32 devices in a mesh: seq: 16 (over z, x, core), fsdp: 2 (over y).
Axes of the slice: x: 2, y: 2, z: 4, core: 2. Of those that a mesh axis runs over, the one named last changes fastest.
Arguments:
- tokens: bfloat16 [8192, 640], P(('seq', 'fsdp')), may hold values from -6 to 6
- positions: int32 [8192], P(('seq', 'fsdp')), may hold values from 0 to 7935, as said below
- cotangent: bfloat16 [8192, 640], P(('seq', 'fsdp')), may hold values from -6 to 6
- in_gain: bfloat16 [640], P('fsdp'), may hold values from 0.25 to 1.75
- w_query: bfloat16 [640, 1024], P('fsdp'), may hold values from -0.25 to 0.25
- w_key: bfloat16 [640, 256], P('fsdp'), may hold values from -0.25 to 0.25
- w_value: bfloat16 [640, 256], P('fsdp'), may hold values from -0.25 to 0.25
- query_gain: bfloat16 [256], P('fsdp'), may hold values from 0.25 to 1.75
- key_gain: bfloat16 [256], P('fsdp'), may hold values from 0.25 to 1.75
- w_out: bfloat16 [1024, 640], P('fsdp'), may hold values from -0.1875 to 0.1875
- attn_gain: bfloat16 [640], P('fsdp'), may hold values from 0.25 to 1.75
- ffn_gain_in: bfloat16 [640], P('fsdp'), may hold values from 0.25 to 1.75
- w_gate: bfloat16 [640, 2048], P('fsdp'), may hold values from -0.25 to 0.25
- w_up: bfloat16 [640, 2048], P('fsdp'), may hold values from -0.25 to 0.25
- w_down: bfloat16 [2048, 640], P('fsdp'), may hold values from -0.125 to 0.125
- ffn_gain_out: bfloat16 [640], P('fsdp'), may hold values from 0.25 to 1.75
Outputs:
- layer_out: bfloat16 [8192, 640], P(('seq', 'fsdp'))
- grad_tokens: float32 [8192, 640], P(('seq', 'fsdp'))
- grad_in_gain: float32 [640], P('fsdp')
- grad_query: float32 [640, 1024], P('fsdp')
- grad_key: float32 [640, 256], P('fsdp')
- grad_value: float32 [640, 256], P('fsdp')
- grad_query_gain: float32 [256], P('fsdp')
- grad_key_gain: float32 [256], P('fsdp')
- grad_w_out: float32 [1024, 640], P('fsdp')
- grad_attn_gain: float32 [640], P('fsdp')
- grad_ffn_gain_in: float32 [640], P('fsdp')
- grad_gate: float32 [640, 2048], P('fsdp')
- grad_up: float32 [640, 2048], P('fsdp')
- grad_down: float32 [2048, 640], P('fsdp')
- grad_ffn_gain_out: float32 [640], P('fsdp')
The draws below stay inside these ranges and needn't reach their ends.
Inputs may be any that keep to these rules, and one draw needn't show every extreme that they name: Sequences lie end to end: one holds 7936 tokens and begins within the first 256 tokens; the others, before and after it, hold 256 tokens together; positions count from 0 in each sequence.
All inputs are finite; a program needn't handle non-finite values.
Results may differ from the reference program's by a relative error of at most 0.017.
Values may be sent and summed in bfloat16 or wider, within the bound.
No kernel may reach another device: no remote copies, remote signals or barrier semaphores. Data moves between devices by JAX's collectives and lax.ppermute only.
A program may use at most 128 MiB of HBM per device.

```python
import math
import jax
import jax.numpy as jnp
from jax import lax

D = 640
HEADS = 4
HEAD_DIM = 256
FF = 2048
WINDOW = 512
TOK_DEV = 256
TOKENS = 8192


def draw_positions(key, part):
    key = jax.random.fold_in(key, 11)
    length_key, start_key = jax.random.split(key)
    first_length = jax.random.randint(length_key, (), 1, TOK_DEV).astype(jnp.int32)
    index_all = jnp.arange(TOKENS, dtype=jnp.int32)
    third_start = first_length + (TOKENS - TOK_DEV)
    random_starts = jax.random.randint(start_key, (TOKENS,), 0, 4) == 0
    outside = (index_all < first_length) | (index_all > third_start)
    is_start = (index_all == 0) | (index_all == first_length) | (index_all == third_start) | outside & random_starts
    start_of = lax.cummax(jnp.where(is_start, index_all, jnp.zeros_like(index_all)), axis=0)
    return (index_all - start_of).astype(jnp.int32)


def levels(key, extent, cuts, low, largest):
    loudness = 1.0
    for position, parts in cuts:
        draws = jax.random.uniform(jax.random.fold_in(jax.random.fold_in(key, 6), position), (parts,), jnp.float32, low / len(cuts), largest / len(cuts))
        loudness = loudness * jnp.repeat(jnp.exp(draws), extent[position] // parts).reshape((-1,) + (1,) * (len(extent) - 1 - position))
    return loudness


def gaussian(stream_key, dims, width, most, cuts=(), kind=jnp.bfloat16):
    values = jax.random.normal(stream_key, dims, jnp.float32) * width
    if len(cuts) > 0:
        values = levels(stream_key, dims, cuts, -0.22, 0.18) * values
    return jnp.clip(values, min=-most, max=most).astype(kind)


def setup_inputs(seed: int = 0) -> dict:
    key_of = jax.random.split(jax.random.key(seed), 17)
    return {
        "tokens": gaussian(key_of[0], (TOKENS, D), 1.0, 6.0, ((0, 32),)),
        "positions": draw_positions(jax.random.fold_in(key_of[16], 71), 0),
        "cotangent": gaussian(key_of[2], (TOKENS, D), 1.0, 6.0, ((0, 32),)),
        "in_gain": jnp.clip(1.0 + 0.15 * jax.random.normal(key_of[3], (D,), jnp.float32), 0.25, 1.75).astype(jnp.bfloat16),
        "w_query": gaussian(key_of[4], (D, HEADS * HEAD_DIM), D ** -0.5, 0.25, ((0, 2),)),
        "w_key": gaussian(key_of[5], (D, HEAD_DIM), D ** -0.5, 0.25, ((0, 2),)),
        "w_value": gaussian(key_of[6], (D, HEAD_DIM), D ** -0.5, 0.25, ((0, 2),)),
        "query_gain": jnp.clip(1.0 + 0.15 * jax.random.normal(key_of[7], (HEAD_DIM,), jnp.float32), 0.25, 1.75).astype(jnp.bfloat16),
        "key_gain": jnp.clip(1.0 + 0.15 * jax.random.normal(key_of[8], (HEAD_DIM,), jnp.float32), 0.25, 1.75).astype(jnp.bfloat16),
        "w_out": gaussian(key_of[9], (HEADS * HEAD_DIM, D), (HEADS * HEAD_DIM) ** -0.5, 0.1875, ((0, 2),)),
        "attn_gain": jnp.clip(1.0 + 0.15 * jax.random.normal(key_of[10], (D,), jnp.float32), 0.25, 1.75).astype(jnp.bfloat16),
        "ffn_gain_in": jnp.clip(1.0 + 0.15 * jax.random.normal(key_of[11], (D,), jnp.float32), 0.25, 1.75).astype(jnp.bfloat16),
        "w_gate": gaussian(key_of[12], (D, FF), D ** -0.5, 0.25, ((0, 2),)),
        "w_up": gaussian(key_of[13], (D, FF), D ** -0.5, 0.25, ((0, 2),)),
        "w_down": gaussian(key_of[14], (FF, D), FF ** -0.5, 0.125, ((0, 2),)),
        "ffn_gain_out": jnp.clip(1.0 + 0.15 * jax.random.normal(key_of[15], (D,), jnp.float32), 0.25, 1.75).astype(jnp.bfloat16),
    }


EPSILON = 1e-06
ROPE_BASE = 10000.0
MASKED = -1e+30

@jax.custom_vjp
def low(v):
    return lax.optimization_barrier(v.astype(jnp.bfloat16)).astype(jnp.float32)

@jax.custom_vjp
def low_back(v):
    return v

def low_keep(v):
    return (low(v), None)

def low_pass(kept, grad):
    return (grad,)

def back_keep(v):
    return (v, None)

def back_low(kept, grad):
    return (low(grad),)
low.defvjp(low_keep, low_pass)
low_back.defvjp(back_keep, back_low)

def norm_scale(values, scales):
    return values * lax.rsqrt(lax.optimization_barrier(jnp.mean(values * values, axis=-1, keepdims=True)) + EPSILON) * scales

def rotate(values, places):
    half_dim = values.shape[-1] // 2
    frequency = ROPE_BASE ** (-(jnp.arange(half_dim, dtype=jnp.float32) * 2.0 / values.shape[-1]))
    angles = places.astype(jnp.float32)[:, None] * frequency[None, :]
    cosine = jnp.cos(angles)[:, None, :]
    sine_part = jnp.sin(angles)[:, None, :]
    first_half = values[..., :half_dim]
    second_half = values[..., half_dim:]
    return jnp.concatenate([first_half * cosine - second_half * sine_part, second_half * cosine + first_half * sine_part], axis=-1)

def gelu_gate(gate_vals, up_vals):
    return jax.nn.gelu(gate_vals, approximate=True) * up_vals

def dot_high(left_side, right_side):
    return jnp.dot(left_side, right_side, precision=lax.Precision.HIGHEST, preferred_element_type=jnp.float32)

def forward(tokens_f, in_gain, w_query, w_key, w_value, query_gain, key_gain, w_out, attn_gain, ffn_gain_in, w_gate, w_up, w_down, ffn_gain_out, positions):
    token_count = tokens_f.shape[0]
    head_dim = w_key.shape[1]
    head_count = w_query.shape[1] // head_dim
    normed = low(norm_scale(tokens_f, in_gain))
    query_raw = low_back(dot_high(normed, w_query)).reshape(token_count, head_count, head_dim)
    queries = low(rotate(norm_scale(query_raw, query_gain), positions))
    key_raw = low_back(dot_high(normed, w_key)).reshape(token_count, 1, head_dim)
    keys_rot = low(rotate(norm_scale(key_raw, key_gain), positions)).reshape(token_count, head_dim)
    valued = low(low_back(dot_high(normed, w_value)))
    padding = jnp.zeros((WINDOW, head_dim), jnp.float32)
    key_pad = jnp.concatenate([padding, keys_rot], axis=0)
    value_pad = jnp.concatenate([padding, valued], axis=0)
    block_rows = math.gcd(token_count, 512)
    block_count = token_count // block_rows
    window_index = jnp.arange(block_count, dtype=jnp.int32)[:, None] * block_rows + jnp.arange(block_rows + WINDOW, dtype=jnp.int32)[None, :]
    key_blocks = key_pad[window_index]
    value_blocks = value_pad[window_index]
    query_blocks = queries.reshape(block_count, block_rows, head_count, head_dim)
    place_blocks = positions.reshape(block_count, block_rows)
    distance = jnp.arange(block_rows, dtype=jnp.int32)[:, None] + WINDOW - jnp.arange(block_rows + WINDOW, dtype=jnp.int32)[None, :]
    score_scale = head_dim ** (-0.5)

    def attend(pieces):
        query_blk, key_blk, value_blk, place_blk = pieces
        allowed = (distance >= 0) & (distance < WINDOW) & (distance <= place_blk[:, None])
        raw_scores = jnp.einsum('qhd,kd->hqk', query_blk, key_blk, precision=lax.Precision.HIGHEST)
        scores = jnp.where(allowed[None], low_back(raw_scores) * score_scale, MASKED)
        attn_probs = low(jax.nn.softmax(scores, axis=-1))
        return jnp.einsum('hqk,kd->qhd', attn_probs, value_blk, precision=lax.Precision.HIGHEST)
    attended = lax.map(jax.checkpoint(attend), (query_blocks, key_blocks, value_blocks, place_blocks))
    attended = low(low_back(attended.reshape(token_count, head_count * head_dim)))

    def finish(pieces):
        attended_blk, tokens_blk = pieces
        projected = low_back(dot_high(attended_blk, w_out))
        residual = tokens_blk + norm_scale(projected, attn_gain)
        ffn_in = low(norm_scale(residual, ffn_gain_in))
        gate_vals = low_back(dot_high(ffn_in, w_gate))
        up_vals = low_back(dot_high(ffn_in, w_up))
        mixed_vals = low(gelu_gate(gate_vals, up_vals))
        down_vals = low_back(dot_high(mixed_vals, w_down))
        return residual + norm_scale(down_vals, ffn_gain_out)
    result = lax.map(jax.checkpoint(finish), (attended.reshape(block_count, block_rows, -1), tokens_f.reshape(block_count, block_rows, -1)))
    return result.reshape(token_count, -1)

def reference(tokens, positions, cotangent, in_gain, w_query, w_key, w_value, query_gain, key_gain, w_out, attn_gain, ffn_gain_in, w_gate, w_up, w_down, ffn_gain_out):
    floats = tuple((source.astype(jnp.float32) for source in (tokens, in_gain, w_query, w_key, w_value, query_gain, key_gain, w_out, attn_gain, ffn_gain_in, w_gate, w_up, w_down, ffn_gain_out)))

    def wrapped(*params):
        return forward(*params, positions)
    result, pullback = jax.vjp(wrapped, *floats)
    gradients = pullback(cotangent.astype(jnp.float32))
    return (result.astype(jnp.bfloat16), gradients[0], gradients[1], gradients[2], gradients[3], gradients[4], gradients[5], gradients[6], gradients[7], gradients[8], gradients[9], gradients[10], gradients[11], gradients[12], gradients[13])
```

```python
import jax
import jax.numpy as jnp
from jax import lax
from jax.sharding import PartitionSpec as P

WINDOW = 512
EPSILON = 1e-06
ROPE_BASE = 10000.0
MASKED = -1e30
LANES = 128
BF16 = jnp.bfloat16
F32 = jnp.float32


def norm_scale(values, scales):
    return values * lax.rsqrt(jnp.mean(values * values, axis=-1, keepdims=True) + EPSILON) * scales


def rotate(values, places):
    half_dim = values.shape[-1] // 2
    frequency = ROPE_BASE ** (-(jnp.arange(half_dim, dtype=F32) * 2.0 / values.shape[-1]))
    angles = places.astype(F32)[:, None] * frequency[None, :]
    cosine = jnp.cos(angles)[:, None, :]
    sine_part = jnp.sin(angles)[:, None, :]
    first_half = values[..., :half_dim]
    second_half = values[..., half_dim:]
    return jnp.concatenate(
        [first_half * cosine - second_half * sine_part, second_half * cosine + first_half * sine_part], axis=-1
    )


def gelu_gate(gate_vals, up_vals):
    return jax.nn.gelu(gate_vals, approximate=True) * up_vals


class Places:
    def __init__(self):
        self.seq = lax.axis_size("seq")
        self.fsdp = lax.axis_size("fsdp")
        self.outer = self.seq // 4
        index = lax.axis_index("seq")
        self.core_at = index % 2
        self.mid_at = (index // 2) % 2
        self.outer_at = index // 4
        self.fsdp_at = lax.axis_index("fsdp")

    def core_swap(self, array):
        return lax.ppermute(array, "seq", [(i, i ^ 1) for i in range(self.seq)])

    def mid_swap(self, array):
        return lax.ppermute(array, "seq", [(i, i ^ 2) for i in range(self.seq)])

    def outer_shift(self, array, by):
        return lax.ppermute(array, "seq", [(i, (i + 4 * by) % self.seq) for i in range(self.seq)])

    def fsdp_shift(self, array, by):
        return lax.ppermute(array, "fsdp", [(i, (i + by) % self.fsdp) for i in range(self.fsdp)])


def pick(array, at):
    return lax.dynamic_index_in_dim(array, at, 0, keepdims=False)


def ordered(pieces, at):
    count = len(pieces)
    if count == 2:
        own, other = pieces
        return jnp.where(at == 0, jnp.stack([own, other]), jnp.stack([other, own]))
    stacked = jnp.stack(pieces)
    return jnp.stack([pick(stacked, (at - j) % count) for j in range(count)])


def gather_rows(here, shard):
    rows = shard.shape[0]
    half_rows = rows // 2
    half = lax.dynamic_slice_in_dim(shard, here.core_at * half_rows, half_rows, 0)
    pieces = [shard]
    for by in range(1, here.fsdp):
        mine = here.fsdp_shift(half, by)
        pieces.append(ordered([mine, here.core_swap(mine)], here.core_at).reshape(shard.shape))
    return ordered(pieces, here.fsdp_at).reshape((here.fsdp * rows,) + shard.shape[1:])


def pack_columns(here, grad):
    rows, columns = grad.shape
    tall, wide = rows // (here.fsdp * here.outer), columns // (4 * LANES)
    cut = grad.astype(BF16).reshape(here.fsdp, here.outer, tall, 2, 2, wide, LANES)
    return cut.transpose(3, 0, 4, 1, 5, 2, 6).reshape(2, here.fsdp, 2, here.outer, wide * tall, LANES)


def unpack_columns(here, packed, rows, columns):
    tall, wide = rows // here.outer, columns // (4 * LANES)
    cut = packed.reshape(2, 2, here.outer, wide, tall, LANES)
    return cut.transpose(2, 4, 0, 1, 3, 5).reshape(rows, columns).astype(F32)


def pack_rows(here, grad):
    rows, columns = grad.shape
    tall, wide = rows // (here.fsdp * here.outer * 4), columns // LANES
    cut = grad.astype(BF16).reshape(here.fsdp, 2, 2, here.outer, tall, wide, LANES)
    return cut.transpose(1, 0, 2, 3, 5, 4, 6).reshape(2, here.fsdp, 2, here.outer, wide * tall, LANES)


def unpack_rows(here, packed, rows, columns):
    tall, wide = rows // (here.outer * 4), columns // LANES
    cut = packed.reshape(2, 2, here.outer, wide, tall, LANES)
    return cut.transpose(0, 1, 2, 4, 3, 5).reshape(rows, columns).astype(F32)


def total(terms):
    out = terms[0].astype(F32)
    for term in terms[1:]:
        out = out + term.astype(F32)
    return out.astype(BF16)


def reduce_chunk(here, packed):
    kept = pick(packed, here.core_at)
    packed = total([kept, here.core_swap(pick(packed, 1 - here.core_at))])
    terms = [pick(packed, here.fsdp_at)]
    for by in range(1, here.fsdp):
        terms.append(here.fsdp_shift(pick(packed, (here.fsdp_at + by) % here.fsdp), by))
    packed = total(terms)
    kept = pick(packed, here.mid_at)
    packed = total([kept, here.mid_swap(pick(packed, 1 - here.mid_at))])
    terms = [pick(packed, here.outer_at)]
    for by in range(1, here.outer):
        terms.append(here.outer_shift(pick(packed, (here.outer_at + by) % here.outer), by))
    own = total(terms)
    packed = ordered([own] + [here.outer_shift(own, by) for by in range(1, here.outer)], here.outer_at)
    packed = ordered([packed, here.mid_swap(packed)], here.mid_at)
    return ordered([packed, here.core_swap(packed)], here.core_at)


def linear_shift(array, by):
    count = lax.axis_size("seq") * lax.axis_size("fsdp")
    return lax.ppermute(array, ("seq", "fsdp"), [(i, i + by) for i in range(count) if 0 <= i + by < count])


def on_device(
    tokens, positions, cotangent, in_gain, w_query, w_key, w_value, query_gain, key_gain, w_out, attn_gain,
    ffn_gain_in, w_gate, w_up, w_down, ffn_gain_out,
):
    here = Places()
    rows = tokens.shape[0]
    head_dim = w_key.shape[1]
    query_cols = w_query.shape[1]
    head_count = query_cols // head_dim
    hops = (WINDOW + rows - 1) // rows
    halo = hops * rows
    gains = (in_gain, query_gain, key_gain, attn_gain, ffn_gain_in, ffn_gain_out)
    cuts = [0]
    for gain in gains:
        cuts.append(cuts[-1] + gain.shape[0])

    qkv_shard = jnp.concatenate([w_query, w_key, w_value], axis=1)
    shard_rows, qkv_cols = qkv_shard.shape
    padded = (shard_rows + 1 + 31) // 32 * 32
    gain_row = jnp.pad(jnp.concatenate(gains), (0, qkv_cols - cuts[-1]))[None]
    first = jnp.concatenate([qkv_shard, jnp.pad(gain_row, ((0, padded - shard_rows - 1), (0, 0)))], axis=0)
    first = gather_rows(here, first).reshape(here.fsdp, padded, qkv_cols)
    full_qkv = first[:, :shard_rows].reshape(-1, qkv_cols)
    gain_rows = first[:, shard_rows].astype(F32)
    gain_in, gain_query, gain_key, gain_attn, gain_ffn_in, gain_ffn_out = (
        gain_rows[:, cuts[i] : cuts[i + 1]].reshape(-1) for i in range(6)
    )
    all_tokens = jnp.concatenate([linear_shift(tokens, by) for by in range(hops, 0, -1)] + [tokens], axis=0)
    full_out = gather_rows(here, w_out)
    full_gate = gather_rows(here, w_gate)
    full_up = gather_rows(here, w_up)
    full_down = gather_rows(here, w_down)

    score_scale = head_dim ** (-0.5)
    tokens_f = tokens.astype(F32)
    all_positions = jnp.concatenate([positions[0] - halo + jnp.arange(halo, dtype=jnp.int32), positions])
    normed_f, pull_in = jax.vjp(norm_scale, all_tokens.astype(F32), gain_in)
    normed_all = normed_f.astype(BF16)
    normed = normed_all[halo:]
    query_raw = jnp.dot(normed, full_qkv[:, :query_cols], preferred_element_type=F32).reshape(
        rows, head_count, head_dim
    )
    kv_raw = jnp.dot(normed_all, full_qkv[:, query_cols:], preferred_element_type=F32)
    key_raw = kv_raw[:, :head_dim].reshape(halo + rows, 1, head_dim)
    values_all = kv_raw[:, head_dim:].astype(BF16)

    queries_f, pull_query = jax.vjp(lambda v, g: rotate(norm_scale(v, g), positions), query_raw, gain_query)
    keys_f, pull_key = jax.vjp(lambda v, g: rotate(norm_scale(v, g), all_positions), key_raw, gain_key)
    queries = queries_f.astype(BF16)
    keys_all = keys_f.reshape(halo + rows, head_dim).astype(BF16)
    distance = jnp.arange(rows)[:, None] + halo - jnp.arange(halo + rows)[None, :]
    allowed = (distance >= 0) & (distance < WINDOW) & (distance <= positions[:, None])
    raw_scores = jnp.einsum("qhd,kd->hqk", queries, keys_all, preferred_element_type=F32)
    scores = jnp.where(allowed[None], raw_scores * score_scale, MASKED)
    top_score = jnp.max(scores, axis=-1, keepdims=True)
    weights = jnp.exp(scores - top_score)
    probs_f = weights / jnp.sum(weights, axis=-1, keepdims=True)
    attn_probs = probs_f.astype(BF16)
    attended = (
        jnp.einsum("hqk,kd->qhd", attn_probs, values_all, preferred_element_type=F32)
        .reshape(rows, query_cols)
        .astype(BF16)
    )
    projected = jnp.dot(attended, full_out, preferred_element_type=F32)
    branch_attn, pull_attn = jax.vjp(norm_scale, projected, gain_attn)
    residual = tokens_f + branch_attn
    ffn_in_f, pull_ffn_in = jax.vjp(norm_scale, residual, gain_ffn_in)
    ffn_in = ffn_in_f.astype(BF16)
    gate_vals = jnp.dot(ffn_in, full_gate, preferred_element_type=F32)
    up_vals = jnp.dot(ffn_in, full_up, preferred_element_type=F32)
    mixed_f, pull_mixed = jax.vjp(gelu_gate, gate_vals, up_vals)
    mixed_vals = mixed_f.astype(BF16)
    down_vals = jnp.dot(mixed_vals, full_down, preferred_element_type=F32)
    branch_ffn, pull_ffn_out = jax.vjp(norm_scale, down_vals, gain_ffn_out)
    layer_out = (residual + branch_ffn).astype(BF16)

    upstream = cotangent.astype(F32)
    d_down_f, grad_ffn_out = pull_ffn_out(upstream)
    d_down = d_down_f.astype(BF16)
    grad_down = jnp.einsum("tf,td->fd", mixed_vals, d_down, preferred_element_type=F32)
    down_chunk = reduce_chunk(here, pack_rows(here, grad_down))
    d_mixed = jnp.einsum("td,fd->tf", d_down, full_down, preferred_element_type=F32)
    d_gate_f, d_up_f = pull_mixed(d_mixed)
    d_gate = d_gate_f.astype(BF16)
    d_up = d_up_f.astype(BF16)
    grad_gate = jnp.einsum("td,tf->df", ffn_in, d_gate, preferred_element_type=F32)
    grad_up = jnp.einsum("td,tf->df", ffn_in, d_up, preferred_element_type=F32)
    gate_chunk = reduce_chunk(
        here, jnp.concatenate([pack_columns(here, grad_gate), pack_columns(here, grad_up)], axis=-2)
    )
    d_ffn_in = jnp.einsum("tf,df->td", d_gate, full_gate, preferred_element_type=F32) + jnp.einsum(
        "tf,df->td", d_up, full_up, preferred_element_type=F32
    )
    d_resid_part, grad_ffn_in = pull_ffn_in(d_ffn_in)
    d_residual = upstream + d_resid_part
    d_proj_f, grad_attn = pull_attn(d_residual)
    d_proj = d_proj_f.astype(BF16)
    grad_out = jnp.einsum("tq,td->qd", attended, d_proj, preferred_element_type=F32)
    d_attended = (
        jnp.einsum("td,qd->tq", d_proj, full_out, preferred_element_type=F32)
        .astype(BF16)
        .reshape(rows, head_count, head_dim)
    )
    d_probs = jnp.einsum("qhd,kd->hqk", d_attended, values_all, preferred_element_type=F32)
    row_terms = jnp.sum(probs_f * d_probs, axis=-1, keepdims=True)
    d_scores = (probs_f * (d_probs - row_terms) * score_scale).astype(BF16)
    d_queries = jnp.einsum("hqk,kd->qhd", d_scores, keys_all, preferred_element_type=F32)
    d_keys = jnp.einsum("hqk,qhd->kd", d_scores, queries, preferred_element_type=F32)
    d_values = jnp.einsum("hqk,qhd->kd", attn_probs, d_attended, preferred_element_type=F32)
    d_query_f, grad_query_gain = pull_query(d_queries)
    d_key_f, grad_key_gain = pull_key(d_keys.reshape(halo + rows, 1, head_dim))
    d_query_raw = d_query_f.reshape(rows, query_cols).astype(BF16)
    d_kv_raw = jnp.concatenate([d_key_f.reshape(halo + rows, head_dim), d_values], axis=1).astype(BF16)
    grad_q = jnp.einsum("td,tq->dq", normed, d_query_raw, preferred_element_type=F32)
    grad_kv = jnp.einsum("td,tq->dq", normed_all, d_kv_raw, preferred_element_type=F32)
    d_normed = jnp.einsum("tq,dq->td", d_kv_raw, full_qkv[:, query_cols:], preferred_element_type=F32)
    d_normed_q = jnp.einsum("tq,dq->td", d_query_raw, full_qkv[:, :query_cols], preferred_element_type=F32)
    d_normed = jnp.concatenate([d_normed[:halo], d_normed[halo:] + d_normed_q], axis=0)
    d_tokens, grad_in = pull_in(d_normed)
    gain_grads = (grad_in, grad_query_gain, grad_key_gain, grad_attn, grad_ffn_in, grad_ffn_out)
    gain_pack = jnp.concatenate([g.reshape(here.fsdp, -1) for g in gain_grads], axis=1)
    gain_piece = cuts[-1] // (4 * here.outer)
    gain_pack = gain_pack.reshape(here.fsdp, 2, 2, here.outer, 1, gain_piece).transpose(1, 0, 2, 3, 4, 5)
    gain_pack = jnp.pad(gain_pack.astype(BF16), ((0, 0),) * 4 + ((0, 15), (0, LANES - gain_piece)))
    out_pack = pack_rows(here, grad_out)
    qkv_pack = pack_columns(here, jnp.concatenate([grad_q, grad_kv], axis=1))
    last_chunk = reduce_chunk(here, jnp.concatenate([out_pack, qkv_pack, gain_pack], axis=-2))

    grad_tokens = d_residual + d_tokens[halo:]
    for by in range(1, hops + 1):
        start = halo - by * rows
        grad_tokens = grad_tokens + linear_shift(d_tokens[start : start + rows].astype(BF16), -by).astype(F32)

    gate_rows = gate_chunk.shape[-2] // 2
    out_rows, qkv_rows = out_pack.shape[-2], qkv_pack.shape[-2]
    total_out = unpack_rows(here, last_chunk[..., :out_rows, :], *w_out.shape)
    total_qkv = unpack_columns(here, last_chunk[..., out_rows : out_rows + qkv_rows, :], shard_rows, qkv_cols)
    total_gains = last_chunk[..., out_rows + qkv_rows, :gain_piece].reshape(-1).astype(F32)
    g = [total_gains[cuts[i] : cuts[i + 1]] for i in range(6)]
    return (
        layer_out,
        grad_tokens,
        g[0],
        total_qkv[:, :query_cols],
        total_qkv[:, query_cols : query_cols + head_dim],
        total_qkv[:, query_cols + head_dim :],
        g[1],
        g[2],
        total_out,
        g[3],
        g[4],
        unpack_columns(here, gate_chunk[..., :gate_rows, :], *w_gate.shape),
        unpack_columns(here, gate_chunk[..., gate_rows:, :], *w_up.shape),
        unpack_rows(here, down_chunk, *w_down.shape),
        g[5],
    )


def solution(mesh):
    tok = P(("seq", "fsdp"), None)
    mat = P("fsdp", None)
    vec = P("fsdp")
    return jax.shard_map(
        on_device,
        mesh=mesh,
        in_specs=(
            tok, P(("seq", "fsdp")), tok, vec, mat, mat, mat, vec, vec, mat, vec, vec, mat, mat, mat, vec,
        ),
        out_specs=(tok, tok, vec, mat, mat, mat, vec, vec, mat, vec, vec, mat, mat, mat, vec),
        check_vma=False,
    )
```

```python
import functools
import math

import jax
import jax.numpy as jnp
from jax import lax
from jax.experimental import pallas as pl
from jax.experimental.pallas import tpu as pltpu
from jax.sharding import PartitionSpec as P

WINDOW = 512
EPSILON = 1e-06
ROPE_BASE = 10000.0
MASKED = -1e30
BF16 = jnp.bfloat16
F32 = jnp.float32
QBLOCK = 128
GELU_A = math.sqrt(2.0 / math.pi)
GELU_B = 0.044715

VMEM = pl.BlockSpec(memory_space=pltpu.VMEM)
SMEM = pl.BlockSpec(memory_space=pltpu.SMEM)
ANY = pl.BlockSpec(memory_space=pl.ANY)


class Places:
    def __init__(self):
        self.seq = lax.axis_size("seq")
        self.fsdp = lax.axis_size("fsdp")
        self.outer = self.seq // 4
        index = lax.axis_index("seq")
        self.core_at = index % 2
        self.mid_at = (index // 2) % 2
        self.outer_at = index // 4
        self.fsdp_at = lax.axis_index("fsdp")
        self.vector = jnp.stack([self.core_at, self.mid_at, self.fsdp_at]).astype(jnp.int32)

    def core_swap(self, array):
        return lax.ppermute(array, "seq", [(i, i ^ 1) for i in range(self.seq)])

    def mid_swap(self, array):
        return lax.ppermute(array, "seq", [(i, i ^ 2) for i in range(self.seq)])

    def outer_shift(self, array, by):
        return lax.ppermute(array, "seq", [(i, (i + 4 * by) % self.seq) for i in range(self.seq)])

    def fsdp_shift(self, array, by):
        return lax.ppermute(array, "fsdp", [(i, (i + by) % self.fsdp) for i in range(self.fsdp)])


def linear_shift(array, by):
    count = lax.axis_size("seq") * lax.axis_size("fsdp")
    return lax.ppermute(array, ("seq", "fsdp"), [(i, i + by) for i in range(count) if 0 <= i + by < count])


def pick(array, at):
    return lax.dynamic_index_in_dim(array, at, 0, keepdims=False)


def ordered(pieces, at):
    count = len(pieces)
    if count == 2:
        own, other = pieces
        return jnp.where(at == 0, jnp.stack([own, other]), jnp.stack([other, own]))
    stacked = jnp.stack(pieces)
    return jnp.stack([pick(stacked, (at - j) % count) for j in range(count)])


def fetch(here, shard, axis):
    half = shard.shape[axis] // 2
    part = lax.dynamic_slice_in_dim(shard, here.core_at * half, half, axis)
    pieces = [shard]
    for by in range(1, here.fsdp):
        mine = here.fsdp_shift(part, by)
        pieces += [mine, here.core_swap(mine)]
    return pieces


def multiple(value, of):
    return pl.multiple_of(value, of)


def place_copies(pieces, whole, sems, at, axis):
    core, fsdp = at[0], at[2]
    count = (len(pieces) + 1) // 2
    rows, columns = pieces[0].shape
    copies = []
    for k, piece in enumerate(pieces):
        by = (k + 1) // 2
        row = multiple(lax.rem(fsdp + (count - by), count) * rows, 16)
        if k == 0:
            target = whole.at[pl.ds(row, rows), :]
        else:
            half = core if k % 2 == 1 else 1 - core
            if axis == 0:
                target = whole.at[pl.ds(multiple(row + half * (rows // 2), 16), rows // 2), :]
            else:
                target = whole.at[pl.ds(row, rows), pl.ds(multiple(half * (columns // 2), 128), columns // 2)]
        copies.append(pltpu.make_async_copy(piece, target, sems.at[k]))
    return copies


def dot(a, b):
    return lax.dot_general(a, b, (((1,), (0,)), ((), ())), preferred_element_type=F32)


def dot_nt(a, b):
    return lax.dot_general(a, b, (((1,), (1,)), ((), ())), preferred_element_type=F32)


def dot_tn(a, b):
    return lax.dot_general(a, b, (((0,), (0,)), ((), ())), preferred_element_type=F32)


def inverse_rms(u):
    return lax.rsqrt(jnp.mean(u * u, axis=-1, keepdims=True) + EPSILON)


def norm_back(u, g, dz):
    r = inverse_rms(u)
    ur = u * r
    gdz = g * dz
    du = r * (gdz - ur * jnp.mean(gdz * ur, axis=-1, keepdims=True))
    return du, jnp.sum(dz * ur, axis=0, keepdims=True)


def params(megabytes=56):
    return pltpu.CompilerParams(vmem_limit_bytes=megabytes * 1024 * 1024)


def cost(flops, bytes_accessed):
    return pl.CostEstimate(flops=int(flops), bytes_accessed=int(bytes_accessed), transcendentals=0)


def shape(dims, kind):
    return jax.ShapeDtypeStruct(tuple(dims), kind)


def attend_kernel(n_tok, n_qkv, heads, *refs):
    at = refs[0]
    toks = refs[1 : 1 + n_tok]
    pos, cosine, sine, gain_in, gain_q, gain_k = refs[1 + n_tok : 7 + n_tok]
    qkv = refs[7 + n_tok : 7 + n_tok + n_qkv]
    normed, q_raw, k_raw, q_st, keys, values, probs, attended, w_full, sems = refs[7 + n_tok + n_qkv :]
    copies = place_copies(qkv, w_full, sems, at, 1)
    for copy in copies:
        copy.start()
    rows = toks[0].shape[0]
    dim = keys.shape[1]
    half = dim // 2
    halo = (n_tok - 1) * rows
    gain = gain_in[...]
    for i, tok in enumerate(toks):
        u = tok[...].astype(F32)
        normed[i * rows : (i + 1) * rows, :] = (u * inverse_rms(u) * gain).astype(BF16)
    for copy in copies:
        copy.wait()

    def turned(u, g, cos, sin):
        u = u * inverse_rms(u) * g
        first, second = u[:, :half], u[:, half:]
        return (first * cos - second * sin).astype(BF16), (second * cos + first * sin).astype(BF16)

    for i in range(n_tok):
        here = slice(i * rows, (i + 1) * rows)
        kv = dot(normed[here, :], w_full[:, heads * dim :])
        k_raw[here, :] = kv[:, :dim]
        values[here, :] = kv[:, dim:].astype(BF16)
        first, second = turned(kv[:, :dim], gain_k[...], cosine[here, :], sine[here, :])
        keys[here, :half] = first
        keys[here, half:] = second
    blocks = rows // QBLOCK
    for h in range(heads):
        u = dot(normed[halo:, :], w_full[:, h * dim : (h + 1) * dim])
        q_raw[:, h * dim : (h + 1) * dim] = u
        first, second = turned(u, gain_q[...], cosine[halo:, :], sine[halo:, :])
        for b in range(blocks):
            start = (b * heads + h) * QBLOCK
            q_st[start : start + QBLOCK, :half] = first[b * QBLOCK : (b + 1) * QBLOCK, :]
            q_st[start : start + QBLOCK, half:] = second[b * QBLOCK : (b + 1) * QBLOCK, :]
    span = WINDOW + QBLOCK
    distance = (
        lax.broadcasted_iota(jnp.int32, (QBLOCK, span), 0)
        + WINDOW
        - lax.broadcasted_iota(jnp.int32, (QBLOCK, span), 1)
    )
    scale = dim ** (-0.5)
    for b in range(blocks):
        first_key = halo - WINDOW + b * QBLOCK
        limit = jnp.minimum(pos[b * QBLOCK : (b + 1) * QBLOCK, :], WINDOW - 1)
        allowed = (distance >= 0) & (distance <= limit)
        for h in range(heads):
            start = (b * heads + h) * QBLOCK
            scores = dot_nt(q_st[start : start + QBLOCK, :], keys[first_key : first_key + span, :]) * scale
            scores = jnp.where(allowed, scores, MASKED)
            weights = jnp.exp(scores - jnp.max(scores, axis=-1, keepdims=True))
            weights = (weights * (1.0 / jnp.sum(weights, axis=-1, keepdims=True))).astype(BF16)
            probs[start : start + QBLOCK, :] = weights
            attended[b * QBLOCK : (b + 1) * QBLOCK, h * dim : (h + 1) * dim] = dot(
                weights, values[first_key : first_key + span, :]
            ).astype(BF16)


def gate_kernel(n_out, n_gate, n_up, *refs):
    at, attended, tokens, gain_attn, gain_ffn = refs[:5]
    refs = refs[5:]
    out_w, gate_w, up_w, refs = (
        refs[:n_out],
        refs[n_out : n_out + n_gate],
        refs[n_out + n_gate : n_out + n_gate + n_up],
        refs[n_out + n_gate + n_up :],
    )
    projected_ref, residual_ref, ffn_in_ref, mixed, gelu_out, gate_slope = refs[:6]
    out_full, gate_full, up_full, out_sems, gate_sems, up_sems = refs[6:]
    groups = (
        place_copies(out_w, out_full, out_sems, at, 0),
        place_copies(gate_w, gate_full, gate_sems, at, 1),
        place_copies(up_w, up_full, up_sems, at, 1),
    )
    for group in groups:
        for copy in group:
            copy.start()
    for copy in groups[0]:
        copy.wait()
    projected = dot(attended[...], out_full[...])
    projected_ref[...] = projected
    residual = tokens[...].astype(F32) + projected * inverse_rms(projected) * gain_attn[...]
    residual_ref[...] = residual
    ffn_in_ref[...] = (residual * inverse_rms(residual) * gain_ffn[...]).astype(BF16)
    for group in groups[1:]:
        for copy in group:
            copy.wait()
    width = 256

    def step(i, _):
        cut = pl.ds(multiple(i * width, width), width)
        gate = dot(ffn_in_ref[...], gate_full[:, cut])
        up = dot(ffn_in_ref[...], up_full[:, cut])
        square = gate * gate
        t = jnp.tanh(GELU_A * gate * (1.0 + GELU_B * square))
        cdf = 0.5 * (1.0 + t)
        act = gate * cdf
        slope = cdf + 0.5 * gate * (1.0 - t * t) * (GELU_A * (1.0 + 3.0 * GELU_B * square))
        mixed[:, cut] = (act * up).astype(BF16)
        gelu_out[:, cut] = act.astype(BF16)
        gate_slope[:, cut] = (up * slope).astype(BF16)
        return 0

    lax.fori_loop(0, gate_full.shape[1] // width, step, 0)


def relative_blocks(at, fsdp):
    for c in range(2):
        core = c + at[0] - 2 * c * at[0]
        for f in range(fsdp):
            row = lax.rem(at[2] + f, fsdp)
            for x in range(2):
                mid = x + at[1] - 2 * x * at[1]
                yield c, f, x, core, row, mid


def down_kernel(n_down, fsdp, *refs):
    at, mixed, residual, cotangent, gain_out = refs[:5]
    down_w = refs[5 : 5 + n_down]
    layer_out, d_down, grad_gain, keep, send = refs[5 + n_down : 10 + n_down]
    down_full, mixed_t, sems = refs[10 + n_down :]
    copies = place_copies(down_w, down_full, sems, at, 0)
    for copy in copies:
        copy.start()
    mixed_t[...] = mixed[...].T
    for copy in copies:
        copy.wait()
    down = dot(mixed[...], down_full[...])
    r = inverse_rms(down)
    gain = gain_out[...]
    layer_out[...] = (residual[...] + down * r * gain).astype(BF16)
    du, dg = norm_back(down, gain, cotangent[...].astype(F32))
    grad_gain[...] = dg
    d_down[...] = du.astype(BF16)
    block = keep.shape[2]
    for c, f, x, core, row, mid in relative_blocks(at, fsdp):
        start = multiple(((row * 2 + core) * 2 + mid) * block, 16)
        target = keep if c == 0 else send
        target[f, x] = dot(mixed_t[pl.ds(start, block), :], d_down[...]).astype(BF16)


def gate_back_kernel(n_down, fsdp, *refs):
    at, d_down, gelu_out, gate_slope, ffn_in = refs[:5]
    down_w = refs[5 : 5 + n_down]
    d_gate, d_up, keep, send = refs[5 + n_down : 9 + n_down]
    down_full, ffn_t, sems = refs[9 + n_down :]
    copies = place_copies(down_w, down_full, sems, at, 0)
    for copy in copies:
        copy.start()
    ffn_t[...] = ffn_in[...].T
    for copy in copies:
        copy.wait()
    width = 256

    def step(i, _):
        cut = pl.ds(multiple(i * width, width), width)
        d_mixed = dot_nt(d_down[...], down_full[cut, :])
        d_gate[:, cut] = (d_mixed * gate_slope[:, cut].astype(F32)).astype(BF16)
        d_up[:, cut] = (d_mixed * gelu_out[:, cut].astype(F32)).astype(BF16)
        return 0

    lax.fori_loop(0, d_gate.shape[1] // width, step, 0)
    tall, wide = keep.shape[2] // 2, keep.shape[3]
    for c, f, x, core, row, mid in relative_blocks(at, fsdp):
        cut = pl.ds(multiple((core * 2 + mid) * wide, 128), wide)
        left = ffn_t[pl.ds(multiple(row * tall, 16), tall), :]
        target = keep if c == 0 else send
        target[f, x, :tall, :] = dot(left, d_gate[:, cut]).astype(BF16)
        target[f, x, tall:, :] = dot(left, d_up[:, cut]).astype(BF16)


def last_kernel(n_out, n_gate, n_up, n_qkv, n_tok, fsdp, heads, *refs):
    (
        at, d_gate, d_up, residual, projected, cotangent, gain_ffn, gain_attn, attended,
        q_raw, k_raw, q_st, keys, values, probs, cosine, sine, gain_q, gain_k, gain_in, normed,
    ) = refs[:21]
    toks = refs[21 : 21 + n_tok]
    refs = refs[21 + n_tok :]
    out_w, gate_w, up_w, qkv_w, refs = (
        refs[:n_out],
        refs[n_out : n_out + n_gate],
        refs[n_out + n_gate : n_out + n_gate + n_up],
        refs[n_out + n_gate + n_up : n_out + n_gate + n_up + n_qkv],
        refs[n_out + n_gate + n_up + n_qkv :],
    )
    grad_tokens, d_halo, g_ffn, g_attn, g_q, g_k, g_in, keep, send = refs[:9]
    (
        out_full, gate_full, up_full, w_full, att_t, normed_t, d_att, d_scores, d_q, d_k, d_v, d_qkv,
        out_sems, gate_sems, up_sems, qkv_sems,
    ) = refs[9:]
    groups = (
        place_copies(gate_w, gate_full, gate_sems, at, 1),
        place_copies(up_w, up_full, up_sems, at, 1),
        place_copies(out_w, out_full, out_sems, at, 0),
        place_copies(qkv_w, w_full, qkv_sems, at, 1),
    )
    for group in groups:
        for copy in group:
            copy.start()
    att_t[...] = attended[...].T
    normed_t[...] = normed[...].T
    for copy in groups[0] + groups[1]:
        copy.wait()
    d_ffn_in = dot_nt(d_gate[...], gate_full[...]) + dot_nt(d_up[...], up_full[...])
    du, dg = norm_back(residual[...], gain_ffn[...], d_ffn_in)
    g_ffn[...] = dg
    d_residual = cotangent[...].astype(F32) + du
    grad_tokens[...] = d_residual
    du, dg = norm_back(projected[...], gain_attn[...], d_residual)
    g_attn[...] = dg
    d_proj = du.astype(BF16)
    rows = toks[0].shape[0]
    halo = (n_tok - 1) * rows
    dim = keys.shape[1]
    half = dim // 2
    blocks = rows // QBLOCK
    span = WINDOW + QBLOCK
    for copy in groups[2]:
        copy.wait()
    for h in range(heads):
        part = dot_nt(d_proj, out_full[h * dim : (h + 1) * dim, :]).astype(BF16)
        for b in range(blocks):
            start = (b * heads + h) * QBLOCK
            d_att[start : start + QBLOCK, :] = part[b * QBLOCK : (b + 1) * QBLOCK, :]
    out_block = att_t.shape[0] // (4 * fsdp)
    tall, wide = normed_t.shape[0] // fsdp, keep.shape[3]
    columns = d_proj.shape[1]
    for c, f, x, core, row, mid in relative_blocks(at, fsdp):
        start = multiple(((row * 2 + core) * 2 + mid) * out_block, 16)
        part = dot(att_t[pl.ds(start, out_block), :], d_proj).astype(BF16)
        target = keep if c == 0 else send
        target[f, x, tall : tall + out_block, :] = part[:, :wide]
        target[f, x, tall + out_block :, : columns - wide] = part[:, wide:]
        target[f, x, tall + out_block :, columns - wide :] = jnp.zeros((out_block, 2 * wide - columns), BF16)
    scale = dim ** (-0.5)
    d_k[...] = jnp.zeros(d_k.shape, F32)
    d_v[...] = jnp.zeros(d_v.shape, F32)
    for b in range(blocks):
        first_key = halo - WINDOW + b * QBLOCK
        here = slice(first_key, first_key + span)
        for h in range(heads):
            start = (b * heads + h) * QBLOCK
            stack = slice(start, start + QBLOCK)
            d_probs = dot_nt(d_att[stack, :], values[here, :])
            p = probs[stack, :].astype(F32)
            row_terms = jnp.sum(p * d_probs, axis=-1, keepdims=True)
            ds = (p * (d_probs - row_terms) * scale).astype(BF16)
            d_scores[h * QBLOCK : (h + 1) * QBLOCK, :] = ds
            d_q[b * QBLOCK : (b + 1) * QBLOCK, h * dim : (h + 1) * dim] = dot(ds, keys[here, :])
        stack = slice(b * heads * QBLOCK, (b + 1) * heads * QBLOCK)
        d_k[here, :] += dot_tn(d_scores[...], q_st[stack, :])
        d_v[here, :] += dot_tn(probs[stack, :], d_att[stack, :])

    def turned_back(u, g, dz, cos, sin):
        first, second = dz[:, :half], dz[:, half:]
        dz = jnp.concatenate([first * cos + second * sin, second * cos - first * sin], axis=1)
        return norm_back(u, g, dz)

    total_q = jnp.zeros((1, dim), F32)
    if halo:
        d_qkv[:halo, : heads * dim] = jnp.zeros((halo, heads * dim), BF16)
    for h in range(heads):
        cut = slice(h * dim, (h + 1) * dim)
        du, dg = turned_back(q_raw[:, cut], gain_q[...], d_q[:, cut], cosine[halo:, :], sine[halo:, :])
        total_q += dg
        d_qkv[halo:, cut] = du.astype(BF16)
    g_q[...] = total_q
    total_k = jnp.zeros((1, dim), F32)
    for i in range(n_tok):
        here = slice(i * rows, (i + 1) * rows)
        du, dg = turned_back(k_raw[here, :], gain_k[...], d_k[here, :], cosine[here, :], sine[here, :])
        total_k += dg
        d_qkv[here, heads * dim : (heads + 1) * dim] = du.astype(BF16)
        d_qkv[here, (heads + 1) * dim :] = d_v[here, :].astype(BF16)
    g_k[...] = total_k
    for c, f, x, core, row, mid in relative_blocks(at, fsdp):
        cut = pl.ds(multiple((core * 2 + mid) * wide, 128), wide)
        left = normed_t[pl.ds(multiple(row * tall, 16), tall), :]
        target = keep if c == 0 else send
        target[f, x, :tall, :] = dot(left, d_qkv[:, cut]).astype(BF16)
    for copy in groups[3]:
        copy.wait()
    total_in = jnp.zeros(g_in.shape, F32)
    for i in range(n_tok):
        here = slice(i * rows, (i + 1) * rows)
        if i < n_tok - 1:
            d_normed = dot_nt(d_qkv[here, heads * dim :], w_full[:, heads * dim :])
        else:
            d_normed = dot_nt(d_qkv[here, :], w_full[...])
        du, dg = norm_back(toks[i][...].astype(F32), gain_in[...], d_normed)
        total_in += dg
        if i < n_tok - 1:
            d_halo[here, :] = du.astype(BF16)
        else:
            grad_tokens[...] += du
    g_in[...] = total_in


def add(*terms):
    out = terms[0].astype(F32)
    for term in terms[1:]:
        out = out + term.astype(F32)
    return out


def reduce_chunk(here, keep, send):
    other = here.core_swap(send)
    n, w = keep.shape[2:]
    arrived = []
    for by in range(1, here.fsdp):
        arrived.append(here.fsdp_shift(add(keep[by], other[by]).astype(BF16), by))
    across = here.mid_swap(add(keep[0, 1], other[0, 1], *[a[1] for a in arrived]).astype(BF16))
    mine = add(keep[0, 0], other[0, 0], *[a[0] for a in arrived], across).astype(BF16)
    mine = mine.reshape(here.outer, n // here.outer, w)
    terms = [pick(mine, here.outer_at)]
    for by in range(1, here.outer):
        terms.append(here.outer_shift(pick(mine, (here.outer_at + by) % here.outer), by))
    own = add(*terms).astype(BF16)
    block = ordered([own] + [here.outer_shift(own, by) for by in range(1, here.outer)], here.outer_at).reshape(n, w)
    across = here.mid_swap(block)
    return [[block, across], [here.core_swap(block), here.core_swap(across)]]


def by_place(here, blocks):
    own = [jnp.where(here.mid_at == 0, a, b) for a, b in blocks]
    other = [jnp.where(here.mid_at == 0, b, a) for a, b in blocks]
    pairs = list(zip(own, other))
    first = [jnp.where(here.core_at == 0, a, b) for a, b in zip(pairs[0], pairs[1])]
    second = [jnp.where(here.core_at == 0, b, a) for a, b in zip(pairs[0], pairs[1])]
    return first + second


def on_device(
    tokens, positions, cotangent, in_gain, w_query, w_key, w_value, query_gain, key_gain, w_out, attn_gain,
    ffn_gain_in, w_gate, w_up, w_down, ffn_gain_out,
):
    here = Places()
    fsdp = here.fsdp
    rows, width = tokens.shape
    dim = w_key.shape[1]
    query_cols = w_query.shape[1]
    heads = query_cols // dim
    hidden = w_gate.shape[1]
    hops = (WINDOW + rows - 1) // rows
    n_tok = hops + 1
    halo = hops * rows
    every = halo + rows
    at = here.vector

    gains = (in_gain, query_gain, key_gain, attn_gain, ffn_gain_in, ffn_gain_out)
    cuts = [0]
    for gain in gains:
        cuts.append(cuts[-1] + gain.shape[0])
    gain_row = jnp.concatenate(gains)
    qkv_w = fetch(here, jnp.concatenate([w_query, w_key, w_value], axis=1), 1)
    gain_rows = ordered([gain_row] + [here.fsdp_shift(gain_row, by) for by in range(1, fsdp)], here.fsdp_at)
    gain_rows = gain_rows.astype(F32)
    gain_in, gain_q, gain_k, gain_attn, gain_ffn, gain_out = (
        gain_rows[:, cuts[i] : cuts[i + 1]].reshape(1, -1) for i in range(6)
    )
    toks = [linear_shift(tokens, by) for by in range(hops, 0, -1)] + [tokens]
    out_w = fetch(here, w_out, 0)
    gate_w = fetch(here, w_gate, 1)
    up_w = fetch(here, w_up, 1)
    down_w = fetch(here, w_down, 0)

    all_positions = jnp.concatenate([positions[0] - halo + jnp.arange(halo, dtype=jnp.int32), positions])
    frequency = ROPE_BASE ** (-(jnp.arange(dim // 2, dtype=F32) * 2.0 / dim))
    angles = all_positions.astype(F32)[:, None] * frequency[None, :]
    cosine, sine = jnp.cos(angles), jnp.sin(angles)

    span = WINDOW + QBLOCK
    weight_bytes = 2 * fsdp * w_gate.size
    normed, q_raw, k_raw, q_st, keys, values, probs, attended = pl.pallas_call(
        functools.partial(attend_kernel, n_tok, len(qkv_w), heads),
        out_shape=(
            shape((every, width), BF16),
            shape((rows, query_cols), F32),
            shape((every, dim), F32),
            shape((heads * rows, dim), BF16),
            shape((every, dim), BF16),
            shape((every, dim), BF16),
            shape((heads * rows, span), BF16),
            shape((rows, query_cols), BF16),
        ),
        in_specs=[SMEM] + [VMEM] * (n_tok + 6) + [ANY] * len(qkv_w),
        out_specs=(VMEM,) * 8,
        scratch_shapes=[
            pltpu.VMEM((width, query_cols + 2 * dim), BF16),
            pltpu.SemaphoreType.DMA((len(qkv_w),)),
        ],
        compiler_params=params(),
        cost_estimate=cost(4e9, 1e7),
        name="attend",
    )(at, *toks, positions[:, None], cosine, sine, gain_in, gain_q, gain_k, *qkv_w)

    projected, residual, ffn_in, mixed, gelu_out, gate_slope = pl.pallas_call(
        functools.partial(gate_kernel, len(out_w), len(gate_w), len(up_w)),
        out_shape=(
            shape((rows, width), F32),
            shape((rows, width), F32),
            shape((rows, width), BF16),
            shape((rows, hidden), BF16),
            shape((rows, hidden), BF16),
            shape((rows, hidden), BF16),
        ),
        in_specs=[SMEM] + [VMEM] * 4 + [ANY] * (len(out_w) + len(gate_w) + len(up_w)),
        out_specs=(VMEM,) * 6,
        scratch_shapes=[
            pltpu.VMEM((query_cols, width), BF16),
            pltpu.VMEM((width, hidden), BF16),
            pltpu.VMEM((width, hidden), BF16),
            pltpu.SemaphoreType.DMA((len(out_w),)),
            pltpu.SemaphoreType.DMA((len(gate_w),)),
            pltpu.SemaphoreType.DMA((len(up_w),)),
        ],
        compiler_params=params(),
        cost_estimate=cost(4e9, 2 * weight_bytes),
        name="gate",
    )(at, attended, tokens, gain_attn, gain_ffn, *out_w, *gate_w, *up_w)

    down_block = w_down.shape[0] // 4
    down_shape = shape((fsdp, 2, down_block, width), BF16)
    layer_out, d_down, g_ffn_out, down_keep, down_send = pl.pallas_call(
        functools.partial(down_kernel, len(down_w), fsdp),
        out_shape=(
            shape((rows, width), BF16),
            shape((rows, width), BF16),
            shape((1, width), F32),
            down_shape,
            down_shape,
        ),
        in_specs=[SMEM] + [VMEM] * 4 + [ANY] * len(down_w),
        out_specs=(VMEM,) * 5,
        scratch_shapes=[
            pltpu.VMEM((hidden, width), BF16),
            pltpu.VMEM((hidden, rows), BF16),
            pltpu.SemaphoreType.DMA((len(down_w),)),
        ],
        compiler_params=params(),
        cost_estimate=cost(4e9, 2 * weight_bytes),
        name="down",
    )(at, mixed, residual, cotangent, gain_out, *down_w)

    gate_shape = shape((fsdp, 2, 2 * w_gate.shape[0], hidden // 4), BF16)
    d_gate, d_up, gate_keep, gate_send = pl.pallas_call(
        functools.partial(gate_back_kernel, len(down_w), fsdp),
        out_shape=(
            shape((rows, hidden), BF16),
            shape((rows, hidden), BF16),
            gate_shape,
            gate_shape,
        ),
        in_specs=[SMEM] + [VMEM] * 4 + [ANY] * len(down_w),
        out_specs=(VMEM,) * 4,
        scratch_shapes=[
            pltpu.VMEM((hidden, width), BF16),
            pltpu.VMEM((width, rows), BF16),
            pltpu.SemaphoreType.DMA((len(down_w),)),
        ],
        compiler_params=params(),
        cost_estimate=cost(6e9, 3 * weight_bytes),
        name="gate_back",
    )(at, d_down, gelu_out, gate_slope, ffn_in, *down_w)

    qkv_cols = query_cols + 2 * dim
    last_wide = qkv_cols // 4
    shard_rows = w_query.shape[0]
    out_block = w_out.shape[0] // 4
    last_shape = shape((fsdp, 2, shard_rows + 2 * out_block, last_wide), BF16)
    grad_tokens, d_halo, g_ffn, g_attn, g_q, g_k, g_in, last_keep, last_send = pl.pallas_call(
        functools.partial(
            last_kernel, len(out_w), len(gate_w), len(up_w), len(qkv_w), n_tok, fsdp, heads
        ),
        out_shape=(
            shape((rows, width), F32),
            shape((halo, width), BF16),
            shape((1, width), F32),
            shape((1, width), F32),
            shape((1, dim), F32),
            shape((1, dim), F32),
            shape((1, width), F32),
            last_shape,
            last_shape,
        ),
        in_specs=[SMEM]
        + [VMEM] * (20 + n_tok)
        + [ANY] * (len(out_w) + len(gate_w) + len(up_w) + len(qkv_w)),
        out_specs=(VMEM,) * 9,
        scratch_shapes=[
            pltpu.VMEM((query_cols, width), BF16),
            pltpu.VMEM((width, hidden), BF16),
            pltpu.VMEM((width, hidden), BF16),
            pltpu.VMEM((width, qkv_cols), BF16),
            pltpu.VMEM((query_cols, rows), BF16),
            pltpu.VMEM((width, every), BF16),
            pltpu.VMEM((heads * rows, dim), BF16),
            pltpu.VMEM((heads * QBLOCK, span), BF16),
            pltpu.VMEM((rows, query_cols), F32),
            pltpu.VMEM((every, dim), F32),
            pltpu.VMEM((every, dim), F32),
            pltpu.VMEM((every, qkv_cols), BF16),
            pltpu.SemaphoreType.DMA((len(out_w),)),
            pltpu.SemaphoreType.DMA((len(gate_w),)),
            pltpu.SemaphoreType.DMA((len(up_w),)),
            pltpu.SemaphoreType.DMA((len(qkv_w),)),
        ],
        compiler_params=params(),
        cost_estimate=cost(15e9, 4 * weight_bytes),
        name="last",
    )(
        at, d_gate, d_up, residual, projected, cotangent, gain_ffn, gain_attn, attended,
        q_raw, k_raw, q_st, keys, values, probs, cosine, sine, gain_q, gain_k, gain_in, normed,
        *toks, *out_w, *gate_w, *up_w, *qkv_w,
    )

    gain_grads = (g_in, g_q, g_k, g_attn, g_ffn, g_ffn_out)
    packed = jnp.concatenate([g.reshape(fsdp, -1) for g in gain_grads], axis=1).astype(BF16)
    corner = 2 * last_wide - width
    per_block = cuts[-1] // 4
    deep = -(-per_block // corner)
    packed = jnp.pad(packed.reshape(fsdp, 4, per_block), ((0, 0), (0, 0), (0, deep * corner - per_block)))
    packed = packed.reshape(fsdp, 2, 2, deep, corner)
    packed = jnp.stack([pick(packed, (here.fsdp_at + f) % fsdp) for f in range(fsdp)])
    packed = jnp.where(here.mid_at == 0, packed, packed[:, :, ::-1])
    corner_at = (0, 0, shard_rows + out_block, width - last_wide)
    last_keep = lax.dynamic_update_slice(last_keep, jnp.where(here.core_at == 0, packed[:, 0], packed[:, 1]), corner_at)
    last_send = lax.dynamic_update_slice(last_send, jnp.where(here.core_at == 0, packed[:, 1], packed[:, 0]), corner_at)

    down_blocks = by_place(here, reduce_chunk(here, down_keep, down_send))
    gate_blocks = by_place(here, reduce_chunk(here, gate_keep, gate_send))
    last_blocks = by_place(here, reduce_chunk(here, last_keep, last_send))

    for by in range(1, hops + 1):
        start = halo - by * rows
        grad_tokens = grad_tokens + linear_shift(d_halo[start : start + rows], -by).astype(F32)

    total_down = jnp.concatenate(down_blocks, axis=0).astype(F32)
    total_gate = jnp.concatenate([b[:shard_rows] for b in gate_blocks], axis=1).astype(F32)
    total_up = jnp.concatenate([b[shard_rows:] for b in gate_blocks], axis=1).astype(F32)
    total_qkv = jnp.concatenate([b[:shard_rows] for b in last_blocks], axis=1).astype(F32)
    middle = shard_rows + out_block
    total_out = jnp.concatenate(
        [jnp.concatenate([b[shard_rows:middle], b[middle:, : width - last_wide]], axis=1) for b in last_blocks],
        axis=0,
    ).astype(F32)
    total_gains = jnp.concatenate(
        [b[middle : middle + deep, width - last_wide :].reshape(-1)[:per_block] for b in last_blocks]
    ).astype(F32)
    g = [total_gains[cuts[i] : cuts[i + 1]] for i in range(6)]
    return (
        layer_out, grad_tokens, g[0],
        total_qkv[:, :query_cols],
        total_qkv[:, query_cols : query_cols + dim],
        total_qkv[:, query_cols + dim :],
        g[1], g[2], total_out, g[3], g[4], total_gate, total_up, total_down, g[5],
    )


def solution(mesh):
    tok = P(("seq", "fsdp"), None)
    mat = P("fsdp", None)
    vec = P("fsdp")
    return jax.shard_map(
        on_device,
        mesh=mesh,
        in_specs=(tok, P(("seq", "fsdp")), tok, vec, mat, mat, mat, vec, vec, mat, vec, vec, mat, mat, mat, vec),
        out_specs=(tok, tok, vec, mat, mat, mat, vec, vec, mat, vec, vec, mat, mat, mat, vec),
        check_vma=False,
    )
```

```python
import functools
import math

import jax
import jax.numpy as jnp
from jax import lax
from jax.experimental import pallas as pl
from jax.experimental.pallas import tpu as pltpu
from jax.sharding import PartitionSpec as P

WINDOW = 512
EPSILON = 1e-06
ROPE_BASE = 10000.0
MASKED = -1e30
BF16 = jnp.bfloat16
F32 = jnp.float32
QBLOCK = 128
LANES = 128
GAIN_ROWS = 32
GELU_A = math.sqrt(2.0 / math.pi)
GELU_B = 0.044715

VMEM = pl.BlockSpec(memory_space=pltpu.VMEM)
SMEM = pl.BlockSpec(memory_space=pltpu.SMEM)
ANY = pl.BlockSpec(memory_space=pl.ANY)


def wrapped(value, size):
    return value & (size - 1) if size & (size - 1) == 0 else lax.rem(value, jnp.int32(size))


class Places:
    def __init__(self):
        self.seq = lax.axis_size("seq")
        self.fsdp = lax.axis_size("fsdp")
        self.outer = self.seq // 4
        index = lax.axis_index("seq").astype(jnp.int32)
        fsdp_at = lax.axis_index("fsdp").astype(jnp.int32)
        outer_at = lax.shift_right_logical(index, 2)
        core_at, mid_at = index & 1, lax.shift_right_logical(index, 1) & 1
        scalars = lax.optimization_barrier(
            (
                core_at,
                mid_at,
                fsdp_at,
                core_at * 2 + mid_at,
                tuple(wrapped(outer_at + by, self.outer) for by in range(self.outer)),
                tuple(wrapped(outer_at - by + self.outer, self.outer) for by in range(self.outer)),
                tuple(wrapped(fsdp_at + by, self.fsdp) for by in range(self.fsdp)),
                tuple(wrapped(fsdp_at - by + self.fsdp, self.fsdp) for by in range(self.fsdp)),
                jnp.stack([core_at, mid_at, fsdp_at]),
            )
        )
        self.core_at, self.mid_at, self.fsdp_at, self.quarter_at = scalars[:4]
        self.outer_ahead, self.outer_behind, self.fsdp_ahead, self.fsdp_behind, self.vector = scalars[4:]

    def core_swap(self, array):
        return lax.ppermute(array, "seq", [(i, i ^ 1) for i in range(self.seq)])

    def mid_swap(self, array):
        return lax.ppermute(array, "seq", [(i, i ^ 2) for i in range(self.seq)])

    def outer_shift(self, array, by):
        return lax.ppermute(array, "seq", [(i, (i + 4 * by) % self.seq) for i in range(self.seq)])

    def fsdp_shift(self, array, by):
        return lax.ppermute(array, "fsdp", [(i, (i + by) % self.fsdp) for i in range(self.fsdp)])


def linear_shift(array, by):
    count = lax.axis_size("seq") * lax.axis_size("fsdp")
    return lax.ppermute(array, ("seq", "fsdp"), [(i, i + by) for i in range(count) if 0 <= i + by < count])


def pick(array, at):
    return lax.dynamic_index_in_dim(array, at, 0, keepdims=False, allow_negative_indices=False)


def ordered(pieces, behind):
    if len(pieces) == 2:
        own, other = pieces
        return jnp.where(behind[0] == 0, jnp.stack([own, other]), jnp.stack([other, own]))
    stacked = jnp.stack(pieces)
    return jnp.stack([pick(stacked, at) for at in behind])


def own_part(here, shards, axis, ways):
    size = sum(shard.shape[axis] for shard in shards) // ways
    place = here.quarter_at if ways == 4 else here.core_at
    if len(shards) == 1:
        return lax.dynamic_slice_in_dim(shards[0], place * size, size, axis, allow_negative_indices=False)
    joined = jnp.concatenate(shards, axis)
    parts = [lax.slice_in_dim(joined, i * size, (i + 1) * size, axis=axis) for i in range(ways)]
    return functools.reduce(lambda rest, i: jnp.where(place == i, parts[i], rest), range(1, ways), parts[0])


def after(value, *earlier):
    return lax.optimization_barrier((value, *earlier))[0]


def over_links(here, part):
    return [here.fsdp_shift(part, by) for by in range(1, here.fsdp)]


def on_chips(here, arrived, ways):
    pieces = []
    for mine in arrived:
        if ways == 4:
            across = here.mid_swap(mine)
            pieces += [mine, across, here.core_swap(mine), here.core_swap(across)]
        else:
            pieces += [mine, here.core_swap(mine)]
    return pieces


def multiple(value, of):
    return pl.multiple_of(value, of)


def place_copies(owned, pieces, whole, sems, at, axis, ways):
    core, mid, fsdp = at[0], at[1], at[2]
    count = 1 + len(pieces) // ways
    rows = owned[0].shape[0]
    copies = []
    column = 0
    own_row = multiple(fsdp * rows, 16)
    for shard in owned:
        wide = shard.shape[1]
        copies.append((shard, whole.at[pl.ds(own_row, rows), pl.ds(column, wide)]))
        column += wide
    for k, piece in enumerate(pieces):
        by = 1 + k // ways
        row = multiple(lax.rem(fsdp + (count - by), count) * rows, 16)
        k = k % ways
        if ways == 4:
            place = (core if k < 2 else 1 - core) * 2 + (mid if k % 2 == 0 else 1 - mid)
        else:
            place = core if k == 0 else 1 - core
        if axis == 0:
            target = whole.at[pl.ds(multiple(row + place * (rows // ways), 16), rows // ways), :]
        else:
            target = whole.at[pl.ds(row, rows), pl.ds(multiple(place * (column // ways), 128), column // ways)]
        copies.append((piece, target))
    return [pltpu.make_async_copy(a, b, sems.at[k]) for k, (a, b) in enumerate(copies)]


def dot(a, b):
    return lax.dot_general(a, b, (((1,), (0,)), ((), ())), preferred_element_type=F32)


def dot_nt(a, b):
    return lax.dot_general(a, b, (((1,), (1,)), ((), ())), preferred_element_type=F32)


def dot_tn(a, b):
    return lax.dot_general(a, b, (((0,), (0,)), ((), ())), preferred_element_type=F32)


def inverse_rms(u):
    return lax.rsqrt(jnp.mean(u * u, axis=-1, keepdims=True) + EPSILON)


def norm_back(u, g, dz):
    r = inverse_rms(u)
    ur = u * r
    gdz = g * dz
    du = r * (gdz - ur * jnp.mean(gdz * ur, axis=-1, keepdims=True))
    return du, jnp.sum(dz * ur, axis=0, keepdims=True)


def params(megabytes=56):
    return pltpu.CompilerParams(vmem_limit_bytes=megabytes * 1024 * 1024)


def cost(flops, bytes_accessed):
    return pl.CostEstimate(flops=int(20 * flops), bytes_accessed=int(20 * bytes_accessed), transcendentals=0)


def shape(dims, kind):
    return jax.ShapeDtypeStruct(tuple(dims), kind)


def attend_kernel(n_tok, n_qkv, heads, *refs):
    at = refs[0]
    toks = refs[1 : 1 + n_tok]
    pos, cosine, sine, gain_in, gain_q, gain_k = refs[1 + n_tok : 7 + n_tok]
    qkv = refs[7 + n_tok : 7 + n_tok + n_qkv]
    normed, q_raw, k_raw, q_st, keys, values, probs, attended, w_full, sems = refs[7 + n_tok + n_qkv :]
    copies = place_copies(qkv[:3], qkv[3:], w_full, sems, at, 1, 4)
    for copy in copies:
        copy.start()
    rows = toks[0].shape[0]
    dim = keys.shape[1]
    half = dim // 2
    halo = (n_tok - 1) * rows
    gain = gain_in[...]
    for i, tok in enumerate(toks):
        u = tok[...].astype(F32)
        normed[i * rows : (i + 1) * rows, :] = (u * inverse_rms(u) * gain).astype(BF16)
    for copy in copies:
        copy.wait()

    def turned(u, g, cos, sin):
        u = u * inverse_rms(u) * g
        first, second = u[:, :half], u[:, half:]
        return (first * cos - second * sin).astype(BF16), (second * cos + first * sin).astype(BF16)

    for i in range(n_tok):
        here = slice(i * rows, (i + 1) * rows)
        kv = dot(normed[here, :], w_full[:, heads * dim :])
        k_raw[here, :] = kv[:, :dim]
        values[here, :] = kv[:, dim:].astype(BF16)
        first, second = turned(kv[:, :dim], gain_k[...], cosine[here, :], sine[here, :])
        keys[here, :half] = first
        keys[here, half:] = second
    blocks = rows // QBLOCK
    for h in range(heads):
        u = dot(normed[halo:, :], w_full[:, h * dim : (h + 1) * dim])
        q_raw[:, h * dim : (h + 1) * dim] = u
        first, second = turned(u, gain_q[...], cosine[halo:, :], sine[halo:, :])
        for b in range(blocks):
            start = (b * heads + h) * QBLOCK
            q_st[start : start + QBLOCK, :half] = first[b * QBLOCK : (b + 1) * QBLOCK, :]
            q_st[start : start + QBLOCK, half:] = second[b * QBLOCK : (b + 1) * QBLOCK, :]
    span = WINDOW + QBLOCK
    distance = (
        lax.broadcasted_iota(jnp.int32, (QBLOCK, span), 0)
        + WINDOW
        - lax.broadcasted_iota(jnp.int32, (QBLOCK, span), 1)
    )
    scale = dim ** (-0.5)
    for b in range(blocks):
        first_key = halo - WINDOW + b * QBLOCK
        limit = jnp.minimum(pos[b * QBLOCK : (b + 1) * QBLOCK, :], WINDOW - 1)
        allowed = (distance >= 0) & (distance <= limit)
        for h in range(heads):
            start = (b * heads + h) * QBLOCK
            scores = dot_nt(q_st[start : start + QBLOCK, :], keys[first_key : first_key + span, :]) * scale
            scores = jnp.where(allowed, scores, MASKED)
            weights = jnp.exp(scores - jnp.max(scores, axis=-1, keepdims=True))
            weights = (weights * (1.0 / jnp.sum(weights, axis=-1, keepdims=True))).astype(BF16)
            probs[start : start + QBLOCK, :] = weights
            attended[b * QBLOCK : (b + 1) * QBLOCK, h * dim : (h + 1) * dim] = dot(
                weights, values[first_key : first_key + span, :]
            ).astype(BF16)


def gate_kernel(n_out, n_gate, n_up, *refs):
    at, attended, tokens, gain_attn, gain_ffn = refs[:5]
    refs = refs[5:]
    out_w, gate_w, up_w, refs = (
        refs[:n_out],
        refs[n_out : n_out + n_gate],
        refs[n_out + n_gate : n_out + n_gate + n_up],
        refs[n_out + n_gate + n_up :],
    )
    projected_ref, residual_ref, ffn_in_ref, mixed, gelu_out, gate_slope = refs[:6]
    out_full, gate_full, up_full, out_sems, gate_sems, up_sems = refs[6:]
    groups = (
        place_copies(out_w[:1], out_w[1:], out_full, out_sems, at, 0, 2),
        place_copies(gate_w[:1], gate_w[1:], gate_full, gate_sems, at, 1, 4),
        place_copies(up_w[:1], up_w[1:], up_full, up_sems, at, 1, 2),
    )
    for group in groups:
        for copy in group:
            copy.start()
    for copy in groups[0]:
        copy.wait()
    projected = dot(attended[...], out_full[...])
    projected_ref[...] = projected
    residual = tokens[...].astype(F32) + projected * inverse_rms(projected) * gain_attn[...]
    residual_ref[...] = residual
    ffn_in_ref[...] = (residual * inverse_rms(residual) * gain_ffn[...]).astype(BF16)
    for group in groups[1:]:
        for copy in group:
            copy.wait()
    width = 256

    def step(i, _):
        cut = pl.ds(multiple(i * width, width), width)
        gate = dot(ffn_in_ref[...], gate_full[:, cut])
        up = dot(ffn_in_ref[...], up_full[:, cut])
        square = gate * gate
        t = jnp.tanh(GELU_A * gate * (1.0 + GELU_B * square))
        cdf = 0.5 * (1.0 + t)
        act = gate * cdf
        slope = cdf + 0.5 * gate * (1.0 - t * t) * (GELU_A * (1.0 + 3.0 * GELU_B * square))
        mixed[:, cut] = (act * up).astype(BF16)
        gelu_out[:, cut] = act.astype(BF16)
        gate_slope[:, cut] = (up * slope).astype(BF16)
        return 0

    lax.fori_loop(0, gate_full.shape[1] // width, step, 0)


def relative_blocks(at, fsdp):
    for c in range(2):
        core = c + at[0] - 2 * c * at[0]
        for f in range(fsdp):
            row = lax.rem(at[2] + f, fsdp)
            for x in range(2):
                mid = x + at[1] - 2 * x * at[1]
                yield c, f, x, core, row, mid


def down_kernel(n_down, fsdp, *refs):
    at, mixed, residual, cotangent, gain_out = refs[:5]
    down_w = refs[5 : 5 + n_down]
    layer_out, d_down, grad_gain, keep, send = refs[5 + n_down : 10 + n_down]
    down_full, mixed_t, sems = refs[10 + n_down :]
    copies = place_copies(down_w[:1], down_w[1:], down_full, sems, at, 0, 4)
    for copy in copies:
        copy.start()
    mixed_t[...] = mixed[...].T
    for copy in copies:
        copy.wait()
    down = dot(mixed[...], down_full[...])
    r = inverse_rms(down)
    gain = gain_out[...]
    layer_out[...] = (residual[...] + down * r * gain).astype(BF16)
    du, dg = norm_back(down, gain, cotangent[...].astype(F32))
    grad_gain[...] = dg
    d_down[...] = du.astype(BF16)
    block = keep.shape[2]
    for c, f, x, core, row, mid in relative_blocks(at, fsdp):
        start = multiple(((row * 2 + core) * 2 + mid) * block, 16)
        target = keep if c == 0 else send
        target[f, x] = dot(mixed_t[pl.ds(start, block), :], d_down[...]).astype(BF16)


def gate_back_kernel(n_down, fsdp, *refs):
    at, d_down, gelu_out, gate_slope, ffn_in = refs[:5]
    down_w = refs[5 : 5 + n_down]
    d_gate, d_up, gate_keep, gate_send, up_keep, up_send = refs[5 + n_down : 11 + n_down]
    down_full, ffn_t, sems = refs[11 + n_down :]
    copies = place_copies(down_w[:1], down_w[1:], down_full, sems, at, 0, 4)
    for copy in copies:
        copy.start()
    ffn_t[...] = ffn_in[...].T
    for copy in copies:
        copy.wait()
    width = 256

    def step(i, _):
        cut = pl.ds(multiple(i * width, width), width)
        d_mixed = dot_nt(d_down[...], down_full[cut, :])
        d_gate[:, cut] = (d_mixed * gate_slope[:, cut].astype(F32)).astype(BF16)
        d_up[:, cut] = (d_mixed * gelu_out[:, cut].astype(F32)).astype(BF16)
        return 0

    lax.fori_loop(0, d_gate.shape[1] // width, step, 0)
    tall, wide = gate_keep.shape[2:]
    for source, targets in ((d_gate, (gate_keep, gate_send)), (d_up, (up_keep, up_send))):
        for c, f, x, core, row, mid in relative_blocks(at, fsdp):
            cut = pl.ds(multiple((core * 2 + mid) * wide, 128), wide)
            left = ffn_t[pl.ds(multiple(row * tall, 16), tall), :]
            targets[c][f, x] = dot(left, source[:, cut]).astype(BF16)


def middle_kernel(n_out, n_gate, n_up, fsdp, heads, *refs):
    at, d_gate, d_up, residual, projected, cotangent, gain_ffn, gain_attn, attended = refs[:9]
    refs = refs[9:]
    out_w, gate_w, up_w, refs = (
        refs[:n_out],
        refs[n_out : n_out + n_gate],
        refs[n_out + n_gate : n_out + n_gate + n_up],
        refs[n_out + n_gate + n_up :],
    )
    d_residual_ref, g_ffn, g_attn, d_att, keep, send = refs[:6]
    out_full, gate_full, up_full, att_t, out_sems, gate_sems, up_sems = refs[6:]
    groups = (
        place_copies(gate_w[:1], gate_w[1:], gate_full, gate_sems, at, 1, 4),
        place_copies(up_w[:1], up_w[1:], up_full, up_sems, at, 1, 2),
        place_copies(out_w[:1], out_w[1:], out_full, out_sems, at, 0, 2),
    )
    for group in groups:
        for copy in group:
            copy.start()
    att_t[...] = attended[...].T
    for copy in groups[0]:
        copy.wait()
    d_ffn_in = dot_nt(d_gate[...], gate_full[...])
    for copy in groups[1]:
        copy.wait()
    d_ffn_in = d_ffn_in + dot_nt(d_up[...], up_full[...])
    du, dg = norm_back(residual[...], gain_ffn[...], d_ffn_in)
    g_ffn[...] = dg
    d_residual = cotangent[...].astype(F32) + du
    d_residual_ref[...] = d_residual
    du, dg = norm_back(projected[...], gain_attn[...], d_residual)
    g_attn[...] = dg
    d_proj = du.astype(BF16)
    rows, dim = d_proj.shape[0], d_att.shape[1]
    for copy in groups[2]:
        copy.wait()
    for h in range(heads):
        part = dot_nt(d_proj, out_full[h * dim : (h + 1) * dim, :]).astype(BF16)
        for b in range(rows // QBLOCK):
            start = (b * heads + h) * QBLOCK
            d_att[start : start + QBLOCK, :] = part[b * QBLOCK : (b + 1) * QBLOCK, :]
    block = keep.shape[2]
    for c, f, x, core, row, mid in relative_blocks(at, fsdp):
        start = multiple(((row * 2 + core) * 2 + mid) * block, 16)
        target = keep if c == 0 else send
        target[f, x] = dot(att_t[pl.ds(start, block), :], d_proj).astype(BF16)


def last_kernel(n_qkv, n_tok, fsdp, heads, *refs):
    (
        at, d_residual, d_att,
        q_raw, k_raw, q_st, keys, values, probs, cosine, sine, gain_q, gain_k, gain_in, normed, g_ffn, g_attn, g_out,
    ) = refs[:18]
    toks = refs[18 : 18 + n_tok]
    refs = refs[18 + n_tok :]
    qkv_w, refs = refs[:n_qkv], refs[n_qkv:]
    grad_tokens, d_halo, keep, send = refs[:4]
    w_full, normed_t, d_scores, d_q, d_k, d_v, d_qkv, gain_rows, qkv_sems = refs[4:]
    copies = place_copies(qkv_w[:3], qkv_w[3:], w_full, qkv_sems, at, 1, 4)
    for copy in copies:
        copy.start()
    normed_t[...] = normed[...].T
    rows = toks[0].shape[0]
    halo = (n_tok - 1) * rows
    dim = keys.shape[1]
    half = dim // 2
    blocks = rows // QBLOCK
    span = WINDOW + QBLOCK
    tall, wide = normed_t.shape[0] // fsdp, keep.shape[3]
    scale = dim ** (-0.5)
    d_k[...] = jnp.zeros(d_k.shape, F32)
    d_v[...] = jnp.zeros(d_v.shape, F32)
    for b in range(blocks):
        first_key = halo - WINDOW + b * QBLOCK
        here = slice(first_key, first_key + span)
        for h in range(heads):
            start = (b * heads + h) * QBLOCK
            stack = slice(start, start + QBLOCK)
            d_probs = dot_nt(d_att[stack, :], values[here, :])
            p = probs[stack, :].astype(F32)
            row_terms = jnp.sum(p * d_probs, axis=-1, keepdims=True)
            ds = (p * (d_probs - row_terms) * scale).astype(BF16)
            d_scores[h * QBLOCK : (h + 1) * QBLOCK, :] = ds
            d_q[b * QBLOCK : (b + 1) * QBLOCK, h * dim : (h + 1) * dim] = dot(ds, keys[here, :])
        stack = slice(b * heads * QBLOCK, (b + 1) * heads * QBLOCK)
        d_k[here, :] += dot_tn(d_scores[...], q_st[stack, :])
        d_v[here, :] += dot_tn(probs[stack, :], d_att[stack, :])

    def turned_back(u, g, dz, cos, sin):
        first, second = dz[:, :half], dz[:, half:]
        dz = jnp.concatenate([first * cos + second * sin, second * cos - first * sin], axis=1)
        return norm_back(u, g, dz)

    total_q = jnp.zeros((1, dim), F32)
    if halo:
        d_qkv[:halo, : heads * dim] = jnp.zeros((halo, heads * dim), BF16)
    for h in range(heads):
        cut = slice(h * dim, (h + 1) * dim)
        du, dg = turned_back(q_raw[:, cut], gain_q[...], d_q[:, cut], cosine[halo:, :], sine[halo:, :])
        total_q += dg
        d_qkv[halo:, cut] = du.astype(BF16)
    total_k = jnp.zeros((1, dim), F32)
    for i in range(n_tok):
        here = slice(i * rows, (i + 1) * rows)
        du, dg = turned_back(k_raw[here, :], gain_k[...], d_k[here, :], cosine[here, :], sine[here, :])
        total_k += dg
        d_qkv[here, heads * dim : (heads + 1) * dim] = du.astype(BF16)
        d_qkv[here, (heads + 1) * dim :] = d_v[here, :].astype(BF16)
    for c, f, x, core, row, mid in relative_blocks(at, fsdp):
        cut = pl.ds(multiple((core * 2 + mid) * wide, 128), wide)
        left = normed_t[pl.ds(multiple(row * tall, 16), tall), :]
        target = keep if c == 0 else send
        target[f, x, :tall, :] = dot(left, d_qkv[:, cut]).astype(BF16)
    for copy in copies:
        copy.wait()
    total_in = jnp.zeros(gain_in.shape, F32)
    for i in range(n_tok):
        here = slice(i * rows, (i + 1) * rows)
        if i < n_tok - 1:
            d_normed = dot_nt(d_qkv[here, heads * dim :], w_full[:, heads * dim :])
        else:
            d_normed = dot_nt(d_qkv[here, :], w_full[...])
        du, dg = norm_back(toks[i][...].astype(F32), gain_in[...], d_normed)
        total_in += dg
        if i < n_tok - 1:
            d_halo[here, :] = du.astype(BF16)
        else:
            grad_tokens[...] = d_residual[...] + du
    gain_rows[...] = jnp.zeros(gain_rows.shape, F32)
    at_row = 0
    for total in (total_in, total_q, total_k, g_attn[...], g_ffn[...], g_out[...]):
        for i in range(total.shape[1] // LANES):
            gain_rows[at_row : at_row + 1, :LANES] = total[:, i * LANES : (i + 1) * LANES]
            at_row += 1
    packed = gain_rows[...].astype(BF16)
    for target in (keep, send):
        for f in range(fsdp):
            for x in range(2):
                target[f, x, tall:, :] = packed


def add(*terms):
    out = terms[0].astype(F32)
    for term in terms[1:]:
        out = out + term.astype(F32)
    return out


class Chunk:
    def __init__(self, here, keep, send):
        self.here, self.keep = here, keep
        self.other = here.core_swap(send)

    def over_fsdp(self, *earlier):
        here = self.here
        parts = [add(self.keep[by], self.other[by]).astype(BF16) for by in range(1, here.fsdp)]
        self.arrived = [here.fsdp_shift(after(part, *earlier), by + 1) for by, part in enumerate(parts)]

    def over_mid(self, *earlier):
        terms = [self.keep[0, 1], self.other[0, 1]] + [a[1] for a in self.arrived]
        self.across = self.here.mid_swap(after(add(*terms).astype(BF16), *earlier))

    def finish(self, *earlier):
        here = self.here
        n, w = self.across.shape
        terms = [self.keep[0, 0], self.other[0, 0]] + [a[0] for a in self.arrived] + [self.across]
        mine = after(add(*terms).astype(BF16), *earlier).reshape(here.outer, n // here.outer, w)
        terms = [pick(mine, here.outer_ahead[0])]
        for by in range(1, here.outer):
            terms.append(here.outer_shift(pick(mine, here.outer_ahead[by]), by))
        own = add(*terms).astype(BF16)
        block = ordered([own] + [here.outer_shift(own, by) for by in range(1, here.outer)], here.outer_behind)
        block = block.reshape(n, w)
        across = here.mid_swap(block)
        return [[block, across], [here.core_swap(block), here.core_swap(across)]]


def by_place(here, blocks):
    own = [jnp.where(here.mid_at == 0, a, b) for a, b in blocks]
    other = [jnp.where(here.mid_at == 0, b, a) for a, b in blocks]
    pairs = list(zip(own, other))
    first = [jnp.where(here.core_at == 0, a, b) for a, b in zip(pairs[0], pairs[1])]
    second = [jnp.where(here.core_at == 0, b, a) for a, b in zip(pairs[0], pairs[1])]
    return first + second


def on_device(
    tokens, positions, cotangent, in_gain, w_query, w_key, w_value, query_gain, key_gain, w_out, attn_gain,
    ffn_gain_in, w_gate, w_up, w_down, ffn_gain_out,
):
    here = Places()
    fsdp = here.fsdp
    rows, width = tokens.shape
    dim = w_key.shape[1]
    query_cols = w_query.shape[1]
    heads = query_cols // dim
    hidden = w_gate.shape[1]
    hops = (WINDOW + rows - 1) // rows
    n_tok = hops + 1
    halo = hops * rows
    every = halo + rows
    at = here.vector

    gains = (in_gain, query_gain, key_gain, attn_gain, ffn_gain_in, ffn_gain_out)
    cuts = [0]
    for gain in gains:
        cuts.append(cuts[-1] + gain.shape[0])
    gain_row = jnp.concatenate(gains)
    gain_rows = ordered([gain_row] + [here.fsdp_shift(gain_row, by) for by in range(1, fsdp)], here.fsdp_behind)
    gain_rows = gain_rows.astype(F32)
    gain_in, gain_q, gain_k, gain_attn, gain_ffn, gain_out = (
        gain_rows[:, cuts[i] : cuts[i + 1]].reshape(1, -1) for i in range(6)
    )
    toks = [linear_shift(tokens, by) for by in range(hops, 0, -1)] + [tokens]
    qkv_w = [w_query, w_key, w_value]
    qkv_w += on_chips(here, over_links(here, own_part(here, qkv_w, 1, 4)), 4)
    out_part = after(own_part(here, [w_out], 0, 2), *toks[:-1])
    out_arrived = over_links(here, out_part)
    gate_part = after(own_part(here, [w_gate], 1, 4), qkv_w[3])
    gate_arrived = over_links(here, gate_part)
    up_part = after(own_part(here, [w_up], 1, 2), out_arrived[0])
    up_arrived = over_links(here, up_part)

    all_positions = jnp.concatenate([positions[0] - halo + jnp.arange(halo, dtype=jnp.int32), positions])
    frequency = ROPE_BASE ** (-(jnp.arange(dim // 2, dtype=F32) * 2.0 / dim))
    angles = all_positions.astype(F32)[:, None] * frequency[None, :]
    cosine, sine = jnp.cos(angles), jnp.sin(angles)

    span = WINDOW + QBLOCK
    weight_bytes = 2 * fsdp * w_gate.size
    normed, q_raw, k_raw, q_st, keys, values, probs, attended = pl.pallas_call(
        functools.partial(attend_kernel, n_tok, len(qkv_w), heads),
        out_shape=(
            shape((every, width), BF16),
            shape((rows, query_cols), F32),
            shape((every, dim), F32),
            shape((heads * rows, dim), BF16),
            shape((every, dim), BF16),
            shape((every, dim), BF16),
            shape((heads * rows, span), BF16),
            shape((rows, query_cols), BF16),
        ),
        in_specs=[SMEM] + [VMEM] * (n_tok + 6) + [ANY] * len(qkv_w),
        out_specs=(VMEM,) * 8,
        scratch_shapes=[
            pltpu.VMEM((width, query_cols + 2 * dim), BF16),
            pltpu.SemaphoreType.DMA((len(qkv_w),)),
        ],
        compiler_params=params(),
        cost_estimate=cost(4e9, 1e7),
        name="attend",
    )(at, *toks, positions[:, None], cosine, sine, gain_in, gain_q, gain_k, *qkv_w)

    down_part = after(own_part(here, [w_down], 0, 4), attended)
    out_w = [w_out] + on_chips(here, [after(a, attended) for a in out_arrived], 2)
    gate_w = [w_gate] + on_chips(here, [after(a, attended) for a in gate_arrived], 4)
    up_w = [w_up] + on_chips(here, [after(a, attended) for a in up_arrived], 2)
    down_w = [w_down] + on_chips(here, over_links(here, down_part), 4)
    projected, residual, ffn_in, mixed, gelu_out, gate_slope = pl.pallas_call(
        functools.partial(gate_kernel, len(out_w), len(gate_w), len(up_w)),
        out_shape=(
            shape((rows, width), F32),
            shape((rows, width), F32),
            shape((rows, width), BF16),
            shape((rows, hidden), BF16),
            shape((rows, hidden), BF16),
            shape((rows, hidden), BF16),
        ),
        in_specs=[SMEM] + [VMEM] * 4 + [ANY] * (len(out_w) + len(gate_w) + len(up_w)),
        out_specs=(VMEM,) * 6,
        scratch_shapes=[
            pltpu.VMEM((query_cols, width), BF16),
            pltpu.VMEM((width, hidden), BF16),
            pltpu.VMEM((width, hidden), BF16),
            pltpu.SemaphoreType.DMA((len(out_w),)),
            pltpu.SemaphoreType.DMA((len(gate_w),)),
            pltpu.SemaphoreType.DMA((len(up_w),)),
        ],
        compiler_params=params(),
        cost_estimate=cost(4e9, 2 * weight_bytes),
        name="gate",
    )(at, attended, tokens, gain_attn, gain_ffn, *out_w, *gate_w, *up_w)

    down_block = w_down.shape[0] // 4
    down_shape = shape((fsdp, 2, down_block, width), BF16)
    layer_out, d_down, g_ffn_out, down_keep, down_send = pl.pallas_call(
        functools.partial(down_kernel, len(down_w), fsdp),
        out_shape=(
            shape((rows, width), BF16),
            shape((rows, width), BF16),
            shape((1, width), F32),
            down_shape,
            down_shape,
        ),
        in_specs=[SMEM] + [VMEM] * 4 + [ANY] * len(down_w),
        out_specs=(VMEM,) * 5,
        scratch_shapes=[
            pltpu.VMEM((hidden, width), BF16),
            pltpu.VMEM((hidden, rows), BF16),
            pltpu.SemaphoreType.DMA((len(down_w),)),
        ],
        compiler_params=params(),
        cost_estimate=cost(4e9, 2 * weight_bytes),
        name="down",
    )(at, mixed, residual, cotangent, gain_out, *down_w)

    down_sum = Chunk(here, down_keep, down_send)
    d_down = after(d_down, down_sum.other)
    gate_shape = shape((fsdp, 2, w_gate.shape[0], hidden // 4), BF16)
    d_gate, d_up, gate_keep, gate_send, up_keep, up_send = pl.pallas_call(
        functools.partial(gate_back_kernel, len(down_w), fsdp),
        out_shape=(
            shape((rows, hidden), BF16),
            shape((rows, hidden), BF16),
            gate_shape,
            gate_shape,
            gate_shape,
            gate_shape,
        ),
        in_specs=[SMEM] + [VMEM] * 4 + [ANY] * len(down_w),
        out_specs=(VMEM,) * 6,
        scratch_shapes=[
            pltpu.VMEM((hidden, width), BF16),
            pltpu.VMEM((width, rows), BF16),
            pltpu.SemaphoreType.DMA((len(down_w),)),
        ],
        compiler_params=params(),
        cost_estimate=cost(6e9, 3 * weight_bytes),
        name="gate_back",
    )(at, d_down, gelu_out, gate_slope, ffn_in, *down_w)

    qkv_cols = query_cols + 2 * dim
    last_wide = qkv_cols // 4
    shard_rows = w_query.shape[0]
    last_shape = shape((fsdp, 2, shard_rows + GAIN_ROWS, last_wide), BF16)
    gate_sum = Chunk(here, gate_keep, gate_send)
    up_sum = Chunk(here, up_keep, up_send)
    down_sum.over_fsdp()
    out_shape = shape((fsdp, 2, w_out.shape[0] // 4, width), BF16)
    d_residual, g_ffn, g_attn, d_att, out_keep, out_send = pl.pallas_call(
        functools.partial(middle_kernel, len(out_w), len(gate_w), len(up_w), fsdp, heads),
        out_shape=(
            shape((rows, width), F32),
            shape((1, width), F32),
            shape((1, width), F32),
            shape((heads * rows, dim), BF16),
            out_shape,
            out_shape,
        ),
        in_specs=[SMEM] + [VMEM] * 8 + [ANY] * (len(out_w) + len(gate_w) + len(up_w)),
        out_specs=(VMEM,) * 6,
        scratch_shapes=[
            pltpu.VMEM((query_cols, width), BF16),
            pltpu.VMEM((width, hidden), BF16),
            pltpu.VMEM((width, hidden), BF16),
            pltpu.VMEM((query_cols, rows), BF16),
            pltpu.SemaphoreType.DMA((len(out_w),)),
            pltpu.SemaphoreType.DMA((len(gate_w),)),
            pltpu.SemaphoreType.DMA((len(up_w),)),
        ],
        compiler_params=params(),
        cost_estimate=cost(6e9, 4 * weight_bytes),
        name="middle",
    )(at, d_gate, d_up, residual, projected, cotangent, gain_ffn, gain_attn, attended, *out_w, *gate_w, *up_w)

    gate_sum.over_fsdp()
    out_sum = Chunk(here, out_keep, out_send)
    d_att = after(d_att, gate_sum.other, up_sum.other, *down_sum.arrived)
    down_sum.over_mid()
    grad_tokens, d_halo, last_keep, last_send = pl.pallas_call(
        functools.partial(last_kernel, len(qkv_w), n_tok, fsdp, heads),
        out_shape=(
            shape((rows, width), F32),
            shape((halo, width), BF16),
            last_shape,
            last_shape,
        ),
        in_specs=[SMEM] + [VMEM] * (17 + n_tok) + [ANY] * len(qkv_w),
        out_specs=(VMEM,) * 4,
        scratch_shapes=[
            pltpu.VMEM((width, qkv_cols), BF16),
            pltpu.VMEM((width, every), BF16),
            pltpu.VMEM((heads * QBLOCK, span), BF16),
            pltpu.VMEM((rows, query_cols), F32),
            pltpu.VMEM((every, dim), F32),
            pltpu.VMEM((every, dim), F32),
            pltpu.VMEM((every, qkv_cols), BF16),
            pltpu.VMEM((GAIN_ROWS, last_wide), F32),
            pltpu.SemaphoreType.DMA((len(qkv_w),)),
        ],
        compiler_params=params(),
        cost_estimate=cost(15e9, 4 * weight_bytes),
        name="last",
    )(
        at, d_residual, d_att,
        q_raw, k_raw, q_st, keys, values, probs, cosine, sine, gain_q, gain_k, gain_in, normed,
        g_ffn, g_attn, g_ffn_out, *toks, *qkv_w,
    )

    last_sum = Chunk(here, last_keep, after(last_send, down_sum.across, *gate_sum.arrived))
    up_sum.over_fsdp()
    gate_sum.over_mid(last_sum.other)
    last_sum.over_fsdp()
    out_sum.over_fsdp(last_sum.other, *up_sum.arrived)
    down_blocks = by_place(here, down_sum.finish(last_sum.other))
    up_sum.over_mid(last_sum.other)
    last_sum.over_mid()
    gate_blocks = by_place(here, gate_sum.finish(*last_sum.arrived))
    out_sum.over_mid()
    up_blocks = by_place(here, up_sum.finish(*out_sum.arrived))
    last_blocks = last_sum.finish()
    total_gains = last_blocks[0][0][shard_rows:, :LANES].astype(F32)
    last_blocks = by_place(here, last_blocks)
    out_blocks = by_place(here, out_sum.finish())

    for by in range(1, hops + 1):
        start = halo - by * rows
        grad_tokens = grad_tokens + linear_shift(d_halo[start : start + rows], -by).astype(F32)

    total_down = jnp.concatenate(down_blocks, axis=0).astype(F32)
    total_gate = jnp.concatenate(gate_blocks, axis=1).astype(F32)
    total_up = jnp.concatenate(up_blocks, axis=1).astype(F32)
    total_qkv = jnp.concatenate([b[:shard_rows] for b in last_blocks], axis=1).astype(F32)
    total_out = jnp.concatenate(out_blocks, axis=0).astype(F32)
    g, at_row = [], 0
    for gain in gains:
        deep = fsdp * gain.shape[0] // total_gains.shape[1]
        total = total_gains[at_row : at_row + deep].reshape(fsdp, gain.shape[0])
        g.append(pick(total, here.fsdp_at))
        at_row += deep
    return (
        layer_out, grad_tokens, g[0],
        total_qkv[:, :query_cols],
        total_qkv[:, query_cols : query_cols + dim],
        total_qkv[:, query_cols + dim :],
        g[1], g[2], total_out, g[3], g[4], total_gate, total_up, total_down, g[5],
    )


def solution(mesh):
    tok = P(("seq", "fsdp"), None)
    mat = P("fsdp", None)
    vec = P("fsdp")
    return jax.shard_map(
        on_device,
        mesh=mesh,
        in_specs=(tok, P(("seq", "fsdp")), tok, vec, mat, mat, mat, vec, vec, mat, vec, vec, mat, mat, mat, vec),
        out_specs=(tok, tok, vec, mat, mat, mat, vec, vec, mat, vec, vec, mat, mat, mat, vec),
        check_vma=False,
    )
```

```python
import functools
import math

import jax
import jax.numpy as jnp
from jax import lax
from jax.experimental import pallas as pl
from jax.experimental.pallas import tpu as pltpu
from jax.sharding import PartitionSpec as P

WINDOW = 512
EPSILON = 1e-06
ROPE_BASE = 10000.0
MASKED = -1e30
BF16 = jnp.bfloat16
F32 = jnp.float32
QBLOCK = 128
LANES = 128
GAIN_ROWS = 32
GELU_A = math.sqrt(2.0 / math.pi)
GELU_B = 0.044715

VMEM = pl.BlockSpec(memory_space=pltpu.VMEM)
SMEM = pl.BlockSpec(memory_space=pltpu.SMEM)
ANY = pl.BlockSpec(memory_space=pl.ANY)


def wrapped(value, size):
    return value & (size - 1) if size & (size - 1) == 0 else lax.rem(value, jnp.int32(size))


class Places:
    def __init__(self):
        self.seq = lax.axis_size("seq")
        self.fsdp = lax.axis_size("fsdp")
        self.outer = self.seq // 4
        self.bits = self.outer.bit_length() - 1
        index = lax.axis_index("seq").astype(jnp.int32)
        fsdp_at = lax.axis_index("fsdp").astype(jnp.int32)
        outer_at = lax.shift_right_logical(index, 2)
        core_at, mid_at = index & 1, lax.shift_right_logical(index, 1) & 1
        scalars = lax.optimization_barrier(
            (
                core_at,
                mid_at,
                fsdp_at,
                core_at * 2 + mid_at,
                tuple(lax.shift_right_logical(outer_at, bit) & 1 for bit in range(self.bits)),
                tuple(1 - (lax.shift_right_logical(outer_at, bit) & 1) for bit in range(self.bits)),
                tuple(wrapped(fsdp_at + by, self.fsdp) for by in range(self.fsdp)),
                tuple(wrapped(fsdp_at - by + self.fsdp, self.fsdp) for by in range(self.fsdp)),
                jnp.stack([core_at, mid_at, fsdp_at]),
            )
        )
        self.core_at, self.mid_at, self.fsdp_at, self.quarter_at = scalars[:4]
        self.bit_at, self.bit_off, self.fsdp_ahead, self.fsdp_behind, self.vector = scalars[4:]

    def core_swap(self, array):
        return lax.ppermute(array, "seq", [(i, i ^ 1) for i in range(self.seq)])

    def mid_swap(self, array):
        return lax.ppermute(array, "seq", [(i, i ^ 2) for i in range(self.seq)])

    def outer_swap(self, array, bit):
        return lax.ppermute(array, "seq", [(i, i ^ (4 << bit)) for i in range(self.seq)])

    def fsdp_shift(self, array, by):
        return lax.ppermute(array, "fsdp", [(i, (i + by) % self.fsdp) for i in range(self.fsdp)])


def linear_shift(array, by):
    count = lax.axis_size("seq") * lax.axis_size("fsdp")
    return lax.ppermute(array, ("seq", "fsdp"), [(i, i + by) for i in range(count) if 0 <= i + by < count])


def pick(array, at):
    return lax.dynamic_index_in_dim(array, at, 0, keepdims=False, allow_negative_indices=False)


def ordered(pieces, behind):
    if len(pieces) == 2:
        own, other = pieces
        return jnp.where(behind[0] == 0, jnp.stack([own, other]), jnp.stack([other, own]))
    stacked = jnp.stack(pieces)
    return jnp.stack([pick(stacked, at) for at in behind])


def own_part(here, shards, axis, ways):
    size = sum(shard.shape[axis] for shard in shards) // ways
    place = here.quarter_at if ways == 4 else here.core_at
    if len(shards) == 1:
        return lax.dynamic_slice_in_dim(shards[0], place * size, size, axis, allow_negative_indices=False)
    parts = []
    for i in range(ways):
        pieces, start = [], 0
        for shard in shards:
            low, high = max(i * size - start, 0), min((i + 1) * size - start, shard.shape[axis])
            if low < high:
                pieces.append(lax.slice_in_dim(shard, low, high, axis=axis))
            start += shard.shape[axis]
        parts.append(jnp.concatenate(pieces, axis))
    return functools.reduce(lambda rest, i: jnp.where(place == i, parts[i], rest), range(1, ways), parts[0])


def after(value, *earlier):
    return lax.optimization_barrier((value, *earlier))[0]


def over_links(here, part):
    return [here.fsdp_shift(part, by) for by in range(1, here.fsdp)]


def on_chips(here, arrived, ways):
    pieces = []
    for mine in arrived:
        if ways == 4:
            across = here.mid_swap(mine)
            pieces += [mine, across, here.core_swap(mine), here.core_swap(across)]
        else:
            pieces += [mine, here.core_swap(mine)]
    return pieces


def multiple(value, of):
    return pl.multiple_of(value, of)


def place_copies(owned, pieces, whole, sems, at, axis, ways):
    core, mid, fsdp = at[0], at[1], at[2]
    count = 1 + len(pieces) // ways
    rows = owned[0].shape[0]
    copies = []
    column = 0
    own_row = multiple(fsdp * rows, 16)
    for shard in owned:
        wide = shard.shape[1]
        copies.append((shard, whole.at[pl.ds(own_row, rows), pl.ds(column, wide)]))
        column += wide
    for k, piece in enumerate(pieces):
        by = 1 + k // ways
        row = multiple(lax.rem(fsdp + (count - by), count) * rows, 16)
        k = k % ways
        if ways == 4:
            place = (core if k < 2 else 1 - core) * 2 + (mid if k % 2 == 0 else 1 - mid)
        else:
            place = core if k == 0 else 1 - core
        if axis == 0:
            target = whole.at[pl.ds(multiple(row + place * (rows // ways), 16), rows // ways), :]
        else:
            target = whole.at[pl.ds(row, rows), pl.ds(multiple(place * (column // ways), 128), column // ways)]
        copies.append((piece, target))
    return [pltpu.make_async_copy(a, b, sems.at[k]) for k, (a, b) in enumerate(copies)]


def dot(a, b):
    return lax.dot_general(a, b, (((1,), (0,)), ((), ())), preferred_element_type=F32)


def dot_nt(a, b):
    return lax.dot_general(a, b, (((1,), (1,)), ((), ())), preferred_element_type=F32)


def dot_tn(a, b):
    return lax.dot_general(a, b, (((0,), (0,)), ((), ())), preferred_element_type=F32)


def inverse_rms(u):
    return lax.rsqrt(jnp.mean(u * u, axis=-1, keepdims=True) + EPSILON)


def norm_back(u, g, dz):
    r = inverse_rms(u)
    ur = u * r
    gdz = g * dz
    du = r * (gdz - ur * jnp.mean(gdz * ur, axis=-1, keepdims=True))
    return du, jnp.sum(dz * ur, axis=0, keepdims=True)


def params(megabytes=56):
    return pltpu.CompilerParams(vmem_limit_bytes=megabytes * 1024 * 1024)


def cost(flops, bytes_accessed):
    return pl.CostEstimate(flops=int(20 * flops), bytes_accessed=int(20 * bytes_accessed), transcendentals=0)


def shape(dims, kind):
    return jax.ShapeDtypeStruct(tuple(dims), kind)


def attend_kernel(n_tok, n_qkv, heads, *refs):
    at = refs[0]
    toks = refs[1 : 1 + n_tok]
    pos, cosine, sine, gain_in, gain_q, gain_k = refs[1 + n_tok : 7 + n_tok]
    qkv = refs[7 + n_tok : 7 + n_tok + n_qkv]
    normed, q_raw, k_raw, q_st, keys, values, probs, attended, w_full, sems = refs[7 + n_tok + n_qkv :]
    copies = place_copies(qkv[:3], qkv[3:], w_full, sems, at, 1, 4)
    for copy in copies:
        copy.start()
    rows = toks[0].shape[0]
    dim = keys.shape[1]
    half = dim // 2
    halo = (n_tok - 1) * rows
    gain = gain_in[...]
    for i, tok in enumerate(toks):
        u = tok[...].astype(F32)
        normed[i * rows : (i + 1) * rows, :] = (u * inverse_rms(u) * gain).astype(BF16)
    for copy in copies:
        copy.wait()

    def turned(u, g, cos, sin):
        u = u * inverse_rms(u) * g
        first, second = u[:, :half], u[:, half:]
        return (first * cos - second * sin).astype(BF16), (second * cos + first * sin).astype(BF16)

    for i in range(n_tok):
        here = slice(i * rows, (i + 1) * rows)
        kv = dot(normed[here, :], w_full[:, heads * dim :])
        k_raw[here, :] = kv[:, :dim]
        values[here, :] = kv[:, dim:].astype(BF16)
        first, second = turned(kv[:, :dim], gain_k[...], cosine[here, :], sine[here, :])
        keys[here, :half] = first
        keys[here, half:] = second
    blocks = rows // QBLOCK
    for h in range(heads):
        u = dot(normed[halo:, :], w_full[:, h * dim : (h + 1) * dim])
        q_raw[:, h * dim : (h + 1) * dim] = u
        first, second = turned(u, gain_q[...], cosine[halo:, :], sine[halo:, :])
        for b in range(blocks):
            start = (b * heads + h) * QBLOCK
            q_st[start : start + QBLOCK, :half] = first[b * QBLOCK : (b + 1) * QBLOCK, :]
            q_st[start : start + QBLOCK, half:] = second[b * QBLOCK : (b + 1) * QBLOCK, :]
    span = WINDOW + QBLOCK
    distance = (
        lax.broadcasted_iota(jnp.int32, (QBLOCK, span), 0)
        + WINDOW
        - lax.broadcasted_iota(jnp.int32, (QBLOCK, span), 1)
    )
    scale = dim ** (-0.5)
    for b in range(blocks):
        first_key = halo - WINDOW + b * QBLOCK
        limit = jnp.minimum(pos[b * QBLOCK : (b + 1) * QBLOCK, :], WINDOW - 1)
        allowed = (distance >= 0) & (distance <= limit)
        for h in range(heads):
            start = (b * heads + h) * QBLOCK
            scores = dot_nt(q_st[start : start + QBLOCK, :], keys[first_key : first_key + span, :]) * scale
            scores = jnp.where(allowed, scores, MASKED)
            weights = jnp.exp(scores - jnp.max(scores, axis=-1, keepdims=True))
            weights = (weights * (1.0 / jnp.sum(weights, axis=-1, keepdims=True))).astype(BF16)
            probs[start : start + QBLOCK, :] = weights
            attended[b * QBLOCK : (b + 1) * QBLOCK, h * dim : (h + 1) * dim] = dot(
                weights, values[first_key : first_key + span, :]
            ).astype(BF16)


def gate_kernel(n_out, n_gate, n_up, *refs):
    at, attended, tokens, gain_attn, gain_ffn = refs[:5]
    refs = refs[5:]
    out_w, gate_w, up_w, refs = (
        refs[:n_out],
        refs[n_out : n_out + n_gate],
        refs[n_out + n_gate : n_out + n_gate + n_up],
        refs[n_out + n_gate + n_up :],
    )
    projected_ref, residual_ref, ffn_in_ref, mixed, gelu_out, gate_slope = refs[:6]
    out_full, gate_full, up_full, out_sems, gate_sems, up_sems = refs[6:]
    groups = (
        place_copies(out_w[:1], out_w[1:], out_full, out_sems, at, 0, 2),
        place_copies(gate_w[:1], gate_w[1:], gate_full, gate_sems, at, 1, 4),
        place_copies(up_w[:1], up_w[1:], up_full, up_sems, at, 1, 4),
    )
    for group in groups:
        for copy in group:
            copy.start()
    for copy in groups[0]:
        copy.wait()
    projected = dot(attended[...], out_full[...])
    projected_ref[...] = projected
    residual = tokens[...].astype(F32) + projected * inverse_rms(projected) * gain_attn[...]
    residual_ref[...] = residual
    ffn_in_ref[...] = (residual * inverse_rms(residual) * gain_ffn[...]).astype(BF16)
    for group in groups[1:]:
        for copy in group:
            copy.wait()
    width = 256

    def step(i, _):
        cut = pl.ds(multiple(i * width, width), width)
        gate = dot(ffn_in_ref[...], gate_full[:, cut])
        up = dot(ffn_in_ref[...], up_full[:, cut])
        square = gate * gate
        t = jnp.tanh(GELU_A * gate * (1.0 + GELU_B * square))
        cdf = 0.5 * (1.0 + t)
        act = gate * cdf
        slope = cdf + 0.5 * gate * (1.0 - t * t) * (GELU_A * (1.0 + 3.0 * GELU_B * square))
        mixed[:, cut] = (act * up).astype(BF16)
        gelu_out[:, cut] = act.astype(BF16)
        gate_slope[:, cut] = (up * slope).astype(BF16)
        return 0

    lax.fori_loop(0, gate_full.shape[1] // width, step, 0)


def relative_blocks(at, fsdp):
    for c in range(2):
        core = c + at[0] - 2 * c * at[0]
        for f in range(fsdp):
            row = lax.rem(at[2] + f, fsdp)
            for x in range(2):
                mid = x + at[1] - 2 * x * at[1]
                yield c, f, x, core, row, mid


def column_blocks(at, fsdp, left_t, right, keep, send):
    tall, wide = left_t.shape[0] // fsdp, keep.shape[3]
    for c, f, x, core, row, mid in relative_blocks(at, fsdp):
        cut = pl.ds(multiple((core * 2 + mid) * wide, 128), wide)
        left = left_t[pl.ds(multiple(row * tall, 16), tall), :]
        target = keep if c == 0 else send
        target[f, x, :tall, :] = dot(left, right[:, cut]).astype(BF16)


def down_kernel(n_down, fsdp, *refs):
    at, mixed, residual, cotangent, gain_out = refs[:5]
    down_w = refs[5 : 5 + n_down]
    layer_out, d_down, grad_gain, keep, send = refs[5 + n_down : 10 + n_down]
    down_full, mixed_t, sems = refs[10 + n_down :]
    copies = place_copies(down_w[:1], down_w[1:], down_full, sems, at, 0, 2)
    for copy in copies:
        copy.start()
    mixed_t[...] = mixed[...].T
    for copy in copies:
        copy.wait()
    down = dot(mixed[...], down_full[...])
    r = inverse_rms(down)
    gain = gain_out[...]
    layer_out[...] = (residual[...] + down * r * gain).astype(BF16)
    du, dg = norm_back(down, gain, cotangent[...].astype(F32))
    grad_gain[...] = dg
    d_down[...] = du.astype(BF16)
    block = keep.shape[2]
    for c, f, x, core, row, mid in relative_blocks(at, fsdp):
        start = multiple(((row * 2 + core) * 2 + mid) * block, 16)
        target = keep if c == 0 else send
        target[f, x] = dot(mixed_t[pl.ds(start, block), :], d_down[...]).astype(BF16)


def gate_back_kernel(n_down, fsdp, *refs):
    at, d_down, gelu_out, gate_slope, ffn_in = refs[:5]
    down_w = refs[5 : 5 + n_down]
    d_gate, d_up, ffn_t, keep, send = refs[5 + n_down : 10 + n_down]
    down_full, sems = refs[10 + n_down :]
    copies = place_copies(down_w[:1], down_w[1:], down_full, sems, at, 0, 2)
    for copy in copies:
        copy.start()
    ffn_t[...] = ffn_in[...].T
    for copy in copies:
        copy.wait()
    width = 256

    def step(i, _):
        cut = pl.ds(multiple(i * width, width), width)
        d_mixed = dot_nt(d_down[...], down_full[cut, :])
        d_gate[:, cut] = (d_mixed * gate_slope[:, cut].astype(F32)).astype(BF16)
        d_up[:, cut] = (d_mixed * gelu_out[:, cut].astype(F32)).astype(BF16)
        return 0

    lax.fori_loop(0, d_gate.shape[1] // width, step, 0)
    column_blocks(at, fsdp, ffn_t, d_gate, keep, send)


def up_back_kernel(fsdp, at, ffn_t, d_up, keep, send):
    column_blocks(at, fsdp, ffn_t, d_up, keep, send)


def middle_kernel(n_out, n_gate, n_up, fsdp, heads, *refs):
    at, d_gate, d_up, residual, projected, cotangent, gain_ffn, gain_attn, attended = refs[:9]
    refs = refs[9:]
    out_w, gate_w, up_w, refs = (
        refs[:n_out],
        refs[n_out : n_out + n_gate],
        refs[n_out + n_gate : n_out + n_gate + n_up],
        refs[n_out + n_gate + n_up :],
    )
    d_residual_ref, g_ffn, g_attn, d_att, keep, send = refs[:6]
    out_full, gate_full, up_full, att_t, out_sems, gate_sems, up_sems = refs[6:]
    groups = (
        place_copies(gate_w[:1], gate_w[1:], gate_full, gate_sems, at, 1, 4),
        place_copies(up_w[:1], up_w[1:], up_full, up_sems, at, 1, 4),
        place_copies(out_w[:1], out_w[1:], out_full, out_sems, at, 0, 2),
    )
    for group in groups:
        for copy in group:
            copy.start()
    att_t[...] = attended[...].T
    for copy in groups[0]:
        copy.wait()
    d_ffn_in = dot_nt(d_gate[...], gate_full[...])
    for copy in groups[1]:
        copy.wait()
    d_ffn_in = d_ffn_in + dot_nt(d_up[...], up_full[...])
    du, dg = norm_back(residual[...], gain_ffn[...], d_ffn_in)
    g_ffn[...] = dg
    d_residual = cotangent[...].astype(F32) + du
    d_residual_ref[...] = d_residual
    du, dg = norm_back(projected[...], gain_attn[...], d_residual)
    g_attn[...] = dg
    d_proj = du.astype(BF16)
    rows, dim = d_proj.shape[0], d_att.shape[1]
    for copy in groups[2]:
        copy.wait()
    for h in range(heads):
        part = dot_nt(d_proj, out_full[h * dim : (h + 1) * dim, :]).astype(BF16)
        for b in range(rows // QBLOCK):
            start = (b * heads + h) * QBLOCK
            d_att[start : start + QBLOCK, :] = part[b * QBLOCK : (b + 1) * QBLOCK, :]
    block = keep.shape[2]
    for c, f, x, core, row, mid in relative_blocks(at, fsdp):
        start = multiple(((row * 2 + core) * 2 + mid) * block, 16)
        target = keep if c == 0 else send
        target[f, x] = dot(att_t[pl.ds(start, block), :], d_proj).astype(BF16)


def attend_back_kernel(halo, heads, d_att, q_st, keys, values, probs, d_q, d_k, d_v, d_scores):
    rows = d_q.shape[0]
    dim = keys.shape[1]
    blocks = rows // QBLOCK
    span = WINDOW + QBLOCK
    scale = dim ** (-0.5)
    d_k[...] = jnp.zeros(d_k.shape, F32)
    d_v[...] = jnp.zeros(d_v.shape, F32)
    for b in range(blocks):
        first_key = halo - WINDOW + b * QBLOCK
        here = slice(first_key, first_key + span)
        for h in range(heads):
            start = (b * heads + h) * QBLOCK
            stack = slice(start, start + QBLOCK)
            d_probs = dot_nt(d_att[stack, :], values[here, :])
            p = probs[stack, :].astype(F32)
            row_terms = jnp.sum(p * d_probs, axis=-1, keepdims=True)
            ds = (p * (d_probs - row_terms) * scale).astype(BF16)
            d_scores[h * QBLOCK : (h + 1) * QBLOCK, :] = ds
            d_q[b * QBLOCK : (b + 1) * QBLOCK, h * dim : (h + 1) * dim] = dot(ds, keys[here, :])
        stack = slice(b * heads * QBLOCK, (b + 1) * heads * QBLOCK)
        d_k[here, :] += dot_tn(d_scores[...], q_st[stack, :])
        d_v[here, :] += dot_tn(probs[stack, :], d_att[stack, :])


def last_kernel(n_qkv, n_tok, fsdp, heads, *refs):
    (
        at, d_residual, d_q, d_k, d_v,
        q_raw, k_raw, cosine, sine, gain_q, gain_k, gain_in, normed, g_ffn, g_attn, g_out,
    ) = refs[:16]
    toks = refs[16 : 16 + n_tok]
    refs = refs[16 + n_tok :]
    qkv_w, refs = refs[:n_qkv], refs[n_qkv:]
    grad_tokens, d_halo, keep, send = refs[:4]
    w_full, normed_t, d_qkv, gain_rows, qkv_sems = refs[4:]
    copies = place_copies(qkv_w[:3], qkv_w[3:], w_full, qkv_sems, at, 1, 4)
    for copy in copies:
        copy.start()
    normed_t[...] = normed[...].T
    rows = toks[0].shape[0]
    halo = (n_tok - 1) * rows
    dim = k_raw.shape[1]
    half = dim // 2
    tall, wide = normed_t.shape[0] // fsdp, keep.shape[3]
    def turned_back(u, g, dz, cos, sin):
        first, second = dz[:, :half], dz[:, half:]
        dz = jnp.concatenate([first * cos + second * sin, second * cos - first * sin], axis=1)
        return norm_back(u, g, dz)

    total_q = jnp.zeros((1, dim), F32)
    if halo:
        d_qkv[:halo, : heads * dim] = jnp.zeros((halo, heads * dim), BF16)
    for h in range(heads):
        cut = slice(h * dim, (h + 1) * dim)
        du, dg = turned_back(q_raw[:, cut], gain_q[...], d_q[:, cut], cosine[halo:, :], sine[halo:, :])
        total_q += dg
        d_qkv[halo:, cut] = du.astype(BF16)
    total_k = jnp.zeros((1, dim), F32)
    for i in range(n_tok):
        here = slice(i * rows, (i + 1) * rows)
        du, dg = turned_back(k_raw[here, :], gain_k[...], d_k[here, :], cosine[here, :], sine[here, :])
        total_k += dg
        d_qkv[here, heads * dim : (heads + 1) * dim] = du.astype(BF16)
        d_qkv[here, (heads + 1) * dim :] = d_v[here, :].astype(BF16)
    column_blocks(at, fsdp, normed_t, d_qkv, keep, send)
    for copy in copies:
        copy.wait()
    total_in = jnp.zeros(gain_in.shape, F32)
    for i in range(n_tok):
        here = slice(i * rows, (i + 1) * rows)
        if i < n_tok - 1:
            d_normed = dot_nt(d_qkv[here, heads * dim :], w_full[:, heads * dim :])
        else:
            d_normed = dot_nt(d_qkv[here, :], w_full[...])
        du, dg = norm_back(toks[i][...].astype(F32), gain_in[...], d_normed)
        total_in += dg
        if i < n_tok - 1:
            d_halo[here, :] = du.astype(BF16)
        else:
            grad_tokens[...] = d_residual[...] + du
    gain_rows[...] = jnp.zeros(gain_rows.shape, F32)
    at_row = 0
    for total in (total_in, total_q, total_k, g_attn[...], g_ffn[...], g_out[...]):
        for i in range(total.shape[1] // LANES):
            gain_rows[at_row : at_row + 1, :LANES] = total[:, i * LANES : (i + 1) * LANES]
            at_row += 1
    packed = gain_rows[...].astype(BF16)
    for target in (keep, send):
        for f in range(fsdp):
            for x in range(2):
                target[f, x, tall:, :] = packed


def add(*terms):
    out = terms[0].astype(F32)
    for term in terms[1:]:
        out = out + term.astype(F32)
    return out


class Chunk:
    def __init__(self, here, keep, send):
        self.here, self.keep = here, keep
        self.other = here.core_swap(send)
        self.sums = []

    def over_fsdp(self, *earlier):
        here = self.here
        parts = [add(self.keep[by], self.other[by]).astype(BF16) for by in range(1, here.fsdp)]
        self.arrived = [here.fsdp_shift(after(part, *earlier), by + 1) for by, part in enumerate(parts)]

    def over_mid(self, *earlier):
        self.arrived = [after(a, *earlier) for a in self.arrived]
        terms = [self.keep[0, 1], self.other[0, 1]] + [a[1] for a in self.arrived]
        self.across = self.here.mid_swap(add(*terms).astype(BF16))

    def gather_sums(self, bit, *earlier):
        here = self.here
        if bit == 0:
            self.across = after(self.across, *earlier)
            terms = [self.keep[0, 0], self.other[0, 0]] + [a[0] for a in self.arrived] + [self.across]
        else:
            terms = [after(self.sums[-1], *earlier)]
        n, w = terms[0].shape
        halves = [term.reshape(2, n // 2, w) for term in terms]
        off = add(*[pick(half, here.bit_off[bit]) for half in halves]).astype(BF16)
        came = here.outer_swap(off, bit)
        self.sums.append(add(*[pick(half, here.bit_at[bit]) for half in halves], came).astype(BF16))

    def finish(self, *earlier, last=()):
        here = self.here
        for bit in range(len(self.sums), here.bits):
            self.gather_sums(bit, *earlier)
        block = self.sums[-1]
        for bit in reversed(range(here.bits)):
            n, w = block.shape
            both = [block, here.outer_swap(block, bit)]
            low, high = jnp.concatenate(both), jnp.concatenate(both[::-1])
            block = jnp.where(here.bit_at[bit] == 0, low, high)
        block = after(block, *last)
        across = here.mid_swap(block)
        return [[block, across], [here.core_swap(block), here.core_swap(across)]]


def by_place(here, blocks):
    own = [jnp.where(here.mid_at == 0, a, b) for a, b in blocks]
    other = [jnp.where(here.mid_at == 0, b, a) for a, b in blocks]
    pairs = list(zip(own, other))
    first = [jnp.where(here.core_at == 0, a, b) for a, b in zip(pairs[0], pairs[1])]
    second = [jnp.where(here.core_at == 0, b, a) for a, b in zip(pairs[0], pairs[1])]
    return first + second


def on_device(
    tokens, positions, cotangent, in_gain, w_query, w_key, w_value, query_gain, key_gain, w_out, attn_gain,
    ffn_gain_in, w_gate, w_up, w_down, ffn_gain_out,
):
    here = Places()
    fsdp = here.fsdp
    rows, width = tokens.shape
    dim = w_key.shape[1]
    query_cols = w_query.shape[1]
    heads = query_cols // dim
    hidden = w_gate.shape[1]
    hops = (WINDOW + rows - 1) // rows
    n_tok = hops + 1
    halo = hops * rows
    every = halo + rows
    at = here.vector

    gains = (in_gain, query_gain, key_gain, attn_gain, ffn_gain_in, ffn_gain_out)
    cuts = [0]
    for gain in gains:
        cuts.append(cuts[-1] + gain.shape[0])
    gain_row = jnp.concatenate(gains)
    gain_rows = ordered([gain_row] + [here.fsdp_shift(gain_row, by) for by in range(1, fsdp)], here.fsdp_behind)
    gain_rows = gain_rows.astype(F32)
    gain_in, gain_q, gain_k, gain_attn, gain_ffn, gain_out = (
        gain_rows[:, cuts[i] : cuts[i + 1]].reshape(1, -1) for i in range(6)
    )
    qkv_w = [w_query, w_key, w_value]
    qkv_part = own_part(here, qkv_w, 1, 4)
    tokens_out = after(tokens, qkv_part)
    toks = [linear_shift(tokens_out, by) for by in range(hops, 0, -1)] + [tokens]
    qkv_w += on_chips(here, over_links(here, qkv_part), 4)
    out_arrived = over_links(here, after(own_part(here, [w_out], 0, 2), *toks[:-1]))
    gate_arrived = over_links(here, after(own_part(here, [w_gate], 1, 4), qkv_w[3]))
    up_arrived = over_links(here, after(own_part(here, [w_up], 1, 4), out_arrived[0]))

    all_positions = jnp.concatenate([positions[0] - halo + jnp.arange(halo, dtype=jnp.int32), positions])
    frequency = ROPE_BASE ** (-(jnp.arange(dim // 2, dtype=F32) * 2.0 / dim))
    angles = all_positions.astype(F32)[:, None] * frequency[None, :]
    cosine, sine = jnp.cos(angles), jnp.sin(angles)

    span = WINDOW + QBLOCK
    weight_bytes = 2 * fsdp * w_gate.size
    normed, q_raw, k_raw, q_st, keys, values, probs, attended = pl.pallas_call(
        functools.partial(attend_kernel, n_tok, len(qkv_w), heads),
        out_shape=(
            shape((every, width), BF16),
            shape((rows, query_cols), F32),
            shape((every, dim), F32),
            shape((heads * rows, dim), BF16),
            shape((every, dim), BF16),
            shape((every, dim), BF16),
            shape((heads * rows, span), BF16),
            shape((rows, query_cols), BF16),
        ),
        in_specs=[SMEM] + [VMEM] * (n_tok + 6) + [ANY] * len(qkv_w),
        out_specs=(VMEM,) * 8,
        scratch_shapes=[
            pltpu.VMEM((width, query_cols + 2 * dim), BF16),
            pltpu.SemaphoreType.DMA((len(qkv_w),)),
        ],
        compiler_params=params(),
        cost_estimate=cost(4e9, 1e7),
        name="attend",
    )(at, *toks, positions[:, None], cosine, sine, gain_in, gain_q, gain_k, *qkv_w)

    down_arrived = over_links(here, after(own_part(here, [w_down], 0, 2), attended))
    out_w = [w_out] + on_chips(here, [after(a, attended) for a in out_arrived], 2)
    gate_w = [w_gate] + on_chips(here, [after(a, attended) for a in gate_arrived], 4)
    up_w = [w_up] + on_chips(here, [after(a, attended) for a in up_arrived], 4)
    projected, residual, ffn_in, mixed, gelu_out, gate_slope = pl.pallas_call(
        functools.partial(gate_kernel, len(out_w), len(gate_w), len(up_w)),
        out_shape=(
            shape((rows, width), F32),
            shape((rows, width), F32),
            shape((rows, width), BF16),
            shape((rows, hidden), BF16),
            shape((rows, hidden), BF16),
            shape((rows, hidden), BF16),
        ),
        in_specs=[SMEM] + [VMEM] * 4 + [ANY] * (len(out_w) + len(gate_w) + len(up_w)),
        out_specs=(VMEM,) * 6,
        scratch_shapes=[
            pltpu.VMEM((query_cols, width), BF16),
            pltpu.VMEM((width, hidden), BF16),
            pltpu.VMEM((width, hidden), BF16),
            pltpu.SemaphoreType.DMA((len(out_w),)),
            pltpu.SemaphoreType.DMA((len(gate_w),)),
            pltpu.SemaphoreType.DMA((len(up_w),)),
        ],
        compiler_params=params(),
        cost_estimate=cost(4e9, 2 * weight_bytes),
        name="gate",
    )(at, attended, tokens, gain_attn, gain_ffn, *out_w, *gate_w, *up_w)

    down_w = [w_down] + on_chips(here, [after(a, mixed) for a in down_arrived], 2)
    down_block = w_down.shape[0] // 4
    down_shape = shape((fsdp, 2, down_block, width), BF16)
    layer_out, d_down, g_ffn_out, down_keep, down_send = pl.pallas_call(
        functools.partial(down_kernel, len(down_w), fsdp),
        out_shape=(
            shape((rows, width), BF16),
            shape((rows, width), BF16),
            shape((1, width), F32),
            down_shape,
            down_shape,
        ),
        in_specs=[SMEM] + [VMEM] * 4 + [ANY] * len(down_w),
        out_specs=(VMEM,) * 5,
        scratch_shapes=[
            pltpu.VMEM((hidden, width), BF16),
            pltpu.VMEM((hidden, rows), BF16),
            pltpu.SemaphoreType.DMA((len(down_w),)),
        ],
        compiler_params=params(),
        cost_estimate=cost(4e9, 2 * weight_bytes),
        name="down",
    )(at, mixed, residual, cotangent, gain_out, *down_w)

    down_sum = Chunk(here, down_keep, down_send)
    gate_shape = shape((fsdp, 2, w_gate.shape[0], hidden // 4), BF16)
    d_gate, d_up, ffn_t, gate_keep, gate_send = pl.pallas_call(
        functools.partial(gate_back_kernel, len(down_w), fsdp),
        out_shape=(
            shape((rows, hidden), BF16),
            shape((rows, hidden), BF16),
            shape((width, rows), BF16),
            gate_shape,
            gate_shape,
        ),
        in_specs=[SMEM] + [VMEM] * 4 + [ANY] * len(down_w),
        out_specs=(VMEM,) * 5,
        scratch_shapes=[
            pltpu.VMEM((hidden, width), BF16),
            pltpu.SemaphoreType.DMA((len(down_w),)),
        ],
        compiler_params=params(),
        cost_estimate=cost(6e9, 3 * weight_bytes),
        name="gate_back",
    )(at, d_down, gelu_out, gate_slope, ffn_in, *down_w)
    gate_sum = Chunk(here, gate_keep, gate_send)
    up_keep, up_send = pl.pallas_call(
        functools.partial(up_back_kernel, fsdp),
        out_shape=(gate_shape, gate_shape),
        in_specs=[SMEM] + [VMEM] * 2,
        out_specs=(VMEM,) * 2,
        compiler_params=params(),
        cost_estimate=cost(6e9, 3 * weight_bytes),
        name="up_back",
    )(at, ffn_t, after(d_up, down_sum.other))
    up_sum = Chunk(here, up_keep, up_send)
    down_sum.over_fsdp(d_gate)
    d_gate = after(d_gate, gate_sum.other, up_keep)

    qkv_cols = query_cols + 2 * dim
    last_wide = qkv_cols // 4
    shard_rows = w_query.shape[0]
    last_shape = shape((fsdp, 2, shard_rows + GAIN_ROWS, last_wide), BF16)
    out_shape = shape((fsdp, 2, w_out.shape[0] // 4, width), BF16)
    d_residual, g_ffn, g_attn, d_att, out_keep, out_send = pl.pallas_call(
        functools.partial(middle_kernel, len(out_w), len(gate_w), len(up_w), fsdp, heads),
        out_shape=(
            shape((rows, width), F32),
            shape((1, width), F32),
            shape((1, width), F32),
            shape((heads * rows, dim), BF16),
            out_shape,
            out_shape,
        ),
        in_specs=[SMEM] + [VMEM] * 8 + [ANY] * (len(out_w) + len(gate_w) + len(up_w)),
        out_specs=(VMEM,) * 6,
        scratch_shapes=[
            pltpu.VMEM((query_cols, width), BF16),
            pltpu.VMEM((width, hidden), BF16),
            pltpu.VMEM((width, hidden), BF16),
            pltpu.VMEM((query_cols, rows), BF16),
            pltpu.SemaphoreType.DMA((len(out_w),)),
            pltpu.SemaphoreType.DMA((len(gate_w),)),
            pltpu.SemaphoreType.DMA((len(up_w),)),
        ],
        compiler_params=params(),
        cost_estimate=cost(6e9, 4 * weight_bytes),
        name="middle",
    )(at, d_gate, d_up, residual, projected, cotangent, gain_ffn, gain_attn, attended, *out_w, *gate_w, *up_w)

    out_sum = Chunk(here, out_keep, out_send)
    gate_sum.over_fsdp(up_keep)
    d_q, d_k, d_v = pl.pallas_call(
        functools.partial(attend_back_kernel, halo, heads),
        out_shape=(shape((rows, query_cols), F32), shape((every, dim), F32), shape((every, dim), F32)),
        in_specs=[VMEM] * 5,
        out_specs=(VMEM,) * 3,
        scratch_shapes=[pltpu.VMEM((heads * QBLOCK, span), BF16)],
        compiler_params=params(),
        cost_estimate=cost(6e9, 3 * weight_bytes),
        name="attend_back",
    )(after(d_att, up_sum.other, *down_sum.arrived), q_st, keys, values, probs)
    down_sum.over_mid(g_ffn)
    up_sum.over_fsdp(g_ffn)
    d_k_token = d_k
    d_q = after(d_q, out_sum.other, down_sum.across, *gate_sum.arrived)
    gate_sum.over_mid(d_k_token)
    out_sum.over_fsdp(d_k_token)
    grad_tokens, d_halo, last_keep, last_send = pl.pallas_call(
        functools.partial(last_kernel, len(qkv_w), n_tok, fsdp, heads),
        out_shape=(
            shape((rows, width), F32),
            shape((halo, width), BF16),
            last_shape,
            last_shape,
        ),
        in_specs=[SMEM] + [VMEM] * (15 + n_tok) + [ANY] * len(qkv_w),
        out_specs=(VMEM,) * 4,
        scratch_shapes=[
            pltpu.VMEM((width, qkv_cols), BF16),
            pltpu.VMEM((width, every), BF16),
            pltpu.VMEM((every, qkv_cols), BF16),
            pltpu.VMEM((GAIN_ROWS, last_wide), F32),
            pltpu.SemaphoreType.DMA((len(qkv_w),)),
        ],
        compiler_params=params(),
        cost_estimate=cost(15e9, 4 * weight_bytes),
        name="last",
    )(
        at, d_residual, d_q, d_k, d_v,
        q_raw, k_raw, cosine, sine, gain_q, gain_k, gain_in, normed, g_ffn, g_attn, g_ffn_out, *toks, *qkv_w,
    )

    last_sum = Chunk(here, last_keep, last_send)
    last_sum.over_fsdp()
    arrived = last_sum.other
    down_blocks = by_place(here, down_sum.finish(arrived))
    gate_blocks = by_place(here, gate_sum.finish(arrived, last=last_sum.arrived))
    up_sum.over_mid(arrived)
    out_sum.over_mid(arrived)
    up_blocks = by_place(here, up_sum.finish())
    out_blocks = by_place(here, out_sum.finish())
    last_sum.over_mid()
    last_blocks = last_sum.finish()
    total_gains = last_blocks[0][0][shard_rows:, :LANES].astype(F32)
    last_blocks = by_place(here, last_blocks)

    for by in range(1, hops + 1):
        start = halo - by * rows
        came = linear_shift(after(d_halo[start : start + rows], arrived), -by)
        grad_tokens = grad_tokens + after(came, *last_sum.arrived).astype(F32)

    total_down = jnp.concatenate(down_blocks, axis=0).astype(F32)
    total_gate = jnp.concatenate(gate_blocks, axis=1).astype(F32)
    total_up = jnp.concatenate(up_blocks, axis=1).astype(F32)
    total_qkv = jnp.concatenate([b[:shard_rows] for b in last_blocks], axis=1).astype(F32)
    total_out = jnp.concatenate(out_blocks, axis=0).astype(F32)
    g, at_row = [], 0
    for gain in gains:
        deep = fsdp * gain.shape[0] // total_gains.shape[1]
        total = total_gains[at_row : at_row + deep].reshape(fsdp, gain.shape[0])
        g.append(pick(total, here.fsdp_at))
        at_row += deep
    return (
        layer_out, grad_tokens, g[0],
        total_qkv[:, :query_cols],
        total_qkv[:, query_cols : query_cols + dim],
        total_qkv[:, query_cols + dim :],
        g[1], g[2], total_out, g[3], g[4], total_gate, total_up, total_down, g[5],
    )


def solution(mesh):
    tok = P(("seq", "fsdp"), None)
    mat = P("fsdp", None)
    vec = P("fsdp")
    return jax.shard_map(
        on_device,
        mesh=mesh,
        in_specs=(tok, P(("seq", "fsdp")), tok, vec, mat, mat, mat, vec, vec, mat, vec, vec, mat, mat, mat, vec),
        out_specs=(tok, tok, vec, mat, mat, mat, vec, vec, mat, vec, vec, mat, mat, mat, vec),
        check_vma=False,
    )
```

```python
import functools
import math

import jax
import jax.numpy as jnp
from jax import lax
from jax.experimental import pallas as pl
from jax.experimental.pallas import tpu as pltpu
from jax.sharding import PartitionSpec as P

WINDOW = 512
EPSILON = 1e-06
ROPE_BASE = 10000.0
MASKED = -1e30
BF16 = jnp.bfloat16
F32 = jnp.float32
QBLOCK = 128
LANES = 128
GAIN_ROWS = 32
GELU_A = math.sqrt(2.0 / math.pi)
GELU_B = 0.044715

VMEM = pl.BlockSpec(memory_space=pltpu.VMEM)
SMEM = pl.BlockSpec(memory_space=pltpu.SMEM)
ANY = pl.BlockSpec(memory_space=pl.ANY)


def wrapped(value, size):
    return value & (size - 1) if size & (size - 1) == 0 else lax.rem(value, jnp.int32(size))


class Places:
    def __init__(self):
        self.seq = lax.axis_size("seq")
        self.fsdp = lax.axis_size("fsdp")
        self.outer = self.seq // 4
        index = lax.axis_index("seq").astype(jnp.int32)
        fsdp_at = lax.axis_index("fsdp").astype(jnp.int32)
        outer_at = lax.shift_right_logical(index, 2)
        core_at, mid_at = index & 1, lax.shift_right_logical(index, 1) & 1
        scalars = lax.optimization_barrier(
            (
                core_at,
                mid_at,
                fsdp_at,
                core_at * 2 + mid_at,
                tuple(wrapped(outer_at + by, self.outer) for by in range(self.outer)),
                tuple(wrapped(outer_at - by + self.outer, self.outer) for by in range(self.outer)),
                tuple(wrapped(fsdp_at + by, self.fsdp) for by in range(self.fsdp)),
                tuple(wrapped(fsdp_at - by + self.fsdp, self.fsdp) for by in range(self.fsdp)),
                jnp.stack([core_at, mid_at, fsdp_at]),
            )
        )
        self.core_at, self.mid_at, self.fsdp_at, self.quarter_at = scalars[:4]
        self.outer_ahead, self.outer_behind, self.fsdp_ahead, self.fsdp_behind, self.vector = scalars[4:]

    def core_swap(self, array):
        return lax.ppermute(array, "seq", [(i, i ^ 1) for i in range(self.seq)])

    def mid_swap(self, array):
        return lax.ppermute(array, "seq", [(i, i ^ 2) for i in range(self.seq)])

    def outer_shift(self, array, by):
        return lax.ppermute(array, "seq", [(i, (i + 4 * by) % self.seq) for i in range(self.seq)])

    def fsdp_shift(self, array, by):
        return lax.ppermute(array, "fsdp", [(i, (i + by) % self.fsdp) for i in range(self.fsdp)])


def linear_shift(array, by):
    count = lax.axis_size("seq") * lax.axis_size("fsdp")
    return lax.ppermute(array, ("seq", "fsdp"), [(i, i + by) for i in range(count) if 0 <= i + by < count])


def pick(array, at):
    return lax.dynamic_index_in_dim(array, at, 0, keepdims=False, allow_negative_indices=False)


def ordered(pieces, behind):
    if len(pieces) == 2:
        own, other = pieces
        return jnp.where(behind[0] == 0, jnp.stack([own, other]), jnp.stack([other, own]))
    stacked = jnp.stack(pieces)
    return jnp.stack([pick(stacked, at) for at in behind])


def own_part(here, shards, axis, ways):
    size = sum(shard.shape[axis] for shard in shards) // ways
    place = here.quarter_at if ways == 4 else here.core_at
    if len(shards) == 1:
        return lax.dynamic_slice_in_dim(shards[0], place * size, size, axis, allow_negative_indices=False)
    parts = []
    for i in range(ways):
        pieces, start = [], 0
        for shard in shards:
            low, high = max(i * size - start, 0), min((i + 1) * size - start, shard.shape[axis])
            if low < high:
                pieces.append(lax.slice_in_dim(shard, low, high, axis=axis))
            start += shard.shape[axis]
        parts.append(jnp.concatenate(pieces, axis))
    return functools.reduce(lambda rest, i: jnp.where(place == i, parts[i], rest), range(1, ways), parts[0])


def after(value, *earlier):
    return lax.optimization_barrier((value, *earlier))[0]


def together(*groups):
    return lax.optimization_barrier(tuple(tuple(group) for group in groups))


def over_links(here, part):
    return [here.fsdp_shift(part, by) for by in range(1, here.fsdp)]


def on_chips(here, arrived, ways):
    pieces = []
    for mine in arrived:
        if ways == 4:
            across = here.mid_swap(mine)
            pieces += [mine, across, here.core_swap(mine), here.core_swap(across)]
        else:
            pieces += [mine, here.core_swap(mine)]
    return pieces


def multiple(value, of):
    return pl.multiple_of(value, of)


def place_copies(owned, pieces, whole, sems, at, axis, ways):
    core, mid, fsdp = at[0], at[1], at[2]
    count = 1 + len(pieces) // ways
    rows = owned[0].shape[0]
    copies = []
    column = 0
    own_row = multiple(fsdp * rows, 16)
    for shard in owned:
        wide = shard.shape[1]
        copies.append((shard, whole.at[pl.ds(own_row, rows), pl.ds(column, wide)]))
        column += wide
    for k, piece in enumerate(pieces):
        by = 1 + k // ways
        row = multiple(lax.rem(fsdp + (count - by), count) * rows, 16)
        k = k % ways
        if ways == 4:
            place = (core if k < 2 else 1 - core) * 2 + (mid if k % 2 == 0 else 1 - mid)
        else:
            place = core if k == 0 else 1 - core
        if axis == 0:
            target = whole.at[pl.ds(multiple(row + place * (rows // ways), 16), rows // ways), :]
        else:
            target = whole.at[pl.ds(row, rows), pl.ds(multiple(place * (column // ways), 128), column // ways)]
        copies.append((piece, target))
    return [pltpu.make_async_copy(a, b, sems.at[k]) for k, (a, b) in enumerate(copies)]


def dot(a, b):
    return lax.dot_general(a, b, (((1,), (0,)), ((), ())), preferred_element_type=F32)


def dot_nt(a, b):
    return lax.dot_general(a, b, (((1,), (1,)), ((), ())), preferred_element_type=F32)


def dot_tn(a, b):
    return lax.dot_general(a, b, (((0,), (0,)), ((), ())), preferred_element_type=F32)


def inverse_rms(u):
    return lax.rsqrt(jnp.mean(u * u, axis=-1, keepdims=True) + EPSILON)


def norm_back(u, g, dz):
    r = inverse_rms(u)
    ur = u * r
    gdz = g * dz
    du = r * (gdz - ur * jnp.mean(gdz * ur, axis=-1, keepdims=True))
    return du, jnp.sum(dz * ur, axis=0, keepdims=True)


def params(megabytes=56):
    return pltpu.CompilerParams(vmem_limit_bytes=megabytes * 1024 * 1024)


def cost(flops, bytes_accessed):
    return pl.CostEstimate(flops=int(20 * flops), bytes_accessed=int(20 * bytes_accessed), transcendentals=0)


def shape(dims, kind):
    return jax.ShapeDtypeStruct(tuple(dims), kind)


def attend_kernel(n_tok, n_qkv, heads, *refs):
    at = refs[0]
    toks = refs[1 : 1 + n_tok]
    pos, cosine, sine, gain_table = refs[1 + n_tok : 5 + n_tok]
    qkv = refs[5 + n_tok : 5 + n_tok + n_qkv]
    normed, q_raw, k_raw, q_st, keys, values, probs, attended, w_full, sems = refs[5 + n_tok + n_qkv :]
    copies = place_copies(qkv[:3], qkv[3:], w_full, sems, at, 1, 2)
    for copy in copies:
        copy.start()
    rows = toks[0].shape[0]
    dim = keys.shape[1]
    half = dim // 2
    halo = (n_tok - 1) * rows
    gain = gain_table[0:1, :]
    gain_q, gain_k = gain_table[1:2, :dim], gain_table[2:3, :dim]
    for i, tok in enumerate(toks):
        u = tok[...].astype(F32)
        normed[i * rows : (i + 1) * rows, :] = (u * inverse_rms(u) * gain).astype(BF16)
    for copy in copies:
        copy.wait()

    def turned(u, g, cos, sin):
        u = u * inverse_rms(u) * g
        first, second = u[:, :half], u[:, half:]
        return (first * cos - second * sin).astype(BF16), (second * cos + first * sin).astype(BF16)

    for i in range(n_tok):
        here = slice(i * rows, (i + 1) * rows)
        kv = dot(normed[here, :], w_full[:, heads * dim :])
        k_raw[here, :] = kv[:, :dim]
        values[here, :] = kv[:, dim:].astype(BF16)
        first, second = turned(kv[:, :dim], gain_k, cosine[here, :], sine[here, :])
        keys[here, :half] = first
        keys[here, half:] = second
    blocks = rows // QBLOCK
    for h in range(heads):
        u = dot(normed[halo:, :], w_full[:, h * dim : (h + 1) * dim])
        q_raw[:, h * dim : (h + 1) * dim] = u
        first, second = turned(u, gain_q, cosine[halo:, :], sine[halo:, :])
        for b in range(blocks):
            start = (b * heads + h) * QBLOCK
            q_st[start : start + QBLOCK, :half] = first[b * QBLOCK : (b + 1) * QBLOCK, :]
            q_st[start : start + QBLOCK, half:] = second[b * QBLOCK : (b + 1) * QBLOCK, :]
    span = WINDOW + QBLOCK
    distance = (
        lax.broadcasted_iota(jnp.int32, (QBLOCK, span), 0)
        + WINDOW
        - lax.broadcasted_iota(jnp.int32, (QBLOCK, span), 1)
    )
    scale = dim ** (-0.5)
    for b in range(blocks):
        first_key = halo - WINDOW + b * QBLOCK
        limit = jnp.minimum(pos[b * QBLOCK : (b + 1) * QBLOCK, :], WINDOW - 1)
        allowed = (distance >= 0) & (distance <= limit)
        for h in range(heads):
            start = (b * heads + h) * QBLOCK
            scores = dot_nt(q_st[start : start + QBLOCK, :], keys[first_key : first_key + span, :]) * scale
            scores = jnp.where(allowed, scores, MASKED)
            weights = jnp.exp(scores - jnp.max(scores, axis=-1, keepdims=True))
            weights = (weights * (1.0 / jnp.sum(weights, axis=-1, keepdims=True))).astype(BF16)
            probs[start : start + QBLOCK, :] = weights
            attended[b * QBLOCK : (b + 1) * QBLOCK, h * dim : (h + 1) * dim] = dot(
                weights, values[first_key : first_key + span, :]
            ).astype(BF16)


def gate_kernel(n_out, n_gate, n_up, *refs):
    at, attended, tokens, gain_table = refs[:4]
    refs = refs[4:]
    out_w, gate_w, up_w, refs = (
        refs[:n_out],
        refs[n_out : n_out + n_gate],
        refs[n_out + n_gate : n_out + n_gate + n_up],
        refs[n_out + n_gate + n_up :],
    )
    projected_ref, residual_ref, ffn_in_ref, mixed, gelu_out, gate_slope = refs[:6]
    out_full, gate_full, up_full, out_sems, gate_sems, up_sems = refs[6:]
    groups = (
        place_copies(out_w[:1], out_w[1:], out_full, out_sems, at, 0, 2),
        place_copies(gate_w[:1], gate_w[1:], gate_full, gate_sems, at, 1, 4),
        place_copies(up_w[:1], up_w[1:], up_full, up_sems, at, 1, 2),
    )
    for group in groups:
        for copy in group:
            copy.start()
    for copy in groups[0]:
        copy.wait()
    projected = dot(attended[...], out_full[...])
    projected_ref[...] = projected
    residual = tokens[...].astype(F32) + projected * inverse_rms(projected) * gain_table[3:4, :]
    residual_ref[...] = residual
    ffn_in_ref[...] = (residual * inverse_rms(residual) * gain_table[4:5, :]).astype(BF16)
    for group in groups[1:]:
        for copy in group:
            copy.wait()
    width = 256

    def step(i, _):
        cut = pl.ds(multiple(i * width, width), width)
        gate = dot(ffn_in_ref[...], gate_full[:, cut])
        up = dot(ffn_in_ref[...], up_full[:, cut])
        square = gate * gate
        t = jnp.tanh(GELU_A * gate * (1.0 + GELU_B * square))
        cdf = 0.5 * (1.0 + t)
        act = gate * cdf
        slope = cdf + 0.5 * gate * (1.0 - t * t) * (GELU_A * (1.0 + 3.0 * GELU_B * square))
        mixed[:, cut] = (act * up).astype(BF16)
        gelu_out[:, cut] = act.astype(BF16)
        gate_slope[:, cut] = (up * slope).astype(BF16)
        return 0

    lax.fori_loop(0, gate_full.shape[1] // width, step, 0)


def relative_blocks(at, fsdp):
    for c in range(2):
        core = c + at[0] - 2 * c * at[0]
        for f in range(fsdp):
            row = lax.rem(at[2] + f, fsdp)
            for x in range(2):
                mid = x + at[1] - 2 * x * at[1]
                yield c, f, x, core, row, mid


def column_blocks(at, fsdp, left_t, right, keep, send):
    tall, wide = left_t.shape[0] // fsdp, keep.shape[3]
    for c, f, x, core, row, mid in relative_blocks(at, fsdp):
        cut = pl.ds(multiple((core * 2 + mid) * wide, 128), wide)
        left = left_t[pl.ds(multiple(row * tall, 16), tall), :]
        target = keep if c == 0 else send
        target[f, x, :tall, :] = dot(left, right[:, cut]).astype(BF16)


def down_kernel(n_down, fsdp, *refs):
    at, mixed, residual, cotangent, gain_table = refs[:5]
    down_w = refs[5 : 5 + n_down]
    layer_out, d_down, grad_gain, keep, send = refs[5 + n_down : 10 + n_down]
    down_full, mixed_t, sems = refs[10 + n_down :]
    copies = place_copies(down_w[:1], down_w[1:], down_full, sems, at, 0, 2)
    for copy in copies:
        copy.start()
    mixed_t[...] = mixed[...].T
    for copy in copies:
        copy.wait()
    down = dot(mixed[...], down_full[...])
    r = inverse_rms(down)
    gain = gain_table[5:6, :]
    layer_out[...] = (residual[...] + down * r * gain).astype(BF16)
    du, dg = norm_back(down, gain, cotangent[...].astype(F32))
    grad_gain[...] = dg
    d_down[...] = du.astype(BF16)
    block = keep.shape[2]
    for c, f, x, core, row, mid in relative_blocks(at, fsdp):
        start = multiple(((row * 2 + core) * 2 + mid) * block, 16)
        target = keep if c == 0 else send
        target[f, x] = dot(mixed_t[pl.ds(start, block), :], d_down[...]).astype(BF16)


def gate_back_kernel(n_down, fsdp, *refs):
    at, d_down, gelu_out, gate_slope, ffn_in = refs[:5]
    down_w = refs[5 : 5 + n_down]
    d_gate, d_up, keep, send, up_keep, up_send = refs[5 + n_down : 11 + n_down]
    down_full, ffn_t, sems = refs[11 + n_down :]
    copies = place_copies(down_w[:1], down_w[1:], down_full, sems, at, 0, 2)
    for copy in copies:
        copy.start()
    ffn_t[...] = ffn_in[...].T
    for copy in copies:
        copy.wait()
    width = 256

    def step(i, _):
        cut = pl.ds(multiple(i * width, width), width)
        d_mixed = dot_nt(d_down[...], down_full[cut, :])
        d_gate[:, cut] = (d_mixed * gate_slope[:, cut].astype(F32)).astype(BF16)
        d_up[:, cut] = (d_mixed * gelu_out[:, cut].astype(F32)).astype(BF16)
        return 0

    lax.fori_loop(0, d_gate.shape[1] // width, step, 0)
    column_blocks(at, fsdp, ffn_t, d_gate, keep, send)
    column_blocks(at, fsdp, ffn_t, d_up, up_keep, up_send)


def middle_kernel(n_out, n_gate, n_up, fsdp, heads, *refs):
    at, d_gate, d_up, residual, projected, cotangent, gain_table, attended = refs[:8]
    refs = refs[8:]
    out_w, gate_w, up_w, refs = (
        refs[:n_out],
        refs[n_out : n_out + n_gate],
        refs[n_out + n_gate : n_out + n_gate + n_up],
        refs[n_out + n_gate + n_up :],
    )
    d_residual_ref, g_ffn, g_attn, d_att, keep, send = refs[:6]
    out_full, gate_full, up_full, att_t, out_sems, gate_sems, up_sems = refs[6:]
    groups = (
        place_copies(gate_w[:1], gate_w[1:], gate_full, gate_sems, at, 1, 4),
        place_copies(up_w[:1], up_w[1:], up_full, up_sems, at, 1, 2),
        place_copies(out_w[:1], out_w[1:], out_full, out_sems, at, 0, 2),
    )
    for group in groups:
        for copy in group:
            copy.start()
    att_t[...] = attended[...].T
    for copy in groups[0]:
        copy.wait()
    d_ffn_in = dot_nt(d_gate[...], gate_full[...])
    for copy in groups[1]:
        copy.wait()
    d_ffn_in = d_ffn_in + dot_nt(d_up[...], up_full[...])
    du, dg = norm_back(residual[...], gain_table[4:5, :], d_ffn_in)
    g_ffn[...] = dg
    d_residual = cotangent[...].astype(F32) + du
    d_residual_ref[...] = d_residual
    du, dg = norm_back(projected[...], gain_table[3:4, :], d_residual)
    g_attn[...] = dg
    d_proj = du.astype(BF16)
    rows, dim = d_proj.shape[0], d_att.shape[1]
    for copy in groups[2]:
        copy.wait()
    for h in range(heads):
        part = dot_nt(d_proj, out_full[h * dim : (h + 1) * dim, :]).astype(BF16)
        for b in range(rows // QBLOCK):
            start = (b * heads + h) * QBLOCK
            d_att[start : start + QBLOCK, :] = part[b * QBLOCK : (b + 1) * QBLOCK, :]
    block = att_t.shape[0] // (4 * fsdp)
    wide = keep.shape[3]
    parts = wide // LANES
    deep = block // parts
    for c, f, x, core, row, mid in relative_blocks(at, fsdp):
        start = multiple(((row * 2 + core) * 2 + mid) * block, 16)
        part = dot(att_t[pl.ds(start, block), :], d_proj).astype(BF16)
        target = keep if c == 0 else send
        target[f, x, :block, :] = part[:, :wide]
        for i in range(parts):
            target[f, x, block:, i * LANES : (i + 1) * LANES] = part[i * deep : (i + 1) * deep, wide:]


def attend_back_kernel(halo, heads, d_att, q_st, keys, values, probs, d_q, d_k, d_v, d_scores):
    rows = d_q.shape[0]
    dim = keys.shape[1]
    blocks = rows // QBLOCK
    span = WINDOW + QBLOCK
    scale = dim ** (-0.5)
    d_k[...] = jnp.zeros(d_k.shape, F32)
    d_v[...] = jnp.zeros(d_v.shape, F32)
    for b in range(blocks):
        first_key = halo - WINDOW + b * QBLOCK
        here = slice(first_key, first_key + span)
        for h in range(heads):
            start = (b * heads + h) * QBLOCK
            stack = slice(start, start + QBLOCK)
            d_probs = dot_nt(d_att[stack, :], values[here, :])
            p = probs[stack, :].astype(F32)
            row_terms = jnp.sum(p * d_probs, axis=-1, keepdims=True)
            ds = (p * (d_probs - row_terms) * scale).astype(BF16)
            d_scores[h * QBLOCK : (h + 1) * QBLOCK, :] = ds
            d_q[b * QBLOCK : (b + 1) * QBLOCK, h * dim : (h + 1) * dim] = dot(ds, keys[here, :])
        stack = slice(b * heads * QBLOCK, (b + 1) * heads * QBLOCK)
        d_k[here, :] += dot_tn(d_scores[...], q_st[stack, :])
        d_v[here, :] += dot_tn(probs[stack, :], d_att[stack, :])


def last_kernel(n_qkv, n_tok, fsdp, heads, *refs):
    (
        at, d_residual, d_q, d_k, d_v,
        q_raw, k_raw, cosine, sine, gain_table, normed, g_ffn, g_attn, g_out,
    ) = refs[:14]
    toks = refs[14 : 14 + n_tok]
    refs = refs[14 + n_tok :]
    qkv_w, refs = refs[:n_qkv], refs[n_qkv:]
    grad_tokens, d_halo, keep, send = refs[:4]
    w_full, normed_t, d_qkv, gain_rows, qkv_sems = refs[4:]
    copies = place_copies(qkv_w[:3], qkv_w[3:], w_full, qkv_sems, at, 1, 2)
    for copy in copies:
        copy.start()
    normed_t[...] = normed[...].T
    rows = toks[0].shape[0]
    halo = (n_tok - 1) * rows
    dim = k_raw.shape[1]
    gain_in, gain_q, gain_k = gain_table[0:1, :], gain_table[1:2, :dim], gain_table[2:3, :dim]
    half = dim // 2
    tall, wide = normed_t.shape[0] // fsdp, keep.shape[3]
    def turned_back(u, g, dz, cos, sin):
        first, second = dz[:, :half], dz[:, half:]
        dz = jnp.concatenate([first * cos + second * sin, second * cos - first * sin], axis=1)
        return norm_back(u, g, dz)

    total_q = jnp.zeros((1, dim), F32)
    if halo:
        d_qkv[:halo, : heads * dim] = jnp.zeros((halo, heads * dim), BF16)
    for h in range(heads):
        cut = slice(h * dim, (h + 1) * dim)
        du, dg = turned_back(q_raw[:, cut], gain_q, d_q[:, cut], cosine[halo:, :], sine[halo:, :])
        total_q += dg
        d_qkv[halo:, cut] = du.astype(BF16)
    total_k = jnp.zeros((1, dim), F32)
    for i in range(n_tok):
        here = slice(i * rows, (i + 1) * rows)
        du, dg = turned_back(k_raw[here, :], gain_k, d_k[here, :], cosine[here, :], sine[here, :])
        total_k += dg
        d_qkv[here, heads * dim : (heads + 1) * dim] = du.astype(BF16)
        d_qkv[here, (heads + 1) * dim :] = d_v[here, :].astype(BF16)
    column_blocks(at, fsdp, normed_t, d_qkv, keep, send)
    for copy in copies:
        copy.wait()
    total_in = jnp.zeros(gain_in.shape, F32)
    for i in range(n_tok):
        here = slice(i * rows, (i + 1) * rows)
        if i < n_tok - 1:
            d_normed = dot_nt(d_qkv[here, heads * dim :], w_full[:, heads * dim :])
        else:
            d_normed = dot_nt(d_qkv[here, :], w_full[...])
        du, dg = norm_back(toks[i][...].astype(F32), gain_in, d_normed)
        total_in += dg
        if i < n_tok - 1:
            d_halo[here, :] = du.astype(BF16)
        else:
            grad_tokens[...] = d_residual[...] + du
    gain_rows[...] = jnp.zeros(gain_rows.shape, F32)
    at_row = 0
    for total in (total_in, total_q, total_k, g_attn[...], g_ffn[...], g_out[...]):
        for i in range(total.shape[1] // LANES):
            gain_rows[at_row : at_row + 1, :LANES] = total[:, i * LANES : (i + 1) * LANES]
            at_row += 1
    packed = gain_rows[...].astype(BF16)
    for target in (keep, send):
        for f in range(fsdp):
            for x in range(2):
                target[f, x, tall:, :] = packed


def add(*terms):
    out = terms[0].astype(F32)
    for term in terms[1:]:
        out = out + term.astype(F32)
    return out


class Chunk:
    def __init__(self, here, keep, send):
        self.here, self.keep = here, keep
        self.other = here.core_swap(send)

    def over_fsdp(self, *earlier):
        here = self.here
        parts = [add(self.keep[by], self.other[by]).astype(BF16) for by in range(1, here.fsdp)]
        self.arrived = [here.fsdp_shift(after(part, *earlier), by + 1) for by, part in enumerate(parts)]

    def over_mid(self, *earlier):
        self.arrived = [after(a, *earlier) for a in self.arrived]
        terms = [self.keep[0, 1], self.other[0, 1]] + [a[1] for a in self.arrived]
        self.across = self.here.mid_swap(add(*terms).astype(BF16))
        self.mine = [self.keep[0, 0], self.other[0, 0]] + [a[0] for a in self.arrived]
        return self.arrived[0] if self.arrived else self.other

    def join(self, below, *earlier):
        for chunk in (self, below):
            chunk.arrived = [after(a, *earlier) for a in chunk.arrived]
        pairs = [
            [[c.keep[0, x], c.other[0, x]] + [a[x] for a in c.arrived] for c in (self, below)] for x in range(2)
        ]
        self.across_sent = jnp.concatenate([add(*terms).astype(BF16) for terms in pairs[1]])
        self.across = self.here.mid_swap(self.across_sent)
        self.mine = [jnp.concatenate([add(*terms).astype(BF16) for terms in pairs[0]])]

    def outer_sums(self, *earlier):
        here = self.here
        self.across = after(self.across, *earlier)
        mine = add(*self.mine, self.across).astype(BF16)
        n, w = mine.shape
        mine = mine.reshape(here.outer, n // here.outer, w)
        self.shares = [pick(mine, here.outer_ahead[0])]
        for by in range(1, here.outer):
            self.shares.append(here.outer_shift(pick(mine, here.outer_ahead[by]), by))
        return self.across

    def outer_gather(self, *earlier):
        here = self.here
        self.shares = list(after(tuple(self.shares), *earlier))
        own = add(*self.shares).astype(BF16)
        self.gathered = [own] + [here.outer_shift(own, by) for by in range(1, here.outer)]
        return self.shares[-1]

    def mid_gather(self, *earlier):
        here = self.here
        self.gathered = list(after(tuple(self.gathered), *earlier))
        block = ordered(self.gathered, here.outer_behind)
        block = block.reshape(-1, block.shape[-1])
        across = here.mid_swap(block)
        self.blocks = [[block, across], [here.core_swap(block), here.core_swap(across)]]
        return self.gathered[-1]


def by_place(here, blocks):
    own = [jnp.where(here.mid_at == 0, a, b) for a, b in blocks]
    other = [jnp.where(here.mid_at == 0, b, a) for a, b in blocks]
    pairs = list(zip(own, other))
    first = [jnp.where(here.core_at == 0, a, b) for a, b in zip(pairs[0], pairs[1])]
    second = [jnp.where(here.core_at == 0, b, a) for a, b in zip(pairs[0], pairs[1])]
    return first + second


def on_device(
    tokens, positions, cotangent, in_gain, w_query, w_key, w_value, query_gain, key_gain, w_out, attn_gain,
    ffn_gain_in, w_gate, w_up, w_down, ffn_gain_out,
):
    here = Places()
    fsdp = here.fsdp
    rows, width = tokens.shape
    dim = w_key.shape[1]
    query_cols = w_query.shape[1]
    heads = query_cols // dim
    hidden = w_gate.shape[1]
    hops = (WINDOW + rows - 1) // rows
    n_tok = hops + 1
    halo = hops * rows
    every = halo + rows
    at = here.vector

    gains = (in_gain, query_gain, key_gain, attn_gain, ffn_gain_in, ffn_gain_out)
    cuts = [0]
    for gain in gains:
        cuts.append(cuts[-1] + gain.shape[0])
    gain_row = jnp.concatenate(gains)
    gain_rows = ordered([gain_row] + [here.fsdp_shift(gain_row, by) for by in range(1, fsdp)], here.fsdp_behind)
    gain_rows = gain_rows.astype(F32)
    gain_table = jnp.concatenate(
        [
            jnp.pad(gain_rows[:, cuts[i] : cuts[i + 1]].reshape(1, -1), ((0, 0), (0, width - fsdp * gains[i].shape[0])))
            for i in range(6)
        ]
        + [jnp.zeros((2, width), F32)],
        axis=0,
    )
    qkv_w = [w_query, w_key, w_value]
    qkv_part = own_part(here, qkv_w, 1, 2)
    tokens_out = after(tokens, qkv_part)
    toks = [linear_shift(tokens_out, by) for by in range(hops, 0, -1)] + [tokens]
    qkv_w += on_chips(here, over_links(here, qkv_part), 2)
    out_arrived = over_links(here, after(own_part(here, [w_out], 0, 2), *toks[:-1]))
    gate_arrived = over_links(here, after(own_part(here, [w_gate], 1, 4), qkv_w[3]))
    up_arrived = over_links(here, after(own_part(here, [w_up], 1, 2), out_arrived[0]))

    all_positions = jnp.concatenate([positions[0] - halo + jnp.arange(halo, dtype=jnp.int32), positions])
    frequency = ROPE_BASE ** (-(jnp.arange(dim // 2, dtype=F32) * 2.0 / dim))
    angles = all_positions.astype(F32)[:, None] * frequency[None, :]
    cosine, sine = jnp.cos(angles), jnp.sin(angles)

    span = WINDOW + QBLOCK
    weight_bytes = 2 * fsdp * w_gate.size
    normed, q_raw, k_raw, q_st, keys, values, probs, attended = pl.pallas_call(
        functools.partial(attend_kernel, n_tok, len(qkv_w), heads),
        out_shape=(
            shape((every, width), BF16),
            shape((rows, query_cols), F32),
            shape((every, dim), F32),
            shape((heads * rows, dim), BF16),
            shape((every, dim), BF16),
            shape((every, dim), BF16),
            shape((heads * rows, span), BF16),
            shape((rows, query_cols), BF16),
        ),
        in_specs=[SMEM] + [VMEM] * (n_tok + 4) + [ANY] * len(qkv_w),
        out_specs=(VMEM,) * 8,
        scratch_shapes=[
            pltpu.VMEM((width, query_cols + 2 * dim), BF16),
            pltpu.SemaphoreType.DMA((len(qkv_w),)),
        ],
        compiler_params=params(),
        cost_estimate=cost(4e9, 1e7),
        name="attend",
    )(at, *toks, positions[:, None], cosine, sine, gain_table, *qkv_w)

    down_arrived = over_links(here, after(own_part(here, [w_down], 0, 2), attended))
    out_w = [w_out] + on_chips(here, [after(a, attended) for a in out_arrived], 2)
    gate_w = [w_gate] + on_chips(here, [after(a, attended) for a in gate_arrived], 4)
    up_w = [w_up] + on_chips(here, [after(a, attended) for a in up_arrived], 2)
    projected, residual, ffn_in, mixed, gelu_out, gate_slope = pl.pallas_call(
        functools.partial(gate_kernel, len(out_w), len(gate_w), len(up_w)),
        out_shape=(
            shape((rows, width), F32),
            shape((rows, width), F32),
            shape((rows, width), BF16),
            shape((rows, hidden), BF16),
            shape((rows, hidden), BF16),
            shape((rows, hidden), BF16),
        ),
        in_specs=[SMEM] + [VMEM] * 3 + [ANY] * (len(out_w) + len(gate_w) + len(up_w)),
        out_specs=(VMEM,) * 6,
        scratch_shapes=[
            pltpu.VMEM((query_cols, width), BF16),
            pltpu.VMEM((width, hidden), BF16),
            pltpu.VMEM((width, hidden), BF16),
            pltpu.SemaphoreType.DMA((len(out_w),)),
            pltpu.SemaphoreType.DMA((len(gate_w),)),
            pltpu.SemaphoreType.DMA((len(up_w),)),
        ],
        compiler_params=params(),
        cost_estimate=cost(4e9, 2 * weight_bytes),
        name="gate",
    )(at, attended, tokens, gain_table, *out_w, *gate_w, *up_w)

    down_w = [w_down] + on_chips(here, [after(a, mixed) for a in down_arrived], 2)
    down_block = w_down.shape[0] // 4
    down_shape = shape((fsdp, 2, down_block, width), BF16)
    layer_out, d_down, g_ffn_out, down_keep, down_send = pl.pallas_call(
        functools.partial(down_kernel, len(down_w), fsdp),
        out_shape=(
            shape((rows, width), BF16),
            shape((rows, width), BF16),
            shape((1, width), F32),
            down_shape,
            down_shape,
        ),
        in_specs=[SMEM] + [VMEM] * 4 + [ANY] * len(down_w),
        out_specs=(VMEM,) * 5,
        scratch_shapes=[
            pltpu.VMEM((hidden, width), BF16),
            pltpu.VMEM((hidden, rows), BF16),
            pltpu.SemaphoreType.DMA((len(down_w),)),
        ],
        compiler_params=params(),
        cost_estimate=cost(4e9, 2 * weight_bytes),
        name="down",
    )(at, mixed, residual, cotangent, gain_table, *down_w)

    down_sum = Chunk(here, down_keep, down_send)
    gate_shape = shape((fsdp, 2, w_gate.shape[0], hidden // 4), BF16)
    d_gate, d_up, gate_keep, gate_send, up_keep, up_send = pl.pallas_call(
        functools.partial(gate_back_kernel, len(down_w), fsdp),
        out_shape=(
            shape((rows, hidden), BF16),
            shape((rows, hidden), BF16),
            gate_shape,
            gate_shape,
            gate_shape,
            gate_shape,
        ),
        in_specs=[SMEM] + [VMEM] * 4 + [ANY] * len(down_w),
        out_specs=(VMEM,) * 6,
        scratch_shapes=[
            pltpu.VMEM((hidden, width), BF16),
            pltpu.VMEM((width, rows), BF16),
            pltpu.SemaphoreType.DMA((len(down_w),)),
        ],
        compiler_params=params(),
        cost_estimate=cost(6e9, 3 * weight_bytes),
        name="gate_back",
    )(at, d_down, gelu_out, gate_slope, ffn_in, *down_w)
    gate_sum = Chunk(here, gate_keep, gate_send)
    up_sum = Chunk(here, up_keep, up_send)
    down_sum.over_fsdp(d_gate)
    d_gate = after(d_gate, down_sum.other)
    qkv_cols = query_cols + 2 * dim
    last_wide = qkv_cols // 4
    shard_rows = w_query.shape[0]
    last_shape = shape((fsdp, 2, shard_rows + GAIN_ROWS, last_wide), BF16)
    out_block = w_out.shape[0] // 4
    out_shape = shape((fsdp, 2, out_block * width // (hidden // 4), hidden // 4), BF16)
    d_residual, g_ffn, g_attn, d_att, out_keep, out_send = pl.pallas_call(
        functools.partial(middle_kernel, len(out_w), len(gate_w), len(up_w), fsdp, heads),
        out_shape=(
            shape((rows, width), F32),
            shape((1, width), F32),
            shape((1, width), F32),
            shape((heads * rows, dim), BF16),
            out_shape,
            out_shape,
        ),
        in_specs=[SMEM] + [VMEM] * 7 + [ANY] * (len(out_w) + len(gate_w) + len(up_w)),
        out_specs=(VMEM,) * 6,
        scratch_shapes=[
            pltpu.VMEM((query_cols, width), BF16),
            pltpu.VMEM((width, hidden), BF16),
            pltpu.VMEM((width, hidden), BF16),
            pltpu.VMEM((query_cols, rows), BF16),
            pltpu.SemaphoreType.DMA((len(out_w),)),
            pltpu.SemaphoreType.DMA((len(gate_w),)),
            pltpu.SemaphoreType.DMA((len(up_w),)),
        ],
        compiler_params=params(),
        cost_estimate=cost(6e9, 4 * weight_bytes),
        name="middle",
    )(at, d_gate, d_up, residual, projected, cotangent, gain_table, attended, *out_w, *gate_w, *up_w)

    out_sum = Chunk(here, out_keep, out_send)
    gate_sum.over_fsdp(g_ffn)
    up_sum.over_fsdp(g_ffn)
    down_sum.over_mid(g_ffn)
    d_q, d_k, d_v = pl.pallas_call(
        functools.partial(attend_back_kernel, halo, heads),
        out_shape=(shape((rows, query_cols), F32), shape((every, dim), F32), shape((every, dim), F32)),
        in_specs=[VMEM] * 5,
        out_specs=(VMEM,) * 3,
        scratch_shapes=[pltpu.VMEM((heads * QBLOCK, span), BF16)],
        compiler_params=params(),
        cost_estimate=cost(6e9, 3 * weight_bytes),
        name="attend_back",
    )(after(d_att, gate_sum.other, up_sum.other, *down_sum.arrived), q_st, keys, values, probs)
    out_sum.over_fsdp(d_k)
    down_sum.outer_sums(d_k)
    d_q = after(d_q, out_sum.other, down_sum.across)
    grad_tokens, d_halo, last_keep, last_send = pl.pallas_call(
        functools.partial(last_kernel, len(qkv_w), n_tok, fsdp, heads),
        out_shape=(
            shape((rows, width), F32),
            shape((halo, width), BF16),
            last_shape,
            last_shape,
        ),
        in_specs=[SMEM] + [VMEM] * (13 + n_tok) + [ANY] * len(qkv_w),
        out_specs=(VMEM,) * 4,
        scratch_shapes=[
            pltpu.VMEM((width, qkv_cols), BF16),
            pltpu.VMEM((width, every), BF16),
            pltpu.VMEM((every, qkv_cols), BF16),
            pltpu.VMEM((GAIN_ROWS, last_wide), F32),
            pltpu.SemaphoreType.DMA((len(qkv_w),)),
        ],
        compiler_params=params(),
        cost_estimate=cost(15e9, 4 * weight_bytes),
        name="last",
    )(
        at, d_residual, d_q, d_k, d_v,
        q_raw, k_raw, cosine, sine, gain_table, normed, g_ffn, g_attn, g_ffn_out, *toks, *qkv_w,
    )

    last_sum = Chunk(here, last_keep, last_send)
    gate_sum.over_mid(last_keep)
    down_sum.outer_sums(last_keep)
    (last_sum.other,), (gate_sum.across,), down_sum.shares, up_sum.arrived, out_sum.arrived = together(
        (last_sum.other,), (gate_sum.across,), down_sum.shares, up_sum.arrived, out_sum.arrived
    )
    last_sum.over_fsdp()
    up_sum.join(out_sum)
    gate_sum.outer_sums()
    down_sum.outer_gather()
    last_sum.arrived, (up_sum.across,), gate_sum.shares, down_sum.gathered = together(
        last_sum.arrived, (up_sum.across,), gate_sum.shares, down_sum.gathered
    )
    last_sum.over_mid()
    up_sum.outer_sums()
    gate_sum.outer_gather()
    down_sum.mid_gather()
    (last_sum.across,), up_sum.shares, gate_sum.gathered, down_last = together(
        (last_sum.across,), up_sum.shares, gate_sum.gathered, down_sum.blocks[0]
    )
    down_sum.blocks[0] = list(down_last)
    last_sum.outer_sums()
    up_sum.outer_gather()
    gate_sum.mid_gather()
    halos = [linear_shift(after(d_halo, last_sum.across)[halo - by * rows :][:rows], -by) for by in range(1, hops + 1)]
    last_sum.shares, up_sum.gathered, gate_last, halos = together(
        last_sum.shares, up_sum.gathered, gate_sum.blocks[0], halos
    )
    gate_sum.blocks[0] = list(gate_last)
    last_sum.outer_gather()
    up_sum.mid_gather()
    last_sum.mid_gather()
    down_blocks, gate_blocks = by_place(here, down_sum.blocks), by_place(here, gate_sum.blocks)
    both_blocks, last_blocks = by_place(here, up_sum.blocks), by_place(here, last_sum.blocks)
    total_gains = last_sum.blocks[0][0][shard_rows:, :LANES].astype(F32)

    for came in halos:
        grad_tokens = grad_tokens + came.astype(F32)

    total_down = jnp.concatenate(down_blocks, axis=0).astype(F32)
    total_gate = jnp.concatenate(gate_blocks, axis=1).astype(F32)
    total_up = jnp.concatenate([b[:shard_rows] for b in both_blocks], axis=1).astype(F32)
    total_qkv = jnp.concatenate([b[:shard_rows] for b in last_blocks], axis=1).astype(F32)
    wide = hidden // 4
    parts = wide // LANES
    total_out = []
    for block in both_blocks:
        below = block[shard_rows + out_block :].reshape(out_block // parts, parts, LANES)
        below = below.transpose(1, 0, 2).reshape(out_block, LANES)
        total_out.append(jnp.concatenate([block[shard_rows : shard_rows + out_block], below], axis=1))
    total_out = jnp.concatenate(total_out, axis=0).astype(F32)
    g, at_row = [], 0
    for gain in gains:
        deep = fsdp * gain.shape[0] // total_gains.shape[1]
        total = total_gains[at_row : at_row + deep].reshape(fsdp, gain.shape[0])
        g.append(pick(total, here.fsdp_at))
        at_row += deep
    return (
        layer_out, grad_tokens, g[0],
        total_qkv[:, :query_cols],
        total_qkv[:, query_cols : query_cols + dim],
        total_qkv[:, query_cols + dim :],
        g[1], g[2], total_out, g[3], g[4], total_gate, total_up, total_down, g[5],
    )


def solution(mesh):
    tok = P(("seq", "fsdp"), None)
    mat = P("fsdp", None)
    vec = P("fsdp")
    return jax.shard_map(
        on_device,
        mesh=mesh,
        in_specs=(tok, P(("seq", "fsdp")), tok, vec, mat, mat, mat, vec, vec, mat, vec, vec, mat, mat, mat, vec),
        out_specs=(tok, tok, vec, mat, mat, mat, vec, vec, mat, vec, vec, mat, mat, mat, vec),
        check_vma=False,
    )
```

```python
import functools
import math

import jax
import jax.numpy as jnp
from jax import lax
from jax.experimental import pallas as pl
from jax.experimental.pallas import tpu as pltpu
from jax.sharding import PartitionSpec as P

WINDOW = 512
EPSILON = 1e-06
ROPE_BASE = 10000.0
MASKED = -1e30
BF16 = jnp.bfloat16
F32 = jnp.float32
QBLOCK = 128
LANES = 128
GAIN_ROWS = 32
GELU_A = math.sqrt(2.0 / math.pi)
GELU_B = 0.044715

VMEM = pl.BlockSpec(memory_space=pltpu.VMEM)
SMEM = pl.BlockSpec(memory_space=pltpu.SMEM)
ANY = pl.BlockSpec(memory_space=pl.ANY)


def wrapped(value, size):
    return value & (size - 1) if size & (size - 1) == 0 else lax.rem(value, jnp.int32(size))


class Places:
    def __init__(self):
        self.seq = lax.axis_size("seq")
        self.fsdp = lax.axis_size("fsdp")
        self.outer = self.seq // 4
        index = lax.axis_index("seq").astype(jnp.int32)
        fsdp_at = lax.axis_index("fsdp").astype(jnp.int32)
        outer_at = lax.shift_right_logical(index, 2)
        core_at, mid_at = index & 1, lax.shift_right_logical(index, 1) & 1
        scalars = lax.optimization_barrier(
            (
                core_at,
                mid_at,
                fsdp_at,
                core_at * 2 + mid_at,
                tuple(wrapped(outer_at + by, self.outer) for by in range(self.outer)),
                tuple(wrapped(outer_at - by + self.outer, self.outer) for by in range(self.outer)),
                tuple(wrapped(fsdp_at + by, self.fsdp) for by in range(self.fsdp)),
                tuple(wrapped(fsdp_at - by + self.fsdp, self.fsdp) for by in range(self.fsdp)),
                jnp.stack([core_at, mid_at, fsdp_at]),
            )
        )
        self.core_at, self.mid_at, self.fsdp_at, self.quarter_at = scalars[:4]
        self.outer_ahead, self.outer_behind, self.fsdp_ahead, self.fsdp_behind, self.vector = scalars[4:]

    def core_swap(self, array):
        return lax.ppermute(array, "seq", [(i, i ^ 1) for i in range(self.seq)])

    def mid_swap(self, array):
        return lax.ppermute(array, "seq", [(i, i ^ 2) for i in range(self.seq)])

    def outer_shift(self, array, by):
        return lax.ppermute(array, "seq", [(i, (i + 4 * by) % self.seq) for i in range(self.seq)])

    def fsdp_shift(self, array, by):
        return lax.ppermute(array, "fsdp", [(i, (i + by) % self.fsdp) for i in range(self.fsdp)])


def linear_shift(array, by):
    count = lax.axis_size("seq") * lax.axis_size("fsdp")
    return lax.ppermute(array, ("seq", "fsdp"), [(i, i + by) for i in range(count) if 0 <= i + by < count])


def pick(array, at):
    return lax.dynamic_index_in_dim(array, at, 0, keepdims=False, allow_negative_indices=False)


def ordered(pieces, behind):
    if len(pieces) == 2:
        own, other = pieces
        return jnp.where(behind[0] == 0, jnp.stack([own, other]), jnp.stack([other, own]))
    stacked = jnp.stack(pieces)
    return jnp.stack([pick(stacked, at) for at in behind])


def own_part(here, shards, axis, ways):
    size = sum(shard.shape[axis] for shard in shards) // ways
    place = here.quarter_at if ways == 4 else here.core_at
    if len(shards) == 1:
        return lax.dynamic_slice_in_dim(shards[0], place * size, size, axis, allow_negative_indices=False)
    parts = []
    for i in range(ways):
        pieces, start = [], 0
        for shard in shards:
            low, high = max(i * size - start, 0), min((i + 1) * size - start, shard.shape[axis])
            if low < high:
                pieces.append(lax.slice_in_dim(shard, low, high, axis=axis))
            start += shard.shape[axis]
        parts.append(jnp.concatenate(pieces, axis))
    return functools.reduce(lambda rest, i: jnp.where(place == i, parts[i], rest), range(1, ways), parts[0])


def after(value, *earlier):
    return lax.optimization_barrier((value, *earlier))[0]


def together(*groups):
    return lax.optimization_barrier(tuple(tuple(group) for group in groups))


def over_links(here, part):
    return [here.fsdp_shift(part, by) for by in range(1, here.fsdp)]


def on_chips(here, arrived, ways):
    pieces = []
    for mine in arrived:
        if ways == 4:
            across = here.mid_swap(mine)
            pieces += [mine, across, here.core_swap(mine), here.core_swap(across)]
        else:
            pieces += [mine, here.core_swap(mine)]
    return pieces


def multiple(value, of):
    return pl.multiple_of(value, of)


def place_copies(owned, pieces, whole, sems, at, axis, ways):
    core, mid, fsdp = at[0], at[1], at[2]
    count = 1 + len(pieces) // ways
    rows = owned[0].shape[0]
    copies = []
    column = 0
    own_row = multiple(fsdp * rows, 16)
    for shard in owned:
        wide = shard.shape[1]
        copies.append((shard, whole.at[pl.ds(own_row, rows), pl.ds(column, wide)]))
        column += wide
    for k, piece in enumerate(pieces):
        by = 1 + k // ways
        row = multiple(lax.rem(fsdp + (count - by), count) * rows, 16)
        k = k % ways
        if ways == 4:
            place = (core if k < 2 else 1 - core) * 2 + (mid if k % 2 == 0 else 1 - mid)
        else:
            place = core if k == 0 else 1 - core
        if axis == 0:
            target = whole.at[pl.ds(multiple(row + place * (rows // ways), 16), rows // ways), :]
        else:
            target = whole.at[pl.ds(row, rows), pl.ds(multiple(place * (column // ways), 128), column // ways)]
        copies.append((piece, target))
    return [pltpu.make_async_copy(a, b, sems.at[k]) for k, (a, b) in enumerate(copies)]


def dot(a, b):
    return lax.dot_general(a, b, (((1,), (0,)), ((), ())), preferred_element_type=F32)


def dot_nt(a, b):
    return lax.dot_general(a, b, (((1,), (1,)), ((), ())), preferred_element_type=F32)


def dot_tn(a, b):
    return lax.dot_general(a, b, (((0,), (0,)), ((), ())), preferred_element_type=F32)


def inverse_rms(u):
    return lax.rsqrt(jnp.mean(u * u, axis=-1, keepdims=True) + EPSILON)


def norm_back(u, g, dz):
    r = inverse_rms(u)
    ur = u * r
    gdz = g * dz
    du = r * (gdz - ur * jnp.mean(gdz * ur, axis=-1, keepdims=True))
    return du, jnp.sum(dz * ur, axis=0, keepdims=True)


def params(megabytes=56):
    return pltpu.CompilerParams(vmem_limit_bytes=megabytes * 1024 * 1024)


def cost(flops, bytes_accessed):
    return pl.CostEstimate(flops=int(20 * flops), bytes_accessed=int(20 * bytes_accessed), transcendentals=0)


def shape(dims, kind):
    return jax.ShapeDtypeStruct(tuple(dims), kind)


def attend_kernel(n_tok, n_qkv, heads, *refs):
    at = refs[0]
    toks = refs[1 : 1 + n_tok]
    pos, cosine, sine, gain_table = refs[1 + n_tok : 5 + n_tok]
    qkv = refs[5 + n_tok : 5 + n_tok + n_qkv]
    normed, q_raw, k_raw, q_st, keys, values, probs, attended, w_full, sems = refs[5 + n_tok + n_qkv :]
    copies = place_copies(qkv[:3], qkv[3:], w_full, sems, at, 1, 4)
    for copy in copies:
        copy.start()
    rows = toks[0].shape[0]
    dim = keys.shape[1]
    half = dim // 2
    halo = (n_tok - 1) * rows
    gain = gain_table[0:1, :]
    gain_q, gain_k = gain_table[1:2, :dim], gain_table[2:3, :dim]
    for i, tok in enumerate(toks):
        u = tok[...].astype(F32)
        normed[i * rows : (i + 1) * rows, :] = (u * inverse_rms(u) * gain).astype(BF16)
    for copy in copies:
        copy.wait()

    def turned(u, g, cos, sin):
        u = u * inverse_rms(u) * g
        first, second = u[:, :half], u[:, half:]
        return (first * cos - second * sin).astype(BF16), (second * cos + first * sin).astype(BF16)

    for i in range(n_tok):
        here = slice(i * rows, (i + 1) * rows)
        kv = dot(normed[here, :], w_full[:, heads * dim :])
        k_raw[here, :] = kv[:, :dim]
        values[here, :] = kv[:, dim:].astype(BF16)
        first, second = turned(kv[:, :dim], gain_k, cosine[here, :], sine[here, :])
        keys[here, :half] = first
        keys[here, half:] = second
    blocks = rows // QBLOCK
    for h in range(heads):
        u = dot(normed[halo:, :], w_full[:, h * dim : (h + 1) * dim])
        q_raw[:, h * dim : (h + 1) * dim] = u
        first, second = turned(u, gain_q, cosine[halo:, :], sine[halo:, :])
        for b in range(blocks):
            start = (b * heads + h) * QBLOCK
            q_st[start : start + QBLOCK, :half] = first[b * QBLOCK : (b + 1) * QBLOCK, :]
            q_st[start : start + QBLOCK, half:] = second[b * QBLOCK : (b + 1) * QBLOCK, :]
    span = WINDOW + QBLOCK
    distance = (
        lax.broadcasted_iota(jnp.int32, (QBLOCK, span), 0)
        + WINDOW
        - lax.broadcasted_iota(jnp.int32, (QBLOCK, span), 1)
    )
    scale = dim ** (-0.5)
    for b in range(blocks):
        first_key = halo - WINDOW + b * QBLOCK
        limit = jnp.minimum(pos[b * QBLOCK : (b + 1) * QBLOCK, :], WINDOW - 1)
        allowed = (distance >= 0) & (distance <= limit)
        for h in range(heads):
            start = (b * heads + h) * QBLOCK
            scores = dot_nt(q_st[start : start + QBLOCK, :], keys[first_key : first_key + span, :]) * scale
            scores = jnp.where(allowed, scores, MASKED)
            weights = jnp.exp(scores - jnp.max(scores, axis=-1, keepdims=True))
            weights = (weights * (1.0 / jnp.sum(weights, axis=-1, keepdims=True))).astype(BF16)
            probs[start : start + QBLOCK, :] = weights
            attended[b * QBLOCK : (b + 1) * QBLOCK, h * dim : (h + 1) * dim] = dot(
                weights, values[first_key : first_key + span, :]
            ).astype(BF16)


def gate_kernel(n_out, n_gate, n_up, *refs):
    at, attended, tokens, gain_table = refs[:4]
    refs = refs[4:]
    out_w, gate_w, up_w, refs = (
        refs[:n_out],
        refs[n_out : n_out + n_gate],
        refs[n_out + n_gate : n_out + n_gate + n_up],
        refs[n_out + n_gate + n_up :],
    )
    projected_ref, residual_ref, ffn_in_ref, mixed, gelu_out, gate_slope = refs[:6]
    out_full, gate_full, up_full, out_sems, gate_sems, up_sems = refs[6:]
    groups = (
        place_copies(out_w[:1], out_w[1:], out_full, out_sems, at, 0, 2),
        place_copies(gate_w[:1], gate_w[1:], gate_full, gate_sems, at, 1, 4),
        place_copies(up_w[:1], up_w[1:], up_full, up_sems, at, 1, 2),
    )
    for group in groups:
        for copy in group:
            copy.start()
    for copy in groups[0]:
        copy.wait()
    projected = dot(attended[...], out_full[...])
    projected_ref[...] = projected
    residual = tokens[...].astype(F32) + projected * inverse_rms(projected) * gain_table[3:4, :]
    residual_ref[...] = residual
    ffn_in_ref[...] = (residual * inverse_rms(residual) * gain_table[4:5, :]).astype(BF16)
    for group in groups[1:]:
        for copy in group:
            copy.wait()
    width = 256

    def step(i, _):
        cut = pl.ds(multiple(i * width, width), width)
        gate = dot(ffn_in_ref[...], gate_full[:, cut])
        up = dot(ffn_in_ref[...], up_full[:, cut])
        square = gate * gate
        t = jnp.tanh(GELU_A * gate * (1.0 + GELU_B * square))
        cdf = 0.5 * (1.0 + t)
        act = gate * cdf
        slope = cdf + 0.5 * gate * (1.0 - t * t) * (GELU_A * (1.0 + 3.0 * GELU_B * square))
        mixed[:, cut] = (act * up).astype(BF16)
        gelu_out[:, cut] = act.astype(BF16)
        gate_slope[:, cut] = (up * slope).astype(BF16)
        return 0

    lax.fori_loop(0, gate_full.shape[1] // width, step, 0)


def relative_blocks(at, fsdp):
    for c in range(2):
        core = c + at[0] - 2 * c * at[0]
        for f in range(fsdp):
            row = lax.rem(at[2] + f, fsdp)
            for x in range(2):
                mid = x + at[1] - 2 * x * at[1]
                yield c, f, x, core, row, mid


def column_blocks(at, fsdp, left_t, right, keep, send):
    tall, wide = left_t.shape[0] // fsdp, keep.shape[3]
    for c, f, x, core, row, mid in relative_blocks(at, fsdp):
        cut = pl.ds(multiple((core * 2 + mid) * wide, 128), wide)
        left = left_t[pl.ds(multiple(row * tall, 16), tall), :]
        target = keep if c == 0 else send
        target[f, x, :tall, :] = dot(left, right[:, cut]).astype(BF16)


def down_kernel(n_down, fsdp, *refs):
    at, mixed, residual, cotangent, gain_table = refs[:5]
    down_w = refs[5 : 5 + n_down]
    layer_out, d_down, grad_gain, keep, send = refs[5 + n_down : 10 + n_down]
    down_full, mixed_t, sems = refs[10 + n_down :]
    copies = place_copies(down_w[:1], down_w[1:], down_full, sems, at, 0, 2)
    for copy in copies:
        copy.start()
    mixed_t[...] = mixed[...].T
    for copy in copies:
        copy.wait()
    down = dot(mixed[...], down_full[...])
    r = inverse_rms(down)
    gain = gain_table[5:6, :]
    layer_out[...] = (residual[...] + down * r * gain).astype(BF16)
    du, dg = norm_back(down, gain, cotangent[...].astype(F32))
    grad_gain[...] = dg
    d_down[...] = du.astype(BF16)
    block = keep.shape[2]
    for c, f, x, core, row, mid in relative_blocks(at, fsdp):
        start = multiple(((row * 2 + core) * 2 + mid) * block, 16)
        target = keep if c == 0 else send
        target[f, x] = dot(mixed_t[pl.ds(start, block), :], d_down[...]).astype(BF16)


def gate_back_kernel(n_down, fsdp, *refs):
    at, d_down, gelu_out, gate_slope, ffn_in = refs[:5]
    down_w = refs[5 : 5 + n_down]
    d_gate, d_up, keep, send, up_keep, up_send = refs[5 + n_down : 11 + n_down]
    down_full, ffn_t, sems = refs[11 + n_down :]
    copies = place_copies(down_w[:1], down_w[1:], down_full, sems, at, 0, 2)
    for copy in copies:
        copy.start()
    ffn_t[...] = ffn_in[...].T
    for copy in copies:
        copy.wait()
    width = 256

    def step(i, _):
        cut = pl.ds(multiple(i * width, width), width)
        d_mixed = dot_nt(d_down[...], down_full[cut, :])
        d_gate[:, cut] = (d_mixed * gate_slope[:, cut].astype(F32)).astype(BF16)
        d_up[:, cut] = (d_mixed * gelu_out[:, cut].astype(F32)).astype(BF16)
        return 0

    lax.fori_loop(0, d_gate.shape[1] // width, step, 0)
    column_blocks(at, fsdp, ffn_t, d_gate, keep, send)
    column_blocks(at, fsdp, ffn_t, d_up, up_keep, up_send)


def middle_kernel(n_out, n_gate, n_up, fsdp, heads, *refs):
    at, d_gate, d_up, residual, projected, cotangent, gain_table, attended = refs[:8]
    refs = refs[8:]
    out_w, gate_w, up_w, refs = (
        refs[:n_out],
        refs[n_out : n_out + n_gate],
        refs[n_out + n_gate : n_out + n_gate + n_up],
        refs[n_out + n_gate + n_up :],
    )
    d_residual_ref, g_ffn, g_attn, d_att, keep, send = refs[:6]
    out_full, gate_full, up_full, att_t, out_sems, gate_sems, up_sems = refs[6:]
    groups = (
        place_copies(gate_w[:1], gate_w[1:], gate_full, gate_sems, at, 1, 4),
        place_copies(up_w[:1], up_w[1:], up_full, up_sems, at, 1, 2),
        place_copies(out_w[:1], out_w[1:], out_full, out_sems, at, 0, 2),
    )
    for group in groups:
        for copy in group:
            copy.start()
    att_t[...] = attended[...].T
    for copy in groups[0]:
        copy.wait()
    d_ffn_in = dot_nt(d_gate[...], gate_full[...])
    for copy in groups[1]:
        copy.wait()
    d_ffn_in = d_ffn_in + dot_nt(d_up[...], up_full[...])
    du, dg = norm_back(residual[...], gain_table[4:5, :], d_ffn_in)
    g_ffn[...] = dg
    d_residual = cotangent[...].astype(F32) + du
    d_residual_ref[...] = d_residual
    du, dg = norm_back(projected[...], gain_table[3:4, :], d_residual)
    g_attn[...] = dg
    d_proj = du.astype(BF16)
    rows, dim = d_proj.shape[0], d_att.shape[1]
    for copy in groups[2]:
        copy.wait()
    for h in range(heads):
        part = dot_nt(d_proj, out_full[h * dim : (h + 1) * dim, :]).astype(BF16)
        for b in range(rows // QBLOCK):
            start = (b * heads + h) * QBLOCK
            d_att[start : start + QBLOCK, :] = part[b * QBLOCK : (b + 1) * QBLOCK, :]
    block = att_t.shape[0] // (4 * fsdp)
    wide = keep.shape[3]
    parts = wide // LANES
    deep = block // parts
    for c, f, x, core, row, mid in relative_blocks(at, fsdp):
        start = multiple(((row * 2 + core) * 2 + mid) * block, 16)
        part = dot(att_t[pl.ds(start, block), :], d_proj).astype(BF16)
        target = keep if c == 0 else send
        target[f, x, :block, :] = part[:, :wide]
        for i in range(parts):
            target[f, x, block:, i * LANES : (i + 1) * LANES] = part[i * deep : (i + 1) * deep, wide:]


def attend_back_kernel(halo, heads, d_att, q_st, keys, values, probs, d_q, d_k, d_v, d_scores):
    rows = d_q.shape[0]
    dim = keys.shape[1]
    blocks = rows // QBLOCK
    span = WINDOW + QBLOCK
    scale = dim ** (-0.5)
    d_k[...] = jnp.zeros(d_k.shape, F32)
    d_v[...] = jnp.zeros(d_v.shape, F32)
    for b in range(blocks):
        first_key = halo - WINDOW + b * QBLOCK
        here = slice(first_key, first_key + span)
        for h in range(heads):
            start = (b * heads + h) * QBLOCK
            stack = slice(start, start + QBLOCK)
            d_probs = dot_nt(d_att[stack, :], values[here, :])
            p = probs[stack, :].astype(F32)
            row_terms = jnp.sum(p * d_probs, axis=-1, keepdims=True)
            ds = (p * (d_probs - row_terms) * scale).astype(BF16)
            d_scores[h * QBLOCK : (h + 1) * QBLOCK, :] = ds
            d_q[b * QBLOCK : (b + 1) * QBLOCK, h * dim : (h + 1) * dim] = dot(ds, keys[here, :])
        stack = slice(b * heads * QBLOCK, (b + 1) * heads * QBLOCK)
        d_k[here, :] += dot_tn(d_scores[...], q_st[stack, :])
        d_v[here, :] += dot_tn(probs[stack, :], d_att[stack, :])


def last_kernel(n_qkv, n_tok, fsdp, heads, *refs):
    (
        at, d_residual, d_q, d_k, d_v,
        q_raw, k_raw, cosine, sine, gain_table, normed, g_ffn, g_attn, g_out,
    ) = refs[:14]
    toks = refs[14 : 14 + n_tok]
    refs = refs[14 + n_tok :]
    qkv_w, refs = refs[:n_qkv], refs[n_qkv:]
    grad_tokens, d_halo, keep, send = refs[:4]
    w_full, normed_t, d_qkv, gain_rows, qkv_sems = refs[4:]
    copies = place_copies(qkv_w[:3], qkv_w[3:], w_full, qkv_sems, at, 1, 4)
    for copy in copies:
        copy.start()
    normed_t[...] = normed[...].T
    rows = toks[0].shape[0]
    halo = (n_tok - 1) * rows
    dim = k_raw.shape[1]
    gain_in, gain_q, gain_k = gain_table[0:1, :], gain_table[1:2, :dim], gain_table[2:3, :dim]
    half = dim // 2
    tall, wide = normed_t.shape[0] // fsdp, keep.shape[3]
    def turned_back(u, g, dz, cos, sin):
        first, second = dz[:, :half], dz[:, half:]
        dz = jnp.concatenate([first * cos + second * sin, second * cos - first * sin], axis=1)
        return norm_back(u, g, dz)

    total_q = jnp.zeros((1, dim), F32)
    if halo:
        d_qkv[:halo, : heads * dim] = jnp.zeros((halo, heads * dim), BF16)
    for h in range(heads):
        cut = slice(h * dim, (h + 1) * dim)
        du, dg = turned_back(q_raw[:, cut], gain_q, d_q[:, cut], cosine[halo:, :], sine[halo:, :])
        total_q += dg
        d_qkv[halo:, cut] = du.astype(BF16)
    total_k = jnp.zeros((1, dim), F32)
    for i in range(n_tok):
        here = slice(i * rows, (i + 1) * rows)
        du, dg = turned_back(k_raw[here, :], gain_k, d_k[here, :], cosine[here, :], sine[here, :])
        total_k += dg
        d_qkv[here, heads * dim : (heads + 1) * dim] = du.astype(BF16)
        d_qkv[here, (heads + 1) * dim :] = d_v[here, :].astype(BF16)
    column_blocks(at, fsdp, normed_t, d_qkv, keep, send)
    for copy in copies:
        copy.wait()
    total_in = jnp.zeros(gain_in.shape, F32)
    for i in range(n_tok):
        here = slice(i * rows, (i + 1) * rows)
        if i < n_tok - 1:
            d_normed = dot_nt(d_qkv[here, heads * dim :], w_full[:, heads * dim :])
        else:
            d_normed = dot_nt(d_qkv[here, :], w_full[...])
        du, dg = norm_back(toks[i][...].astype(F32), gain_in, d_normed)
        total_in += dg
        if i < n_tok - 1:
            d_halo[here, :] = du.astype(BF16)
        else:
            grad_tokens[...] = d_residual[...] + du
    gain_rows[...] = jnp.zeros(gain_rows.shape, F32)
    at_row = 0
    for total in (total_in, total_q, total_k, g_attn[...], g_ffn[...], g_out[...]):
        for i in range(total.shape[1] // LANES):
            gain_rows[at_row : at_row + 1, :LANES] = total[:, i * LANES : (i + 1) * LANES]
            at_row += 1
    packed = gain_rows[...].astype(BF16)
    for target in (keep, send):
        for f in range(fsdp):
            for x in range(2):
                target[f, x, tall:, :] = packed


def add(*terms):
    out = terms[0].astype(F32)
    for term in terms[1:]:
        out = out + term.astype(F32)
    return out


class Chunk:
    def __init__(self, here, keep, send):
        self.here, self.keep = here, keep
        self.other = here.core_swap(send)

    def over_fsdp(self, *earlier):
        here = self.here
        parts = [add(self.keep[by], self.other[by]).astype(BF16) for by in range(1, here.fsdp)]
        self.arrived = [here.fsdp_shift(after(part, *earlier), by + 1) for by, part in enumerate(parts)]

    def over_mid(self, *earlier):
        self.arrived = [after(a, *earlier) for a in self.arrived]
        terms = [self.keep[0, 1], self.other[0, 1]] + [a[1] for a in self.arrived]
        self.across = self.here.mid_swap(add(*terms).astype(BF16))
        self.mine = [self.keep[0, 0], self.other[0, 0]] + [a[0] for a in self.arrived]
        return self.arrived[0] if self.arrived else self.other

    def join(self, below, *earlier):
        for chunk in (self, below):
            chunk.arrived = [after(a, *earlier) for a in chunk.arrived]
        pairs = [
            [[c.keep[0, x], c.other[0, x]] + [a[x] for a in c.arrived] for c in (self, below)] for x in range(2)
        ]
        self.across_sent = jnp.concatenate([add(*terms).astype(BF16) for terms in pairs[1]])
        self.across = self.here.mid_swap(self.across_sent)
        self.mine = [jnp.concatenate([add(*terms).astype(BF16) for terms in pairs[0]])]

    def outer_sums(self, *earlier):
        here = self.here
        self.across = after(self.across, *earlier)
        mine = add(*self.mine, self.across).astype(BF16)
        n, w = mine.shape
        mine = mine.reshape(here.outer, n // here.outer, w)
        self.shares = [pick(mine, here.outer_ahead[0])]
        for by in range(1, here.outer):
            self.shares.append(here.outer_shift(pick(mine, here.outer_ahead[by]), by))
        return self.across

    def outer_gather(self, *earlier):
        here = self.here
        self.shares = list(after(tuple(self.shares), *earlier))
        own = add(*self.shares).astype(BF16)
        self.gathered = [own] + [here.outer_shift(own, by) for by in range(1, here.outer)]
        return self.shares[-1]

    def mid_gather(self, *earlier):
        here = self.here
        self.gathered = list(after(tuple(self.gathered), *earlier))
        block = ordered(self.gathered, here.outer_behind)
        block = block.reshape(-1, block.shape[-1])
        across = here.mid_swap(block)
        self.blocks = [[block, across], [here.core_swap(block), here.core_swap(across)]]
        return self.gathered[-1]


def by_place(here, blocks):
    own = [jnp.where(here.mid_at == 0, a, b) for a, b in blocks]
    other = [jnp.where(here.mid_at == 0, b, a) for a, b in blocks]
    pairs = list(zip(own, other))
    first = [jnp.where(here.core_at == 0, a, b) for a, b in zip(pairs[0], pairs[1])]
    second = [jnp.where(here.core_at == 0, b, a) for a, b in zip(pairs[0], pairs[1])]
    return first + second


def on_device(
    tokens, positions, cotangent, in_gain, w_query, w_key, w_value, query_gain, key_gain, w_out, attn_gain,
    ffn_gain_in, w_gate, w_up, w_down, ffn_gain_out,
):
    here = Places()
    fsdp = here.fsdp
    rows, width = tokens.shape
    dim = w_key.shape[1]
    query_cols = w_query.shape[1]
    heads = query_cols // dim
    hidden = w_gate.shape[1]
    hops = (WINDOW + rows - 1) // rows
    n_tok = hops + 1
    halo = hops * rows
    every = halo + rows
    at = here.vector

    gains = (in_gain, query_gain, key_gain, attn_gain, ffn_gain_in, ffn_gain_out)
    cuts = [0]
    for gain in gains:
        cuts.append(cuts[-1] + gain.shape[0])
    gain_row = jnp.concatenate(gains)
    gain_rows = ordered([gain_row] + [here.fsdp_shift(gain_row, by) for by in range(1, fsdp)], here.fsdp_behind)
    gain_rows = gain_rows.astype(F32)
    gain_table = jnp.concatenate(
        [
            jnp.pad(gain_rows[:, cuts[i] : cuts[i + 1]].reshape(1, -1), ((0, 0), (0, width - fsdp * gains[i].shape[0])))
            for i in range(6)
        ]
        + [jnp.zeros((2, width), F32)],
        axis=0,
    )
    qkv_w = [w_query, w_key, w_value]
    qkv_part = own_part(here, qkv_w, 1, 4)
    tokens_out = after(tokens, qkv_part)
    toks = [linear_shift(tokens_out, by) for by in range(hops, 0, -1)] + [tokens]
    qkv_w += on_chips(here, over_links(here, qkv_part), 4)
    out_arrived = over_links(here, after(own_part(here, [w_out], 0, 2), *toks[:-1]))
    gate_arrived = over_links(here, after(own_part(here, [w_gate], 1, 4), qkv_w[3]))

    all_positions = jnp.concatenate([positions[0] - halo + jnp.arange(halo, dtype=jnp.int32), positions])
    frequency = ROPE_BASE ** (-(jnp.arange(dim // 2, dtype=F32) * 2.0 / dim))
    angles = all_positions.astype(F32)[:, None] * frequency[None, :]
    cosine, sine = jnp.cos(angles), jnp.sin(angles)

    span = WINDOW + QBLOCK
    weight_bytes = 2 * fsdp * w_gate.size
    normed, q_raw, k_raw, q_st, keys, values, probs, attended = pl.pallas_call(
        functools.partial(attend_kernel, n_tok, len(qkv_w), heads),
        out_shape=(
            shape((every, width), BF16),
            shape((rows, query_cols), F32),
            shape((every, dim), F32),
            shape((heads * rows, dim), BF16),
            shape((every, dim), BF16),
            shape((every, dim), BF16),
            shape((heads * rows, span), BF16),
            shape((rows, query_cols), BF16),
        ),
        in_specs=[SMEM] + [VMEM] * (n_tok + 4) + [ANY] * len(qkv_w),
        out_specs=(VMEM,) * 8,
        scratch_shapes=[
            pltpu.VMEM((width, query_cols + 2 * dim), BF16),
            pltpu.SemaphoreType.DMA((len(qkv_w),)),
        ],
        compiler_params=params(),
        cost_estimate=cost(4e9, 1e7),
        name="attend",
    )(at, *toks, positions[:, None], cosine, sine, gain_table, *qkv_w)

    up_part = after(own_part(here, [w_up], 1, 2), attended, *gate_arrived, *out_arrived)
    up_arrived = over_links(here, up_part)
    down_arrived = over_links(here, after(own_part(here, [w_down], 0, 2), attended))
    out_w = [w_out] + on_chips(here, [after(a, attended) for a in out_arrived], 2)
    gate_w = [w_gate] + on_chips(here, [after(a, attended) for a in gate_arrived], 4)
    up_w = [w_up] + on_chips(here, up_arrived, 2)
    projected, residual, ffn_in, mixed, gelu_out, gate_slope = pl.pallas_call(
        functools.partial(gate_kernel, len(out_w), len(gate_w), len(up_w)),
        out_shape=(
            shape((rows, width), F32),
            shape((rows, width), F32),
            shape((rows, width), BF16),
            shape((rows, hidden), BF16),
            shape((rows, hidden), BF16),
            shape((rows, hidden), BF16),
        ),
        in_specs=[SMEM] + [VMEM] * 3 + [ANY] * (len(out_w) + len(gate_w) + len(up_w)),
        out_specs=(VMEM,) * 6,
        scratch_shapes=[
            pltpu.VMEM((query_cols, width), BF16),
            pltpu.VMEM((width, hidden), BF16),
            pltpu.VMEM((width, hidden), BF16),
            pltpu.SemaphoreType.DMA((len(out_w),)),
            pltpu.SemaphoreType.DMA((len(gate_w),)),
            pltpu.SemaphoreType.DMA((len(up_w),)),
        ],
        compiler_params=params(),
        cost_estimate=cost(4e9, 2 * weight_bytes),
        name="gate",
    )(at, attended, tokens, gain_table, *out_w, *gate_w, *up_w)

    down_w = [w_down] + on_chips(here, [after(a, mixed) for a in down_arrived], 2)
    down_block = w_down.shape[0] // 4
    down_shape = shape((fsdp, 2, down_block, width), BF16)
    layer_out, d_down, g_ffn_out, down_keep, down_send = pl.pallas_call(
        functools.partial(down_kernel, len(down_w), fsdp),
        out_shape=(
            shape((rows, width), BF16),
            shape((rows, width), BF16),
            shape((1, width), F32),
            down_shape,
            down_shape,
        ),
        in_specs=[SMEM] + [VMEM] * 4 + [ANY] * len(down_w),
        out_specs=(VMEM,) * 5,
        scratch_shapes=[
            pltpu.VMEM((hidden, width), BF16),
            pltpu.VMEM((hidden, rows), BF16),
            pltpu.SemaphoreType.DMA((len(down_w),)),
        ],
        compiler_params=params(),
        cost_estimate=cost(4e9, 2 * weight_bytes),
        name="down",
    )(at, mixed, residual, cotangent, gain_table, *down_w)

    down_sum = Chunk(here, down_keep, down_send)
    gate_shape = shape((fsdp, 2, w_gate.shape[0], hidden // 4), BF16)
    d_gate, d_up, gate_keep, gate_send, up_keep, up_send = pl.pallas_call(
        functools.partial(gate_back_kernel, len(down_w), fsdp),
        out_shape=(
            shape((rows, hidden), BF16),
            shape((rows, hidden), BF16),
            gate_shape,
            gate_shape,
            gate_shape,
            gate_shape,
        ),
        in_specs=[SMEM] + [VMEM] * 4 + [ANY] * len(down_w),
        out_specs=(VMEM,) * 6,
        scratch_shapes=[
            pltpu.VMEM((hidden, width), BF16),
            pltpu.VMEM((width, rows), BF16),
            pltpu.SemaphoreType.DMA((len(down_w),)),
        ],
        compiler_params=params(),
        cost_estimate=cost(6e9, 3 * weight_bytes),
        name="gate_back",
    )(at, d_down, gelu_out, gate_slope, ffn_in, *down_w)
    gate_sum = Chunk(here, gate_keep, gate_send)
    up_sum = Chunk(here, up_keep, up_send)
    down_sum.over_fsdp(d_gate)
    d_gate = after(d_gate, down_sum.other)
    qkv_cols = query_cols + 2 * dim
    last_wide = qkv_cols // 4
    shard_rows = w_query.shape[0]
    last_shape = shape((fsdp, 2, shard_rows + GAIN_ROWS, last_wide), BF16)
    out_block = w_out.shape[0] // 4
    out_shape = shape((fsdp, 2, out_block * width // (hidden // 4), hidden // 4), BF16)
    d_residual, g_ffn, g_attn, d_att, out_keep, out_send = pl.pallas_call(
        functools.partial(middle_kernel, len(out_w), len(gate_w), len(up_w), fsdp, heads),
        out_shape=(
            shape((rows, width), F32),
            shape((1, width), F32),
            shape((1, width), F32),
            shape((heads * rows, dim), BF16),
            out_shape,
            out_shape,
        ),
        in_specs=[SMEM] + [VMEM] * 7 + [ANY] * (len(out_w) + len(gate_w) + len(up_w)),
        out_specs=(VMEM,) * 6,
        scratch_shapes=[
            pltpu.VMEM((query_cols, width), BF16),
            pltpu.VMEM((width, hidden), BF16),
            pltpu.VMEM((width, hidden), BF16),
            pltpu.VMEM((query_cols, rows), BF16),
            pltpu.SemaphoreType.DMA((len(out_w),)),
            pltpu.SemaphoreType.DMA((len(gate_w),)),
            pltpu.SemaphoreType.DMA((len(up_w),)),
        ],
        compiler_params=params(),
        cost_estimate=cost(6e9, 4 * weight_bytes),
        name="middle",
    )(at, d_gate, d_up, residual, projected, cotangent, gain_table, attended, *out_w, *gate_w, *up_w)

    out_sum = Chunk(here, out_keep, out_send)
    gate_sum.over_fsdp(g_ffn)
    up_sum.over_fsdp(g_ffn)
    down_sum.over_mid(g_ffn)
    d_q, d_k, d_v = pl.pallas_call(
        functools.partial(attend_back_kernel, halo, heads),
        out_shape=(shape((rows, query_cols), F32), shape((every, dim), F32), shape((every, dim), F32)),
        in_specs=[VMEM] * 5,
        out_specs=(VMEM,) * 3,
        scratch_shapes=[pltpu.VMEM((heads * QBLOCK, span), BF16)],
        compiler_params=params(),
        cost_estimate=cost(6e9, 3 * weight_bytes),
        name="attend_back",
    )(after(d_att, gate_sum.other, up_sum.other, *down_sum.arrived), q_st, keys, values, probs)
    out_sum.over_fsdp(d_k)
    down_sum.outer_sums(d_k)
    d_q = after(d_q, out_sum.other, down_sum.across)
    grad_tokens, d_halo, last_keep, last_send = pl.pallas_call(
        functools.partial(last_kernel, len(qkv_w), n_tok, fsdp, heads),
        out_shape=(
            shape((rows, width), F32),
            shape((halo, width), BF16),
            last_shape,
            last_shape,
        ),
        in_specs=[SMEM] + [VMEM] * (13 + n_tok) + [ANY] * len(qkv_w),
        out_specs=(VMEM,) * 4,
        scratch_shapes=[
            pltpu.VMEM((width, qkv_cols), BF16),
            pltpu.VMEM((width, every), BF16),
            pltpu.VMEM((every, qkv_cols), BF16),
            pltpu.VMEM((GAIN_ROWS, last_wide), F32),
            pltpu.SemaphoreType.DMA((len(qkv_w),)),
        ],
        compiler_params=params(),
        cost_estimate=cost(15e9, 4 * weight_bytes),
        name="last",
    )(
        at, d_residual, d_q, d_k, d_v,
        q_raw, k_raw, cosine, sine, gain_table, normed, g_ffn, g_attn, g_ffn_out, *toks, *qkv_w,
    )

    last_sum = Chunk(here, last_keep, last_send)
    down_sum.outer_sums(last_keep)
    gate_sum.over_mid(last_keep, *up_sum.arrived)
    (last_sum.other,), (gate_sum.across,), down_sum.shares, out_sum.arrived = together(
        (last_sum.other,), (gate_sum.across,), down_sum.shares, out_sum.arrived
    )
    last_sum.over_fsdp()
    up_sum.join(out_sum)
    gate_sum.outer_sums()
    down_sum.outer_gather()
    last_sum.arrived, (up_sum.across,), gate_sum.shares, down_sum.gathered = together(
        last_sum.arrived, (up_sum.across,), gate_sum.shares, down_sum.gathered
    )
    last_sum.over_mid()
    up_sum.outer_sums()
    gate_sum.outer_gather()
    down_sum.mid_gather()
    (last_sum.across,), up_sum.shares, gate_sum.gathered, down_last = together(
        (last_sum.across,), up_sum.shares, gate_sum.gathered, down_sum.blocks[0]
    )
    down_sum.blocks[0] = list(down_last)
    last_sum.outer_sums()
    up_sum.outer_gather()
    gate_sum.mid_gather()
    last_sum.shares, up_sum.gathered, gate_last = together(last_sum.shares, up_sum.gathered, gate_sum.blocks[0])
    gate_sum.blocks[0] = list(gate_last)
    last_sum.outer_gather()
    up_sum.mid_gather()
    d_halo = after(d_halo, *last_sum.shares)
    halos = [linear_shift(d_halo[halo - by * rows :][:rows], -by) for by in range(1, hops + 1)]
    last_sum.mid_gather()
    down_blocks, gate_blocks = by_place(here, down_sum.blocks), by_place(here, gate_sum.blocks)
    both_blocks, last_blocks = by_place(here, up_sum.blocks), by_place(here, last_sum.blocks)
    total_gains = last_sum.blocks[0][0][shard_rows:, :LANES].astype(F32)

    for came in halos:
        grad_tokens = grad_tokens + came.astype(F32)

    total_down = jnp.concatenate(down_blocks, axis=0).astype(F32)
    total_gate = jnp.concatenate(gate_blocks, axis=1).astype(F32)
    total_up = jnp.concatenate([b[:shard_rows] for b in both_blocks], axis=1).astype(F32)
    total_qkv = jnp.concatenate([b[:shard_rows] for b in last_blocks], axis=1).astype(F32)
    wide = hidden // 4
    parts = wide // LANES
    total_out = []
    for block in both_blocks:
        below = block[shard_rows + out_block :].reshape(out_block // parts, parts, LANES)
        below = below.transpose(1, 0, 2).reshape(out_block, LANES)
        total_out.append(jnp.concatenate([block[shard_rows : shard_rows + out_block], below], axis=1))
    total_out = jnp.concatenate(total_out, axis=0).astype(F32)
    g, at_row = [], 0
    for gain in gains:
        deep = fsdp * gain.shape[0] // total_gains.shape[1]
        total = total_gains[at_row : at_row + deep].reshape(fsdp, gain.shape[0])
        g.append(pick(total, here.fsdp_at))
        at_row += deep
    return (
        layer_out, grad_tokens, g[0],
        total_qkv[:, :query_cols],
        total_qkv[:, query_cols : query_cols + dim],
        total_qkv[:, query_cols + dim :],
        g[1], g[2], total_out, g[3], g[4], total_gate, total_up, total_down, g[5],
    )


def solution(mesh):
    tok = P(("seq", "fsdp"), None)
    mat = P("fsdp", None)
    vec = P("fsdp")
    return jax.shard_map(
        on_device,
        mesh=mesh,
        in_specs=(tok, P(("seq", "fsdp")), tok, vec, mat, mat, mat, vec, vec, mat, vec, vec, mat, mat, mat, vec),
        out_specs=(tok, tok, vec, mat, mat, mat, vec, vec, mat, vec, vec, mat, mat, mat, vec),
        check_vma=False,
    )
```

```python
import functools
import math

import jax
import jax.numpy as jnp
from jax import lax
from jax.experimental import pallas as pl
from jax.experimental.pallas import tpu as pltpu
from jax.sharding import PartitionSpec as P

WINDOW = 512
EPSILON = 1e-06
ROPE_BASE = 10000.0
MASKED = -1e30
BF16 = jnp.bfloat16
F32 = jnp.float32
QBLOCK = 128
LANES = 128
GAIN_ROWS = 32
GELU_A = math.sqrt(2.0 / math.pi)
GELU_B = 0.044715

VMEM = pl.BlockSpec(memory_space=pltpu.VMEM)
SMEM = pl.BlockSpec(memory_space=pltpu.SMEM)
ANY = pl.BlockSpec(memory_space=pl.ANY)


def wrapped(value, size):
    return value & (size - 1) if size & (size - 1) == 0 else lax.rem(value, jnp.int32(size))


class Places:
    def __init__(self):
        self.seq = lax.axis_size("seq")
        self.fsdp = lax.axis_size("fsdp")
        self.outer = self.seq // 4
        index = lax.axis_index("seq").astype(jnp.int32)
        fsdp_at = lax.axis_index("fsdp").astype(jnp.int32)
        outer_at = lax.shift_right_logical(index, 2)
        core_at, mid_at = index & 1, lax.shift_right_logical(index, 1) & 1
        scalars = lax.optimization_barrier(
            (
                core_at,
                mid_at,
                fsdp_at,
                core_at * 2 + mid_at,
                tuple(wrapped(outer_at + by, self.outer) for by in range(self.outer)),
                tuple(wrapped(outer_at - by + self.outer, self.outer) for by in range(self.outer)),
                tuple(wrapped(fsdp_at + by, self.fsdp) for by in range(self.fsdp)),
                tuple(wrapped(fsdp_at - by + self.fsdp, self.fsdp) for by in range(self.fsdp)),
                jnp.stack([core_at, mid_at, fsdp_at]),
            )
        )
        self.core_at, self.mid_at, self.fsdp_at, self.quarter_at = scalars[:4]
        self.outer_ahead, self.outer_behind, self.fsdp_ahead, self.fsdp_behind, self.vector = scalars[4:]

    def core_swap(self, array):
        return lax.ppermute(array, "seq", [(i, i ^ 1) for i in range(self.seq)])

    def mid_swap(self, array):
        return lax.ppermute(array, "seq", [(i, i ^ 2) for i in range(self.seq)])

    def outer_shift(self, array, by):
        return lax.ppermute(array, "seq", [(i, (i + 4 * by) % self.seq) for i in range(self.seq)])

    def fsdp_shift(self, array, by):
        return lax.ppermute(array, "fsdp", [(i, (i + by) % self.fsdp) for i in range(self.fsdp)])


def linear_shift(array, by):
    count = lax.axis_size("seq") * lax.axis_size("fsdp")
    return lax.ppermute(array, ("seq", "fsdp"), [(i, i + by) for i in range(count) if 0 <= i + by < count])


def pick(array, at):
    return lax.dynamic_index_in_dim(array, at, 0, keepdims=False, allow_negative_indices=False)


def ordered(pieces, behind):
    if len(pieces) == 2:
        own, other = pieces
        return jnp.where(behind[0] == 0, jnp.stack([own, other]), jnp.stack([other, own]))
    stacked = jnp.stack(pieces)
    return jnp.stack([pick(stacked, at) for at in behind])


def own_part(here, shards, axis, ways):
    size = sum(shard.shape[axis] for shard in shards) // ways
    place = here.quarter_at if ways == 4 else here.core_at
    if len(shards) == 1:
        return lax.dynamic_slice_in_dim(shards[0], place * size, size, axis, allow_negative_indices=False)
    parts = []
    for i in range(ways):
        pieces, start = [], 0
        for shard in shards:
            low, high = max(i * size - start, 0), min((i + 1) * size - start, shard.shape[axis])
            if low < high:
                pieces.append(lax.slice_in_dim(shard, low, high, axis=axis))
            start += shard.shape[axis]
        parts.append(jnp.concatenate(pieces, axis))
    return functools.reduce(lambda rest, i: jnp.where(place == i, parts[i], rest), range(1, ways), parts[0])


def after(value, *earlier):
    return lax.optimization_barrier((value, *earlier))[0]


def together(*groups):
    return lax.optimization_barrier(tuple(tuple(group) for group in groups))


def over_links(here, part):
    return [here.fsdp_shift(part, by) for by in range(1, here.fsdp)]


def on_chips(here, arrived, ways):
    pieces = []
    for mine in arrived:
        if ways == 4:
            across = here.mid_swap(mine)
            pieces += [mine, across, here.core_swap(mine), here.core_swap(across)]
        else:
            pieces += [mine, here.core_swap(mine)]
    return pieces


def multiple(value, of):
    return pl.multiple_of(value, of)


def place_copies(owned, pieces, whole, sems, at, axis, ways):
    core, mid, fsdp = at[0], at[1], at[2]
    count = 1 + len(pieces) // ways
    rows = owned[0].shape[0]
    copies = []
    column = 0
    own_row = multiple(fsdp * rows, 16)
    for shard in owned:
        wide = shard.shape[1]
        copies.append((shard, whole.at[pl.ds(own_row, rows), pl.ds(column, wide)]))
        column += wide
    for k, piece in enumerate(pieces):
        by = 1 + k // ways
        row = multiple(lax.rem(fsdp + (count - by), count) * rows, 16)
        k = k % ways
        if ways == 4:
            place = (core if k < 2 else 1 - core) * 2 + (mid if k % 2 == 0 else 1 - mid)
        else:
            place = core if k == 0 else 1 - core
        if axis == 0:
            target = whole.at[pl.ds(multiple(row + place * (rows // ways), 16), rows // ways), :]
        else:
            target = whole.at[pl.ds(row, rows), pl.ds(multiple(place * (column // ways), 128), column // ways)]
        copies.append((piece, target))
    return [pltpu.make_async_copy(a, b, sems.at[k]) for k, (a, b) in enumerate(copies)]


def dot(a, b):
    return lax.dot_general(a, b, (((1,), (0,)), ((), ())), preferred_element_type=F32)


def dot_nt(a, b):
    return lax.dot_general(a, b, (((1,), (1,)), ((), ())), preferred_element_type=F32)


def dot_tn(a, b):
    return lax.dot_general(a, b, (((0,), (0,)), ((), ())), preferred_element_type=F32)


def inverse_rms(u):
    return lax.rsqrt(jnp.mean(u * u, axis=-1, keepdims=True) + EPSILON)


def norm_back(u, g, dz):
    r = inverse_rms(u)
    ur = u * r
    gdz = g * dz
    du = r * (gdz - ur * jnp.mean(gdz * ur, axis=-1, keepdims=True))
    return du, jnp.sum(dz * ur, axis=0, keepdims=True)


def params(megabytes=56):
    return pltpu.CompilerParams(vmem_limit_bytes=megabytes * 1024 * 1024)


def cost(flops, bytes_accessed):
    return pl.CostEstimate(flops=int(20 * flops), bytes_accessed=int(20 * bytes_accessed), transcendentals=0)


def shape(dims, kind):
    return jax.ShapeDtypeStruct(tuple(dims), kind)


def attend_kernel(n_tok, n_qkv, heads, *refs):
    at = refs[0]
    toks = refs[1 : 1 + n_tok]
    pos, cosine, sine, gain_table = refs[1 + n_tok : 5 + n_tok]
    qkv = refs[5 + n_tok : 5 + n_tok + n_qkv]
    normed, q_raw, k_raw, q_st, keys, values, probs, attended, w_full, sems = refs[5 + n_tok + n_qkv :]
    copies = place_copies(qkv[:3], qkv[3:], w_full, sems, at, 1, 4)
    for copy in copies:
        copy.start()
    rows = toks[0].shape[0]
    dim = keys.shape[1]
    half = dim // 2
    halo = (n_tok - 1) * rows
    gain = gain_table[0:1, :]
    gain_q, gain_k = gain_table[1:2, :dim], gain_table[2:3, :dim]
    for i, tok in enumerate(toks):
        u = tok[...].astype(F32)
        normed[i * rows : (i + 1) * rows, :] = (u * inverse_rms(u) * gain).astype(BF16)
    for copy in copies:
        copy.wait()

    def turned(u, g, cos, sin):
        u = u * inverse_rms(u) * g
        first, second = u[:, :half], u[:, half:]
        return (first * cos - second * sin).astype(BF16), (second * cos + first * sin).astype(BF16)

    for i in range(n_tok):
        here = slice(i * rows, (i + 1) * rows)
        kv = dot(normed[here, :], w_full[:, heads * dim :])
        k_raw[here, :] = kv[:, :dim]
        values[here, :] = kv[:, dim:].astype(BF16)
        first, second = turned(kv[:, :dim], gain_k, cosine[here, :], sine[here, :])
        keys[here, :half] = first
        keys[here, half:] = second
    blocks = rows // QBLOCK
    for h in range(heads):
        u = dot(normed[halo:, :], w_full[:, h * dim : (h + 1) * dim])
        q_raw[:, h * dim : (h + 1) * dim] = u
        first, second = turned(u, gain_q, cosine[halo:, :], sine[halo:, :])
        for b in range(blocks):
            start = (b * heads + h) * QBLOCK
            q_st[start : start + QBLOCK, :half] = first[b * QBLOCK : (b + 1) * QBLOCK, :]
            q_st[start : start + QBLOCK, half:] = second[b * QBLOCK : (b + 1) * QBLOCK, :]
    span = WINDOW + QBLOCK
    distance = (
        lax.broadcasted_iota(jnp.int32, (QBLOCK, span), 0)
        + WINDOW
        - lax.broadcasted_iota(jnp.int32, (QBLOCK, span), 1)
    )
    scale = dim ** (-0.5)
    for b in range(blocks):
        first_key = halo - WINDOW + b * QBLOCK
        limit = jnp.minimum(pos[b * QBLOCK : (b + 1) * QBLOCK, :], WINDOW - 1)
        allowed = (distance >= 0) & (distance <= limit)
        for h in range(heads):
            start = (b * heads + h) * QBLOCK
            scores = dot_nt(q_st[start : start + QBLOCK, :], keys[first_key : first_key + span, :]) * scale
            scores = jnp.where(allowed, scores, MASKED)
            weights = jnp.exp(scores - jnp.max(scores, axis=-1, keepdims=True))
            weights = (weights * (1.0 / jnp.sum(weights, axis=-1, keepdims=True))).astype(BF16)
            probs[start : start + QBLOCK, :] = weights
            attended[b * QBLOCK : (b + 1) * QBLOCK, h * dim : (h + 1) * dim] = dot(
                weights, values[first_key : first_key + span, :]
            ).astype(BF16)


def gate_kernel(n_out, n_gate, n_up, *refs):
    at, attended, tokens, gain_table = refs[:4]
    refs = refs[4:]
    out_w, gate_w, up_w, refs = (
        refs[:n_out],
        refs[n_out : n_out + n_gate],
        refs[n_out + n_gate : n_out + n_gate + n_up],
        refs[n_out + n_gate + n_up :],
    )
    projected_ref, residual_ref, ffn_in_ref, mixed, gelu_out, gate_slope = refs[:6]
    out_full, gate_full, up_full, out_sems, gate_sems, up_sems = refs[6:]
    groups = (
        place_copies(out_w[:1], out_w[1:], out_full, out_sems, at, 0, 2),
        place_copies(gate_w[:1], gate_w[1:], gate_full, gate_sems, at, 1, 4),
        place_copies(up_w[:1], up_w[1:], up_full, up_sems, at, 1, 2),
    )
    for group in groups:
        for copy in group:
            copy.start()
    for copy in groups[0]:
        copy.wait()
    projected = dot(attended[...], out_full[...])
    projected_ref[...] = projected
    residual = tokens[...].astype(F32) + projected * inverse_rms(projected) * gain_table[3:4, :]
    residual_ref[...] = residual
    ffn_in_ref[...] = (residual * inverse_rms(residual) * gain_table[4:5, :]).astype(BF16)
    for group in groups[1:]:
        for copy in group:
            copy.wait()
    width = 256

    def step(i, _):
        cut = pl.ds(multiple(i * width, width), width)
        gate = dot(ffn_in_ref[...], gate_full[:, cut])
        up = dot(ffn_in_ref[...], up_full[:, cut])
        square = gate * gate
        t = jnp.tanh(GELU_A * gate * (1.0 + GELU_B * square))
        cdf = 0.5 * (1.0 + t)
        act = gate * cdf
        slope = cdf + 0.5 * gate * (1.0 - t * t) * (GELU_A * (1.0 + 3.0 * GELU_B * square))
        mixed[:, cut] = (act * up).astype(BF16)
        gelu_out[:, cut] = act.astype(BF16)
        gate_slope[:, cut] = (up * slope).astype(BF16)
        return 0

    lax.fori_loop(0, gate_full.shape[1] // width, step, 0)


def relative_blocks(at, fsdp):
    for c in range(2):
        core = c + at[0] - 2 * c * at[0]
        for f in range(fsdp):
            row = lax.rem(at[2] + f, fsdp)
            for x in range(2):
                mid = x + at[1] - 2 * x * at[1]
                yield c, f, x, core, row, mid


def column_blocks(at, fsdp, left_t, right, keep, send):
    tall, wide = left_t.shape[0] // fsdp, keep.shape[3]
    for c, f, x, core, row, mid in relative_blocks(at, fsdp):
        cut = pl.ds(multiple((core * 2 + mid) * wide, 128), wide)
        left = left_t[pl.ds(multiple(row * tall, 16), tall), :]
        target = keep if c == 0 else send
        target[f, x, :tall, :] = dot(left, right[:, cut]).astype(BF16)


def down_kernel(n_down, fsdp, *refs):
    at, mixed, residual, cotangent, gain_table = refs[:5]
    down_w = refs[5 : 5 + n_down]
    layer_out, d_down, grad_gain, keep, send = refs[5 + n_down : 10 + n_down]
    down_full, mixed_t, sems = refs[10 + n_down :]
    copies = place_copies(down_w[:1], down_w[1:], down_full, sems, at, 0, 2)
    for copy in copies:
        copy.start()
    mixed_t[...] = mixed[...].T
    for copy in copies:
        copy.wait()
    down = dot(mixed[...], down_full[...])
    r = inverse_rms(down)
    gain = gain_table[5:6, :]
    layer_out[...] = (residual[...] + down * r * gain).astype(BF16)
    du, dg = norm_back(down, gain, cotangent[...].astype(F32))
    grad_gain[...] = dg
    d_down[...] = du.astype(BF16)
    block = keep.shape[2]
    for c, f, x, core, row, mid in relative_blocks(at, fsdp):
        start = multiple(((row * 2 + core) * 2 + mid) * block, 16)
        target = keep if c == 0 else send
        target[f, x] = dot(mixed_t[pl.ds(start, block), :], d_down[...]).astype(BF16)


def gate_back_kernel(n_down, fsdp, *refs):
    at, d_down, gelu_out, gate_slope, ffn_in = refs[:5]
    down_w = refs[5 : 5 + n_down]
    d_gate, d_up, keep, send, up_keep, up_send = refs[5 + n_down : 11 + n_down]
    down_full, ffn_t, sems = refs[11 + n_down :]
    copies = place_copies(down_w[:1], down_w[1:], down_full, sems, at, 0, 2)
    for copy in copies:
        copy.start()
    ffn_t[...] = ffn_in[...].T
    for copy in copies:
        copy.wait()
    width = 256

    def step(i, _):
        cut = pl.ds(multiple(i * width, width), width)
        d_mixed = dot_nt(d_down[...], down_full[cut, :])
        d_gate[:, cut] = (d_mixed * gate_slope[:, cut].astype(F32)).astype(BF16)
        d_up[:, cut] = (d_mixed * gelu_out[:, cut].astype(F32)).astype(BF16)
        return 0

    lax.fori_loop(0, d_gate.shape[1] // width, step, 0)
    column_blocks(at, fsdp, ffn_t, d_gate, keep, send)
    column_blocks(at, fsdp, ffn_t, d_up, up_keep, up_send)


def middle_kernel(n_out, n_gate, n_up, fsdp, heads, *refs):
    at, d_gate, d_up, residual, projected, cotangent, gain_table, attended = refs[:8]
    refs = refs[8:]
    out_w, gate_w, up_w, refs = (
        refs[:n_out],
        refs[n_out : n_out + n_gate],
        refs[n_out + n_gate : n_out + n_gate + n_up],
        refs[n_out + n_gate + n_up :],
    )
    d_residual_ref, g_ffn, g_attn, d_att, keep, send = refs[:6]
    out_full, gate_full, up_full, att_t, out_sems, gate_sems, up_sems = refs[6:]
    groups = (
        place_copies(gate_w[:1], gate_w[1:], gate_full, gate_sems, at, 1, 4),
        place_copies(up_w[:1], up_w[1:], up_full, up_sems, at, 1, 2),
        place_copies(out_w[:1], out_w[1:], out_full, out_sems, at, 0, 2),
    )
    for group in groups:
        for copy in group:
            copy.start()
    att_t[...] = attended[...].T
    for copy in groups[0]:
        copy.wait()
    d_ffn_in = dot_nt(d_gate[...], gate_full[...])
    for copy in groups[1]:
        copy.wait()
    d_ffn_in = d_ffn_in + dot_nt(d_up[...], up_full[...])
    du, dg = norm_back(residual[...], gain_table[4:5, :], d_ffn_in)
    g_ffn[...] = dg
    d_residual = cotangent[...].astype(F32) + du
    d_residual_ref[...] = d_residual
    du, dg = norm_back(projected[...], gain_table[3:4, :], d_residual)
    g_attn[...] = dg
    d_proj = du.astype(BF16)
    rows, dim = d_proj.shape[0], d_att.shape[1]
    for copy in groups[2]:
        copy.wait()
    for h in range(heads):
        part = dot_nt(d_proj, out_full[h * dim : (h + 1) * dim, :]).astype(BF16)
        for b in range(rows // QBLOCK):
            start = (b * heads + h) * QBLOCK
            d_att[start : start + QBLOCK, :] = part[b * QBLOCK : (b + 1) * QBLOCK, :]
    block = att_t.shape[0] // (4 * fsdp)
    wide = keep.shape[3]
    parts = wide // LANES
    deep = block // parts
    for c, f, x, core, row, mid in relative_blocks(at, fsdp):
        start = multiple(((row * 2 + core) * 2 + mid) * block, 16)
        part = dot(att_t[pl.ds(start, block), :], d_proj).astype(BF16)
        target = keep if c == 0 else send
        target[f, x, :block, :] = part[:, :wide]
        for i in range(parts):
            target[f, x, block:, i * LANES : (i + 1) * LANES] = part[i * deep : (i + 1) * deep, wide:]


def attend_back_kernel(halo, heads, d_att, q_st, keys, values, probs, d_q, d_k, d_v, d_scores):
    rows = d_q.shape[0]
    dim = keys.shape[1]
    blocks = rows // QBLOCK
    span = WINDOW + QBLOCK
    scale = dim ** (-0.5)
    d_k[...] = jnp.zeros(d_k.shape, F32)
    d_v[...] = jnp.zeros(d_v.shape, F32)
    for b in range(blocks):
        first_key = halo - WINDOW + b * QBLOCK
        here = slice(first_key, first_key + span)
        for h in range(heads):
            start = (b * heads + h) * QBLOCK
            stack = slice(start, start + QBLOCK)
            d_probs = dot_nt(d_att[stack, :], values[here, :])
            p = probs[stack, :].astype(F32)
            row_terms = jnp.sum(p * d_probs, axis=-1, keepdims=True)
            ds = (p * (d_probs - row_terms) * scale).astype(BF16)
            d_scores[h * QBLOCK : (h + 1) * QBLOCK, :] = ds
            d_q[b * QBLOCK : (b + 1) * QBLOCK, h * dim : (h + 1) * dim] = dot(ds, keys[here, :])
        stack = slice(b * heads * QBLOCK, (b + 1) * heads * QBLOCK)
        d_k[here, :] += dot_tn(d_scores[...], q_st[stack, :])
        d_v[here, :] += dot_tn(probs[stack, :], d_att[stack, :])


def last_kernel(n_qkv, n_tok, fsdp, heads, *refs):
    (
        at, d_residual, d_q, d_k, d_v,
        q_raw, k_raw, cosine, sine, gain_table, normed, g_ffn, g_attn, g_out,
    ) = refs[:14]
    toks = refs[14 : 14 + n_tok]
    refs = refs[14 + n_tok :]
    qkv_w, refs = refs[:n_qkv], refs[n_qkv:]
    grad_tokens, d_halo, keep, send = refs[:4]
    w_full, normed_t, d_qkv, gain_rows, qkv_sems = refs[4:]
    copies = place_copies(qkv_w[:3], qkv_w[3:], w_full, qkv_sems, at, 1, 4)
    for copy in copies:
        copy.start()
    normed_t[...] = normed[...].T
    rows = toks[0].shape[0]
    halo = (n_tok - 1) * rows
    dim = k_raw.shape[1]
    gain_in, gain_q, gain_k = gain_table[0:1, :], gain_table[1:2, :dim], gain_table[2:3, :dim]
    half = dim // 2
    tall, wide = normed_t.shape[0] // fsdp, keep.shape[3]
    def turned_back(u, g, dz, cos, sin):
        first, second = dz[:, :half], dz[:, half:]
        dz = jnp.concatenate([first * cos + second * sin, second * cos - first * sin], axis=1)
        return norm_back(u, g, dz)

    total_q = jnp.zeros((1, dim), F32)
    if halo:
        d_qkv[:halo, : heads * dim] = jnp.zeros((halo, heads * dim), BF16)
    for h in range(heads):
        cut = slice(h * dim, (h + 1) * dim)
        du, dg = turned_back(q_raw[:, cut], gain_q, d_q[:, cut], cosine[halo:, :], sine[halo:, :])
        total_q += dg
        d_qkv[halo:, cut] = du.astype(BF16)
    total_k = jnp.zeros((1, dim), F32)
    for i in range(n_tok):
        here = slice(i * rows, (i + 1) * rows)
        du, dg = turned_back(k_raw[here, :], gain_k, d_k[here, :], cosine[here, :], sine[here, :])
        total_k += dg
        d_qkv[here, heads * dim : (heads + 1) * dim] = du.astype(BF16)
        d_qkv[here, (heads + 1) * dim :] = d_v[here, :].astype(BF16)
    column_blocks(at, fsdp, normed_t, d_qkv, keep, send)
    for copy in copies:
        copy.wait()
    total_in = jnp.zeros(gain_in.shape, F32)
    for i in range(n_tok):
        here = slice(i * rows, (i + 1) * rows)
        if i < n_tok - 1:
            d_normed = dot_nt(d_qkv[here, heads * dim :], w_full[:, heads * dim :])
        else:
            d_normed = dot_nt(d_qkv[here, :], w_full[...])
        du, dg = norm_back(toks[i][...].astype(F32), gain_in, d_normed)
        total_in += dg
        if i < n_tok - 1:
            d_halo[here, :] = du.astype(BF16)
        else:
            grad_tokens[...] = d_residual[...] + du
    gain_rows[...] = jnp.zeros(gain_rows.shape, F32)
    at_row = 0
    for total in (total_in, total_q, total_k, g_attn[...], g_ffn[...], g_out[...]):
        for i in range(total.shape[1] // LANES):
            gain_rows[at_row : at_row + 1, :LANES] = total[:, i * LANES : (i + 1) * LANES]
            at_row += 1
    packed = gain_rows[...].astype(BF16)
    for target in (keep, send):
        for f in range(fsdp):
            for x in range(2):
                target[f, x, tall:, :] = packed


def add(*terms):
    out = terms[0].astype(F32)
    for term in terms[1:]:
        out = out + term.astype(F32)
    return out


class Chunk:
    def __init__(self, here, keep, send):
        self.here, self.keep = here, keep
        self.other = here.core_swap(send)

    def over_fsdp(self, *earlier):
        here = self.here
        parts = [add(self.keep[by], self.other[by]).astype(BF16) for by in range(1, here.fsdp)]
        self.arrived = [here.fsdp_shift(after(part, *earlier), by + 1) for by, part in enumerate(parts)]

    def over_mid(self, *earlier):
        self.arrived = [after(a, *earlier) for a in self.arrived]
        terms = [self.keep[0, 1], self.other[0, 1]] + [a[1] for a in self.arrived]
        self.across = self.here.mid_swap(add(*terms).astype(BF16))
        self.mine = [self.keep[0, 0], self.other[0, 0]] + [a[0] for a in self.arrived]
        return self.arrived[0] if self.arrived else self.other

    def join(self, below, *earlier):
        for chunk in (self, below):
            chunk.arrived = [after(a, *earlier) for a in chunk.arrived]
        pairs = [
            [[c.keep[0, x], c.other[0, x]] + [a[x] for a in c.arrived] for c in (self, below)] for x in range(2)
        ]
        self.across_sent = jnp.concatenate([add(*terms).astype(BF16) for terms in pairs[1]])
        self.across = self.here.mid_swap(self.across_sent)
        self.mine = [jnp.concatenate([add(*terms).astype(BF16) for terms in pairs[0]])]

    def outer_sums(self, *earlier):
        here = self.here
        self.across = after(self.across, *earlier)
        mine = add(*self.mine, self.across).astype(BF16)
        n, w = mine.shape
        mine = mine.reshape(here.outer, n // here.outer, w)
        self.shares = [pick(mine, here.outer_ahead[0])]
        for by in range(1, here.outer):
            self.shares.append(here.outer_shift(pick(mine, here.outer_ahead[by]), by))
        return self.across

    def outer_gather(self, *earlier):
        here = self.here
        self.shares = list(after(tuple(self.shares), *earlier))
        own = add(*self.shares).astype(BF16)
        self.gathered = [own] + [here.outer_shift(own, by) for by in range(1, here.outer)]
        return self.shares[-1]

    def mid_gather(self, *earlier):
        here = self.here
        self.gathered = list(after(tuple(self.gathered), *earlier))
        block = ordered(self.gathered, here.outer_behind)
        block = block.reshape(-1, block.shape[-1])
        across = here.mid_swap(block)
        self.blocks = [[block, across], [here.core_swap(block), here.core_swap(across)]]
        return self.gathered[-1]


def by_place(here, blocks):
    own = [jnp.where(here.mid_at == 0, a, b) for a, b in blocks]
    other = [jnp.where(here.mid_at == 0, b, a) for a, b in blocks]
    pairs = list(zip(own, other))
    first = [jnp.where(here.core_at == 0, a, b) for a, b in zip(pairs[0], pairs[1])]
    second = [jnp.where(here.core_at == 0, b, a) for a, b in zip(pairs[0], pairs[1])]
    return first + second


def on_device(
    tokens, positions, cotangent, in_gain, w_query, w_key, w_value, query_gain, key_gain, w_out, attn_gain,
    ffn_gain_in, w_gate, w_up, w_down, ffn_gain_out,
):
    here = Places()
    fsdp = here.fsdp
    rows, width = tokens.shape
    dim = w_key.shape[1]
    query_cols = w_query.shape[1]
    heads = query_cols // dim
    hidden = w_gate.shape[1]
    hops = (WINDOW + rows - 1) // rows
    n_tok = hops + 1
    halo = hops * rows
    every = halo + rows
    at = here.vector

    gains = (in_gain, query_gain, key_gain, attn_gain, ffn_gain_in, ffn_gain_out)
    cuts = [0]
    for gain in gains:
        cuts.append(cuts[-1] + gain.shape[0])
    gain_row = jnp.concatenate(gains)
    gain_rows = ordered([gain_row] + [here.fsdp_shift(gain_row, by) for by in range(1, fsdp)], here.fsdp_behind)
    gain_rows = gain_rows.astype(F32)
    gain_table = jnp.concatenate(
        [
            jnp.pad(gain_rows[:, cuts[i] : cuts[i + 1]].reshape(1, -1), ((0, 0), (0, width - fsdp * gains[i].shape[0])))
            for i in range(6)
        ]
        + [jnp.zeros((2, width), F32)],
        axis=0,
    )
    qkv_w = [w_query, w_key, w_value]
    qkv_part = own_part(here, qkv_w, 1, 4)
    tokens_out = after(tokens, qkv_part)
    toks = [linear_shift(tokens_out, by) for by in range(hops, 0, -1)] + [tokens]
    qkv_w += on_chips(here, over_links(here, qkv_part), 4)
    out_arrived = over_links(here, after(own_part(here, [w_out], 0, 2), *toks[:-1]))
    gate_arrived = over_links(here, after(own_part(here, [w_gate], 1, 4), qkv_w[3]))
    up_arrived = over_links(here, after(own_part(here, [w_up], 1, 2), *gate_arrived))

    all_positions = jnp.concatenate([positions[0] - halo + jnp.arange(halo, dtype=jnp.int32), positions])
    frequency = ROPE_BASE ** (-(jnp.arange(dim // 2, dtype=F32) * 2.0 / dim))
    angles = all_positions.astype(F32)[:, None] * frequency[None, :]
    cosine, sine = jnp.cos(angles), jnp.sin(angles)

    span = WINDOW + QBLOCK
    weight_bytes = 2 * fsdp * w_gate.size
    normed, q_raw, k_raw, q_st, keys, values, probs, attended = pl.pallas_call(
        functools.partial(attend_kernel, n_tok, len(qkv_w), heads),
        out_shape=(
            shape((every, width), BF16),
            shape((rows, query_cols), F32),
            shape((every, dim), F32),
            shape((heads * rows, dim), BF16),
            shape((every, dim), BF16),
            shape((every, dim), BF16),
            shape((heads * rows, span), BF16),
            shape((rows, query_cols), BF16),
        ),
        in_specs=[SMEM] + [VMEM] * (n_tok + 4) + [ANY] * len(qkv_w),
        out_specs=(VMEM,) * 8,
        scratch_shapes=[
            pltpu.VMEM((width, query_cols + 2 * dim), BF16),
            pltpu.SemaphoreType.DMA((len(qkv_w),)),
        ],
        compiler_params=params(),
        cost_estimate=cost(4e9, 1e7),
        name="attend",
    )(at, *toks, after(positions[:, None], *gate_arrived), cosine, sine, gain_table, *qkv_w)

    down_arrived = over_links(here, after(own_part(here, [w_down], 0, 2), attended))
    out_w = [w_out] + on_chips(here, [after(a, attended) for a in out_arrived], 2)
    gate_w = [w_gate] + on_chips(here, gate_arrived, 4)
    up_w = [w_up] + on_chips(here, [after(a, attended) for a in up_arrived], 2)
    projected, residual, ffn_in, mixed, gelu_out, gate_slope = pl.pallas_call(
        functools.partial(gate_kernel, len(out_w), len(gate_w), len(up_w)),
        out_shape=(
            shape((rows, width), F32),
            shape((rows, width), F32),
            shape((rows, width), BF16),
            shape((rows, hidden), BF16),
            shape((rows, hidden), BF16),
            shape((rows, hidden), BF16),
        ),
        in_specs=[SMEM] + [VMEM] * 3 + [ANY] * (len(out_w) + len(gate_w) + len(up_w)),
        out_specs=(VMEM,) * 6,
        scratch_shapes=[
            pltpu.VMEM((query_cols, width), BF16),
            pltpu.VMEM((width, hidden), BF16),
            pltpu.VMEM((width, hidden), BF16),
            pltpu.SemaphoreType.DMA((len(out_w),)),
            pltpu.SemaphoreType.DMA((len(gate_w),)),
            pltpu.SemaphoreType.DMA((len(up_w),)),
        ],
        compiler_params=params(),
        cost_estimate=cost(4e9, 2 * weight_bytes),
        name="gate",
    )(at, attended, tokens, gain_table, *out_w, *gate_w, *up_w)

    down_w = [w_down] + on_chips(here, [after(a, mixed) for a in down_arrived], 2)
    down_block = w_down.shape[0] // 4
    down_shape = shape((fsdp, 2, down_block, width), BF16)
    layer_out, d_down, g_ffn_out, down_keep, down_send = pl.pallas_call(
        functools.partial(down_kernel, len(down_w), fsdp),
        out_shape=(
            shape((rows, width), BF16),
            shape((rows, width), BF16),
            shape((1, width), F32),
            down_shape,
            down_shape,
        ),
        in_specs=[SMEM] + [VMEM] * 4 + [ANY] * len(down_w),
        out_specs=(VMEM,) * 5,
        scratch_shapes=[
            pltpu.VMEM((hidden, width), BF16),
            pltpu.VMEM((hidden, rows), BF16),
            pltpu.SemaphoreType.DMA((len(down_w),)),
        ],
        compiler_params=params(),
        cost_estimate=cost(4e9, 2 * weight_bytes),
        name="down",
    )(at, mixed, residual, cotangent, gain_table, *down_w)

    down_sum = Chunk(here, down_keep, down_send)
    gate_shape = shape((fsdp, 2, w_gate.shape[0], hidden // 4), BF16)
    d_gate, d_up, gate_keep, gate_send, up_keep, up_send = pl.pallas_call(
        functools.partial(gate_back_kernel, len(down_w), fsdp),
        out_shape=(
            shape((rows, hidden), BF16),
            shape((rows, hidden), BF16),
            gate_shape,
            gate_shape,
            gate_shape,
            gate_shape,
        ),
        in_specs=[SMEM] + [VMEM] * 4 + [ANY] * len(down_w),
        out_specs=(VMEM,) * 6,
        scratch_shapes=[
            pltpu.VMEM((hidden, width), BF16),
            pltpu.VMEM((width, rows), BF16),
            pltpu.SemaphoreType.DMA((len(down_w),)),
        ],
        compiler_params=params(),
        cost_estimate=cost(6e9, 3 * weight_bytes),
        name="gate_back",
    )(at, d_down, gelu_out, gate_slope, ffn_in, *down_w)
    gate_sum = Chunk(here, gate_keep, gate_send)
    up_sum = Chunk(here, up_keep, up_send)
    down_sum.over_fsdp(d_gate)
    d_gate = after(d_gate, down_sum.other)
    qkv_cols = query_cols + 2 * dim
    last_wide = qkv_cols // 4
    shard_rows = w_query.shape[0]
    last_shape = shape((fsdp, 2, shard_rows + GAIN_ROWS, last_wide), BF16)
    out_block = w_out.shape[0] // 4
    out_shape = shape((fsdp, 2, out_block * width // (hidden // 4), hidden // 4), BF16)
    d_residual, g_ffn, g_attn, d_att, out_keep, out_send = pl.pallas_call(
        functools.partial(middle_kernel, len(out_w), len(gate_w), len(up_w), fsdp, heads),
        out_shape=(
            shape((rows, width), F32),
            shape((1, width), F32),
            shape((1, width), F32),
            shape((heads * rows, dim), BF16),
            out_shape,
            out_shape,
        ),
        in_specs=[SMEM] + [VMEM] * 7 + [ANY] * (len(out_w) + len(gate_w) + len(up_w)),
        out_specs=(VMEM,) * 6,
        scratch_shapes=[
            pltpu.VMEM((query_cols, width), BF16),
            pltpu.VMEM((width, hidden), BF16),
            pltpu.VMEM((width, hidden), BF16),
            pltpu.VMEM((query_cols, rows), BF16),
            pltpu.SemaphoreType.DMA((len(out_w),)),
            pltpu.SemaphoreType.DMA((len(gate_w),)),
            pltpu.SemaphoreType.DMA((len(up_w),)),
        ],
        compiler_params=params(),
        cost_estimate=cost(6e9, 4 * weight_bytes),
        name="middle",
    )(at, d_gate, d_up, residual, projected, cotangent, gain_table, attended, *out_w, *gate_w, *up_w)

    out_sum = Chunk(here, out_keep, out_send)
    gate_sum.over_fsdp(g_ffn)
    up_sum.over_fsdp(g_ffn)
    down_sum.over_mid(g_ffn)
    d_q, d_k, d_v = pl.pallas_call(
        functools.partial(attend_back_kernel, halo, heads),
        out_shape=(shape((rows, query_cols), F32), shape((every, dim), F32), shape((every, dim), F32)),
        in_specs=[VMEM] * 5,
        out_specs=(VMEM,) * 3,
        scratch_shapes=[pltpu.VMEM((heads * QBLOCK, span), BF16)],
        compiler_params=params(),
        cost_estimate=cost(6e9, 3 * weight_bytes),
        name="attend_back",
    )(after(d_att, gate_sum.other, up_sum.other, *down_sum.arrived), q_st, keys, values, probs)
    out_sum.over_fsdp(d_k)
    down_sum.outer_sums(d_k)
    d_q = after(d_q, out_sum.other, down_sum.across)
    grad_tokens, d_halo, last_keep, last_send = pl.pallas_call(
        functools.partial(last_kernel, len(qkv_w), n_tok, fsdp, heads),
        out_shape=(
            shape((rows, width), F32),
            shape((halo, width), BF16),
            last_shape,
            last_shape,
        ),
        in_specs=[SMEM] + [VMEM] * (13 + n_tok) + [ANY] * len(qkv_w),
        out_specs=(VMEM,) * 4,
        scratch_shapes=[
            pltpu.VMEM((width, qkv_cols), BF16),
            pltpu.VMEM((width, every), BF16),
            pltpu.VMEM((every, qkv_cols), BF16),
            pltpu.VMEM((GAIN_ROWS, last_wide), F32),
            pltpu.SemaphoreType.DMA((len(qkv_w),)),
        ],
        compiler_params=params(),
        cost_estimate=cost(15e9, 4 * weight_bytes),
        name="last",
    )(
        at, d_residual, d_q, d_k, d_v,
        q_raw, k_raw, cosine, sine, gain_table, normed, g_ffn, g_attn, g_ffn_out, *toks, *qkv_w,
    )

    last_sum = Chunk(here, last_keep, last_send)
    down_sum.outer_sums(last_keep)
    gate_sum.over_mid(last_keep, *up_sum.arrived)
    (last_sum.other,), (gate_sum.across,), down_sum.shares, out_sum.arrived = together(
        (last_sum.other,), (gate_sum.across,), down_sum.shares, out_sum.arrived
    )
    last_sum.over_fsdp()
    up_sum.join(out_sum)
    gate_sum.outer_sums()
    down_sum.outer_gather()
    last_sum.arrived, (up_sum.across,), gate_sum.shares, down_sum.gathered = together(
        last_sum.arrived, (up_sum.across,), gate_sum.shares, down_sum.gathered
    )
    last_sum.over_mid()
    up_sum.outer_sums()
    gate_sum.outer_gather()
    down_sum.mid_gather()
    (last_sum.across,), up_sum.shares, gate_sum.gathered, down_last = together(
        (last_sum.across,), up_sum.shares, gate_sum.gathered, down_sum.blocks[0]
    )
    down_sum.blocks[0] = list(down_last)
    last_sum.outer_sums()
    up_sum.outer_gather()
    gate_sum.mid_gather()
    last_sum.shares, up_sum.gathered, gate_last = together(last_sum.shares, up_sum.gathered, gate_sum.blocks[0])
    gate_sum.blocks[0] = list(gate_last)
    last_sum.outer_gather()
    up_sum.mid_gather()
    last_sum.mid_gather(up_sum.blocks[0][1])
    d_halo = after(d_halo, up_sum.blocks[0][1])
    halos = [linear_shift(d_halo[halo - by * rows :][:rows], -by) for by in range(1, hops + 1)]
    down_blocks, gate_blocks = by_place(here, down_sum.blocks), by_place(here, gate_sum.blocks)
    both_blocks, last_blocks = by_place(here, up_sum.blocks), by_place(here, last_sum.blocks)
    total_gains = last_sum.blocks[0][0][shard_rows:, :LANES].astype(F32)

    for came in halos:
        grad_tokens = grad_tokens + came.astype(F32)

    total_down = jnp.concatenate(down_blocks, axis=0).astype(F32)
    total_gate = jnp.concatenate(gate_blocks, axis=1).astype(F32)
    total_up = jnp.concatenate([b[:shard_rows] for b in both_blocks], axis=1).astype(F32)
    total_qkv = jnp.concatenate([b[:shard_rows] for b in last_blocks], axis=1).astype(F32)
    wide = hidden // 4
    parts = wide // LANES
    total_out = []
    for block in both_blocks:
        below = block[shard_rows + out_block :].reshape(out_block // parts, parts, LANES)
        below = below.transpose(1, 0, 2).reshape(out_block, LANES)
        total_out.append(jnp.concatenate([block[shard_rows : shard_rows + out_block], below], axis=1))
    total_out = jnp.concatenate(total_out, axis=0).astype(F32)
    g, at_row = [], 0
    for gain in gains:
        deep = fsdp * gain.shape[0] // total_gains.shape[1]
        total = total_gains[at_row : at_row + deep].reshape(fsdp, gain.shape[0])
        g.append(pick(total, here.fsdp_at))
        at_row += deep
    return (
        layer_out, grad_tokens, g[0],
        total_qkv[:, :query_cols],
        total_qkv[:, query_cols : query_cols + dim],
        total_qkv[:, query_cols + dim :],
        g[1], g[2], total_out, g[3], g[4], total_gate, total_up, total_down, g[5],
    )


def solution(mesh):
    tok = P(("seq", "fsdp"), None)
    mat = P("fsdp", None)
    vec = P("fsdp")
    return jax.shard_map(
        on_device,
        mesh=mesh,
        in_specs=(tok, P(("seq", "fsdp")), tok, vec, mat, mat, mat, vec, vec, mat, vec, vec, mat, mat, mat, vec),
        out_specs=(tok, tok, vec, mat, mat, mat, vec, vec, mat, vec, vec, mat, mat, mat, vec),
        check_vma=False,
    )
```

```python
import functools
import math

import jax
import jax.numpy as jnp
from jax import lax
from jax.experimental import pallas as pl
from jax.experimental.pallas import tpu as pltpu
from jax.sharding import PartitionSpec as P

WINDOW = 512
EPSILON = 1e-06
ROPE_BASE = 10000.0
MASKED = -1e30
BF16 = jnp.bfloat16
F32 = jnp.float32
QBLOCK = 128
LANES = 128
GAIN_ROWS = 32
GELU_A = math.sqrt(2.0 / math.pi)
GELU_B = 0.044715

VMEM = pl.BlockSpec(memory_space=pltpu.VMEM)
SMEM = pl.BlockSpec(memory_space=pltpu.SMEM)
ANY = pl.BlockSpec(memory_space=pl.ANY)


def wrapped(value, size):
    return value & (size - 1) if size & (size - 1) == 0 else lax.rem(value, jnp.int32(size))


class Places:
    def __init__(self):
        self.seq = lax.axis_size("seq")
        self.fsdp = lax.axis_size("fsdp")
        self.outer = self.seq // 4
        index = lax.axis_index("seq").astype(jnp.int32)
        fsdp_at = lax.axis_index("fsdp").astype(jnp.int32)
        outer_at = lax.shift_right_logical(index, 2)
        core_at, mid_at = index & 1, lax.shift_right_logical(index, 1) & 1
        scalars = lax.optimization_barrier(
            (
                core_at,
                mid_at,
                fsdp_at,
                core_at * 2 + mid_at,
                tuple(wrapped(outer_at + by, self.outer) for by in range(self.outer)),
                tuple(wrapped(outer_at - by + self.outer, self.outer) for by in range(self.outer)),
                tuple(wrapped(fsdp_at + by, self.fsdp) for by in range(self.fsdp)),
                tuple(wrapped(fsdp_at - by + self.fsdp, self.fsdp) for by in range(self.fsdp)),
                jnp.stack([core_at, mid_at, fsdp_at]),
            )
        )
        self.core_at, self.mid_at, self.fsdp_at, self.quarter_at = scalars[:4]
        self.outer_ahead, self.outer_behind, self.fsdp_ahead, self.fsdp_behind, self.vector = scalars[4:]

    def core_swap(self, array):
        return lax.ppermute(array, "seq", [(i, i ^ 1) for i in range(self.seq)])

    def mid_swap(self, array):
        return lax.ppermute(array, "seq", [(i, i ^ 2) for i in range(self.seq)])

    def outer_shift(self, array, by):
        return lax.ppermute(array, "seq", [(i, (i + 4 * by) % self.seq) for i in range(self.seq)])

    def fsdp_shift(self, array, by):
        return lax.ppermute(array, "fsdp", [(i, (i + by) % self.fsdp) for i in range(self.fsdp)])


def linear_shift(array, by):
    count = lax.axis_size("seq") * lax.axis_size("fsdp")
    return lax.ppermute(array, ("seq", "fsdp"), [(i, i + by) for i in range(count) if 0 <= i + by < count])


def pick(array, at):
    return lax.dynamic_index_in_dim(array, at, 0, keepdims=False, allow_negative_indices=False)


def ordered(pieces, behind):
    if len(pieces) == 2:
        own, other = pieces
        return jnp.where(behind[0] == 0, jnp.stack([own, other]), jnp.stack([other, own]))
    stacked = jnp.stack(pieces)
    return jnp.stack([pick(stacked, at) for at in behind])


def own_part(here, shards, axis, ways):
    size = sum(shard.shape[axis] for shard in shards) // ways
    place = here.quarter_at if ways == 4 else here.core_at
    if len(shards) == 1:
        return lax.dynamic_slice_in_dim(shards[0], place * size, size, axis, allow_negative_indices=False)
    parts = []
    for i in range(ways):
        pieces, start = [], 0
        for shard in shards:
            low, high = max(i * size - start, 0), min((i + 1) * size - start, shard.shape[axis])
            if low < high:
                pieces.append(lax.slice_in_dim(shard, low, high, axis=axis))
            start += shard.shape[axis]
        parts.append(jnp.concatenate(pieces, axis))
    return functools.reduce(lambda rest, i: jnp.where(place == i, parts[i], rest), range(1, ways), parts[0])


def after(value, *earlier):
    return lax.optimization_barrier((value, *earlier))[0]


def together(*groups):
    return lax.optimization_barrier(tuple(tuple(group) for group in groups))


def over_links(here, part):
    return [here.fsdp_shift(part, by) for by in range(1, here.fsdp)]


def on_chips(here, arrived, ways):
    pieces = []
    for mine in arrived:
        if ways == 4:
            across = here.mid_swap(mine)
            pieces += [mine, across, here.core_swap(mine), here.core_swap(across)]
        else:
            pieces += [mine, here.core_swap(mine)]
    return pieces


def multiple(value, of):
    return pl.multiple_of(value, of)


def place_copies(owned, pieces, whole, sems, at, axis, ways):
    core, mid, fsdp = at[0], at[1], at[2]
    count = 1 + len(pieces) // ways
    rows = owned[0].shape[0]
    copies = []
    column = 0
    own_row = multiple(fsdp * rows, 16)
    for shard in owned:
        wide = shard.shape[1]
        copies.append((shard, whole.at[pl.ds(own_row, rows), pl.ds(column, wide)]))
        column += wide
    for k, piece in enumerate(pieces):
        by = 1 + k // ways
        row = multiple(lax.rem(fsdp + (count - by), count) * rows, 16)
        k = k % ways
        if ways == 4:
            place = (core if k < 2 else 1 - core) * 2 + (mid if k % 2 == 0 else 1 - mid)
        else:
            place = core if k == 0 else 1 - core
        if axis == 0:
            target = whole.at[pl.ds(multiple(row + place * (rows // ways), 16), rows // ways), :]
        else:
            target = whole.at[pl.ds(row, rows), pl.ds(multiple(place * (column // ways), 128), column // ways)]
        copies.append((piece, target))
    return [pltpu.make_async_copy(a, b, sems.at[k]) for k, (a, b) in enumerate(copies)]


def dot(a, b):
    return lax.dot_general(a, b, (((1,), (0,)), ((), ())), preferred_element_type=F32)


def dot_nt(a, b):
    return lax.dot_general(a, b, (((1,), (1,)), ((), ())), preferred_element_type=F32)


def dot_tn(a, b):
    return lax.dot_general(a, b, (((0,), (0,)), ((), ())), preferred_element_type=F32)


def inverse_rms(u):
    return lax.rsqrt(jnp.mean(u * u, axis=-1, keepdims=True) + EPSILON)


def norm_back(u, g, dz):
    r = inverse_rms(u)
    ur = u * r
    gdz = g * dz
    du = r * (gdz - ur * jnp.mean(gdz * ur, axis=-1, keepdims=True))
    return du, jnp.sum(dz * ur, axis=0, keepdims=True)


class Writer:
    def __init__(self, sems):
        self.sems, self.copies = sems, []

    def put(self, source, target):
        copy = pltpu.make_async_copy(source, target, self.sems.at[len(self.copies)])
        copy.start()
        self.copies.append(copy)

    def wait(self):
        for copy in self.copies:
            copy.wait()


def params(megabytes=56):
    return pltpu.CompilerParams(vmem_limit_bytes=megabytes * 1024 * 1024)


def cost(flops, bytes_accessed):
    return pl.CostEstimate(flops=int(20 * flops), bytes_accessed=int(20 * bytes_accessed), transcendentals=0)


def shape(dims, kind):
    return jax.ShapeDtypeStruct(tuple(dims), kind)


def attend_kernel(n_tok, n_qkv, heads, *refs):
    at = refs[0]
    toks = refs[1 : 1 + n_tok]
    pos, cosine, sine, gain_table = refs[1 + n_tok : 5 + n_tok]
    qkv = refs[5 + n_tok : 5 + n_tok + n_qkv]
    results, refs = refs[5 + n_tok + n_qkv : 13 + n_tok + n_qkv], refs[13 + n_tok + n_qkv :]
    normed_out, q_raw_out, k_raw_out, q_st_out, keys_out, values_out, probs_out, attended_out = results
    normed, q_raw, k_raw, q_st, keys, values, probs, attended, w_full, sems, out_sems = refs
    writer = Writer(out_sems)
    copies = place_copies(qkv[:3], qkv[3:], w_full, sems, at, 1, 4)
    for copy in copies:
        copy.start()
    rows = toks[0].shape[0]
    dim = keys.shape[1]
    half = dim // 2
    halo = (n_tok - 1) * rows
    gain = gain_table[0:1, :]
    gain_q, gain_k = gain_table[1:2, :dim], gain_table[2:3, :dim]
    for i, tok in enumerate(toks):
        u = tok[...].astype(F32)
        normed[i * rows : (i + 1) * rows, :] = (u * inverse_rms(u) * gain).astype(BF16)
    writer.put(normed, normed_out)
    for copy in copies:
        copy.wait()

    def turned(u, g, cos, sin):
        u = u * inverse_rms(u) * g
        first, second = u[:, :half], u[:, half:]
        return (first * cos - second * sin).astype(BF16), (second * cos + first * sin).astype(BF16)

    for i in range(n_tok):
        here = slice(i * rows, (i + 1) * rows)
        kv = dot(normed[here, :], w_full[:, heads * dim :])
        k_raw[here, :] = kv[:, :dim]
        values[here, :] = kv[:, dim:].astype(BF16)
        first, second = turned(kv[:, :dim], gain_k, cosine[here, :], sine[here, :])
        keys[here, :half] = first
        keys[here, half:] = second
    writer.put(k_raw, k_raw_out)
    writer.put(keys, keys_out)
    writer.put(values, values_out)
    blocks = rows // QBLOCK
    for h in range(heads):
        u = dot(normed[halo:, :], w_full[:, h * dim : (h + 1) * dim])
        q_raw[:, h * dim : (h + 1) * dim] = u
        first, second = turned(u, gain_q, cosine[halo:, :], sine[halo:, :])
        for b in range(blocks):
            start = (b * heads + h) * QBLOCK
            q_st[start : start + QBLOCK, :half] = first[b * QBLOCK : (b + 1) * QBLOCK, :]
            q_st[start : start + QBLOCK, half:] = second[b * QBLOCK : (b + 1) * QBLOCK, :]
    writer.put(q_raw, q_raw_out)
    writer.put(q_st, q_st_out)
    span = WINDOW + QBLOCK
    distance = (
        lax.broadcasted_iota(jnp.int32, (QBLOCK, span), 0)
        + WINDOW
        - lax.broadcasted_iota(jnp.int32, (QBLOCK, span), 1)
    )
    scale = dim ** (-0.5)
    for b in range(blocks):
        first_key = halo - WINDOW + b * QBLOCK
        limit = jnp.minimum(pos[b * QBLOCK : (b + 1) * QBLOCK, :], WINDOW - 1)
        allowed = (distance >= 0) & (distance <= limit)
        for h in range(heads):
            start = (b * heads + h) * QBLOCK
            scores = dot_nt(q_st[start : start + QBLOCK, :], keys[first_key : first_key + span, :]) * scale
            scores = jnp.where(allowed, scores, MASKED)
            weights = jnp.exp(scores - jnp.max(scores, axis=-1, keepdims=True))
            weights = (weights * (1.0 / jnp.sum(weights, axis=-1, keepdims=True))).astype(BF16)
            probs[start : start + QBLOCK, :] = weights
            attended[b * QBLOCK : (b + 1) * QBLOCK, h * dim : (h + 1) * dim] = dot(
                weights, values[first_key : first_key + span, :]
            ).astype(BF16)
        here = pl.ds(b * heads * QBLOCK, heads * QBLOCK)
        writer.put(probs.at[here, :], probs_out.at[here, :])
    writer.put(attended, attended_out)
    writer.wait()


def gate_kernel(n_out, n_gate, n_up, *refs):
    at, attended, tokens, gain_table = refs[:4]
    refs = refs[4:]
    out_w, gate_w, up_w, refs = (
        refs[:n_out],
        refs[n_out : n_out + n_gate],
        refs[n_out + n_gate : n_out + n_gate + n_up],
        refs[n_out + n_gate + n_up :],
    )
    projected_out, residual_out, ffn_in_ref, mixed_out, gelu_out_out, gate_slope_out = refs[:6]
    (
        projected_ref, residual_ref, mixed, gelu_out, gate_slope,
        out_full, gate_full, up_full, out_sems, gate_sems, up_sems, write_sems,
    ) = refs[6:]
    writer = Writer(write_sems)
    groups = (
        place_copies(out_w[:1], out_w[1:], out_full, out_sems, at, 0, 2),
        place_copies(gate_w[:1], gate_w[1:], gate_full, gate_sems, at, 1, 4),
        place_copies(up_w[:1], up_w[1:], up_full, up_sems, at, 1, 2),
    )
    for group in groups:
        for copy in group:
            copy.start()
    for copy in groups[0]:
        copy.wait()
    projected = dot(attended[...], out_full[...])
    projected_ref[...] = projected
    residual = tokens[...].astype(F32) + projected * inverse_rms(projected) * gain_table[3:4, :]
    residual_ref[...] = residual
    ffn_in_ref[...] = (residual * inverse_rms(residual) * gain_table[4:5, :]).astype(BF16)
    writer.put(projected_ref, projected_out)
    writer.put(residual_ref, residual_out)
    width = gate_full.shape[1] // 4
    for k in range(4):
        waits = groups[1][1 + k :: 4] + (groups[2][1 + k // 2 :: 2] if k % 2 == 0 else [])
        if k == 0:
            waits = groups[1][:1] + groups[2][:1] + waits
        for copy in waits:
            copy.wait()
        core = at[0] if k < 2 else 1 - at[0]
        mid = at[1] if k % 2 == 0 else 1 - at[1]
        cut = pl.ds(multiple((core * 2 + mid) * width, width), width)
        gate = dot(ffn_in_ref[...], gate_full[:, cut])
        up = dot(ffn_in_ref[...], up_full[:, cut])
        square = gate * gate
        t = jnp.tanh(GELU_A * gate * (1.0 + GELU_B * square))
        cdf = 0.5 * (1.0 + t)
        act = gate * cdf
        slope = cdf + 0.5 * gate * (1.0 - t * t) * (GELU_A * (1.0 + 3.0 * GELU_B * square))
        mixed[:, cut] = (act * up).astype(BF16)
        gelu_out[:, cut] = act.astype(BF16)
        gate_slope[:, cut] = (up * slope).astype(BF16)
        writer.put(mixed.at[:, cut], mixed_out.at[:, cut])
        writer.put(gelu_out.at[:, cut], gelu_out_out.at[:, cut])
        writer.put(gate_slope.at[:, cut], gate_slope_out.at[:, cut])
    writer.wait()


def relative_blocks(at, fsdp):
    for c in (1, 0):
        core = c + at[0] - 2 * c * at[0]
        for f in range(fsdp):
            row = lax.rem(at[2] + f, fsdp)
            for x in range(2):
                mid = x + at[1] - 2 * x * at[1]
                yield c, f, x, core, row, mid


def column_blocks(at, fsdp, left_t, right, keep, send, results=None, writer=None):
    tall, wide = left_t.shape[0] // fsdp, keep.shape[3]
    for c, f, x, core, row, mid in relative_blocks(at, fsdp):
        cut = pl.ds(multiple((core * 2 + mid) * wide, 128), wide)
        left = left_t[pl.ds(multiple(row * tall, 16), tall), :]
        target = keep if c == 0 else send
        target[f, x, :tall, :] = dot(left, right[:, cut]).astype(BF16)
        if writer is not None:
            writer.put(target.at[f, x], results[c].at[f, x])


def row_pieces(at, fsdp, whole, copies, step):
    rows = whole.shape[0] // fsdp
    total = None
    for k, copy in enumerate(copies):
        copy.wait()
        by = (k + 1) // 2
        start = lax.rem(at[2] + (fsdp - by), fsdp) * rows
        size = rows
        if k > 0:
            size = rows // 2
            start = start + (at[0] if k % 2 == 1 else 1 - at[0]) * size
        part = step(pl.ds(multiple(start, 128), size))
        total = part if total is None else total + part
    return total


def down_kernel(n_down, fsdp, *refs):
    at, mixed, residual, cotangent, gain_table = refs[:5]
    down_w = refs[5 : 5 + n_down]
    layer_out, d_down, grad_gain, keep_out, send_out = refs[5 + n_down : 10 + n_down]
    keep, send, down_full, mixed_t, sems, write_sems = refs[10 + n_down :]
    writer = Writer(write_sems)
    copies = place_copies(down_w[:1], down_w[1:], down_full, sems, at, 0, 2)
    for copy in copies:
        copy.start()
    mixed_t[...] = mixed[...].T
    down = row_pieces(at, fsdp, down_full, copies, lambda cut: dot(mixed[:, cut], down_full[cut, :]))
    r = inverse_rms(down)
    gain = gain_table[5:6, :]
    layer_out[...] = (residual[...] + down * r * gain).astype(BF16)
    du, dg = norm_back(down, gain, cotangent[...].astype(F32))
    grad_gain[...] = dg
    d_down[...] = du.astype(BF16)
    block = keep.shape[2]
    for c, f, x, core, row, mid in relative_blocks(at, fsdp):
        start = multiple(((row * 2 + core) * 2 + mid) * block, 16)
        target = keep if c == 0 else send
        target[f, x] = dot(mixed_t[pl.ds(start, block), :], d_down[...]).astype(BF16)
        writer.put(target.at[f, x], (keep_out if c == 0 else send_out).at[f, x])
    writer.wait()


def gate_back_kernel(n_down, fsdp, *refs):
    at, d_down, gelu_out, gate_slope, ffn_in = refs[:5]
    down_w = refs[5 : 5 + n_down]
    d_gate_out, d_up_out, *results = refs[5 + n_down : 11 + n_down]
    d_gate, d_up, keep, send, up_keep, up_send, down_full, ffn_t, sems, write_sems = refs[11 + n_down :]
    writer = Writer(write_sems)
    copies = place_copies(down_w[:1], down_w[1:], down_full, sems, at, 0, 2)
    for copy in copies:
        copy.start()
    ffn_t[...] = ffn_in[...].T

    def step(cut):
        d_mixed = dot_nt(d_down[...], down_full[cut, :])
        d_gate[:, cut] = (d_mixed * gate_slope[:, cut].astype(F32)).astype(BF16)
        d_up[:, cut] = (d_mixed * gelu_out[:, cut].astype(F32)).astype(BF16)
        return 0

    row_pieces(at, fsdp, down_full, copies, step)
    writer.put(d_gate, d_gate_out)
    writer.put(d_up, d_up_out)
    column_blocks(at, fsdp, ffn_t, d_gate, keep, send, results[:2], writer)
    column_blocks(at, fsdp, ffn_t, d_up, up_keep, up_send, results[2:], writer)
    writer.wait()


def middle_kernel(n_out, n_gate, n_up, fsdp, heads, *refs):
    at, d_gate, d_up, residual, projected, cotangent, gain_table, attended = refs[:8]
    refs = refs[8:]
    out_w, gate_w, up_w, refs = (
        refs[:n_out],
        refs[n_out : n_out + n_gate],
        refs[n_out + n_gate : n_out + n_gate + n_up],
        refs[n_out + n_gate + n_up :],
    )
    d_residual_ref, g_ffn, g_attn, d_att, keep, send = refs[:6]
    out_full, gate_full, up_full, att_t, out_sems, gate_sems, up_sems = refs[6:]
    groups = (
        place_copies(gate_w[:1], gate_w[1:], gate_full, gate_sems, at, 1, 4),
        place_copies(up_w[:1], up_w[1:], up_full, up_sems, at, 1, 2),
        place_copies(out_w[:1], out_w[1:], out_full, out_sems, at, 0, 2),
    )
    for group in groups:
        for copy in group:
            copy.start()
    att_t[...] = attended[...].T
    for copy in groups[0]:
        copy.wait()
    d_ffn_in = dot_nt(d_gate[...], gate_full[...])
    for copy in groups[1]:
        copy.wait()
    d_ffn_in = d_ffn_in + dot_nt(d_up[...], up_full[...])
    du, dg = norm_back(residual[...], gain_table[4:5, :], d_ffn_in)
    g_ffn[...] = dg
    d_residual = cotangent[...].astype(F32) + du
    d_residual_ref[...] = d_residual
    du, dg = norm_back(projected[...], gain_table[3:4, :], d_residual)
    g_attn[...] = dg
    d_proj = du.astype(BF16)
    rows, dim = d_proj.shape[0], d_att.shape[1]
    for copy in groups[2]:
        copy.wait()
    for h in range(heads):
        part = dot_nt(d_proj, out_full[h * dim : (h + 1) * dim, :]).astype(BF16)
        for b in range(rows // QBLOCK):
            start = (b * heads + h) * QBLOCK
            d_att[start : start + QBLOCK, :] = part[b * QBLOCK : (b + 1) * QBLOCK, :]
    block = att_t.shape[0] // (4 * fsdp)
    wide = keep.shape[3]
    parts = wide // LANES
    deep = block // parts
    for c, f, x, core, row, mid in relative_blocks(at, fsdp):
        start = multiple(((row * 2 + core) * 2 + mid) * block, 16)
        part = dot(att_t[pl.ds(start, block), :], d_proj).astype(BF16)
        target = keep if c == 0 else send
        target[f, x, :block, :] = part[:, :wide]
        for i in range(parts):
            target[f, x, block:, i * LANES : (i + 1) * LANES] = part[i * deep : (i + 1) * deep, wide:]


def attend_back_kernel(halo, heads, d_att, q_st, keys, values, probs, d_q, d_k, d_v, d_scores):
    rows = d_q.shape[0]
    dim = keys.shape[1]
    blocks = rows // QBLOCK
    span = WINDOW + QBLOCK
    scale = dim ** (-0.5)
    d_k[...] = jnp.zeros(d_k.shape, F32)
    d_v[...] = jnp.zeros(d_v.shape, F32)
    for b in range(blocks):
        first_key = halo - WINDOW + b * QBLOCK
        here = slice(first_key, first_key + span)
        for h in range(heads):
            start = (b * heads + h) * QBLOCK
            stack = slice(start, start + QBLOCK)
            d_probs = dot_nt(d_att[stack, :], values[here, :])
            p = probs[stack, :].astype(F32)
            row_terms = jnp.sum(p * d_probs, axis=-1, keepdims=True)
            ds = (p * (d_probs - row_terms) * scale).astype(BF16)
            d_scores[h * QBLOCK : (h + 1) * QBLOCK, :] = ds
            d_q[b * QBLOCK : (b + 1) * QBLOCK, h * dim : (h + 1) * dim] = dot(ds, keys[here, :])
        stack = slice(b * heads * QBLOCK, (b + 1) * heads * QBLOCK)
        d_k[here, :] += dot_tn(d_scores[...], q_st[stack, :])
        d_v[here, :] += dot_tn(probs[stack, :], d_att[stack, :])


def last_kernel(n_qkv, n_tok, fsdp, heads, *refs):
    (
        at, d_residual, d_q, d_k, d_v,
        q_raw, k_raw, cosine, sine, gain_table, normed, g_ffn, g_attn, g_out,
    ) = refs[:14]
    toks = refs[14 : 14 + n_tok]
    refs = refs[14 + n_tok :]
    qkv_w, refs = refs[:n_qkv], refs[n_qkv:]
    grad_tokens, d_halo, keep, send = refs[:4]
    w_full, normed_t, d_qkv, gain_rows, qkv_sems = refs[4:]
    copies = place_copies(qkv_w[:3], qkv_w[3:], w_full, qkv_sems, at, 1, 4)
    for copy in copies:
        copy.start()
    normed_t[...] = normed[...].T
    rows = toks[0].shape[0]
    halo = (n_tok - 1) * rows
    dim = k_raw.shape[1]
    gain_in, gain_q, gain_k = gain_table[0:1, :], gain_table[1:2, :dim], gain_table[2:3, :dim]
    half = dim // 2
    tall, wide = normed_t.shape[0] // fsdp, keep.shape[3]
    def turned_back(u, g, dz, cos, sin):
        first, second = dz[:, :half], dz[:, half:]
        dz = jnp.concatenate([first * cos + second * sin, second * cos - first * sin], axis=1)
        return norm_back(u, g, dz)

    total_q = jnp.zeros((1, dim), F32)
    if halo:
        d_qkv[:halo, : heads * dim] = jnp.zeros((halo, heads * dim), BF16)
    for h in range(heads):
        cut = slice(h * dim, (h + 1) * dim)
        du, dg = turned_back(q_raw[:, cut], gain_q, d_q[:, cut], cosine[halo:, :], sine[halo:, :])
        total_q += dg
        d_qkv[halo:, cut] = du.astype(BF16)
    total_k = jnp.zeros((1, dim), F32)
    for i in range(n_tok):
        here = slice(i * rows, (i + 1) * rows)
        du, dg = turned_back(k_raw[here, :], gain_k, d_k[here, :], cosine[here, :], sine[here, :])
        total_k += dg
        d_qkv[here, heads * dim : (heads + 1) * dim] = du.astype(BF16)
        d_qkv[here, (heads + 1) * dim :] = d_v[here, :].astype(BF16)
    column_blocks(at, fsdp, normed_t, d_qkv, keep, send)
    for copy in copies:
        copy.wait()
    total_in = jnp.zeros(gain_in.shape, F32)
    for i in range(n_tok):
        here = slice(i * rows, (i + 1) * rows)
        if i < n_tok - 1:
            d_normed = dot_nt(d_qkv[here, heads * dim :], w_full[:, heads * dim :])
        else:
            d_normed = dot_nt(d_qkv[here, :], w_full[...])
        du, dg = norm_back(toks[i][...].astype(F32), gain_in, d_normed)
        total_in += dg
        if i < n_tok - 1:
            d_halo[here, :] = du.astype(BF16)
        else:
            grad_tokens[...] = d_residual[...] + du
    gain_rows[...] = jnp.zeros(gain_rows.shape, F32)
    at_row = 0
    for total in (total_in, total_q, total_k, g_attn[...], g_ffn[...], g_out[...]):
        for i in range(total.shape[1] // LANES):
            gain_rows[at_row : at_row + 1, :LANES] = total[:, i * LANES : (i + 1) * LANES]
            at_row += 1
    packed = gain_rows[...].astype(BF16)
    for target in (keep, send):
        for f in range(fsdp):
            for x in range(2):
                target[f, x, tall:, :] = packed


def add(*terms):
    out = terms[0].astype(F32)
    for term in terms[1:]:
        out = out + term.astype(F32)
    return out


class Chunk:
    def __init__(self, here, keep, send):
        self.here, self.keep = here, keep
        self.other = here.core_swap(send)

    def over_fsdp(self, *earlier):
        here = self.here
        parts = [add(self.keep[by], self.other[by]).astype(BF16) for by in range(1, here.fsdp)]
        self.arrived = [here.fsdp_shift(after(part, *earlier), by + 1) for by, part in enumerate(parts)]

    def over_mid(self, *earlier):
        self.arrived = [after(a, *earlier) for a in self.arrived]
        terms = [self.keep[0, 1], self.other[0, 1]] + [a[1] for a in self.arrived]
        self.across = self.here.mid_swap(add(*terms).astype(BF16))
        self.mine = [self.keep[0, 0], self.other[0, 0]] + [a[0] for a in self.arrived]
        return self.arrived[0] if self.arrived else self.other

    def join(self, below, *earlier):
        for chunk in (self, below):
            chunk.arrived = [after(a, *earlier) for a in chunk.arrived]
        pairs = [
            [[c.keep[0, x], c.other[0, x]] + [a[x] for a in c.arrived] for c in (self, below)] for x in range(2)
        ]
        self.across_sent = jnp.concatenate([add(*terms).astype(BF16) for terms in pairs[1]])
        self.across = self.here.mid_swap(self.across_sent)
        self.mine = [jnp.concatenate([add(*terms).astype(BF16) for terms in pairs[0]])]

    def outer_sums(self, *earlier):
        here = self.here
        self.across = after(self.across, *earlier)
        mine = add(*self.mine, self.across).astype(BF16)
        n, w = mine.shape
        mine = mine.reshape(here.outer, n // here.outer, w)
        self.shares = [pick(mine, here.outer_ahead[0])]
        for by in range(1, here.outer):
            self.shares.append(here.outer_shift(pick(mine, here.outer_ahead[by]), by))
        return self.across

    def outer_gather(self, *earlier):
        here = self.here
        self.shares = list(after(tuple(self.shares), *earlier))
        own = add(*self.shares).astype(BF16)
        self.gathered = [own] + [here.outer_shift(own, by) for by in range(1, here.outer)]
        return self.shares[-1]

    def mid_gather(self, *earlier):
        here = self.here
        self.gathered = list(after(tuple(self.gathered), *earlier))
        block = ordered(self.gathered, here.outer_behind)
        block = block.reshape(-1, block.shape[-1])
        across = here.mid_swap(block)
        self.blocks = [[block, across], [here.core_swap(block), here.core_swap(across)]]
        return self.gathered[-1]


def by_place(here, blocks):
    own = [jnp.where(here.mid_at == 0, a, b) for a, b in blocks]
    other = [jnp.where(here.mid_at == 0, b, a) for a, b in blocks]
    pairs = list(zip(own, other))
    first = [jnp.where(here.core_at == 0, a, b) for a, b in zip(pairs[0], pairs[1])]
    second = [jnp.where(here.core_at == 0, b, a) for a, b in zip(pairs[0], pairs[1])]
    return first + second


def on_device(
    tokens, positions, cotangent, in_gain, w_query, w_key, w_value, query_gain, key_gain, w_out, attn_gain,
    ffn_gain_in, w_gate, w_up, w_down, ffn_gain_out,
):
    here = Places()
    fsdp = here.fsdp
    rows, width = tokens.shape
    dim = w_key.shape[1]
    query_cols = w_query.shape[1]
    heads = query_cols // dim
    hidden = w_gate.shape[1]
    hops = (WINDOW + rows - 1) // rows
    n_tok = hops + 1
    halo = hops * rows
    every = halo + rows
    at = here.vector

    gains = (in_gain, query_gain, key_gain, attn_gain, ffn_gain_in, ffn_gain_out)
    cuts = [0]
    for gain in gains:
        cuts.append(cuts[-1] + gain.shape[0])
    gain_row = jnp.concatenate(gains)
    gain_rows = ordered([gain_row] + [here.fsdp_shift(gain_row, by) for by in range(1, fsdp)], here.fsdp_behind)
    gain_rows = gain_rows.astype(F32)
    gain_table = jnp.concatenate(
        [
            jnp.pad(gain_rows[:, cuts[i] : cuts[i + 1]].reshape(1, -1), ((0, 0), (0, width - fsdp * gains[i].shape[0])))
            for i in range(6)
        ]
        + [jnp.zeros((2, width), F32)],
        axis=0,
    )
    qkv_w = [w_query, w_key, w_value]
    qkv_part = own_part(here, qkv_w, 1, 4)
    tokens_out = after(tokens, qkv_part)
    toks = [linear_shift(tokens_out, by) for by in range(hops, 0, -1)] + [tokens]
    qkv_w += on_chips(here, over_links(here, qkv_part), 4)
    out_arrived = over_links(here, after(own_part(here, [w_out], 0, 2), *toks[:-1]))
    gate_arrived = over_links(here, after(own_part(here, [w_gate], 1, 4), qkv_w[3]))
    up_arrived = over_links(here, after(own_part(here, [w_up], 1, 2), *gate_arrived))

    all_positions = jnp.concatenate([positions[0] - halo + jnp.arange(halo, dtype=jnp.int32), positions])
    frequency = ROPE_BASE ** (-(jnp.arange(dim // 2, dtype=F32) * 2.0 / dim))
    angles = all_positions.astype(F32)[:, None] * frequency[None, :]
    cosine, sine = jnp.cos(angles), jnp.sin(angles)

    span = WINDOW + QBLOCK
    weight_bytes = 2 * fsdp * w_gate.size
    normed, q_raw, k_raw, q_st, keys, values, probs, attended = pl.pallas_call(
        functools.partial(attend_kernel, n_tok, len(qkv_w), heads),
        out_shape=(
            shape((every, width), BF16),
            shape((rows, query_cols), F32),
            shape((every, dim), F32),
            shape((heads * rows, dim), BF16),
            shape((every, dim), BF16),
            shape((every, dim), BF16),
            shape((heads * rows, span), BF16),
            shape((rows, query_cols), BF16),
        ),
        in_specs=[SMEM] + [VMEM] * (n_tok + 4) + [ANY] * len(qkv_w),
        out_specs=(ANY,) * 8,
        scratch_shapes=[
            pltpu.VMEM((every, width), BF16),
            pltpu.VMEM((rows, query_cols), F32),
            pltpu.VMEM((every, dim), F32),
            pltpu.VMEM((heads * rows, dim), BF16),
            pltpu.VMEM((every, dim), BF16),
            pltpu.VMEM((every, dim), BF16),
            pltpu.VMEM((heads * rows, WINDOW + QBLOCK), BF16),
            pltpu.VMEM((rows, query_cols), BF16),
            pltpu.VMEM((width, query_cols + 2 * dim), BF16),
            pltpu.SemaphoreType.DMA((len(qkv_w),)),
            pltpu.SemaphoreType.DMA((7 + rows // QBLOCK,)),
        ],
        compiler_params=params(),
        cost_estimate=cost(4e9, 1e7),
        name="attend",
    )(at, *toks, after(positions[:, None], *gate_arrived), cosine, sine, gain_table, *qkv_w)

    down_arrived = over_links(here, after(own_part(here, [w_down], 0, 2), attended))
    out_w = [w_out] + on_chips(here, [after(a, attended) for a in out_arrived], 2)
    gate_w = [w_gate] + on_chips(here, gate_arrived, 4)
    up_w = [w_up] + on_chips(here, [after(a, attended) for a in up_arrived], 2)
    projected, residual, ffn_in, mixed, gelu_out, gate_slope = pl.pallas_call(
        functools.partial(gate_kernel, len(out_w), len(gate_w), len(up_w)),
        out_shape=(
            shape((rows, width), F32),
            shape((rows, width), F32),
            shape((rows, width), BF16),
            shape((rows, hidden), BF16),
            shape((rows, hidden), BF16),
            shape((rows, hidden), BF16),
        ),
        in_specs=[SMEM] + [VMEM] * 3 + [ANY] * (len(out_w) + len(gate_w) + len(up_w)),
        out_specs=(ANY, ANY, VMEM, ANY, ANY, ANY),
        scratch_shapes=[
            pltpu.VMEM((rows, width), F32),
            pltpu.VMEM((rows, width), F32),
            pltpu.VMEM((rows, hidden), BF16),
            pltpu.VMEM((rows, hidden), BF16),
            pltpu.VMEM((rows, hidden), BF16),
            pltpu.VMEM((query_cols, width), BF16),
            pltpu.VMEM((width, hidden), BF16),
            pltpu.VMEM((width, hidden), BF16),
            pltpu.SemaphoreType.DMA((len(out_w),)),
            pltpu.SemaphoreType.DMA((len(gate_w),)),
            pltpu.SemaphoreType.DMA((len(up_w),)),
            pltpu.SemaphoreType.DMA((14,)),
        ],
        compiler_params=params(),
        cost_estimate=cost(4e9, 2 * weight_bytes),
        name="gate",
    )(at, attended, tokens, gain_table, *out_w, *gate_w, *up_w)

    down_w = [w_down] + on_chips(here, [after(a, mixed) for a in down_arrived], 2)
    down_block = w_down.shape[0] // 4
    down_shape = shape((fsdp, 2, down_block, width), BF16)
    layer_out, d_down, g_ffn_out, down_keep, down_send = pl.pallas_call(
        functools.partial(down_kernel, len(down_w), fsdp),
        out_shape=(
            shape((rows, width), BF16),
            shape((rows, width), BF16),
            shape((1, width), F32),
            down_shape,
            down_shape,
        ),
        in_specs=[SMEM] + [VMEM] * 4 + [ANY] * len(down_w),
        out_specs=(VMEM, VMEM, VMEM, ANY, ANY),
        scratch_shapes=[
            pltpu.VMEM(down_shape.shape, BF16),
            pltpu.VMEM(down_shape.shape, BF16),
            pltpu.VMEM((hidden, width), BF16),
            pltpu.VMEM((hidden, rows), BF16),
            pltpu.SemaphoreType.DMA((len(down_w),)),
            pltpu.SemaphoreType.DMA((4 * fsdp,)),
        ],
        compiler_params=params(),
        cost_estimate=cost(4e9, 2 * weight_bytes),
        name="down",
    )(at, mixed, residual, cotangent, gain_table, *down_w)

    down_sum = Chunk(here, down_keep, down_send)
    gate_shape = shape((fsdp, 2, w_gate.shape[0], hidden // 4), BF16)
    d_gate, d_up, gate_keep, gate_send, up_keep, up_send = pl.pallas_call(
        functools.partial(gate_back_kernel, len(down_w), fsdp),
        out_shape=(
            shape((rows, hidden), BF16),
            shape((rows, hidden), BF16),
            gate_shape,
            gate_shape,
            gate_shape,
            gate_shape,
        ),
        in_specs=[SMEM] + [VMEM] * 4 + [ANY] * len(down_w),
        out_specs=(ANY,) * 6,
        scratch_shapes=[
            pltpu.VMEM((rows, hidden), BF16),
            pltpu.VMEM((rows, hidden), BF16),
            pltpu.VMEM(gate_shape.shape, BF16),
            pltpu.VMEM(gate_shape.shape, BF16),
            pltpu.VMEM(gate_shape.shape, BF16),
            pltpu.VMEM(gate_shape.shape, BF16),
            pltpu.VMEM((hidden, width), BF16),
            pltpu.VMEM((width, rows), BF16),
            pltpu.SemaphoreType.DMA((len(down_w),)),
            pltpu.SemaphoreType.DMA((2 + 8 * fsdp,)),
        ],
        compiler_params=params(),
        cost_estimate=cost(6e9, 3 * weight_bytes),
        name="gate_back",
    )(at, d_down, gelu_out, gate_slope, ffn_in, *down_w)
    gate_sum = Chunk(here, gate_keep, gate_send)
    up_sum = Chunk(here, up_keep, up_send)
    down_sum.over_fsdp(d_gate)
    d_gate = after(d_gate, down_sum.other)
    qkv_cols = query_cols + 2 * dim
    last_wide = qkv_cols // 4
    shard_rows = w_query.shape[0]
    last_shape = shape((fsdp, 2, shard_rows + GAIN_ROWS, last_wide), BF16)
    out_block = w_out.shape[0] // 4
    out_shape = shape((fsdp, 2, out_block * width // (hidden // 4), hidden // 4), BF16)
    d_residual, g_ffn, g_attn, d_att, out_keep, out_send = pl.pallas_call(
        functools.partial(middle_kernel, len(out_w), len(gate_w), len(up_w), fsdp, heads),
        out_shape=(
            shape((rows, width), F32),
            shape((1, width), F32),
            shape((1, width), F32),
            shape((heads * rows, dim), BF16),
            out_shape,
            out_shape,
        ),
        in_specs=[SMEM] + [VMEM] * 7 + [ANY] * (len(out_w) + len(gate_w) + len(up_w)),
        out_specs=(VMEM,) * 6,
        scratch_shapes=[
            pltpu.VMEM((query_cols, width), BF16),
            pltpu.VMEM((width, hidden), BF16),
            pltpu.VMEM((width, hidden), BF16),
            pltpu.VMEM((query_cols, rows), BF16),
            pltpu.SemaphoreType.DMA((len(out_w),)),
            pltpu.SemaphoreType.DMA((len(gate_w),)),
            pltpu.SemaphoreType.DMA((len(up_w),)),
        ],
        compiler_params=params(),
        cost_estimate=cost(6e9, 4 * weight_bytes),
        name="middle",
    )(at, d_gate, d_up, residual, projected, cotangent, gain_table, attended, *out_w, *gate_w, *up_w)

    out_sum = Chunk(here, out_keep, out_send)
    gate_sum.over_fsdp(g_ffn)
    up_sum.over_fsdp(g_ffn)
    down_sum.over_mid(g_ffn)
    d_q, d_k, d_v = pl.pallas_call(
        functools.partial(attend_back_kernel, halo, heads),
        out_shape=(shape((rows, query_cols), F32), shape((every, dim), F32), shape((every, dim), F32)),
        in_specs=[VMEM] * 5,
        out_specs=(VMEM,) * 3,
        scratch_shapes=[pltpu.VMEM((heads * QBLOCK, span), BF16)],
        compiler_params=params(),
        cost_estimate=cost(6e9, 3 * weight_bytes),
        name="attend_back",
    )(after(d_att, gate_sum.other, up_sum.other, *down_sum.arrived), q_st, keys, values, probs)
    out_sum.over_fsdp(d_k)
    down_sum.outer_sums(d_k)
    down_sum.outer_sums(d_k)
    d_q = after(d_q, out_sum.other, down_sum.across)
    grad_tokens, d_halo, last_keep, last_send = pl.pallas_call(
        functools.partial(last_kernel, len(qkv_w), n_tok, fsdp, heads),
        out_shape=(
            shape((rows, width), F32),
            shape((halo, width), BF16),
            last_shape,
            last_shape,
        ),
        in_specs=[SMEM] + [VMEM] * (13 + n_tok) + [ANY] * len(qkv_w),
        out_specs=(VMEM,) * 4,
        scratch_shapes=[
            pltpu.VMEM((width, qkv_cols), BF16),
            pltpu.VMEM((width, every), BF16),
            pltpu.VMEM((every, qkv_cols), BF16),
            pltpu.VMEM((GAIN_ROWS, last_wide), F32),
            pltpu.SemaphoreType.DMA((len(qkv_w),)),
        ],
        compiler_params=params(),
        cost_estimate=cost(15e9, 4 * weight_bytes),
        name="last",
    )(
        at, d_residual, d_q, d_k, d_v,
        q_raw, k_raw, cosine, sine, gain_table, normed, g_ffn, g_attn, g_ffn_out, *toks, *qkv_w,
    )

    last_sum = Chunk(here, last_keep, last_send)
    gate_sum.over_mid(last_keep, *up_sum.arrived, *down_sum.shares[1:])
    down_sum.outer_gather(last_keep)
    (last_sum.other,), (gate_sum.across,), down_sum.gathered, out_sum.arrived = together(
        (last_sum.other,), (gate_sum.across,), down_sum.gathered, out_sum.arrived
    )
    last_sum.over_fsdp()
    up_sum.join(out_sum)
    gate_sum.outer_sums()
    last_sum.arrived, (up_sum.across,), gate_sum.shares, down_sum.gathered = together(
        last_sum.arrived, (up_sum.across,), gate_sum.shares, down_sum.gathered
    )
    last_sum.over_mid()
    up_sum.outer_sums()
    gate_sum.outer_gather()
    down_sum.mid_gather()
    (last_sum.across,), up_sum.shares, gate_sum.gathered, down_last = together(
        (last_sum.across,), up_sum.shares, gate_sum.gathered, down_sum.blocks[0]
    )
    down_sum.blocks[0] = list(down_last)
    last_sum.outer_sums()
    up_sum.outer_gather()
    gate_sum.mid_gather()
    last_sum.shares, up_sum.gathered, gate_last = together(last_sum.shares, up_sum.gathered, gate_sum.blocks[0])
    gate_sum.blocks[0] = list(gate_last)
    last_sum.outer_gather()
    up_sum.mid_gather()
    last_sum.mid_gather(up_sum.blocks[0][1])
    d_halo = after(d_halo, up_sum.blocks[0][1])
    halos = [linear_shift(d_halo[halo - by * rows :][:rows], -by) for by in range(1, hops + 1)]
    down_blocks, gate_blocks = by_place(here, down_sum.blocks), by_place(here, gate_sum.blocks)
    both_blocks = by_place(here, up_sum.blocks)

    for came in halos:
        grad_tokens = grad_tokens + came.astype(F32)

    total_down = jnp.concatenate(down_blocks, axis=0).astype(F32)
    total_gate = jnp.concatenate(gate_blocks, axis=1).astype(F32)
    total_up = jnp.concatenate([b[:shard_rows] for b in both_blocks], axis=1).astype(F32)
    wide = hidden // 4
    parts = wide // LANES
    total_out = []
    for block in both_blocks:
        below = block[shard_rows + out_block :].reshape(out_block // parts, parts, LANES)
        below = below.transpose(1, 0, 2).reshape(out_block, LANES)
        total_out.append(jnp.concatenate([block[shard_rows : shard_rows + out_block], below], axis=1))
    total_out = jnp.concatenate(total_out, axis=0).astype(F32)
    last_blocks = [[after(b, total_gate, total_up, total_out, total_down) for b in pair] for pair in last_sum.blocks]
    total_gains = last_blocks[0][0][shard_rows:, :LANES].astype(F32)
    last_blocks = by_place(here, last_blocks)
    total_qkv = jnp.concatenate([b[:shard_rows] for b in last_blocks], axis=1).astype(F32)
    g, at_row = [], 0
    for gain in gains:
        deep = fsdp * gain.shape[0] // total_gains.shape[1]
        total = total_gains[at_row : at_row + deep].reshape(fsdp, gain.shape[0])
        g.append(pick(total, here.fsdp_at))
        at_row += deep
    return (
        layer_out, grad_tokens, g[0],
        total_qkv[:, :query_cols],
        total_qkv[:, query_cols : query_cols + dim],
        total_qkv[:, query_cols + dim :],
        g[1], g[2], total_out, g[3], g[4], total_gate, total_up, total_down, g[5],
    )


def solution(mesh):
    tok = P(("seq", "fsdp"), None)
    mat = P("fsdp", None)
    vec = P("fsdp")
    return jax.shard_map(
        on_device,
        mesh=mesh,
        in_specs=(tok, P(("seq", "fsdp")), tok, vec, mat, mat, mat, vec, vec, mat, vec, vec, mat, mat, mat, vec),
        out_specs=(tok, tok, vec, mat, mat, mat, vec, vec, mat, vec, vec, mat, mat, mat, vec),
        check_vma=False,
    )
```

```python
import functools
import math

import jax
import jax.numpy as jnp
from jax import lax
from jax.experimental import pallas as pl
from jax.experimental.pallas import tpu as pltpu
from jax.sharding import PartitionSpec as P

WINDOW = 512
EPSILON = 1e-06
ROPE_BASE = 10000.0
MASKED = -1e30
BF16 = jnp.bfloat16
F32 = jnp.float32
QBLOCK = 128
LANES = 128
GAIN_ROWS = 32
GELU_A = math.sqrt(2.0 / math.pi)
GELU_B = 0.044715

VMEM = pl.BlockSpec(memory_space=pltpu.VMEM)
SMEM = pl.BlockSpec(memory_space=pltpu.SMEM)
ANY = pl.BlockSpec(memory_space=pl.ANY)


def wrapped(value, size):
    return value & (size - 1) if size & (size - 1) == 0 else lax.rem(value, jnp.int32(size))


class Places:
    def __init__(self):
        self.seq = lax.axis_size("seq")
        self.fsdp = lax.axis_size("fsdp")
        self.outer = self.seq // 4
        index = lax.axis_index("seq").astype(jnp.int32)
        fsdp_at = lax.axis_index("fsdp").astype(jnp.int32)
        outer_at = lax.shift_right_logical(index, 2)
        core_at, mid_at = index & 1, lax.shift_right_logical(index, 1) & 1
        scalars = lax.optimization_barrier(
            (
                core_at,
                mid_at,
                fsdp_at,
                core_at * 2 + mid_at,
                tuple(wrapped(outer_at + by, self.outer) for by in range(self.outer)),
                tuple(wrapped(outer_at - by + self.outer, self.outer) for by in range(self.outer)),
                tuple(wrapped(fsdp_at + by, self.fsdp) for by in range(self.fsdp)),
                tuple(wrapped(fsdp_at - by + self.fsdp, self.fsdp) for by in range(self.fsdp)),
                jnp.stack([core_at, mid_at, fsdp_at]),
            )
        )
        self.core_at, self.mid_at, self.fsdp_at, self.quarter_at = scalars[:4]
        self.outer_ahead, self.outer_behind, self.fsdp_ahead, self.fsdp_behind, self.vector = scalars[4:]

    def core_swap(self, array):
        return lax.ppermute(array, "seq", [(i, i ^ 1) for i in range(self.seq)])

    def mid_swap(self, array):
        return lax.ppermute(array, "seq", [(i, i ^ 2) for i in range(self.seq)])

    def outer_shift(self, array, by):
        return lax.ppermute(array, "seq", [(i, (i + 4 * by) % self.seq) for i in range(self.seq)])

    def fsdp_shift(self, array, by):
        return lax.ppermute(array, "fsdp", [(i, (i + by) % self.fsdp) for i in range(self.fsdp)])


def linear_shift(array, by):
    count = lax.axis_size("seq") * lax.axis_size("fsdp")
    return lax.ppermute(array, ("seq", "fsdp"), [(i, i + by) for i in range(count) if 0 <= i + by < count])


def pick(array, at):
    return lax.dynamic_index_in_dim(array, at, 0, keepdims=False, allow_negative_indices=False)


def ordered(pieces, behind):
    if len(pieces) == 2:
        own, other = pieces
        return jnp.where(behind[0] == 0, jnp.stack([own, other]), jnp.stack([other, own]))
    stacked = jnp.stack(pieces)
    return jnp.stack([pick(stacked, at) for at in behind])


def own_part(here, shards, axis, ways):
    size = sum(shard.shape[axis] for shard in shards) // ways
    place = here.quarter_at if ways == 4 else here.core_at
    if len(shards) == 1:
        return lax.dynamic_slice_in_dim(shards[0], place * size, size, axis, allow_negative_indices=False)
    parts = []
    for i in range(ways):
        pieces, start = [], 0
        for shard in shards:
            low, high = max(i * size - start, 0), min((i + 1) * size - start, shard.shape[axis])
            if low < high:
                pieces.append(lax.slice_in_dim(shard, low, high, axis=axis))
            start += shard.shape[axis]
        parts.append(jnp.concatenate(pieces, axis))
    return functools.reduce(lambda rest, i: jnp.where(place == i, parts[i], rest), range(1, ways), parts[0])


def after(value, *earlier):
    return lax.optimization_barrier((value, *earlier))[0]


def together(*groups):
    return lax.optimization_barrier(tuple(tuple(group) for group in groups))


def over_links(here, part):
    return [here.fsdp_shift(part, by) for by in range(1, here.fsdp)]


def on_chips(here, arrived, ways):
    pieces = []
    for mine in arrived:
        if ways == 4:
            across = here.mid_swap(mine)
            pieces += [mine, across, here.core_swap(mine), here.core_swap(across)]
        else:
            pieces += [mine, here.core_swap(mine)]
    return pieces


def multiple(value, of):
    return pl.multiple_of(value, of)


def place_copies(owned, pieces, whole, sems, at, axis, ways):
    core, mid, fsdp = at[0], at[1], at[2]
    count = 1 + len(pieces) // ways
    rows = owned[0].shape[0]
    copies = []
    column = 0
    own_row = multiple(fsdp * rows, 16)
    for shard in owned:
        wide = shard.shape[1]
        copies.append((shard, whole.at[pl.ds(own_row, rows), pl.ds(column, wide)]))
        column += wide
    for k, piece in enumerate(pieces):
        by = 1 + k // ways
        row = multiple(lax.rem(fsdp + (count - by), count) * rows, 16)
        k = k % ways
        if ways == 4:
            place = (core if k < 2 else 1 - core) * 2 + (mid if k % 2 == 0 else 1 - mid)
        else:
            place = core if k == 0 else 1 - core
        if axis == 0:
            target = whole.at[pl.ds(multiple(row + place * (rows // ways), 16), rows // ways), :]
        else:
            target = whole.at[pl.ds(row, rows), pl.ds(multiple(place * (column // ways), 128), column // ways)]
        copies.append((piece, target))
    return [pltpu.make_async_copy(a, b, sems.at[k]) for k, (a, b) in enumerate(copies)]


def dot(a, b):
    return lax.dot_general(a, b, (((1,), (0,)), ((), ())), preferred_element_type=F32)


def dot_nt(a, b):
    return lax.dot_general(a, b, (((1,), (1,)), ((), ())), preferred_element_type=F32)


def dot_tn(a, b):
    return lax.dot_general(a, b, (((0,), (0,)), ((), ())), preferred_element_type=F32)


def inverse_rms(u):
    return lax.rsqrt(jnp.mean(u * u, axis=-1, keepdims=True) + EPSILON)


def norm_back(u, g, dz):
    r = inverse_rms(u)
    ur = u * r
    gdz = g * dz
    du = r * (gdz - ur * jnp.mean(gdz * ur, axis=-1, keepdims=True))
    return du, jnp.sum(dz * ur, axis=0, keepdims=True)


class Writer:
    def __init__(self, sems):
        self.sems, self.copies = sems, []

    def put(self, source, target):
        copy = pltpu.make_async_copy(source, target, self.sems.at[len(self.copies)])
        copy.start()
        self.copies.append(copy)

    def wait(self):
        for copy in self.copies:
            copy.wait()


def params(megabytes=56):
    return pltpu.CompilerParams(vmem_limit_bytes=megabytes * 1024 * 1024)


def cost(flops, bytes_accessed):
    return pl.CostEstimate(flops=int(20 * flops), bytes_accessed=int(20 * bytes_accessed), transcendentals=0)


def shape(dims, kind):
    return jax.ShapeDtypeStruct(tuple(dims), kind)


def attend_kernel(n_tok, n_qkv, heads, *refs):
    at = refs[0]
    toks = refs[1 : 1 + n_tok]
    pos, cosine, sine, gain_table = refs[1 + n_tok : 5 + n_tok]
    qkv = refs[5 + n_tok : 5 + n_tok + n_qkv]
    normed, q_raw, k_raw, q_st, keys, values, probs, attended, w_full, sems = refs[5 + n_tok + n_qkv :]
    copies = place_copies(qkv[:3], qkv[3:], w_full, sems, at, 1, 4)
    for copy in copies:
        copy.start()
    rows = toks[0].shape[0]
    dim = keys.shape[1]
    half = dim // 2
    halo = (n_tok - 1) * rows
    gain = gain_table[0:1, :]
    gain_q, gain_k = gain_table[1:2, :dim], gain_table[2:3, :dim]
    for i, tok in enumerate(toks):
        u = tok[...].astype(F32)
        normed[i * rows : (i + 1) * rows, :] = (u * inverse_rms(u) * gain).astype(BF16)
    for copy in copies:
        copy.wait()

    def turned(u, g, cos, sin):
        u = u * inverse_rms(u) * g
        first, second = u[:, :half], u[:, half:]
        return (first * cos - second * sin).astype(BF16), (second * cos + first * sin).astype(BF16)

    for i in range(n_tok):
        here = slice(i * rows, (i + 1) * rows)
        kv = dot(normed[here, :], w_full[:, heads * dim :])
        k_raw[here, :] = kv[:, :dim]
        values[here, :] = kv[:, dim:].astype(BF16)
        first, second = turned(kv[:, :dim], gain_k, cosine[here, :], sine[here, :])
        keys[here, :half] = first
        keys[here, half:] = second
    blocks = rows // QBLOCK
    for h in range(heads):
        u = dot(normed[halo:, :], w_full[:, h * dim : (h + 1) * dim])
        q_raw[:, h * dim : (h + 1) * dim] = u
        first, second = turned(u, gain_q, cosine[halo:, :], sine[halo:, :])
        for b in range(blocks):
            start = (b * heads + h) * QBLOCK
            q_st[start : start + QBLOCK, :half] = first[b * QBLOCK : (b + 1) * QBLOCK, :]
            q_st[start : start + QBLOCK, half:] = second[b * QBLOCK : (b + 1) * QBLOCK, :]
    span = WINDOW + QBLOCK
    distance = (
        lax.broadcasted_iota(jnp.int32, (QBLOCK, span), 0)
        + WINDOW
        - lax.broadcasted_iota(jnp.int32, (QBLOCK, span), 1)
    )
    scale = dim ** (-0.5)
    for b in range(blocks):
        first_key = halo - WINDOW + b * QBLOCK
        limit = jnp.minimum(pos[b * QBLOCK : (b + 1) * QBLOCK, :], WINDOW - 1)
        allowed = (distance >= 0) & (distance <= limit)
        for h in range(heads):
            start = (b * heads + h) * QBLOCK
            scores = dot_nt(q_st[start : start + QBLOCK, :], keys[first_key : first_key + span, :]) * scale
            scores = jnp.where(allowed, scores, MASKED)
            weights = jnp.exp(scores - jnp.max(scores, axis=-1, keepdims=True))
            weights = (weights * (1.0 / jnp.sum(weights, axis=-1, keepdims=True))).astype(BF16)
            probs[start : start + QBLOCK, :] = weights
            attended[b * QBLOCK : (b + 1) * QBLOCK, h * dim : (h + 1) * dim] = dot(
                weights, values[first_key : first_key + span, :]
            ).astype(BF16)


def gate_kernel(n_out, n_gate, n_up, *refs):
    at, attended, tokens, gain_table = refs[:4]
    refs = refs[4:]
    out_w, gate_w, up_w, refs = (
        refs[:n_out],
        refs[n_out : n_out + n_gate],
        refs[n_out + n_gate : n_out + n_gate + n_up],
        refs[n_out + n_gate + n_up :],
    )
    projected_out, residual_out, ffn_in_ref, mixed_out, gelu_out_out, gate_slope_out = refs[:6]
    (
        projected_ref, residual_ref, mixed, gelu_out, gate_slope,
        out_full, gate_full, up_full, out_sems, gate_sems, up_sems, write_sems,
    ) = refs[6:]
    writer = Writer(write_sems)
    groups = (
        place_copies(out_w[:1], out_w[1:], out_full, out_sems, at, 0, 2),
        place_copies(gate_w[:1], gate_w[1:], gate_full, gate_sems, at, 1, 4),
        place_copies(up_w[:1], up_w[1:], up_full, up_sems, at, 1, 2),
    )
    for group in groups:
        for copy in group:
            copy.start()
    for copy in groups[0]:
        copy.wait()
    projected = dot(attended[...], out_full[...])
    projected_ref[...] = projected
    residual = tokens[...].astype(F32) + projected * inverse_rms(projected) * gain_table[3:4, :]
    residual_ref[...] = residual
    ffn_in_ref[...] = (residual * inverse_rms(residual) * gain_table[4:5, :]).astype(BF16)
    writer.put(projected_ref, projected_out)
    writer.put(residual_ref, residual_out)
    width = gate_full.shape[1] // 4
    for k in range(4):
        waits = groups[1][1 + k :: 4] + (groups[2][1 + k // 2 :: 2] if k % 2 == 0 else [])
        if k == 0:
            waits = groups[1][:1] + groups[2][:1] + waits
        for copy in waits:
            copy.wait()
        core = at[0] if k < 2 else 1 - at[0]
        mid = at[1] if k % 2 == 0 else 1 - at[1]
        cut = pl.ds(multiple((core * 2 + mid) * width, width), width)
        gate = dot(ffn_in_ref[...], gate_full[:, cut])
        up = dot(ffn_in_ref[...], up_full[:, cut])
        square = gate * gate
        t = jnp.tanh(GELU_A * gate * (1.0 + GELU_B * square))
        cdf = 0.5 * (1.0 + t)
        act = gate * cdf
        slope = cdf + 0.5 * gate * (1.0 - t * t) * (GELU_A * (1.0 + 3.0 * GELU_B * square))
        mixed[:, cut] = (act * up).astype(BF16)
        gelu_out[:, cut] = act.astype(BF16)
        gate_slope[:, cut] = (up * slope).astype(BF16)
        writer.put(mixed.at[:, cut], mixed_out.at[:, cut])
        writer.put(gelu_out.at[:, cut], gelu_out_out.at[:, cut])
        writer.put(gate_slope.at[:, cut], gate_slope_out.at[:, cut])
    writer.wait()


def relative_blocks(at, fsdp):
    for c in range(2):
        core = c + at[0] - 2 * c * at[0]
        for f in range(fsdp):
            row = lax.rem(at[2] + f, fsdp)
            for x in range(2):
                mid = x + at[1] - 2 * x * at[1]
                yield c, f, x, core, row, mid


def column_blocks(at, fsdp, left_t, right, keep, send):
    tall, wide = left_t.shape[0] // fsdp, keep.shape[3]
    for c, f, x, core, row, mid in relative_blocks(at, fsdp):
        cut = pl.ds(multiple((core * 2 + mid) * wide, 128), wide)
        left = left_t[pl.ds(multiple(row * tall, 16), tall), :]
        target = keep if c == 0 else send
        target[f, x, :tall, :] = dot(left, right[:, cut]).astype(BF16)


def down_kernel(n_down, fsdp, *refs):
    at, mixed, residual, cotangent, gain_table = refs[:5]
    down_w = refs[5 : 5 + n_down]
    layer_out, d_down, grad_gain, keep, send = refs[5 + n_down : 10 + n_down]
    down_full, mixed_t, sems = refs[10 + n_down :]
    copies = place_copies(down_w[:1], down_w[1:], down_full, sems, at, 0, 2)
    for copy in copies:
        copy.start()
    mixed_t[...] = mixed[...].T
    for copy in copies:
        copy.wait()
    down = dot(mixed[...], down_full[...])
    r = inverse_rms(down)
    gain = gain_table[5:6, :]
    layer_out[...] = (residual[...] + down * r * gain).astype(BF16)
    du, dg = norm_back(down, gain, cotangent[...].astype(F32))
    grad_gain[...] = dg
    d_down[...] = du.astype(BF16)
    block = keep.shape[2]
    for c, f, x, core, row, mid in relative_blocks(at, fsdp):
        start = multiple(((row * 2 + core) * 2 + mid) * block, 16)
        target = keep if c == 0 else send
        target[f, x] = dot(mixed_t[pl.ds(start, block), :], d_down[...]).astype(BF16)


def gate_back_kernel(n_down, fsdp, *refs):
    at, d_down, gelu_out, gate_slope, ffn_in = refs[:5]
    down_w = refs[5 : 5 + n_down]
    d_gate, d_up, keep, send, up_keep, up_send = refs[5 + n_down : 11 + n_down]
    down_full, ffn_t, sems = refs[11 + n_down :]
    copies = place_copies(down_w[:1], down_w[1:], down_full, sems, at, 0, 2)
    for copy in copies:
        copy.start()
    ffn_t[...] = ffn_in[...].T
    for copy in copies:
        copy.wait()
    width = 256

    def step(i, _):
        cut = pl.ds(multiple(i * width, width), width)
        d_mixed = dot_nt(d_down[...], down_full[cut, :])
        d_gate[:, cut] = (d_mixed * gate_slope[:, cut].astype(F32)).astype(BF16)
        d_up[:, cut] = (d_mixed * gelu_out[:, cut].astype(F32)).astype(BF16)
        return 0

    lax.fori_loop(0, d_gate.shape[1] // width, step, 0)
    column_blocks(at, fsdp, ffn_t, d_gate, keep, send)
    column_blocks(at, fsdp, ffn_t, d_up, up_keep, up_send)


def middle_kernel(n_out, n_gate, n_up, fsdp, heads, *refs):
    at, d_gate, d_up, residual, projected, cotangent, gain_table, attended = refs[:8]
    refs = refs[8:]
    out_w, gate_w, up_w, refs = (
        refs[:n_out],
        refs[n_out : n_out + n_gate],
        refs[n_out + n_gate : n_out + n_gate + n_up],
        refs[n_out + n_gate + n_up :],
    )
    d_residual_ref, g_ffn, g_attn, d_att, keep, send = refs[:6]
    out_full, gate_full, up_full, att_t, out_sems, gate_sems, up_sems = refs[6:]
    groups = (
        place_copies(gate_w[:1], gate_w[1:], gate_full, gate_sems, at, 1, 4),
        place_copies(up_w[:1], up_w[1:], up_full, up_sems, at, 1, 2),
        place_copies(out_w[:1], out_w[1:], out_full, out_sems, at, 0, 2),
    )
    for group in groups:
        for copy in group:
            copy.start()
    att_t[...] = attended[...].T
    for copy in groups[0]:
        copy.wait()
    d_ffn_in = dot_nt(d_gate[...], gate_full[...])
    for copy in groups[1]:
        copy.wait()
    d_ffn_in = d_ffn_in + dot_nt(d_up[...], up_full[...])
    du, dg = norm_back(residual[...], gain_table[4:5, :], d_ffn_in)
    g_ffn[...] = dg
    d_residual = cotangent[...].astype(F32) + du
    d_residual_ref[...] = d_residual
    du, dg = norm_back(projected[...], gain_table[3:4, :], d_residual)
    g_attn[...] = dg
    d_proj = du.astype(BF16)
    rows, dim = d_proj.shape[0], d_att.shape[1]
    for copy in groups[2]:
        copy.wait()
    for h in range(heads):
        part = dot_nt(d_proj, out_full[h * dim : (h + 1) * dim, :]).astype(BF16)
        for b in range(rows // QBLOCK):
            start = (b * heads + h) * QBLOCK
            d_att[start : start + QBLOCK, :] = part[b * QBLOCK : (b + 1) * QBLOCK, :]
    block = att_t.shape[0] // (4 * fsdp)
    wide = keep.shape[3]
    parts = wide // LANES
    deep = block // parts
    for c, f, x, core, row, mid in relative_blocks(at, fsdp):
        start = multiple(((row * 2 + core) * 2 + mid) * block, 16)
        part = dot(att_t[pl.ds(start, block), :], d_proj).astype(BF16)
        target = keep if c == 0 else send
        target[f, x, :block, :] = part[:, :wide]
        for i in range(parts):
            target[f, x, block:, i * LANES : (i + 1) * LANES] = part[i * deep : (i + 1) * deep, wide:]


def attend_back_kernel(halo, heads, d_att, q_st, keys, values, probs, d_q, d_k, d_v, d_scores):
    rows = d_q.shape[0]
    dim = keys.shape[1]
    blocks = rows // QBLOCK
    span = WINDOW + QBLOCK
    scale = dim ** (-0.5)
    d_k[...] = jnp.zeros(d_k.shape, F32)
    d_v[...] = jnp.zeros(d_v.shape, F32)
    for b in range(blocks):
        first_key = halo - WINDOW + b * QBLOCK
        here = slice(first_key, first_key + span)
        for h in range(heads):
            start = (b * heads + h) * QBLOCK
            stack = slice(start, start + QBLOCK)
            d_probs = dot_nt(d_att[stack, :], values[here, :])
            p = probs[stack, :].astype(F32)
            row_terms = jnp.sum(p * d_probs, axis=-1, keepdims=True)
            ds = (p * (d_probs - row_terms) * scale).astype(BF16)
            d_scores[h * QBLOCK : (h + 1) * QBLOCK, :] = ds
            d_q[b * QBLOCK : (b + 1) * QBLOCK, h * dim : (h + 1) * dim] = dot(ds, keys[here, :])
        stack = slice(b * heads * QBLOCK, (b + 1) * heads * QBLOCK)
        d_k[here, :] += dot_tn(d_scores[...], q_st[stack, :])
        d_v[here, :] += dot_tn(probs[stack, :], d_att[stack, :])


def last_kernel(n_qkv, n_tok, fsdp, heads, *refs):
    (
        at, d_residual, d_q, d_k, d_v,
        q_raw, k_raw, cosine, sine, gain_table, normed, g_ffn, g_attn, g_out,
    ) = refs[:14]
    toks = refs[14 : 14 + n_tok]
    refs = refs[14 + n_tok :]
    qkv_w, refs = refs[:n_qkv], refs[n_qkv:]
    grad_tokens, d_halo, keep, send = refs[:4]
    w_full, normed_t, d_qkv, gain_rows, qkv_sems = refs[4:]
    copies = place_copies(qkv_w[:3], qkv_w[3:], w_full, qkv_sems, at, 1, 4)
    for copy in copies:
        copy.start()
    normed_t[...] = normed[...].T
    rows = toks[0].shape[0]
    halo = (n_tok - 1) * rows
    dim = k_raw.shape[1]
    gain_in, gain_q, gain_k = gain_table[0:1, :], gain_table[1:2, :dim], gain_table[2:3, :dim]
    half = dim // 2
    tall, wide = normed_t.shape[0] // fsdp, keep.shape[3]
    def turned_back(u, g, dz, cos, sin):
        first, second = dz[:, :half], dz[:, half:]
        dz = jnp.concatenate([first * cos + second * sin, second * cos - first * sin], axis=1)
        return norm_back(u, g, dz)

    total_q = jnp.zeros((1, dim), F32)
    if halo:
        d_qkv[:halo, : heads * dim] = jnp.zeros((halo, heads * dim), BF16)
    for h in range(heads):
        cut = slice(h * dim, (h + 1) * dim)
        du, dg = turned_back(q_raw[:, cut], gain_q, d_q[:, cut], cosine[halo:, :], sine[halo:, :])
        total_q += dg
        d_qkv[halo:, cut] = du.astype(BF16)
    total_k = jnp.zeros((1, dim), F32)
    for i in range(n_tok):
        here = slice(i * rows, (i + 1) * rows)
        du, dg = turned_back(k_raw[here, :], gain_k, d_k[here, :], cosine[here, :], sine[here, :])
        total_k += dg
        d_qkv[here, heads * dim : (heads + 1) * dim] = du.astype(BF16)
        d_qkv[here, (heads + 1) * dim :] = d_v[here, :].astype(BF16)
    column_blocks(at, fsdp, normed_t, d_qkv, keep, send)
    for copy in copies:
        copy.wait()
    total_in = jnp.zeros(gain_in.shape, F32)
    for i in range(n_tok):
        here = slice(i * rows, (i + 1) * rows)
        if i < n_tok - 1:
            d_normed = dot_nt(d_qkv[here, heads * dim :], w_full[:, heads * dim :])
        else:
            d_normed = dot_nt(d_qkv[here, :], w_full[...])
        du, dg = norm_back(toks[i][...].astype(F32), gain_in, d_normed)
        total_in += dg
        if i < n_tok - 1:
            d_halo[here, :] = du.astype(BF16)
        else:
            grad_tokens[...] = d_residual[...] + du
    gain_rows[...] = jnp.zeros(gain_rows.shape, F32)
    at_row = 0
    for total in (total_in, total_q, total_k, g_attn[...], g_ffn[...], g_out[...]):
        for i in range(total.shape[1] // LANES):
            gain_rows[at_row : at_row + 1, :LANES] = total[:, i * LANES : (i + 1) * LANES]
            at_row += 1
    packed = gain_rows[...].astype(BF16)
    for target in (keep, send):
        for f in range(fsdp):
            for x in range(2):
                target[f, x, tall:, :] = packed


def add(*terms):
    out = terms[0].astype(F32)
    for term in terms[1:]:
        out = out + term.astype(F32)
    return out


class Chunk:
    def __init__(self, here, keep, send):
        self.here, self.keep = here, keep
        self.other = here.core_swap(send)

    def over_fsdp(self, *earlier):
        here = self.here
        parts = [add(self.keep[by], self.other[by]).astype(BF16) for by in range(1, here.fsdp)]
        self.arrived = [here.fsdp_shift(after(part, *earlier), by + 1) for by, part in enumerate(parts)]

    def over_mid(self, *earlier):
        self.arrived = [after(a, *earlier) for a in self.arrived]
        terms = [self.keep[0, 1], self.other[0, 1]] + [a[1] for a in self.arrived]
        self.across = self.here.mid_swap(add(*terms).astype(BF16))
        self.mine = [self.keep[0, 0], self.other[0, 0]] + [a[0] for a in self.arrived]
        return self.arrived[0] if self.arrived else self.other

    def join(self, below, *earlier):
        for chunk in (self, below):
            chunk.arrived = [after(a, *earlier) for a in chunk.arrived]
        pairs = [
            [[c.keep[0, x], c.other[0, x]] + [a[x] for a in c.arrived] for c in (self, below)] for x in range(2)
        ]
        self.across_sent = jnp.concatenate([add(*terms).astype(BF16) for terms in pairs[1]])
        self.across = self.here.mid_swap(self.across_sent)
        self.mine = [jnp.concatenate([add(*terms).astype(BF16) for terms in pairs[0]])]

    def outer_sums(self, *earlier):
        here = self.here
        self.across = after(self.across, *earlier)
        mine = add(*self.mine, self.across).astype(BF16)
        n, w = mine.shape
        mine = mine.reshape(here.outer, n // here.outer, w)
        self.shares = [pick(mine, here.outer_ahead[0])]
        for by in range(1, here.outer):
            self.shares.append(here.outer_shift(pick(mine, here.outer_ahead[by]), by))
        return self.across

    def outer_gather(self, *earlier):
        here = self.here
        self.shares = list(after(tuple(self.shares), *earlier))
        own = add(*self.shares).astype(BF16)
        self.gathered = [own] + [here.outer_shift(own, by) for by in range(1, here.outer)]
        return self.shares[-1]

    def mid_gather(self, *earlier, hold=()):
        here = self.here
        self.gathered = list(after(tuple(self.gathered), *earlier))
        block = ordered(self.gathered, here.outer_behind)
        block = block.reshape(-1, block.shape[-1])
        across = after(here.mid_swap(block), *hold)
        self.blocks = [[block, across], [here.core_swap(block), here.core_swap(across)]]
        return self.gathered[-1]


def by_place(here, blocks):
    own = [jnp.where(here.mid_at == 0, a, b) for a, b in blocks]
    other = [jnp.where(here.mid_at == 0, b, a) for a, b in blocks]
    pairs = list(zip(own, other))
    first = [jnp.where(here.core_at == 0, a, b) for a, b in zip(pairs[0], pairs[1])]
    second = [jnp.where(here.core_at == 0, b, a) for a, b in zip(pairs[0], pairs[1])]
    return first + second


def on_device(
    tokens, positions, cotangent, in_gain, w_query, w_key, w_value, query_gain, key_gain, w_out, attn_gain,
    ffn_gain_in, w_gate, w_up, w_down, ffn_gain_out,
):
    here = Places()
    fsdp = here.fsdp
    rows, width = tokens.shape
    dim = w_key.shape[1]
    query_cols = w_query.shape[1]
    heads = query_cols // dim
    hidden = w_gate.shape[1]
    hops = (WINDOW + rows - 1) // rows
    n_tok = hops + 1
    halo = hops * rows
    every = halo + rows
    at = here.vector

    gains = (in_gain, query_gain, key_gain, attn_gain, ffn_gain_in, ffn_gain_out)
    cuts = [0]
    for gain in gains:
        cuts.append(cuts[-1] + gain.shape[0])
    gain_row = jnp.concatenate(gains)
    gain_rows = ordered([gain_row] + [here.fsdp_shift(gain_row, by) for by in range(1, fsdp)], here.fsdp_behind)
    gain_rows = gain_rows.astype(F32)
    gain_table = jnp.concatenate(
        [
            jnp.pad(gain_rows[:, cuts[i] : cuts[i + 1]].reshape(1, -1), ((0, 0), (0, width - fsdp * gains[i].shape[0])))
            for i in range(6)
        ]
        + [jnp.zeros((2, width), F32)],
        axis=0,
    )
    qkv_w = [w_query, w_key, w_value]
    qkv_part = own_part(here, qkv_w, 1, 4)
    tokens_out = after(tokens, qkv_part)
    toks = [linear_shift(tokens_out, by) for by in range(hops, 0, -1)] + [tokens]
    qkv_w += on_chips(here, over_links(here, qkv_part), 4)
    out_arrived = over_links(here, after(own_part(here, [w_out], 0, 2), *toks[:-1]))
    gate_arrived = over_links(here, after(own_part(here, [w_gate], 1, 4), qkv_w[3]))
    up_arrived = over_links(here, after(own_part(here, [w_up], 1, 2), *gate_arrived))

    all_positions = jnp.concatenate([positions[0] - halo + jnp.arange(halo, dtype=jnp.int32), positions])
    frequency = ROPE_BASE ** (-(jnp.arange(dim // 2, dtype=F32) * 2.0 / dim))
    angles = all_positions.astype(F32)[:, None] * frequency[None, :]
    cosine, sine = jnp.cos(angles), jnp.sin(angles)

    span = WINDOW + QBLOCK
    weight_bytes = 2 * fsdp * w_gate.size
    normed, q_raw, k_raw, q_st, keys, values, probs, attended = pl.pallas_call(
        functools.partial(attend_kernel, n_tok, len(qkv_w), heads),
        out_shape=(
            shape((every, width), BF16),
            shape((rows, query_cols), F32),
            shape((every, dim), F32),
            shape((heads * rows, dim), BF16),
            shape((every, dim), BF16),
            shape((every, dim), BF16),
            shape((heads * rows, span), BF16),
            shape((rows, query_cols), BF16),
        ),
        in_specs=[SMEM] + [VMEM] * (n_tok + 4) + [ANY] * len(qkv_w),
        out_specs=(VMEM,) * 8,
        scratch_shapes=[
            pltpu.VMEM((width, query_cols + 2 * dim), BF16),
            pltpu.SemaphoreType.DMA((len(qkv_w),)),
        ],
        compiler_params=params(),
        cost_estimate=cost(4e9, 1e7),
        name="attend",
    )(at, *toks, after(positions[:, None], *gate_arrived), cosine, sine, gain_table, *qkv_w)

    down_arrived = over_links(here, after(own_part(here, [w_down], 0, 2), attended))
    out_w = [w_out] + on_chips(here, [after(a, attended) for a in out_arrived], 2)
    gate_w = [w_gate] + on_chips(here, gate_arrived, 4)
    up_w = [w_up] + on_chips(here, [after(a, attended) for a in up_arrived], 2)
    projected, residual, ffn_in, mixed, gelu_out, gate_slope = pl.pallas_call(
        functools.partial(gate_kernel, len(out_w), len(gate_w), len(up_w)),
        out_shape=(
            shape((rows, width), F32),
            shape((rows, width), F32),
            shape((rows, width), BF16),
            shape((rows, hidden), BF16),
            shape((rows, hidden), BF16),
            shape((rows, hidden), BF16),
        ),
        in_specs=[SMEM] + [VMEM] * 3 + [ANY] * (len(out_w) + len(gate_w) + len(up_w)),
        out_specs=(ANY, ANY, VMEM, ANY, ANY, ANY),
        scratch_shapes=[
            pltpu.VMEM((rows, width), F32),
            pltpu.VMEM((rows, width), F32),
            pltpu.VMEM((rows, hidden), BF16),
            pltpu.VMEM((rows, hidden), BF16),
            pltpu.VMEM((rows, hidden), BF16),
            pltpu.VMEM((query_cols, width), BF16),
            pltpu.VMEM((width, hidden), BF16),
            pltpu.VMEM((width, hidden), BF16),
            pltpu.SemaphoreType.DMA((len(out_w),)),
            pltpu.SemaphoreType.DMA((len(gate_w),)),
            pltpu.SemaphoreType.DMA((len(up_w),)),
            pltpu.SemaphoreType.DMA((14,)),
        ],
        compiler_params=params(),
        cost_estimate=cost(4e9, 2 * weight_bytes),
        name="gate",
    )(at, attended, tokens, gain_table, *out_w, *gate_w, *up_w)

    down_w = [w_down] + on_chips(here, [after(a, mixed) for a in down_arrived], 2)
    down_block = w_down.shape[0] // 4
    down_shape = shape((fsdp, 2, down_block, width), BF16)
    layer_out, d_down, g_ffn_out, down_keep, down_send = pl.pallas_call(
        functools.partial(down_kernel, len(down_w), fsdp),
        out_shape=(
            shape((rows, width), BF16),
            shape((rows, width), BF16),
            shape((1, width), F32),
            down_shape,
            down_shape,
        ),
        in_specs=[SMEM] + [VMEM] * 4 + [ANY] * len(down_w),
        out_specs=(VMEM,) * 5,
        scratch_shapes=[
            pltpu.VMEM((hidden, width), BF16),
            pltpu.VMEM((hidden, rows), BF16),
            pltpu.SemaphoreType.DMA((len(down_w),)),
        ],
        compiler_params=params(),
        cost_estimate=cost(4e9, 2 * weight_bytes),
        name="down",
    )(at, mixed, residual, cotangent, gain_table, *down_w)

    down_sum = Chunk(here, down_keep, down_send)
    gate_shape = shape((fsdp, 2, w_gate.shape[0], hidden // 4), BF16)
    d_gate, d_up, gate_keep, gate_send, up_keep, up_send = pl.pallas_call(
        functools.partial(gate_back_kernel, len(down_w), fsdp),
        out_shape=(
            shape((rows, hidden), BF16),
            shape((rows, hidden), BF16),
            gate_shape,
            gate_shape,
            gate_shape,
            gate_shape,
        ),
        in_specs=[SMEM] + [VMEM] * 4 + [ANY] * len(down_w),
        out_specs=(VMEM,) * 6,
        scratch_shapes=[
            pltpu.VMEM((hidden, width), BF16),
            pltpu.VMEM((width, rows), BF16),
            pltpu.SemaphoreType.DMA((len(down_w),)),
        ],
        compiler_params=params(),
        cost_estimate=cost(6e9, 3 * weight_bytes),
        name="gate_back",
    )(at, d_down, gelu_out, gate_slope, ffn_in, *down_w)
    gate_sum = Chunk(here, gate_keep, gate_send)
    up_sum = Chunk(here, up_keep, up_send)
    down_sum.over_fsdp(d_gate)
    d_gate = after(d_gate, down_sum.other)
    qkv_cols = query_cols + 2 * dim
    last_wide = qkv_cols // 4
    shard_rows = w_query.shape[0]
    last_shape = shape((fsdp, 2, shard_rows + GAIN_ROWS, last_wide), BF16)
    out_block = w_out.shape[0] // 4
    out_shape = shape((fsdp, 2, out_block * width // (hidden // 4), hidden // 4), BF16)
    d_residual, g_ffn, g_attn, d_att, out_keep, out_send = pl.pallas_call(
        functools.partial(middle_kernel, len(out_w), len(gate_w), len(up_w), fsdp, heads),
        out_shape=(
            shape((rows, width), F32),
            shape((1, width), F32),
            shape((1, width), F32),
            shape((heads * rows, dim), BF16),
            out_shape,
            out_shape,
        ),
        in_specs=[SMEM] + [VMEM] * 7 + [ANY] * (len(out_w) + len(gate_w) + len(up_w)),
        out_specs=(VMEM,) * 6,
        scratch_shapes=[
            pltpu.VMEM((query_cols, width), BF16),
            pltpu.VMEM((width, hidden), BF16),
            pltpu.VMEM((width, hidden), BF16),
            pltpu.VMEM((query_cols, rows), BF16),
            pltpu.SemaphoreType.DMA((len(out_w),)),
            pltpu.SemaphoreType.DMA((len(gate_w),)),
            pltpu.SemaphoreType.DMA((len(up_w),)),
        ],
        compiler_params=params(),
        cost_estimate=cost(6e9, 4 * weight_bytes),
        name="middle",
    )(at, d_gate, d_up, residual, projected, cotangent, gain_table, attended, *out_w, *gate_w, *up_w)

    out_sum = Chunk(here, out_keep, out_send)
    gate_sum.over_fsdp(g_ffn)
    up_sum.over_fsdp(g_ffn)
    down_sum.over_mid(g_ffn)
    d_q, d_k, d_v = pl.pallas_call(
        functools.partial(attend_back_kernel, halo, heads),
        out_shape=(shape((rows, query_cols), F32), shape((every, dim), F32), shape((every, dim), F32)),
        in_specs=[VMEM] * 5,
        out_specs=(VMEM,) * 3,
        scratch_shapes=[pltpu.VMEM((heads * QBLOCK, span), BF16)],
        compiler_params=params(),
        cost_estimate=cost(6e9, 3 * weight_bytes),
        name="attend_back",
    )(after(d_att, gate_sum.other, up_sum.other, *down_sum.arrived), q_st, keys, values, probs)
    out_sum.over_fsdp(d_k)
    down_sum.outer_sums(d_k)
    d_q = after(d_q, out_sum.other, down_sum.across)
    grad_tokens, d_halo, last_keep, last_send = pl.pallas_call(
        functools.partial(last_kernel, len(qkv_w), n_tok, fsdp, heads),
        out_shape=(
            shape((rows, width), F32),
            shape((halo, width), BF16),
            last_shape,
            last_shape,
        ),
        in_specs=[SMEM] + [VMEM] * (13 + n_tok) + [ANY] * len(qkv_w),
        out_specs=(VMEM,) * 4,
        scratch_shapes=[
            pltpu.VMEM((width, qkv_cols), BF16),
            pltpu.VMEM((width, every), BF16),
            pltpu.VMEM((every, qkv_cols), BF16),
            pltpu.VMEM((GAIN_ROWS, last_wide), F32),
            pltpu.SemaphoreType.DMA((len(qkv_w),)),
        ],
        compiler_params=params(),
        cost_estimate=cost(15e9, 4 * weight_bytes),
        name="last",
    )(
        at, d_residual, d_q, d_k, d_v,
        q_raw, k_raw, cosine, sine, gain_table, normed, g_ffn, g_attn, g_ffn_out, *toks, *qkv_w,
    )

    last_sum = Chunk(here, last_keep, last_send)
    down_sum.outer_sums(last_keep)
    gate_sum.over_mid(last_keep, *up_sum.arrived)
    down_sum.outer_gather()
    (last_sum.other,), (gate_sum.across,), down_sum.gathered, out_sum.arrived = together(
        (last_sum.other,), (gate_sum.across,), down_sum.gathered, out_sum.arrived
    )
    last_sum.over_fsdp()
    up_sum.join(out_sum)
    gate_sum.outer_sums()
    last_sum.arrived, (up_sum.across,), gate_sum.shares, down_sum.gathered = together(
        last_sum.arrived, (up_sum.across,), gate_sum.shares, down_sum.gathered
    )
    last_sum.over_mid()
    up_sum.outer_sums()
    gate_sum.outer_gather()
    down_sum.mid_gather()
    (last_sum.across,), up_sum.shares, gate_sum.gathered, down_last = together(
        (last_sum.across,), up_sum.shares, gate_sum.gathered, down_sum.blocks[0]
    )
    down_sum.blocks[0] = list(down_last)
    last_sum.outer_sums()
    up_sum.outer_gather()
    gate_sum.mid_gather()
    last_sum.shares, up_sum.gathered, gate_last = together(last_sum.shares, up_sum.gathered, gate_sum.blocks[0])
    gate_sum.blocks[0] = list(gate_last)
    last_sum.outer_gather()
    up_sum.mid_gather()
    down_blocks, gate_blocks = by_place(here, down_sum.blocks), by_place(here, gate_sum.blocks)
    both_blocks = by_place(here, up_sum.blocks)
    total_down = jnp.concatenate(down_blocks, axis=0).astype(F32)
    total_gate = jnp.concatenate(gate_blocks, axis=1).astype(F32)
    total_up = jnp.concatenate([b[:shard_rows] for b in both_blocks], axis=1).astype(F32)
    wide = hidden // 4
    parts = wide // LANES
    total_out = []
    for block in both_blocks:
        below = block[shard_rows + out_block :].reshape(out_block // parts, parts, LANES)
        below = below.transpose(1, 0, 2).reshape(out_block, LANES)
        total_out.append(jnp.concatenate([block[shard_rows : shard_rows + out_block], below], axis=1))
    total_out = jnp.concatenate(total_out, axis=0).astype(F32)
    last_sum.mid_gather(up_sum.blocks[0][1], hold=(total_up, total_out))
    d_halo = after(d_halo, last_sum.blocks[0][1])
    for by in range(1, hops + 1):
        came = linear_shift(d_halo[halo - by * rows :][:rows], -by)
        grad_tokens = grad_tokens + after(came, last_sum.blocks[1][1]).astype(F32)
    total_gains = last_sum.blocks[0][0][shard_rows:, :LANES].astype(F32)
    last_blocks = by_place(here, last_sum.blocks)
    total_qkv = jnp.concatenate([b[:shard_rows] for b in last_blocks], axis=1).astype(F32)
    g, at_row = [], 0
    for gain in gains:
        deep = fsdp * gain.shape[0] // total_gains.shape[1]
        total = total_gains[at_row : at_row + deep].reshape(fsdp, gain.shape[0])
        g.append(pick(total, here.fsdp_at))
        at_row += deep
    return (
        layer_out, grad_tokens, g[0],
        total_qkv[:, :query_cols],
        total_qkv[:, query_cols : query_cols + dim],
        total_qkv[:, query_cols + dim :],
        g[1], g[2], total_out, g[3], g[4], total_gate, total_up, total_down, g[5],
    )


def solution(mesh):
    tok = P(("seq", "fsdp"), None)
    mat = P("fsdp", None)
    vec = P("fsdp")
    return jax.shard_map(
        on_device,
        mesh=mesh,
        in_specs=(tok, P(("seq", "fsdp")), tok, vec, mat, mat, mat, vec, vec, mat, vec, vec, mat, mat, mat, vec),
        out_specs=(tok, tok, vec, mat, mat, mat, vec, vec, mat, vec, vec, mat, mat, mat, vec),
        check_vma=False,
    )
```

```python
import functools
import math

import jax
import jax.numpy as jnp
from jax import lax
from jax.experimental import pallas as pl
from jax.experimental.pallas import tpu as pltpu
from jax.sharding import PartitionSpec as P

WINDOW = 512
EPSILON = 1e-06
ROPE_BASE = 10000.0
MASKED = -1e30
BF16 = jnp.bfloat16
F32 = jnp.float32
QBLOCK = 128
LANES = 128
GAIN_ROWS = 32
GELU_A = math.sqrt(2.0 / math.pi)
GELU_B = 0.044715

VMEM = pl.BlockSpec(memory_space=pltpu.VMEM)
SMEM = pl.BlockSpec(memory_space=pltpu.SMEM)
ANY = pl.BlockSpec(memory_space=pl.ANY)


def wrapped(value, size):
    return value & (size - 1) if size & (size - 1) == 0 else lax.rem(value, jnp.int32(size))


class Places:
    def __init__(self):
        self.seq = lax.axis_size("seq")
        self.fsdp = lax.axis_size("fsdp")
        self.outer = self.seq // 4
        index = lax.axis_index("seq").astype(jnp.int32)
        fsdp_at = lax.axis_index("fsdp").astype(jnp.int32)
        outer_at = lax.shift_right_logical(index, 2)
        core_at, mid_at = index & 1, lax.shift_right_logical(index, 1) & 1
        scalars = lax.optimization_barrier(
            (
                core_at,
                mid_at,
                fsdp_at,
                core_at * 2 + mid_at,
                tuple(wrapped(outer_at + by, self.outer) for by in range(self.outer)),
                tuple(wrapped(outer_at - by + self.outer, self.outer) for by in range(self.outer)),
                tuple(wrapped(fsdp_at + by, self.fsdp) for by in range(self.fsdp)),
                tuple(wrapped(fsdp_at - by + self.fsdp, self.fsdp) for by in range(self.fsdp)),
                jnp.stack([core_at, mid_at, fsdp_at]),
            )
        )
        self.core_at, self.mid_at, self.fsdp_at, self.quarter_at = scalars[:4]
        self.outer_ahead, self.outer_behind, self.fsdp_ahead, self.fsdp_behind, self.vector = scalars[4:]

    def core_swap(self, array):
        return lax.ppermute(array, "seq", [(i, i ^ 1) for i in range(self.seq)])

    def mid_swap(self, array):
        return lax.ppermute(array, "seq", [(i, i ^ 2) for i in range(self.seq)])

    def outer_shift(self, array, by):
        return lax.ppermute(array, "seq", [(i, (i + 4 * by) % self.seq) for i in range(self.seq)])

    def fsdp_shift(self, array, by):
        return lax.ppermute(array, "fsdp", [(i, (i + by) % self.fsdp) for i in range(self.fsdp)])


def linear_shift(array, by):
    count = lax.axis_size("seq") * lax.axis_size("fsdp")
    return lax.ppermute(array, ("seq", "fsdp"), [(i, i + by) for i in range(count) if 0 <= i + by < count])


def pick(array, at):
    return lax.dynamic_index_in_dim(array, at, 0, keepdims=False, allow_negative_indices=False)


def ordered(pieces, behind):
    if len(pieces) == 2:
        own, other = pieces
        return jnp.where(behind[0] == 0, jnp.stack([own, other]), jnp.stack([other, own]))
    stacked = jnp.stack(pieces)
    return jnp.stack([pick(stacked, at) for at in behind])


def own_part(here, shards, axis, ways):
    size = sum(shard.shape[axis] for shard in shards) // ways
    place = here.quarter_at if ways == 4 else here.core_at
    if len(shards) == 1:
        return lax.dynamic_slice_in_dim(shards[0], place * size, size, axis, allow_negative_indices=False)
    parts = []
    for i in range(ways):
        pieces, start = [], 0
        for shard in shards:
            low, high = max(i * size - start, 0), min((i + 1) * size - start, shard.shape[axis])
            if low < high:
                pieces.append(lax.slice_in_dim(shard, low, high, axis=axis))
            start += shard.shape[axis]
        parts.append(jnp.concatenate(pieces, axis))
    return functools.reduce(lambda rest, i: jnp.where(place == i, parts[i], rest), range(1, ways), parts[0])


def after(value, *earlier):
    return lax.optimization_barrier((value, *earlier))[0]


def together(*groups):
    return lax.optimization_barrier(tuple(tuple(group) for group in groups))


def over_links(here, part):
    return [here.fsdp_shift(part, by) for by in range(1, here.fsdp)]


def on_chips(here, arrived, ways):
    pieces = []
    for mine in arrived:
        if ways == 4:
            across = here.mid_swap(mine)
            pieces += [mine, across, here.core_swap(mine), here.core_swap(across)]
        else:
            pieces += [mine, here.core_swap(mine)]
    return pieces


def multiple(value, of):
    return pl.multiple_of(value, of)


def place_copies(owned, pieces, whole, sems, at, axis, ways):
    core, mid, fsdp = at[0], at[1], at[2]
    count = 1 + len(pieces) // ways
    rows = owned[0].shape[0]
    copies = []
    column = 0
    own_row = multiple(fsdp * rows, 16)
    for shard in owned:
        wide = shard.shape[1]
        copies.append((shard, whole.at[pl.ds(own_row, rows), pl.ds(column, wide)]))
        column += wide
    for k, piece in enumerate(pieces):
        by = 1 + k // ways
        row = multiple(lax.rem(fsdp + (count - by), count) * rows, 16)
        k = k % ways
        if ways == 4:
            place = (core if k < 2 else 1 - core) * 2 + (mid if k % 2 == 0 else 1 - mid)
        else:
            place = core if k == 0 else 1 - core
        if axis == 0:
            target = whole.at[pl.ds(multiple(row + place * (rows // ways), 16), rows // ways), :]
        else:
            target = whole.at[pl.ds(row, rows), pl.ds(multiple(place * (column // ways), 128), column // ways)]
        copies.append((piece, target))
    return [pltpu.make_async_copy(a, b, sems.at[k]) for k, (a, b) in enumerate(copies)]


def dot(a, b):
    return lax.dot_general(a, b, (((1,), (0,)), ((), ())), preferred_element_type=F32)


def dot_nt(a, b):
    return lax.dot_general(a, b, (((1,), (1,)), ((), ())), preferred_element_type=F32)


def dot_tn(a, b):
    return lax.dot_general(a, b, (((0,), (0,)), ((), ())), preferred_element_type=F32)


def inverse_rms(u):
    return lax.rsqrt(jnp.mean(u * u, axis=-1, keepdims=True) + EPSILON)


def norm_back(u, g, dz):
    r = inverse_rms(u)
    ur = u * r
    gdz = g * dz
    du = r * (gdz - ur * jnp.mean(gdz * ur, axis=-1, keepdims=True))
    return du, jnp.sum(dz * ur, axis=0, keepdims=True)


class Writer:
    def __init__(self, sems):
        self.sems, self.copies = sems, []

    def put(self, source, target):
        copy = pltpu.make_async_copy(source, target, self.sems.at[len(self.copies)])
        copy.start()
        self.copies.append(copy)

    def wait(self):
        for copy in self.copies:
            copy.wait()


def params(megabytes=56):
    return pltpu.CompilerParams(vmem_limit_bytes=megabytes * 1024 * 1024)


def cost(flops, bytes_accessed):
    return pl.CostEstimate(flops=int(20 * flops), bytes_accessed=int(20 * bytes_accessed), transcendentals=0)


def shape(dims, kind):
    return jax.ShapeDtypeStruct(tuple(dims), kind)


def attend_kernel(n_tok, n_qkv, heads, *refs):
    at = refs[0]
    toks = refs[1 : 1 + n_tok]
    pos, cosine, sine, gain_table = refs[1 + n_tok : 5 + n_tok]
    qkv = refs[5 + n_tok : 5 + n_tok + n_qkv]
    normed, q_raw, k_raw, q_st, keys, values, probs, attended, w_full, sems = refs[5 + n_tok + n_qkv :]
    copies = place_copies(qkv[:3], qkv[3:], w_full, sems, at, 1, 4)
    for copy in copies:
        copy.start()
    rows = toks[0].shape[0]
    dim = keys.shape[1]
    half = dim // 2
    halo = (n_tok - 1) * rows
    gain = gain_table[0:1, :]
    gain_q, gain_k = gain_table[1:2, :dim], gain_table[2:3, :dim]
    for i, tok in enumerate(toks):
        u = tok[...].astype(F32)
        normed[i * rows : (i + 1) * rows, :] = (u * inverse_rms(u) * gain).astype(BF16)
    for copy in copies:
        copy.wait()

    def turned(u, g, cos, sin):
        u = u * inverse_rms(u) * g
        first, second = u[:, :half], u[:, half:]
        return (first * cos - second * sin).astype(BF16), (second * cos + first * sin).astype(BF16)

    for i in range(n_tok):
        here = slice(i * rows, (i + 1) * rows)
        kv = dot(normed[here, :], w_full[:, heads * dim :])
        k_raw[here, :] = kv[:, :dim]
        values[here, :] = kv[:, dim:].astype(BF16)
        first, second = turned(kv[:, :dim], gain_k, cosine[here, :], sine[here, :])
        keys[here, :half] = first
        keys[here, half:] = second
    blocks = rows // QBLOCK
    for h in range(heads):
        u = dot(normed[halo:, :], w_full[:, h * dim : (h + 1) * dim])
        q_raw[:, h * dim : (h + 1) * dim] = u
        first, second = turned(u, gain_q, cosine[halo:, :], sine[halo:, :])
        for b in range(blocks):
            start = (b * heads + h) * QBLOCK
            q_st[start : start + QBLOCK, :half] = first[b * QBLOCK : (b + 1) * QBLOCK, :]
            q_st[start : start + QBLOCK, half:] = second[b * QBLOCK : (b + 1) * QBLOCK, :]
    span = WINDOW + QBLOCK
    distance = (
        lax.broadcasted_iota(jnp.int32, (QBLOCK, span), 0)
        + WINDOW
        - lax.broadcasted_iota(jnp.int32, (QBLOCK, span), 1)
    )
    scale = dim ** (-0.5)
    for b in range(blocks):
        first_key = halo - WINDOW + b * QBLOCK
        limit = jnp.minimum(pos[b * QBLOCK : (b + 1) * QBLOCK, :], WINDOW - 1)
        allowed = (distance >= 0) & (distance <= limit)
        for h in range(heads):
            start = (b * heads + h) * QBLOCK
            scores = dot_nt(q_st[start : start + QBLOCK, :], keys[first_key : first_key + span, :]) * scale
            scores = jnp.where(allowed, scores, MASKED)
            weights = jnp.exp(scores - jnp.max(scores, axis=-1, keepdims=True))
            weights = (weights * (1.0 / jnp.sum(weights, axis=-1, keepdims=True))).astype(BF16)
            probs[start : start + QBLOCK, :] = weights
            attended[b * QBLOCK : (b + 1) * QBLOCK, h * dim : (h + 1) * dim] = dot(
                weights, values[first_key : first_key + span, :]
            ).astype(BF16)


def gate_kernel(n_out, n_gate, n_up, *refs):
    at, attended, tokens, gain_table = refs[:4]
    refs = refs[4:]
    out_w, gate_w, up_w, refs = (
        refs[:n_out],
        refs[n_out : n_out + n_gate],
        refs[n_out + n_gate : n_out + n_gate + n_up],
        refs[n_out + n_gate + n_up :],
    )
    projected_out, residual_out, ffn_in_ref, mixed_out, gelu_out_out, gate_slope_out = refs[:6]
    (
        projected_ref, residual_ref, mixed, gelu_out, gate_slope,
        out_full, gate_full, up_full, out_sems, gate_sems, up_sems, write_sems,
    ) = refs[6:]
    writer = Writer(write_sems)
    groups = (
        place_copies(out_w[:1], out_w[1:], out_full, out_sems, at, 0, 2),
        place_copies(gate_w[:1], gate_w[1:], gate_full, gate_sems, at, 1, 4),
        place_copies(up_w[:1], up_w[1:], up_full, up_sems, at, 1, 2),
    )
    for group in groups:
        for copy in group:
            copy.start()
    for copy in groups[0]:
        copy.wait()
    projected = dot(attended[...], out_full[...])
    projected_ref[...] = projected
    residual = tokens[...].astype(F32) + projected * inverse_rms(projected) * gain_table[3:4, :]
    residual_ref[...] = residual
    ffn_in_ref[...] = (residual * inverse_rms(residual) * gain_table[4:5, :]).astype(BF16)
    writer.put(projected_ref, projected_out)
    writer.put(residual_ref, residual_out)
    width = gate_full.shape[1] // 4
    for k in range(4):
        waits = groups[1][1 + k :: 4] + (groups[2][1 + k // 2 :: 2] if k % 2 == 0 else [])
        if k == 0:
            waits = groups[1][:1] + groups[2][:1] + waits
        for copy in waits:
            copy.wait()
        core = at[0] if k < 2 else 1 - at[0]
        mid = at[1] if k % 2 == 0 else 1 - at[1]
        cut = pl.ds(multiple((core * 2 + mid) * width, width), width)
        gate = dot(ffn_in_ref[...], gate_full[:, cut])
        up = dot(ffn_in_ref[...], up_full[:, cut])
        square = gate * gate
        t = jnp.tanh(GELU_A * gate * (1.0 + GELU_B * square))
        cdf = 0.5 * (1.0 + t)
        act = gate * cdf
        slope = cdf + 0.5 * gate * (1.0 - t * t) * (GELU_A * (1.0 + 3.0 * GELU_B * square))
        mixed[:, cut] = (act * up).astype(BF16)
        gelu_out[:, cut] = act.astype(BF16)
        gate_slope[:, cut] = (up * slope).astype(BF16)
        writer.put(mixed.at[:, cut], mixed_out.at[:, cut])
        writer.put(gelu_out.at[:, cut], gelu_out_out.at[:, cut])
        writer.put(gate_slope.at[:, cut], gate_slope_out.at[:, cut])
    writer.wait()


def relative_blocks(at, fsdp):
    for c in range(2):
        core = c + at[0] - 2 * c * at[0]
        for f in range(fsdp):
            row = lax.rem(at[2] + f, fsdp)
            for x in range(2):
                mid = x + at[1] - 2 * x * at[1]
                yield c, f, x, core, row, mid


def column_blocks(at, fsdp, left_t, right, keep, send):
    tall, wide = left_t.shape[0] // fsdp, keep.shape[3]
    for c, f, x, core, row, mid in relative_blocks(at, fsdp):
        cut = pl.ds(multiple((core * 2 + mid) * wide, 128), wide)
        left = left_t[pl.ds(multiple(row * tall, 16), tall), :]
        target = keep if c == 0 else send
        target[f, x, :tall, :] = dot(left, right[:, cut]).astype(BF16)


def down_kernel(n_down, fsdp, *refs):
    at, mixed, residual, cotangent, gain_table = refs[:5]
    down_w = refs[5 : 5 + n_down]
    layer_out, d_down, grad_gain, keep, send = refs[5 + n_down : 10 + n_down]
    down_full, mixed_t, sems = refs[10 + n_down :]
    copies = place_copies(down_w[:1], down_w[1:], down_full, sems, at, 0, 2)
    for copy in copies:
        copy.start()
    mixed_t[...] = mixed[...].T
    for copy in copies:
        copy.wait()
    down = dot(mixed[...], down_full[...])
    r = inverse_rms(down)
    gain = gain_table[5:6, :]
    layer_out[...] = (residual[...] + down * r * gain).astype(BF16)
    du, dg = norm_back(down, gain, cotangent[...].astype(F32))
    grad_gain[...] = dg
    d_down[...] = du.astype(BF16)
    block = keep.shape[2]
    for c, f, x, core, row, mid in relative_blocks(at, fsdp):
        start = multiple(((row * 2 + core) * 2 + mid) * block, 16)
        target = keep if c == 0 else send
        target[f, x] = dot(mixed_t[pl.ds(start, block), :], d_down[...]).astype(BF16)


def gate_back_kernel(n_down, fsdp, *refs):
    at, d_down, gelu_out, gate_slope, ffn_in = refs[:5]
    down_w = refs[5 : 5 + n_down]
    d_gate, d_up, keep, send, up_keep, up_send = refs[5 + n_down : 11 + n_down]
    down_full, ffn_t, sems = refs[11 + n_down :]
    copies = place_copies(down_w[:1], down_w[1:], down_full, sems, at, 0, 2)
    for copy in copies:
        copy.start()
    ffn_t[...] = ffn_in[...].T
    for copy in copies:
        copy.wait()
    width = 256

    def step(i, _):
        cut = pl.ds(multiple(i * width, width), width)
        d_mixed = dot_nt(d_down[...], down_full[cut, :])
        d_gate[:, cut] = (d_mixed * gate_slope[:, cut].astype(F32)).astype(BF16)
        d_up[:, cut] = (d_mixed * gelu_out[:, cut].astype(F32)).astype(BF16)
        return 0

    lax.fori_loop(0, d_gate.shape[1] // width, step, 0)
    column_blocks(at, fsdp, ffn_t, d_gate, keep, send)
    column_blocks(at, fsdp, ffn_t, d_up, up_keep, up_send)


def middle_kernel(n_out, n_gate, n_up, fsdp, heads, *refs):
    at, d_gate, d_up, residual, projected, cotangent, gain_table, attended = refs[:8]
    refs = refs[8:]
    out_w, gate_w, up_w, refs = (
        refs[:n_out],
        refs[n_out : n_out + n_gate],
        refs[n_out + n_gate : n_out + n_gate + n_up],
        refs[n_out + n_gate + n_up :],
    )
    d_residual_ref, g_ffn, g_attn, d_att, keep, send = refs[:6]
    out_full, gate_full, up_full, att_t, out_sems, gate_sems, up_sems = refs[6:]
    groups = (
        place_copies(gate_w[:1], gate_w[1:], gate_full, gate_sems, at, 1, 4),
        place_copies(up_w[:1], up_w[1:], up_full, up_sems, at, 1, 2),
        place_copies(out_w[:1], out_w[1:], out_full, out_sems, at, 0, 2),
    )
    for group in groups:
        for copy in group:
            copy.start()
    att_t[...] = attended[...].T
    for copy in groups[0]:
        copy.wait()
    d_ffn_in = dot_nt(d_gate[...], gate_full[...])
    for copy in groups[1]:
        copy.wait()
    d_ffn_in = d_ffn_in + dot_nt(d_up[...], up_full[...])
    du, dg = norm_back(residual[...], gain_table[4:5, :], d_ffn_in)
    g_ffn[...] = dg
    d_residual = cotangent[...].astype(F32) + du
    d_residual_ref[...] = d_residual
    du, dg = norm_back(projected[...], gain_table[3:4, :], d_residual)
    g_attn[...] = dg
    d_proj = du.astype(BF16)
    rows, dim = d_proj.shape[0], d_att.shape[1]
    for copy in groups[2]:
        copy.wait()
    for h in range(heads):
        part = dot_nt(d_proj, out_full[h * dim : (h + 1) * dim, :]).astype(BF16)
        for b in range(rows // QBLOCK):
            start = (b * heads + h) * QBLOCK
            d_att[start : start + QBLOCK, :] = part[b * QBLOCK : (b + 1) * QBLOCK, :]
    block = att_t.shape[0] // (4 * fsdp)
    wide = keep.shape[3]
    parts = wide // LANES
    deep = block // parts
    for c, f, x, core, row, mid in relative_blocks(at, fsdp):
        start = multiple(((row * 2 + core) * 2 + mid) * block, 16)
        part = dot(att_t[pl.ds(start, block), :], d_proj).astype(BF16)
        target = keep if c == 0 else send
        target[f, x, :block, :] = part[:, :wide]
        for i in range(parts):
            target[f, x, block:, i * LANES : (i + 1) * LANES] = part[i * deep : (i + 1) * deep, wide:]


def attend_back_kernel(halo, heads, d_att, q_st, keys, values, probs, d_q, d_k, d_v, d_scores):
    rows = d_q.shape[0]
    dim = keys.shape[1]
    blocks = rows // QBLOCK
    span = WINDOW + QBLOCK
    scale = dim ** (-0.5)
    d_k[...] = jnp.zeros(d_k.shape, F32)
    d_v[...] = jnp.zeros(d_v.shape, F32)
    for b in range(blocks):
        first_key = halo - WINDOW + b * QBLOCK
        here = slice(first_key, first_key + span)
        for h in range(heads):
            start = (b * heads + h) * QBLOCK
            stack = slice(start, start + QBLOCK)
            d_probs = dot_nt(d_att[stack, :], values[here, :])
            p = probs[stack, :].astype(F32)
            row_terms = jnp.sum(p * d_probs, axis=-1, keepdims=True)
            ds = (p * (d_probs - row_terms) * scale).astype(BF16)
            d_scores[h * QBLOCK : (h + 1) * QBLOCK, :] = ds
            d_q[b * QBLOCK : (b + 1) * QBLOCK, h * dim : (h + 1) * dim] = dot(ds, keys[here, :])
        stack = slice(b * heads * QBLOCK, (b + 1) * heads * QBLOCK)
        d_k[here, :] += dot_tn(d_scores[...], q_st[stack, :])
        d_v[here, :] += dot_tn(probs[stack, :], d_att[stack, :])


def last_kernel(n_qkv, n_tok, fsdp, heads, *refs):
    (
        at, d_residual, d_q, d_k, d_v,
        q_raw, k_raw, cosine, sine, gain_table, normed, g_ffn, g_attn, g_out,
    ) = refs[:14]
    toks = refs[14 : 14 + n_tok]
    refs = refs[14 + n_tok :]
    qkv_w, refs = refs[:n_qkv], refs[n_qkv:]
    grad_tokens, d_halo, keep, send = refs[:4]
    w_full, normed_t, d_qkv, gain_rows, qkv_sems = refs[4:]
    copies = place_copies(qkv_w[:3], qkv_w[3:], w_full, qkv_sems, at, 1, 4)
    for copy in copies:
        copy.start()
    normed_t[...] = normed[...].T
    rows = toks[0].shape[0]
    halo = (n_tok - 1) * rows
    dim = k_raw.shape[1]
    gain_in, gain_q, gain_k = gain_table[0:1, :], gain_table[1:2, :dim], gain_table[2:3, :dim]
    half = dim // 2
    tall, wide = normed_t.shape[0] // fsdp, keep.shape[3]
    def turned_back(u, g, dz, cos, sin):
        first, second = dz[:, :half], dz[:, half:]
        dz = jnp.concatenate([first * cos + second * sin, second * cos - first * sin], axis=1)
        return norm_back(u, g, dz)

    total_q = jnp.zeros((1, dim), F32)
    if halo:
        d_qkv[:halo, : heads * dim] = jnp.zeros((halo, heads * dim), BF16)
    for h in range(heads):
        cut = slice(h * dim, (h + 1) * dim)
        du, dg = turned_back(q_raw[:, cut], gain_q, d_q[:, cut], cosine[halo:, :], sine[halo:, :])
        total_q += dg
        d_qkv[halo:, cut] = du.astype(BF16)
    total_k = jnp.zeros((1, dim), F32)
    for i in range(n_tok):
        here = slice(i * rows, (i + 1) * rows)
        du, dg = turned_back(k_raw[here, :], gain_k, d_k[here, :], cosine[here, :], sine[here, :])
        total_k += dg
        d_qkv[here, heads * dim : (heads + 1) * dim] = du.astype(BF16)
        d_qkv[here, (heads + 1) * dim :] = d_v[here, :].astype(BF16)
    column_blocks(at, fsdp, normed_t, d_qkv, keep, send)
    for copy in copies:
        copy.wait()
    total_in = jnp.zeros(gain_in.shape, F32)
    for i in range(n_tok):
        here = slice(i * rows, (i + 1) * rows)
        if i < n_tok - 1:
            d_normed = dot_nt(d_qkv[here, heads * dim :], w_full[:, heads * dim :])
        else:
            d_normed = dot_nt(d_qkv[here, :], w_full[...])
        du, dg = norm_back(toks[i][...].astype(F32), gain_in, d_normed)
        total_in += dg
        if i < n_tok - 1:
            d_halo[here, :] = du.astype(BF16)
        else:
            grad_tokens[...] = d_residual[...] + du
    gain_rows[...] = jnp.zeros(gain_rows.shape, F32)
    at_row = 0
    for total in (total_in, total_q, total_k, g_attn[...], g_ffn[...], g_out[...]):
        for i in range(total.shape[1] // LANES):
            gain_rows[at_row : at_row + 1, :LANES] = total[:, i * LANES : (i + 1) * LANES]
            at_row += 1
    packed = gain_rows[...].astype(BF16)
    for target in (keep, send):
        for f in range(fsdp):
            for x in range(2):
                target[f, x, tall:, :] = packed


def add(*terms):
    out = terms[0].astype(F32)
    for term in terms[1:]:
        out = out + term.astype(F32)
    return out


class Chunk:
    def __init__(self, here, keep, send):
        self.here, self.keep = here, keep
        self.other = here.core_swap(send)

    def over_fsdp(self, *earlier):
        here = self.here
        parts = [add(self.keep[by], self.other[by]).astype(BF16) for by in range(1, here.fsdp)]
        self.arrived = [here.fsdp_shift(after(part, *earlier), by + 1) for by, part in enumerate(parts)]

    def over_mid(self, *earlier):
        self.arrived = [after(a, *earlier) for a in self.arrived]
        terms = [self.keep[0, 1], self.other[0, 1]] + [a[1] for a in self.arrived]
        self.across = self.here.mid_swap(add(*terms).astype(BF16))
        self.mine = [self.keep[0, 0], self.other[0, 0]] + [a[0] for a in self.arrived]
        return self.arrived[0] if self.arrived else self.other

    def join(self, below, *earlier):
        for chunk in (self, below):
            chunk.arrived = [after(a, *earlier) for a in chunk.arrived]
        pairs = [
            [[c.keep[0, x], c.other[0, x]] + [a[x] for a in c.arrived] for c in (self, below)] for x in range(2)
        ]
        self.across_sent = jnp.concatenate([add(*terms).astype(BF16) for terms in pairs[1]])
        self.across = self.here.mid_swap(self.across_sent)
        self.mine = [jnp.concatenate([add(*terms).astype(BF16) for terms in pairs[0]])]

    def outer_sums(self, *earlier):
        here = self.here
        self.across = after(self.across, *earlier)
        mine = add(*self.mine, self.across).astype(BF16)
        n, w = mine.shape
        mine = mine.reshape(here.outer, n // here.outer, w)
        self.shares = [pick(mine, here.outer_ahead[0])]
        for by in range(1, here.outer):
            self.shares.append(here.outer_shift(pick(mine, here.outer_ahead[by]), by))
        return self.across

    def outer_gather(self, *earlier):
        here = self.here
        self.shares = list(after(tuple(self.shares), *earlier))
        own = add(*self.shares).astype(BF16)
        self.gathered = [own] + [here.outer_shift(own, by) for by in range(1, here.outer)]
        return self.shares[-1]

    def mid_gather(self, *earlier):
        here = self.here
        self.gathered = list(after(tuple(self.gathered), *earlier))
        block = ordered(self.gathered, here.outer_behind)
        block = block.reshape(-1, block.shape[-1])
        across = here.mid_swap(block)
        self.blocks = [[block, across], None]

    def core_gather(self, *earlier):
        own = after(tuple(self.blocks[0]), *earlier)
        self.blocks = [list(own), [self.here.core_swap(block) for block in own]]


def by_place(here, blocks):
    own = [jnp.where(here.mid_at == 0, a, b) for a, b in blocks]
    other = [jnp.where(here.mid_at == 0, b, a) for a, b in blocks]
    pairs = list(zip(own, other))
    first = [jnp.where(here.core_at == 0, a, b) for a, b in zip(pairs[0], pairs[1])]
    second = [jnp.where(here.core_at == 0, b, a) for a, b in zip(pairs[0], pairs[1])]
    return first + second


def last_columns(blocks, start, count):
    wide = blocks[0].shape[1]
    pieces = []
    for i, block in enumerate(blocks):
        low, high = max(start - i * wide, 0), min(start + count - i * wide, wide)
        if low < high:
            pieces.append(block[:, low:high])
    return jnp.concatenate(pieces, axis=1).astype(F32)


def on_device(
    tokens, positions, cotangent, in_gain, w_query, w_key, w_value, query_gain, key_gain, w_out, attn_gain,
    ffn_gain_in, w_gate, w_up, w_down, ffn_gain_out,
):
    here = Places()
    fsdp = here.fsdp
    rows, width = tokens.shape
    dim = w_key.shape[1]
    query_cols = w_query.shape[1]
    heads = query_cols // dim
    hidden = w_gate.shape[1]
    hops = (WINDOW + rows - 1) // rows
    n_tok = hops + 1
    halo = hops * rows
    every = halo + rows
    at = here.vector

    gains = (in_gain, query_gain, key_gain, attn_gain, ffn_gain_in, ffn_gain_out)
    cuts = [0]
    for gain in gains:
        cuts.append(cuts[-1] + gain.shape[0])
    gain_row = jnp.concatenate(gains)
    gain_rows = ordered([gain_row] + [here.fsdp_shift(gain_row, by) for by in range(1, fsdp)], here.fsdp_behind)
    gain_rows = gain_rows.astype(F32)
    gain_table = jnp.concatenate(
        [
            jnp.pad(gain_rows[:, cuts[i] : cuts[i + 1]].reshape(1, -1), ((0, 0), (0, width - fsdp * gains[i].shape[0])))
            for i in range(6)
        ]
        + [jnp.zeros((2, width), F32)],
        axis=0,
    )
    qkv_w = [w_query, w_key, w_value]
    qkv_part = own_part(here, qkv_w, 1, 4)
    tokens_out = after(tokens, qkv_part)
    toks = [linear_shift(tokens_out, by) for by in range(hops, 0, -1)] + [tokens]
    qkv_w += on_chips(here, over_links(here, qkv_part), 4)
    out_arrived = over_links(here, after(own_part(here, [w_out], 0, 2), *toks[:-1]))
    gate_arrived = over_links(here, after(own_part(here, [w_gate], 1, 4), qkv_w[3]))
    up_arrived = over_links(here, after(own_part(here, [w_up], 1, 2), *gate_arrived))

    all_positions = jnp.concatenate([positions[0] - halo + jnp.arange(halo, dtype=jnp.int32), positions])
    frequency = ROPE_BASE ** (-(jnp.arange(dim // 2, dtype=F32) * 2.0 / dim))
    angles = all_positions.astype(F32)[:, None] * frequency[None, :]
    cosine, sine = jnp.cos(angles), jnp.sin(angles)

    span = WINDOW + QBLOCK
    weight_bytes = 2 * fsdp * w_gate.size
    normed, q_raw, k_raw, q_st, keys, values, probs, attended = pl.pallas_call(
        functools.partial(attend_kernel, n_tok, len(qkv_w), heads),
        out_shape=(
            shape((every, width), BF16),
            shape((rows, query_cols), F32),
            shape((every, dim), F32),
            shape((heads * rows, dim), BF16),
            shape((every, dim), BF16),
            shape((every, dim), BF16),
            shape((heads * rows, span), BF16),
            shape((rows, query_cols), BF16),
        ),
        in_specs=[SMEM] + [VMEM] * (n_tok + 4) + [ANY] * len(qkv_w),
        out_specs=(VMEM,) * 8,
        scratch_shapes=[
            pltpu.VMEM((width, query_cols + 2 * dim), BF16),
            pltpu.SemaphoreType.DMA((len(qkv_w),)),
        ],
        compiler_params=params(),
        cost_estimate=cost(4e9, 1e7),
        name="attend",
    )(at, *toks, after(positions[:, None], *gate_arrived), cosine, sine, gain_table, *qkv_w)

    down_arrived = over_links(here, after(own_part(here, [w_down], 0, 2), attended))
    out_w = [w_out] + on_chips(here, [after(a, attended) for a in out_arrived], 2)
    gate_w = [w_gate] + on_chips(here, gate_arrived, 4)
    up_w = [w_up] + on_chips(here, [after(a, attended) for a in up_arrived], 2)
    projected, residual, ffn_in, mixed, gelu_out, gate_slope = pl.pallas_call(
        functools.partial(gate_kernel, len(out_w), len(gate_w), len(up_w)),
        out_shape=(
            shape((rows, width), F32),
            shape((rows, width), F32),
            shape((rows, width), BF16),
            shape((rows, hidden), BF16),
            shape((rows, hidden), BF16),
            shape((rows, hidden), BF16),
        ),
        in_specs=[SMEM] + [VMEM] * 3 + [ANY] * (len(out_w) + len(gate_w) + len(up_w)),
        out_specs=(ANY, ANY, VMEM, ANY, ANY, ANY),
        scratch_shapes=[
            pltpu.VMEM((rows, width), F32),
            pltpu.VMEM((rows, width), F32),
            pltpu.VMEM((rows, hidden), BF16),
            pltpu.VMEM((rows, hidden), BF16),
            pltpu.VMEM((rows, hidden), BF16),
            pltpu.VMEM((query_cols, width), BF16),
            pltpu.VMEM((width, hidden), BF16),
            pltpu.VMEM((width, hidden), BF16),
            pltpu.SemaphoreType.DMA((len(out_w),)),
            pltpu.SemaphoreType.DMA((len(gate_w),)),
            pltpu.SemaphoreType.DMA((len(up_w),)),
            pltpu.SemaphoreType.DMA((14,)),
        ],
        compiler_params=params(),
        cost_estimate=cost(4e9, 2 * weight_bytes),
        name="gate",
    )(at, attended, tokens, gain_table, *out_w, *gate_w, *up_w)

    down_w = [w_down] + on_chips(here, [after(a, mixed) for a in down_arrived], 2)
    down_block = w_down.shape[0] // 4
    down_shape = shape((fsdp, 2, down_block, width), BF16)
    layer_out, d_down, g_ffn_out, down_keep, down_send = pl.pallas_call(
        functools.partial(down_kernel, len(down_w), fsdp),
        out_shape=(
            shape((rows, width), BF16),
            shape((rows, width), BF16),
            shape((1, width), F32),
            down_shape,
            down_shape,
        ),
        in_specs=[SMEM] + [VMEM] * 4 + [ANY] * len(down_w),
        out_specs=(VMEM,) * 5,
        scratch_shapes=[
            pltpu.VMEM((hidden, width), BF16),
            pltpu.VMEM((hidden, rows), BF16),
            pltpu.SemaphoreType.DMA((len(down_w),)),
        ],
        compiler_params=params(),
        cost_estimate=cost(4e9, 2 * weight_bytes),
        name="down",
    )(at, mixed, residual, cotangent, gain_table, *down_w)

    down_sum = Chunk(here, down_keep, down_send)
    gate_shape = shape((fsdp, 2, w_gate.shape[0], hidden // 4), BF16)
    d_gate, d_up, gate_keep, gate_send, up_keep, up_send = pl.pallas_call(
        functools.partial(gate_back_kernel, len(down_w), fsdp),
        out_shape=(
            shape((rows, hidden), BF16),
            shape((rows, hidden), BF16),
            gate_shape,
            gate_shape,
            gate_shape,
            gate_shape,
        ),
        in_specs=[SMEM] + [VMEM] * 4 + [ANY] * len(down_w),
        out_specs=(VMEM,) * 6,
        scratch_shapes=[
            pltpu.VMEM((hidden, width), BF16),
            pltpu.VMEM((width, rows), BF16),
            pltpu.SemaphoreType.DMA((len(down_w),)),
        ],
        compiler_params=params(),
        cost_estimate=cost(6e9, 3 * weight_bytes),
        name="gate_back",
    )(at, d_down, gelu_out, gate_slope, ffn_in, *down_w)
    gate_sum = Chunk(here, gate_keep, gate_send)
    up_sum = Chunk(here, up_keep, up_send)
    down_sum.over_fsdp(d_gate)
    d_gate = after(d_gate, down_sum.other)
    qkv_cols = query_cols + 2 * dim
    last_wide = qkv_cols // 4
    shard_rows = w_query.shape[0]
    last_shape = shape((fsdp, 2, shard_rows + GAIN_ROWS, last_wide), BF16)
    out_block = w_out.shape[0] // 4
    out_shape = shape((fsdp, 2, out_block * width // (hidden // 4), hidden // 4), BF16)
    d_residual, g_ffn, g_attn, d_att, out_keep, out_send = pl.pallas_call(
        functools.partial(middle_kernel, len(out_w), len(gate_w), len(up_w), fsdp, heads),
        out_shape=(
            shape((rows, width), F32),
            shape((1, width), F32),
            shape((1, width), F32),
            shape((heads * rows, dim), BF16),
            out_shape,
            out_shape,
        ),
        in_specs=[SMEM] + [VMEM] * 7 + [ANY] * (len(out_w) + len(gate_w) + len(up_w)),
        out_specs=(VMEM,) * 6,
        scratch_shapes=[
            pltpu.VMEM((query_cols, width), BF16),
            pltpu.VMEM((width, hidden), BF16),
            pltpu.VMEM((width, hidden), BF16),
            pltpu.VMEM((query_cols, rows), BF16),
            pltpu.SemaphoreType.DMA((len(out_w),)),
            pltpu.SemaphoreType.DMA((len(gate_w),)),
            pltpu.SemaphoreType.DMA((len(up_w),)),
        ],
        compiler_params=params(),
        cost_estimate=cost(6e9, 4 * weight_bytes),
        name="middle",
    )(at, d_gate, d_up, residual, projected, cotangent, gain_table, attended, *out_w, *gate_w, *up_w)

    out_sum = Chunk(here, out_keep, out_send)
    gate_sum.over_fsdp(g_ffn)
    up_sum.over_fsdp(g_ffn)
    down_sum.over_mid(g_ffn)
    d_q, d_k, d_v = pl.pallas_call(
        functools.partial(attend_back_kernel, halo, heads),
        out_shape=(shape((rows, query_cols), F32), shape((every, dim), F32), shape((every, dim), F32)),
        in_specs=[VMEM] * 5,
        out_specs=(VMEM,) * 3,
        scratch_shapes=[pltpu.VMEM((heads * QBLOCK, span), BF16)],
        compiler_params=params(),
        cost_estimate=cost(6e9, 3 * weight_bytes),
        name="attend_back",
    )(after(d_att, gate_sum.other, up_sum.other, *down_sum.arrived), q_st, keys, values, probs)
    out_sum.over_fsdp(d_k)
    down_sum.outer_sums(d_k)
    d_q = after(d_q, out_sum.other, down_sum.across)
    grad_tokens, d_halo, last_keep, last_send = pl.pallas_call(
        functools.partial(last_kernel, len(qkv_w), n_tok, fsdp, heads),
        out_shape=(
            shape((rows, width), F32),
            shape((halo, width), BF16),
            last_shape,
            last_shape,
        ),
        in_specs=[SMEM] + [VMEM] * (13 + n_tok) + [ANY] * len(qkv_w),
        out_specs=(VMEM,) * 4,
        scratch_shapes=[
            pltpu.VMEM((width, qkv_cols), BF16),
            pltpu.VMEM((width, every), BF16),
            pltpu.VMEM((every, qkv_cols), BF16),
            pltpu.VMEM((GAIN_ROWS, last_wide), F32),
            pltpu.SemaphoreType.DMA((len(qkv_w),)),
        ],
        compiler_params=params(),
        cost_estimate=cost(15e9, 4 * weight_bytes),
        name="last",
    )(
        at, d_residual, d_q, d_k, d_v,
        q_raw, k_raw, cosine, sine, gain_table, normed, g_ffn, g_attn, g_ffn_out, *toks, *qkv_w,
    )

    last_sum = Chunk(here, last_keep, last_send)
    down_sum.outer_sums(last_keep)
    gate_sum.over_mid(last_keep, *up_sum.arrived)
    (last_sum.other,), (gate_sum.across,), down_sum.shares, out_sum.arrived = together(
        (last_sum.other,), (gate_sum.across,), down_sum.shares, out_sum.arrived
    )
    last_sum.over_fsdp()
    up_sum.join(out_sum)
    gate_sum.outer_sums()
    down_sum.outer_gather()
    last_sum.arrived, (up_sum.across,), gate_sum.shares, down_sum.gathered = together(
        last_sum.arrived, (up_sum.across,), gate_sum.shares, down_sum.gathered
    )
    last_sum.over_mid()
    up_sum.outer_sums()
    gate_sum.outer_gather()
    down_sum.mid_gather()
    (last_sum.across,), up_sum.shares, gate_sum.gathered, down_last = together(
        (last_sum.across,), up_sum.shares, gate_sum.gathered, down_sum.blocks[0]
    )
    down_sum.blocks[0] = list(down_last)
    last_sum.outer_sums()
    up_sum.outer_gather()
    gate_sum.mid_gather()
    last_sum.shares, up_sum.gathered, gate_last = together(last_sum.shares, up_sum.gathered, gate_sum.blocks[0])
    gate_sum.blocks[0] = list(gate_last)
    last_sum.outer_gather()
    up_sum.mid_gather()
    last_sum.mid_gather(up_sum.blocks[0][1])
    d_halo = after(d_halo, up_sum.blocks[0][1])
    halos = [linear_shift(d_halo[halo - by * rows :][:rows], -by) for by in range(1, hops + 1)]
    up_sum.core_gather()
    down_sum.core_gather(up_sum.blocks[0][1])
    gate_sum.core_gather(up_sum.blocks[0][1])
    down_blocks, gate_blocks = by_place(here, down_sum.blocks), by_place(here, gate_sum.blocks)
    total_down = jnp.concatenate(down_blocks, axis=0).astype(F32)
    total_gate = jnp.concatenate(gate_blocks, axis=1).astype(F32)
    last_sum.core_gather(total_down, total_gate)
    up_blocks = by_place(here, [[b[:shard_rows] for b in pair] for pair in up_sum.blocks])
    beside = by_place(here, [[b[shard_rows : shard_rows + out_block] for b in pair] for pair in up_sum.blocks])
    below = by_place(here, [[b[shard_rows + out_block :] for b in pair] for pair in up_sum.blocks])
    last_blocks = by_place(here, [[b[:shard_rows] for b in pair] for pair in last_sum.blocks])
    total_gains = last_sum.blocks[0][0][shard_rows:, :LANES].astype(F32)
    total_up = jnp.concatenate(up_blocks, axis=1).astype(F32)
    parts = hidden // 4 // LANES
    total_out = []
    for left, right in zip(beside, below):
        right = jnp.concatenate([right[:, i * LANES : (i + 1) * LANES] for i in range(parts)])
        total_out.append(jnp.concatenate([left, right], axis=1))
    total_out = jnp.concatenate(total_out, axis=0).astype(F32)

    for came in halos:
        grad_tokens = grad_tokens + after(came, total_up, total_out).astype(F32)

    total_qkv = [last_columns(last_blocks, 0, query_cols)]
    total_qkv += [last_columns(last_blocks, query_cols + i * dim, dim) for i in range(2)]
    g, at_row = [], 0
    for gain in gains:
        deep = fsdp * gain.shape[0] // total_gains.shape[1]
        total = total_gains[at_row : at_row + deep].reshape(fsdp, gain.shape[0])
        g.append(pick(total, here.fsdp_at))
        at_row += deep
    return (
        layer_out, grad_tokens, g[0],
        *total_qkv,
        g[1], g[2], total_out, g[3], g[4], total_gate, total_up, total_down, g[5],
    )


def solution(mesh):
    tok = P(("seq", "fsdp"), None)
    mat = P("fsdp", None)
    vec = P("fsdp")
    return jax.shard_map(
        on_device,
        mesh=mesh,
        in_specs=(tok, P(("seq", "fsdp")), tok, vec, mat, mat, mat, vec, vec, mat, vec, vec, mat, mat, mat, vec),
        out_specs=(tok, tok, vec, mat, mat, mat, vec, vec, mat, vec, vec, mat, mat, mat, vec),
        check_vma=False,
    )
```

```python
import functools
import math

import jax
import jax.numpy as jnp
from jax import lax
from jax.experimental import pallas as pl
from jax.experimental.pallas import tpu as pltpu
from jax.sharding import PartitionSpec as P

WINDOW = 512
EPSILON = 1e-06
ROPE_BASE = 10000.0
MASKED = -1e30
BF16 = jnp.bfloat16
F32 = jnp.float32
QBLOCK = 128
LANES = 128
GAIN_ROWS = 32
GELU_A = math.sqrt(2.0 / math.pi)
GELU_B = 0.044715

VMEM = pl.BlockSpec(memory_space=pltpu.VMEM)
SMEM = pl.BlockSpec(memory_space=pltpu.SMEM)
ANY = pl.BlockSpec(memory_space=pl.ANY)


def wrapped(value, size):
    return value & (size - 1) if size & (size - 1) == 0 else lax.rem(value, jnp.int32(size))


class Places:
    def __init__(self):
        self.seq = lax.axis_size("seq")
        self.fsdp = lax.axis_size("fsdp")
        self.outer = self.seq // 4
        index = lax.axis_index("seq").astype(jnp.int32)
        fsdp_at = lax.axis_index("fsdp").astype(jnp.int32)
        outer_at = lax.shift_right_logical(index, 2)
        core_at, mid_at = index & 1, lax.shift_right_logical(index, 1) & 1
        scalars = lax.optimization_barrier(
            (
                core_at,
                mid_at,
                fsdp_at,
                core_at * 2 + mid_at,
                tuple(wrapped(outer_at + by, self.outer) for by in range(self.outer)),
                tuple(wrapped(outer_at - by + self.outer, self.outer) for by in range(self.outer)),
                tuple(wrapped(fsdp_at + by, self.fsdp) for by in range(self.fsdp)),
                tuple(wrapped(fsdp_at - by + self.fsdp, self.fsdp) for by in range(self.fsdp)),
                jnp.stack([core_at, mid_at, fsdp_at]),
            )
        )
        self.core_at, self.mid_at, self.fsdp_at, self.quarter_at = scalars[:4]
        self.outer_ahead, self.outer_behind, self.fsdp_ahead, self.fsdp_behind, self.vector = scalars[4:]

    def core_swap(self, array):
        return lax.ppermute(array, "seq", [(i, i ^ 1) for i in range(self.seq)])

    def mid_swap(self, array):
        return lax.ppermute(array, "seq", [(i, i ^ 2) for i in range(self.seq)])

    def outer_shift(self, array, by):
        return lax.ppermute(array, "seq", [(i, (i + 4 * by) % self.seq) for i in range(self.seq)])

    def fsdp_shift(self, array, by):
        return lax.ppermute(array, "fsdp", [(i, (i + by) % self.fsdp) for i in range(self.fsdp)])


def linear_shift(array, by):
    count = lax.axis_size("seq") * lax.axis_size("fsdp")
    return lax.ppermute(array, ("seq", "fsdp"), [(i, i + by) for i in range(count) if 0 <= i + by < count])


def pick(array, at):
    return lax.dynamic_index_in_dim(array, at, 0, keepdims=False, allow_negative_indices=False)


def ordered(pieces, behind):
    if len(pieces) == 2:
        own, other = pieces
        return jnp.where(behind[0] == 0, jnp.stack([own, other]), jnp.stack([other, own]))
    stacked = jnp.stack(pieces)
    return jnp.stack([pick(stacked, at) for at in behind])


def own_part(here, shards, axis, ways):
    size = sum(shard.shape[axis] for shard in shards) // ways
    place = here.quarter_at if ways == 4 else here.core_at
    if len(shards) == 1:
        return lax.dynamic_slice_in_dim(shards[0], place * size, size, axis, allow_negative_indices=False)
    parts = []
    for i in range(ways):
        pieces, start = [], 0
        for shard in shards:
            low, high = max(i * size - start, 0), min((i + 1) * size - start, shard.shape[axis])
            if low < high:
                pieces.append(lax.slice_in_dim(shard, low, high, axis=axis))
            start += shard.shape[axis]
        parts.append(jnp.concatenate(pieces, axis))
    return functools.reduce(lambda rest, i: jnp.where(place == i, parts[i], rest), range(1, ways), parts[0])


def after(value, *earlier):
    return lax.optimization_barrier((value, *earlier))[0]


def together(*groups):
    return lax.optimization_barrier(tuple(tuple(group) for group in groups))


def over_links(here, part):
    return [here.fsdp_shift(part, by) for by in range(1, here.fsdp)]


def on_chips(here, arrived, ways):
    pieces = []
    for mine in arrived:
        if ways == 4:
            across = here.mid_swap(mine)
            pieces += [mine, across, here.core_swap(mine), here.core_swap(across)]
        else:
            pieces += [mine, here.core_swap(mine)]
    return pieces


def multiple(value, of):
    return pl.multiple_of(value, of)


def place_copies(owned, pieces, whole, sems, at, axis, ways):
    core, mid, fsdp = at[0], at[1], at[2]
    count = 1 + len(pieces) // ways
    rows = owned[0].shape[0]
    copies = []
    column = 0
    own_row = multiple(fsdp * rows, 16)
    for shard in owned:
        wide = shard.shape[1]
        copies.append((shard, whole.at[pl.ds(own_row, rows), pl.ds(column, wide)]))
        column += wide
    for k, piece in enumerate(pieces):
        by = 1 + k // ways
        row = multiple(lax.rem(fsdp + (count - by), count) * rows, 16)
        k = k % ways
        if ways == 4:
            place = (core if k < 2 else 1 - core) * 2 + (mid if k % 2 == 0 else 1 - mid)
        else:
            place = core if k == 0 else 1 - core
        if axis == 0:
            target = whole.at[pl.ds(multiple(row + place * (rows // ways), 16), rows // ways), :]
        else:
            target = whole.at[pl.ds(row, rows), pl.ds(multiple(place * (column // ways), 128), column // ways)]
        copies.append((piece, target))
    return [pltpu.make_async_copy(a, b, sems.at[k]) for k, (a, b) in enumerate(copies)]


def dot(a, b):
    return lax.dot_general(a, b, (((1,), (0,)), ((), ())), preferred_element_type=F32)


def dot_nt(a, b):
    return lax.dot_general(a, b, (((1,), (1,)), ((), ())), preferred_element_type=F32)


def dot_tn(a, b):
    return lax.dot_general(a, b, (((0,), (0,)), ((), ())), preferred_element_type=F32)


def inverse_rms(u):
    return lax.rsqrt(jnp.mean(u * u, axis=-1, keepdims=True) + EPSILON)


def norm_back(u, g, dz):
    r = inverse_rms(u)
    ur = u * r
    gdz = g * dz
    du = r * (gdz - ur * jnp.mean(gdz * ur, axis=-1, keepdims=True))
    return du, jnp.sum(dz * ur, axis=0, keepdims=True)


class Writer:
    def __init__(self, sems):
        self.sems, self.copies = sems, []

    def put(self, source, target):
        copy = pltpu.make_async_copy(source, target, self.sems.at[len(self.copies)])
        copy.start()
        self.copies.append(copy)

    def wait(self):
        for copy in self.copies:
            copy.wait()


def params(megabytes=56):
    return pltpu.CompilerParams(vmem_limit_bytes=megabytes * 1024 * 1024)


def cost(flops, bytes_accessed):
    return pl.CostEstimate(flops=int(20 * flops), bytes_accessed=int(20 * bytes_accessed), transcendentals=0)


def shape(dims, kind):
    return jax.ShapeDtypeStruct(tuple(dims), kind)


def attend_kernel(n_tok, n_qkv, heads, *refs):
    at = refs[0]
    toks = refs[1 : 1 + n_tok]
    pos, cosine, sine, gain_table = refs[1 + n_tok : 5 + n_tok]
    qkv = refs[5 + n_tok : 5 + n_tok + n_qkv]
    normed, q_raw, k_raw, q_st, keys, values, probs, attended, w_full, sems = refs[5 + n_tok + n_qkv :]
    copies = place_copies(qkv[:3], qkv[3:], w_full, sems, at, 1, 4)
    for copy in copies:
        copy.start()
    rows = toks[0].shape[0]
    dim = keys.shape[1]
    half = dim // 2
    halo = (n_tok - 1) * rows
    gain = gain_table[0:1, :]
    gain_q, gain_k = gain_table[1:2, :dim], gain_table[2:3, :dim]
    for i, tok in enumerate(toks):
        u = tok[...].astype(F32)
        normed[i * rows : (i + 1) * rows, :] = (u * inverse_rms(u) * gain).astype(BF16)
    for copy in copies:
        copy.wait()

    def turned(u, g, cos, sin):
        u = u * inverse_rms(u) * g
        first, second = u[:, :half], u[:, half:]
        return (first * cos - second * sin).astype(BF16), (second * cos + first * sin).astype(BF16)

    for i in range(n_tok):
        here = slice(i * rows, (i + 1) * rows)
        kv = dot(normed[here, :], w_full[:, heads * dim :])
        k_raw[here, :] = kv[:, :dim]
        values[here, :] = kv[:, dim:].astype(BF16)
        first, second = turned(kv[:, :dim], gain_k, cosine[here, :], sine[here, :])
        keys[here, :half] = first
        keys[here, half:] = second
    blocks = rows // QBLOCK
    for h in range(heads):
        u = dot(normed[halo:, :], w_full[:, h * dim : (h + 1) * dim])
        q_raw[:, h * dim : (h + 1) * dim] = u
        first, second = turned(u, gain_q, cosine[halo:, :], sine[halo:, :])
        for b in range(blocks):
            start = (b * heads + h) * QBLOCK
            q_st[start : start + QBLOCK, :half] = first[b * QBLOCK : (b + 1) * QBLOCK, :]
            q_st[start : start + QBLOCK, half:] = second[b * QBLOCK : (b + 1) * QBLOCK, :]
    span = WINDOW + QBLOCK
    distance = (
        lax.broadcasted_iota(jnp.int32, (QBLOCK, span), 0)
        + WINDOW
        - lax.broadcasted_iota(jnp.int32, (QBLOCK, span), 1)
    )
    scale = dim ** (-0.5)
    for b in range(blocks):
        first_key = halo - WINDOW + b * QBLOCK
        limit = jnp.minimum(pos[b * QBLOCK : (b + 1) * QBLOCK, :], WINDOW - 1)
        allowed = (distance >= 0) & (distance <= limit)
        for h in range(heads):
            start = (b * heads + h) * QBLOCK
            scores = dot_nt(q_st[start : start + QBLOCK, :], keys[first_key : first_key + span, :]) * scale
            scores = jnp.where(allowed, scores, MASKED)
            weights = jnp.exp(scores - jnp.max(scores, axis=-1, keepdims=True))
            weights = (weights * (1.0 / jnp.sum(weights, axis=-1, keepdims=True))).astype(BF16)
            probs[start : start + QBLOCK, :] = weights
            attended[b * QBLOCK : (b + 1) * QBLOCK, h * dim : (h + 1) * dim] = dot(
                weights, values[first_key : first_key + span, :]
            ).astype(BF16)


def gate_kernel(n_out, n_gate, n_up, *refs):
    at, attended, tokens, gain_table = refs[:4]
    refs = refs[4:]
    out_w, gate_w, up_w, refs = (
        refs[:n_out],
        refs[n_out : n_out + n_gate],
        refs[n_out + n_gate : n_out + n_gate + n_up],
        refs[n_out + n_gate + n_up :],
    )
    projected_out, residual_out, ffn_in_ref, mixed_out, gelu_out_out, gate_slope_out = refs[:6]
    (
        projected_ref, residual_ref, mixed, gelu_out, gate_slope,
        out_full, gate_full, up_full, out_sems, gate_sems, up_sems, write_sems,
    ) = refs[6:]
    writer = Writer(write_sems)
    groups = (
        place_copies(out_w[:1], out_w[1:], out_full, out_sems, at, 0, 2),
        place_copies(gate_w[:1], gate_w[1:], gate_full, gate_sems, at, 1, 4),
        place_copies(up_w[:1], up_w[1:], up_full, up_sems, at, 1, 2),
    )
    for group in groups:
        for copy in group:
            copy.start()
    for copy in groups[0]:
        copy.wait()
    projected = dot(attended[...], out_full[...])
    projected_ref[...] = projected
    residual = tokens[...].astype(F32) + projected * inverse_rms(projected) * gain_table[3:4, :]
    residual_ref[...] = residual
    ffn_in_ref[...] = (residual * inverse_rms(residual) * gain_table[4:5, :]).astype(BF16)
    writer.put(projected_ref, projected_out)
    writer.put(residual_ref, residual_out)
    width = gate_full.shape[1] // 4
    for k in range(4):
        waits = groups[1][1 + k :: 4] + (groups[2][1 + k // 2 :: 2] if k % 2 == 0 else [])
        if k == 0:
            waits = groups[1][:1] + groups[2][:1] + waits
        for copy in waits:
            copy.wait()
        core = at[0] if k < 2 else 1 - at[0]
        mid = at[1] if k % 2 == 0 else 1 - at[1]
        cut = pl.ds(multiple((core * 2 + mid) * width, width), width)
        gate = dot(ffn_in_ref[...], gate_full[:, cut])
        up = dot(ffn_in_ref[...], up_full[:, cut])
        square = gate * gate
        t = jnp.tanh(GELU_A * gate * (1.0 + GELU_B * square))
        cdf = 0.5 * (1.0 + t)
        act = gate * cdf
        slope = cdf + 0.5 * gate * (1.0 - t * t) * (GELU_A * (1.0 + 3.0 * GELU_B * square))
        mixed[:, cut] = (act * up).astype(BF16)
        gelu_out[:, cut] = act.astype(BF16)
        gate_slope[:, cut] = (up * slope).astype(BF16)
        writer.put(mixed.at[:, cut], mixed_out.at[:, cut])
        writer.put(gelu_out.at[:, cut], gelu_out_out.at[:, cut])
        writer.put(gate_slope.at[:, cut], gate_slope_out.at[:, cut])
    writer.wait()


def relative_blocks(at, fsdp):
    for c in range(2):
        core = c + at[0] - 2 * c * at[0]
        for f in range(fsdp):
            row = lax.rem(at[2] + f, fsdp)
            for x in range(2):
                mid = x + at[1] - 2 * x * at[1]
                yield c, f, x, core, row, mid


def column_blocks(at, fsdp, left_t, right, keep, send):
    tall, wide = left_t.shape[0] // fsdp, keep.shape[3]
    for c, f, x, core, row, mid in relative_blocks(at, fsdp):
        cut = pl.ds(multiple((core * 2 + mid) * wide, 128), wide)
        left = left_t[pl.ds(multiple(row * tall, 16), tall), :]
        target = keep if c == 0 else send
        target[f, x, :tall, :] = dot(left, right[:, cut]).astype(BF16)


def down_kernel(n_down, fsdp, *refs):
    at, mixed, residual, cotangent, gain_table = refs[:5]
    down_w = refs[5 : 5 + n_down]
    layer_out, d_down, grad_gain, keep, send = refs[5 + n_down : 10 + n_down]
    down_full, mixed_t, sems = refs[10 + n_down :]
    copies = place_copies(down_w[:1], down_w[1:], down_full, sems, at, 0, 2)
    for copy in copies:
        copy.start()
    mixed_t[...] = mixed[...].T
    for copy in copies:
        copy.wait()
    down = dot(mixed[...], down_full[...])
    r = inverse_rms(down)
    gain = gain_table[5:6, :]
    layer_out[...] = (residual[...] + down * r * gain).astype(BF16)
    du, dg = norm_back(down, gain, cotangent[...].astype(F32))
    grad_gain[...] = dg
    d_down[...] = du.astype(BF16)
    block = keep.shape[2]
    for c, f, x, core, row, mid in relative_blocks(at, fsdp):
        start = multiple(((row * 2 + core) * 2 + mid) * block, 16)
        target = keep if c == 0 else send
        target[f, x] = dot(mixed_t[pl.ds(start, block), :], d_down[...]).astype(BF16)


def gate_back_kernel(n_down, fsdp, *refs):
    at, d_down, gelu_out, gate_slope, ffn_in = refs[:5]
    down_w = refs[5 : 5 + n_down]
    d_gate, d_up, keep, send, up_keep, up_send = refs[5 + n_down : 11 + n_down]
    down_full, ffn_t, sems = refs[11 + n_down :]
    copies = place_copies(down_w[:1], down_w[1:], down_full, sems, at, 0, 2)
    for copy in copies:
        copy.start()
    ffn_t[...] = ffn_in[...].T
    for copy in copies:
        copy.wait()
    width = 256

    def step(i, _):
        cut = pl.ds(multiple(i * width, width), width)
        d_mixed = dot_nt(d_down[...], down_full[cut, :])
        d_gate[:, cut] = (d_mixed * gate_slope[:, cut].astype(F32)).astype(BF16)
        d_up[:, cut] = (d_mixed * gelu_out[:, cut].astype(F32)).astype(BF16)
        return 0

    lax.fori_loop(0, d_gate.shape[1] // width, step, 0)
    column_blocks(at, fsdp, ffn_t, d_gate, keep, send)
    column_blocks(at, fsdp, ffn_t, d_up, up_keep, up_send)


def middle_kernel(n_out, n_gate, n_up, fsdp, heads, *refs):
    at, d_gate, d_up, residual, projected, cotangent, gain_table, attended = refs[:8]
    refs = refs[8:]
    out_w, gate_w, up_w, refs = (
        refs[:n_out],
        refs[n_out : n_out + n_gate],
        refs[n_out + n_gate : n_out + n_gate + n_up],
        refs[n_out + n_gate + n_up :],
    )
    d_residual_ref, g_ffn, g_attn, d_att, keep, send = refs[:6]
    out_full, gate_full, up_full, att_t, out_sems, gate_sems, up_sems = refs[6:]
    groups = (
        place_copies(gate_w[:1], gate_w[1:], gate_full, gate_sems, at, 1, 4),
        place_copies(up_w[:1], up_w[1:], up_full, up_sems, at, 1, 2),
        place_copies(out_w[:1], out_w[1:], out_full, out_sems, at, 0, 2),
    )
    for group in groups:
        for copy in group:
            copy.start()
    att_t[...] = attended[...].T
    for copy in groups[0]:
        copy.wait()
    d_ffn_in = dot_nt(d_gate[...], gate_full[...])
    for copy in groups[1]:
        copy.wait()
    d_ffn_in = d_ffn_in + dot_nt(d_up[...], up_full[...])
    du, dg = norm_back(residual[...], gain_table[4:5, :], d_ffn_in)
    g_ffn[...] = dg
    d_residual = cotangent[...].astype(F32) + du
    d_residual_ref[...] = d_residual
    du, dg = norm_back(projected[...], gain_table[3:4, :], d_residual)
    g_attn[...] = dg
    d_proj = du.astype(BF16)
    rows, dim = d_proj.shape[0], d_att.shape[1]
    for copy in groups[2]:
        copy.wait()
    for h in range(heads):
        part = dot_nt(d_proj, out_full[h * dim : (h + 1) * dim, :]).astype(BF16)
        for b in range(rows // QBLOCK):
            start = (b * heads + h) * QBLOCK
            d_att[start : start + QBLOCK, :] = part[b * QBLOCK : (b + 1) * QBLOCK, :]
    block = att_t.shape[0] // (4 * fsdp)
    wide = keep.shape[3]
    parts = wide // LANES
    deep = block // parts
    for c, f, x, core, row, mid in relative_blocks(at, fsdp):
        start = multiple(((row * 2 + core) * 2 + mid) * block, 16)
        part = dot(att_t[pl.ds(start, block), :], d_proj).astype(BF16)
        target = keep if c == 0 else send
        target[f, x, :block, :] = part[:, :wide]
        for i in range(parts):
            target[f, x, block:, i * LANES : (i + 1) * LANES] = part[i * deep : (i + 1) * deep, wide:]


def attend_back_kernel(halo, heads, d_att, q_st, keys, values, probs, d_q, d_k, d_v, d_scores):
    rows = d_q.shape[0]
    dim = keys.shape[1]
    blocks = rows // QBLOCK
    span = WINDOW + QBLOCK
    scale = dim ** (-0.5)
    d_k[...] = jnp.zeros(d_k.shape, F32)
    d_v[...] = jnp.zeros(d_v.shape, F32)
    for b in range(blocks):
        first_key = halo - WINDOW + b * QBLOCK
        here = slice(first_key, first_key + span)
        for h in range(heads):
            start = (b * heads + h) * QBLOCK
            stack = slice(start, start + QBLOCK)
            d_probs = dot_nt(d_att[stack, :], values[here, :])
            p = probs[stack, :].astype(F32)
            row_terms = jnp.sum(p * d_probs, axis=-1, keepdims=True)
            ds = (p * (d_probs - row_terms) * scale).astype(BF16)
            d_scores[h * QBLOCK : (h + 1) * QBLOCK, :] = ds
            d_q[b * QBLOCK : (b + 1) * QBLOCK, h * dim : (h + 1) * dim] = dot(ds, keys[here, :])
        stack = slice(b * heads * QBLOCK, (b + 1) * heads * QBLOCK)
        d_k[here, :] += dot_tn(d_scores[...], q_st[stack, :])
        d_v[here, :] += dot_tn(probs[stack, :], d_att[stack, :])


def last_kernel(n_qkv, n_tok, fsdp, heads, *refs):
    (
        at, d_residual, d_q, d_k, d_v,
        q_raw, k_raw, cosine, sine, gain_table, normed, g_ffn, g_attn, g_out,
    ) = refs[:14]
    toks = refs[14 : 14 + n_tok]
    refs = refs[14 + n_tok :]
    qkv_w, refs = refs[:n_qkv], refs[n_qkv:]
    grad_tokens, d_halo, keep, send = refs[:4]
    w_full, normed_t, d_qkv, gain_rows, qkv_sems = refs[4:]
    copies = place_copies(qkv_w[:3], qkv_w[3:], w_full, qkv_sems, at, 1, 4)
    for copy in copies:
        copy.start()
    normed_t[...] = normed[...].T
    rows = toks[0].shape[0]
    halo = (n_tok - 1) * rows
    dim = k_raw.shape[1]
    gain_in, gain_q, gain_k = gain_table[0:1, :], gain_table[1:2, :dim], gain_table[2:3, :dim]
    half = dim // 2
    tall, wide = normed_t.shape[0] // fsdp, keep.shape[3]
    def turned_back(u, g, dz, cos, sin):
        first, second = dz[:, :half], dz[:, half:]
        dz = jnp.concatenate([first * cos + second * sin, second * cos - first * sin], axis=1)
        return norm_back(u, g, dz)

    total_q = jnp.zeros((1, dim), F32)
    if halo:
        d_qkv[:halo, : heads * dim] = jnp.zeros((halo, heads * dim), BF16)
    for h in range(heads):
        cut = slice(h * dim, (h + 1) * dim)
        du, dg = turned_back(q_raw[:, cut], gain_q, d_q[:, cut], cosine[halo:, :], sine[halo:, :])
        total_q += dg
        d_qkv[halo:, cut] = du.astype(BF16)
    total_k = jnp.zeros((1, dim), F32)
    for i in range(n_tok):
        here = slice(i * rows, (i + 1) * rows)
        du, dg = turned_back(k_raw[here, :], gain_k, d_k[here, :], cosine[here, :], sine[here, :])
        total_k += dg
        d_qkv[here, heads * dim : (heads + 1) * dim] = du.astype(BF16)
        d_qkv[here, (heads + 1) * dim :] = d_v[here, :].astype(BF16)
    column_blocks(at, fsdp, normed_t, d_qkv, keep, send)
    for copy in copies:
        copy.wait()
    total_in = jnp.zeros(gain_in.shape, F32)
    for i in range(n_tok):
        here = slice(i * rows, (i + 1) * rows)
        if i < n_tok - 1:
            d_normed = dot_nt(d_qkv[here, heads * dim :], w_full[:, heads * dim :])
        else:
            d_normed = dot_nt(d_qkv[here, :], w_full[...])
        du, dg = norm_back(toks[i][...].astype(F32), gain_in, d_normed)
        total_in += dg
        if i < n_tok - 1:
            d_halo[here, :] = du.astype(BF16)
        else:
            grad_tokens[...] = d_residual[...] + du
    gain_rows[...] = jnp.zeros(gain_rows.shape, F32)
    at_row = 0
    for total in (total_in, total_q, total_k, g_attn[...], g_ffn[...], g_out[...]):
        for i in range(total.shape[1] // LANES):
            gain_rows[at_row : at_row + 1, :LANES] = total[:, i * LANES : (i + 1) * LANES]
            at_row += 1
    packed = gain_rows[...].astype(BF16)
    for target in (keep, send):
        for f in range(fsdp):
            for x in range(2):
                target[f, x, tall:, :] = packed


def add(*terms):
    out = terms[0].astype(F32)
    for term in terms[1:]:
        out = out + term.astype(F32)
    return out


class Chunk:
    def __init__(self, here, keep, send):
        self.here, self.keep = here, keep
        self.other = here.core_swap(send)

    def over_fsdp(self, *earlier):
        here = self.here
        parts = [add(self.keep[by], self.other[by]).astype(BF16) for by in range(1, here.fsdp)]
        self.arrived = [here.fsdp_shift(after(part, *earlier), by + 1) for by, part in enumerate(parts)]

    def over_mid(self, *earlier):
        self.arrived = [after(a, *earlier) for a in self.arrived]
        terms = [self.keep[0, 1], self.other[0, 1]] + [a[1] for a in self.arrived]
        self.across = self.here.mid_swap(add(*terms).astype(BF16))
        self.mine = [self.keep[0, 0], self.other[0, 0]] + [a[0] for a in self.arrived]
        return self.arrived[0] if self.arrived else self.other

    def join(self, below, *earlier):
        for chunk in (self, below):
            chunk.arrived = [after(a, *earlier) for a in chunk.arrived]
        pairs = [
            [[c.keep[0, x], c.other[0, x]] + [a[x] for a in c.arrived] for c in (self, below)] for x in range(2)
        ]
        self.across_sent = jnp.concatenate([add(*terms).astype(BF16) for terms in pairs[1]])
        self.across = self.here.mid_swap(self.across_sent)
        self.mine = [jnp.concatenate([add(*terms).astype(BF16) for terms in pairs[0]])]

    def outer_sums(self, *earlier):
        here = self.here
        self.across = after(self.across, *earlier)
        mine = add(*self.mine, self.across).astype(BF16)
        n, w = mine.shape
        mine = mine.reshape(here.outer, n // here.outer, w)
        self.shares = [pick(mine, here.outer_ahead[0])]
        for by in range(1, here.outer):
            self.shares.append(here.outer_shift(pick(mine, here.outer_ahead[by]), by))
        return self.across

    def outer_gather(self, *earlier):
        here = self.here
        self.shares = list(after(tuple(self.shares), *earlier))
        own = add(*self.shares).astype(BF16)
        self.gathered = [own] + [here.outer_shift(own, by) for by in range(1, here.outer)]
        return self.shares[-1]

    def mid_gather(self, *earlier):
        here = self.here
        self.gathered = list(after(tuple(self.gathered), *earlier))
        block = ordered(self.gathered, here.outer_behind)
        block = block.reshape(-1, block.shape[-1])
        across = here.mid_swap(block)
        self.blocks = [[block, across], [here.core_swap(block), here.core_swap(across)]]
        return self.gathered[-1]


def by_place(here, blocks):
    own = [jnp.where(here.mid_at == 0, a, b) for a, b in blocks]
    other = [jnp.where(here.mid_at == 0, b, a) for a, b in blocks]
    pairs = list(zip(own, other))
    first = [jnp.where(here.core_at == 0, a, b) for a, b in zip(pairs[0], pairs[1])]
    second = [jnp.where(here.core_at == 0, b, a) for a, b in zip(pairs[0], pairs[1])]
    return first + second


def last_columns(blocks, start, count):
    wide = blocks[0].shape[1]
    pieces = []
    for i, block in enumerate(blocks):
        low, high = max(start - i * wide, 0), min(start + count - i * wide, wide)
        if low < high:
            pieces.append(block[:, low:high])
    return jnp.concatenate(pieces, axis=1).astype(F32)


def on_device(
    tokens, positions, cotangent, in_gain, w_query, w_key, w_value, query_gain, key_gain, w_out, attn_gain,
    ffn_gain_in, w_gate, w_up, w_down, ffn_gain_out,
):
    here = Places()
    fsdp = here.fsdp
    rows, width = tokens.shape
    dim = w_key.shape[1]
    query_cols = w_query.shape[1]
    heads = query_cols // dim
    hidden = w_gate.shape[1]
    hops = (WINDOW + rows - 1) // rows
    n_tok = hops + 1
    halo = hops * rows
    every = halo + rows
    at = here.vector

    gains = (in_gain, query_gain, key_gain, attn_gain, ffn_gain_in, ffn_gain_out)
    cuts = [0]
    for gain in gains:
        cuts.append(cuts[-1] + gain.shape[0])
    gain_row = jnp.concatenate(gains)
    gain_rows = ordered([gain_row] + [here.fsdp_shift(gain_row, by) for by in range(1, fsdp)], here.fsdp_behind)
    gain_rows = gain_rows.astype(F32)
    gain_table = jnp.concatenate(
        [
            jnp.pad(gain_rows[:, cuts[i] : cuts[i + 1]].reshape(1, -1), ((0, 0), (0, width - fsdp * gains[i].shape[0])))
            for i in range(6)
        ]
        + [jnp.zeros((2, width), F32)],
        axis=0,
    )
    qkv_w = [w_query, w_key, w_value]
    qkv_part = own_part(here, qkv_w, 1, 4)
    tokens_out = after(tokens, qkv_part)
    toks = [linear_shift(tokens_out, by) for by in range(hops, 0, -1)] + [tokens]
    qkv_w += on_chips(here, over_links(here, qkv_part), 4)
    out_arrived = over_links(here, after(own_part(here, [w_out], 0, 2), *toks[:-1]))
    gate_arrived = over_links(here, after(own_part(here, [w_gate], 1, 4), qkv_w[3]))
    up_arrived = over_links(here, after(own_part(here, [w_up], 1, 2), *gate_arrived))
    down_arrived = over_links(here, after(own_part(here, [w_down], 0, 2), *gate_arrived))

    all_positions = jnp.concatenate([positions[0] - halo + jnp.arange(halo, dtype=jnp.int32), positions])
    frequency = ROPE_BASE ** (-(jnp.arange(dim // 2, dtype=F32) * 2.0 / dim))
    angles = all_positions.astype(F32)[:, None] * frequency[None, :]
    cosine, sine = jnp.cos(angles), jnp.sin(angles)

    span = WINDOW + QBLOCK
    weight_bytes = 2 * fsdp * w_gate.size
    normed, q_raw, k_raw, q_st, keys, values, probs, attended = pl.pallas_call(
        functools.partial(attend_kernel, n_tok, len(qkv_w), heads),
        out_shape=(
            shape((every, width), BF16),
            shape((rows, query_cols), F32),
            shape((every, dim), F32),
            shape((heads * rows, dim), BF16),
            shape((every, dim), BF16),
            shape((every, dim), BF16),
            shape((heads * rows, span), BF16),
            shape((rows, query_cols), BF16),
        ),
        in_specs=[SMEM] + [VMEM] * (n_tok + 4) + [ANY] * len(qkv_w),
        out_specs=(VMEM,) * 8,
        scratch_shapes=[
            pltpu.VMEM((width, query_cols + 2 * dim), BF16),
            pltpu.SemaphoreType.DMA((len(qkv_w),)),
        ],
        compiler_params=params(),
        cost_estimate=cost(4e9, 1e7),
        name="attend",
    )(at, *toks, after(positions[:, None], *gate_arrived), cosine, sine, gain_table, *qkv_w)

    out_w = [w_out] + on_chips(here, [after(a, attended) for a in out_arrived], 2)
    gate_w = [w_gate] + on_chips(here, gate_arrived, 4)
    up_w = [w_up] + on_chips(here, [after(a, attended) for a in up_arrived], 2)
    projected, residual, ffn_in, mixed, gelu_out, gate_slope = pl.pallas_call(
        functools.partial(gate_kernel, len(out_w), len(gate_w), len(up_w)),
        out_shape=(
            shape((rows, width), F32),
            shape((rows, width), F32),
            shape((rows, width), BF16),
            shape((rows, hidden), BF16),
            shape((rows, hidden), BF16),
            shape((rows, hidden), BF16),
        ),
        in_specs=[SMEM] + [VMEM] * 3 + [ANY] * (len(out_w) + len(gate_w) + len(up_w)),
        out_specs=(ANY, ANY, VMEM, ANY, ANY, ANY),
        scratch_shapes=[
            pltpu.VMEM((rows, width), F32),
            pltpu.VMEM((rows, width), F32),
            pltpu.VMEM((rows, hidden), BF16),
            pltpu.VMEM((rows, hidden), BF16),
            pltpu.VMEM((rows, hidden), BF16),
            pltpu.VMEM((query_cols, width), BF16),
            pltpu.VMEM((width, hidden), BF16),
            pltpu.VMEM((width, hidden), BF16),
            pltpu.SemaphoreType.DMA((len(out_w),)),
            pltpu.SemaphoreType.DMA((len(gate_w),)),
            pltpu.SemaphoreType.DMA((len(up_w),)),
            pltpu.SemaphoreType.DMA((14,)),
        ],
        compiler_params=params(),
        cost_estimate=cost(1e6, 1e3),
        name="gate",
    )(at, attended, tokens, gain_table, *out_w, *gate_w, *up_w)

    down_w = [w_down] + on_chips(here, [after(a, mixed) for a in down_arrived], 2)
    down_block = w_down.shape[0] // 4
    down_shape = shape((fsdp, 2, down_block, width), BF16)
    layer_out, d_down, g_ffn_out, down_keep, down_send = pl.pallas_call(
        functools.partial(down_kernel, len(down_w), fsdp),
        out_shape=(
            shape((rows, width), BF16),
            shape((rows, width), BF16),
            shape((1, width), F32),
            down_shape,
            down_shape,
        ),
        in_specs=[SMEM] + [VMEM] * 4 + [ANY] * len(down_w),
        out_specs=(VMEM,) * 5,
        scratch_shapes=[
            pltpu.VMEM((hidden, width), BF16),
            pltpu.VMEM((hidden, rows), BF16),
            pltpu.SemaphoreType.DMA((len(down_w),)),
        ],
        compiler_params=params(),
        cost_estimate=cost(4e9, 2 * weight_bytes),
        name="down",
    )(at, mixed, residual, cotangent, gain_table, *down_w)

    down_sum = Chunk(here, down_keep, down_send)
    gate_shape = shape((fsdp, 2, w_gate.shape[0], hidden // 4), BF16)
    d_gate, d_up, gate_keep, gate_send, up_keep, up_send = pl.pallas_call(
        functools.partial(gate_back_kernel, len(down_w), fsdp),
        out_shape=(
            shape((rows, hidden), BF16),
            shape((rows, hidden), BF16),
            gate_shape,
            gate_shape,
            gate_shape,
            gate_shape,
        ),
        in_specs=[SMEM] + [VMEM] * 4 + [ANY] * len(down_w),
        out_specs=(VMEM,) * 6,
        scratch_shapes=[
            pltpu.VMEM((hidden, width), BF16),
            pltpu.VMEM((width, rows), BF16),
            pltpu.SemaphoreType.DMA((len(down_w),)),
        ],
        compiler_params=params(),
        cost_estimate=cost(6e9, 3 * weight_bytes),
        name="gate_back",
    )(at, d_down, gelu_out, gate_slope, ffn_in, *down_w)
    gate_sum = Chunk(here, gate_keep, gate_send)
    up_sum = Chunk(here, up_keep, up_send)
    down_sum.over_fsdp(d_gate)
    d_gate = after(d_gate, down_sum.other)
    qkv_cols = query_cols + 2 * dim
    last_wide = qkv_cols // 4
    shard_rows = w_query.shape[0]
    last_shape = shape((fsdp, 2, shard_rows + GAIN_ROWS, last_wide), BF16)
    out_block = w_out.shape[0] // 4
    out_shape = shape((fsdp, 2, out_block * width // (hidden // 4), hidden // 4), BF16)
    d_residual, g_ffn, g_attn, d_att, out_keep, out_send = pl.pallas_call(
        functools.partial(middle_kernel, len(out_w), len(gate_w), len(up_w), fsdp, heads),
        out_shape=(
            shape((rows, width), F32),
            shape((1, width), F32),
            shape((1, width), F32),
            shape((heads * rows, dim), BF16),
            out_shape,
            out_shape,
        ),
        in_specs=[SMEM] + [VMEM] * 7 + [ANY] * (len(out_w) + len(gate_w) + len(up_w)),
        out_specs=(VMEM,) * 6,
        scratch_shapes=[
            pltpu.VMEM((query_cols, width), BF16),
            pltpu.VMEM((width, hidden), BF16),
            pltpu.VMEM((width, hidden), BF16),
            pltpu.VMEM((query_cols, rows), BF16),
            pltpu.SemaphoreType.DMA((len(out_w),)),
            pltpu.SemaphoreType.DMA((len(gate_w),)),
            pltpu.SemaphoreType.DMA((len(up_w),)),
        ],
        compiler_params=params(),
        cost_estimate=cost(6e9, 4 * weight_bytes),
        name="middle",
    )(at, d_gate, d_up, residual, projected, cotangent, gain_table, attended, *out_w, *gate_w, *up_w)

    out_sum = Chunk(here, out_keep, out_send)
    gate_sum.over_fsdp(g_ffn)
    up_sum.over_fsdp(g_ffn)
    down_sum.over_mid(g_ffn)
    d_q, d_k, d_v = pl.pallas_call(
        functools.partial(attend_back_kernel, halo, heads),
        out_shape=(shape((rows, query_cols), F32), shape((every, dim), F32), shape((every, dim), F32)),
        in_specs=[VMEM] * 5,
        out_specs=(VMEM,) * 3,
        scratch_shapes=[pltpu.VMEM((heads * QBLOCK, span), BF16)],
        compiler_params=params(),
        cost_estimate=cost(6e9, 3 * weight_bytes),
        name="attend_back",
    )(after(d_att, gate_sum.other, up_sum.other, *down_sum.arrived), q_st, keys, values, probs)
    out_sum.over_fsdp(d_k)
    down_sum.outer_sums(d_k)
    d_q = after(d_q, out_sum.other, down_sum.across)
    grad_tokens, d_halo, last_keep, last_send = pl.pallas_call(
        functools.partial(last_kernel, len(qkv_w), n_tok, fsdp, heads),
        out_shape=(
            shape((rows, width), F32),
            shape((halo, width), BF16),
            last_shape,
            last_shape,
        ),
        in_specs=[SMEM] + [VMEM] * (13 + n_tok) + [ANY] * len(qkv_w),
        out_specs=(VMEM,) * 4,
        scratch_shapes=[
            pltpu.VMEM((width, qkv_cols), BF16),
            pltpu.VMEM((width, every), BF16),
            pltpu.VMEM((every, qkv_cols), BF16),
            pltpu.VMEM((GAIN_ROWS, last_wide), F32),
            pltpu.SemaphoreType.DMA((len(qkv_w),)),
        ],
        compiler_params=params(),
        cost_estimate=cost(15e9, 4 * weight_bytes),
        name="last",
    )(
        at, d_residual, d_q, d_k, d_v,
        q_raw, k_raw, cosine, sine, gain_table, normed, g_ffn, g_attn, g_ffn_out, *toks, *qkv_w,
    )

    last_sum = Chunk(here, last_keep, last_send)
    down_sum.outer_sums(last_keep)
    gate_sum.over_mid(last_keep, *up_sum.arrived)
    (last_sum.other,), (gate_sum.across,), down_sum.shares, out_sum.arrived = together(
        (last_sum.other,), (gate_sum.across,), down_sum.shares, out_sum.arrived
    )
    last_sum.over_fsdp()
    up_sum.join(out_sum)
    gate_sum.outer_sums()
    down_sum.outer_gather()
    last_sum.arrived, (up_sum.across,), gate_sum.shares, down_sum.gathered = together(
        last_sum.arrived, (up_sum.across,), gate_sum.shares, down_sum.gathered
    )
    last_sum.over_mid()
    up_sum.outer_sums()
    gate_sum.outer_gather()
    down_sum.mid_gather()
    (last_sum.across,), up_sum.shares, gate_sum.gathered, down_last = together(
        (last_sum.across,), up_sum.shares, gate_sum.gathered, down_sum.blocks[0]
    )
    down_sum.blocks[0] = list(down_last)
    last_sum.outer_sums()
    up_sum.outer_gather()
    gate_sum.mid_gather()
    last_sum.shares, up_sum.gathered, gate_last = together(last_sum.shares, up_sum.gathered, gate_sum.blocks[0])
    gate_sum.blocks[0] = list(gate_last)
    last_sum.outer_gather()
    up_sum.mid_gather()
    last_sum.mid_gather(up_sum.blocks[0][1])
    d_halo = after(d_halo, up_sum.blocks[0][1])
    halos = [linear_shift(d_halo[halo - by * rows :][:rows], -by) for by in range(1, hops + 1)]
    down_blocks, gate_blocks = by_place(here, down_sum.blocks), by_place(here, gate_sum.blocks)
    both_blocks, last_blocks = by_place(here, up_sum.blocks), by_place(here, last_sum.blocks)
    total_gains = last_sum.blocks[0][0][shard_rows:, :LANES].astype(F32)

    for came in halos:
        grad_tokens = grad_tokens + came.astype(F32)

    total_down = jnp.concatenate(down_blocks, axis=0).astype(F32)
    total_gate = jnp.concatenate(gate_blocks, axis=1).astype(F32)
    total_up = jnp.concatenate([b[:shard_rows] for b in both_blocks], axis=1).astype(F32)
    last_blocks = [b[:shard_rows] for b in last_blocks]
    total_qkv = [last_columns(last_blocks, 0, query_cols)]
    total_qkv += [last_columns(last_blocks, query_cols + i * dim, dim) for i in range(2)]
    wide = hidden // 4
    parts = wide // LANES
    total_out = []
    for block in both_blocks:
        below = block[shard_rows + out_block :].reshape(out_block // parts, parts, LANES)
        below = below.transpose(1, 0, 2).reshape(out_block, LANES)
        total_out.append(jnp.concatenate([block[shard_rows : shard_rows + out_block], below], axis=1))
    total_out = jnp.concatenate(total_out, axis=0).astype(F32)
    g, at_row = [], 0
    for gain in gains:
        deep = fsdp * gain.shape[0] // total_gains.shape[1]
        total = total_gains[at_row : at_row + deep].reshape(fsdp, gain.shape[0])
        g.append(pick(total, here.fsdp_at))
        at_row += deep
    return (
        layer_out, grad_tokens, g[0],
        *total_qkv,
        g[1], g[2], total_out, g[3], g[4], total_gate, total_up, total_down, g[5],
    )


def solution(mesh):
    tok = P(("seq", "fsdp"), None)
    mat = P("fsdp", None)
    vec = P("fsdp")
    return jax.shard_map(
        on_device,
        mesh=mesh,
        in_specs=(tok, P(("seq", "fsdp")), tok, vec, mat, mat, mat, vec, vec, mat, vec, vec, mat, mat, mat, vec),
        out_specs=(tok, tok, vec, mat, mat, mat, vec, vec, mat, vec, vec, mat, mat, mat, vec),
        check_vma=False,
    )
```

```python
import functools
import math

import jax
import jax.numpy as jnp
from jax import lax
from jax.experimental import pallas as pl
from jax.experimental.pallas import tpu as pltpu
from jax.sharding import PartitionSpec as P

WINDOW = 512
EPSILON = 1e-06
ROPE_BASE = 10000.0
MASKED = -1e30
BF16 = jnp.bfloat16
F32 = jnp.float32
QBLOCK = 128
LANES = 128
GAIN_ROWS = 32
GELU_A = math.sqrt(2.0 / math.pi)
GELU_B = 0.044715

VMEM = pl.BlockSpec(memory_space=pltpu.VMEM)
SMEM = pl.BlockSpec(memory_space=pltpu.SMEM)
ANY = pl.BlockSpec(memory_space=pl.ANY)


def wrapped(value, size):
    return value & (size - 1) if size & (size - 1) == 0 else lax.rem(value, jnp.int32(size))


class Places:
    def __init__(self):
        self.seq = lax.axis_size("seq")
        self.fsdp = lax.axis_size("fsdp")
        self.outer = self.seq // 4
        index = lax.axis_index("seq").astype(jnp.int32)
        fsdp_at = lax.axis_index("fsdp").astype(jnp.int32)
        outer_at = lax.shift_right_logical(index, 2)
        core_at, mid_at = index & 1, lax.shift_right_logical(index, 1) & 1
        scalars = lax.optimization_barrier(
            (
                core_at,
                mid_at,
                fsdp_at,
                core_at * 2 + mid_at,
                tuple(wrapped(outer_at + by, self.outer) for by in range(self.outer)),
                tuple(wrapped(outer_at - by + self.outer, self.outer) for by in range(self.outer)),
                tuple(wrapped(fsdp_at + by, self.fsdp) for by in range(self.fsdp)),
                tuple(wrapped(fsdp_at - by + self.fsdp, self.fsdp) for by in range(self.fsdp)),
                jnp.stack([core_at, mid_at, fsdp_at]),
            )
        )
        self.core_at, self.mid_at, self.fsdp_at, self.quarter_at = scalars[:4]
        self.outer_ahead, self.outer_behind, self.fsdp_ahead, self.fsdp_behind, self.vector = scalars[4:]

    def core_swap(self, array):
        return lax.ppermute(array, "seq", [(i, i ^ 1) for i in range(self.seq)])

    def mid_swap(self, array):
        return lax.ppermute(array, "seq", [(i, i ^ 2) for i in range(self.seq)])

    def outer_shift(self, array, by):
        return lax.ppermute(array, "seq", [(i, (i + 4 * by) % self.seq) for i in range(self.seq)])

    def fsdp_shift(self, array, by):
        return lax.ppermute(array, "fsdp", [(i, (i + by) % self.fsdp) for i in range(self.fsdp)])


def linear_shift(array, by):
    count = lax.axis_size("seq") * lax.axis_size("fsdp")
    return lax.ppermute(array, ("seq", "fsdp"), [(i, i + by) for i in range(count) if 0 <= i + by < count])


def pick(array, at):
    return lax.dynamic_index_in_dim(array, at, 0, keepdims=False, allow_negative_indices=False)


def ordered(pieces, behind):
    if len(pieces) == 2:
        own, other = pieces
        return jnp.where(behind[0] == 0, jnp.stack([own, other]), jnp.stack([other, own]))
    stacked = jnp.stack(pieces)
    return jnp.stack([pick(stacked, at) for at in behind])


def own_part(here, shards, axis, ways):
    size = sum(shard.shape[axis] for shard in shards) // ways
    place = here.quarter_at if ways == 4 else here.core_at
    if len(shards) == 1:
        return lax.dynamic_slice_in_dim(shards[0], place * size, size, axis, allow_negative_indices=False)
    parts = []
    for i in range(ways):
        pieces, start = [], 0
        for shard in shards:
            low, high = max(i * size - start, 0), min((i + 1) * size - start, shard.shape[axis])
            if low < high:
                pieces.append(lax.slice_in_dim(shard, low, high, axis=axis))
            start += shard.shape[axis]
        parts.append(jnp.concatenate(pieces, axis))
    return functools.reduce(lambda rest, i: jnp.where(place == i, parts[i], rest), range(1, ways), parts[0])


def after(value, *earlier):
    return lax.optimization_barrier((value, *earlier))[0]


def together(*groups):
    return lax.optimization_barrier(tuple(tuple(group) for group in groups))


def over_links(here, part):
    return [here.fsdp_shift(part, by) for by in range(1, here.fsdp)]


def on_chips(here, arrived, ways):
    pieces = []
    for mine in arrived:
        if ways == 4:
            across = here.mid_swap(mine)
            pieces += [mine, across, here.core_swap(mine), here.core_swap(across)]
        else:
            pieces += [mine, here.core_swap(mine)]
    return pieces


def multiple(value, of):
    return pl.multiple_of(value, of)


def place_copies(owned, pieces, whole, sems, at, axis, ways):
    core, mid, fsdp = at[0], at[1], at[2]
    count = 1 + len(pieces) // ways
    rows = owned[0].shape[0]
    copies = []
    column = 0
    own_row = multiple(fsdp * rows, 16)
    for shard in owned:
        wide = shard.shape[1]
        copies.append((shard, whole.at[pl.ds(own_row, rows), pl.ds(column, wide)]))
        column += wide
    for k, piece in enumerate(pieces):
        by = 1 + k // ways
        row = multiple(lax.rem(fsdp + (count - by), count) * rows, 16)
        k = k % ways
        if ways == 4:
            place = (core if k < 2 else 1 - core) * 2 + (mid if k % 2 == 0 else 1 - mid)
        else:
            place = core if k == 0 else 1 - core
        if axis == 0:
            target = whole.at[pl.ds(multiple(row + place * (rows // ways), 16), rows // ways), :]
        else:
            target = whole.at[pl.ds(row, rows), pl.ds(multiple(place * (column // ways), 128), column // ways)]
        copies.append((piece, target))
    return [pltpu.make_async_copy(a, b, sems.at[k]) for k, (a, b) in enumerate(copies)]


def dot(a, b):
    return lax.dot_general(a, b, (((1,), (0,)), ((), ())), preferred_element_type=F32)


def dot_nt(a, b):
    return lax.dot_general(a, b, (((1,), (1,)), ((), ())), preferred_element_type=F32)


def dot_tn(a, b):
    return lax.dot_general(a, b, (((0,), (0,)), ((), ())), preferred_element_type=F32)


def inverse_rms(u):
    return lax.rsqrt(jnp.mean(u * u, axis=-1, keepdims=True) + EPSILON)


def norm_back(u, g, dz):
    r = inverse_rms(u)
    ur = u * r
    gdz = g * dz
    du = r * (gdz - ur * jnp.mean(gdz * ur, axis=-1, keepdims=True))
    return du, jnp.sum(dz * ur, axis=0, keepdims=True)


class Writer:
    def __init__(self, sems):
        self.sems, self.copies = sems, []

    def put(self, source, target):
        copy = pltpu.make_async_copy(source, target, self.sems.at[len(self.copies)])
        copy.start()
        self.copies.append(copy)

    def wait(self):
        for copy in self.copies:
            copy.wait()


def params(megabytes=56):
    return pltpu.CompilerParams(vmem_limit_bytes=megabytes * 1024 * 1024)


def cost(flops, bytes_accessed):
    return pl.CostEstimate(flops=int(20 * flops), bytes_accessed=int(20 * bytes_accessed), transcendentals=0)


def shape(dims, kind):
    return jax.ShapeDtypeStruct(tuple(dims), kind)


def attend_kernel(n_tok, n_qkv, heads, *refs):
    at = refs[0]
    toks = refs[1 : 1 + n_tok]
    pos, cosine, sine, gain_table = refs[1 + n_tok : 5 + n_tok]
    qkv = refs[5 + n_tok : 5 + n_tok + n_qkv]
    normed, q_raw, k_raw, q_st, keys, values, probs, attended, w_full, sems = refs[5 + n_tok + n_qkv :]
    copies = place_copies(qkv[:3], qkv[3:], w_full, sems, at, 1, 4)
    for copy in copies:
        copy.start()
    rows = toks[0].shape[0]
    dim = keys.shape[1]
    half = dim // 2
    halo = (n_tok - 1) * rows
    gain = gain_table[0:1, :]
    gain_q, gain_k = gain_table[1:2, :dim], gain_table[2:3, :dim]
    for i, tok in enumerate(toks):
        u = tok[...].astype(F32)
        normed[i * rows : (i + 1) * rows, :] = (u * inverse_rms(u) * gain).astype(BF16)
    for copy in copies:
        copy.wait()

    def turned(u, g, cos, sin):
        u = u * inverse_rms(u) * g
        first, second = u[:, :half], u[:, half:]
        return (first * cos - second * sin).astype(BF16), (second * cos + first * sin).astype(BF16)

    for i in range(n_tok):
        here = slice(i * rows, (i + 1) * rows)
        kv = dot(normed[here, :], w_full[:, heads * dim :])
        k_raw[here, :] = kv[:, :dim]
        values[here, :] = kv[:, dim:].astype(BF16)
        first, second = turned(kv[:, :dim], gain_k, cosine[here, :], sine[here, :])
        keys[here, :half] = first
        keys[here, half:] = second
    blocks = rows // QBLOCK
    for h in range(heads):
        u = dot(normed[halo:, :], w_full[:, h * dim : (h + 1) * dim])
        q_raw[:, h * dim : (h + 1) * dim] = u
        first, second = turned(u, gain_q, cosine[halo:, :], sine[halo:, :])
        for b in range(blocks):
            start = (b * heads + h) * QBLOCK
            q_st[start : start + QBLOCK, :half] = first[b * QBLOCK : (b + 1) * QBLOCK, :]
            q_st[start : start + QBLOCK, half:] = second[b * QBLOCK : (b + 1) * QBLOCK, :]
    span = WINDOW + QBLOCK
    distance = (
        lax.broadcasted_iota(jnp.int32, (QBLOCK, span), 0)
        + WINDOW
        - lax.broadcasted_iota(jnp.int32, (QBLOCK, span), 1)
    )
    scale = dim ** (-0.5)
    for b in range(blocks):
        first_key = halo - WINDOW + b * QBLOCK
        limit = jnp.minimum(pos[b * QBLOCK : (b + 1) * QBLOCK, :], WINDOW - 1)
        allowed = (distance >= 0) & (distance <= limit)
        for h in range(heads):
            start = (b * heads + h) * QBLOCK
            scores = dot_nt(q_st[start : start + QBLOCK, :], keys[first_key : first_key + span, :]) * scale
            scores = jnp.where(allowed, scores, MASKED)
            weights = jnp.exp(scores - jnp.max(scores, axis=-1, keepdims=True))
            weights = (weights * (1.0 / jnp.sum(weights, axis=-1, keepdims=True))).astype(BF16)
            probs[start : start + QBLOCK, :] = weights
            attended[b * QBLOCK : (b + 1) * QBLOCK, h * dim : (h + 1) * dim] = dot(
                weights, values[first_key : first_key + span, :]
            ).astype(BF16)


def gate_kernel(n_out, n_gate, n_up, *refs):
    at, attended, tokens, gain_table = refs[:4]
    refs = refs[4:]
    out_w, gate_w, up_w, refs = (
        refs[:n_out],
        refs[n_out : n_out + n_gate],
        refs[n_out + n_gate : n_out + n_gate + n_up],
        refs[n_out + n_gate + n_up :],
    )
    projected_out, residual_out, ffn_in_ref, mixed_out, gelu_out_out, gate_slope_out = refs[:6]
    (
        projected_ref, residual_ref, mixed, gelu_out, gate_slope,
        out_full, gate_full, up_full, out_sems, gate_sems, up_sems, write_sems,
    ) = refs[6:]
    writer = Writer(write_sems)
    groups = (
        place_copies(out_w[:1], out_w[1:], out_full, out_sems, at, 0, 2),
        place_copies(gate_w[:1], gate_w[1:], gate_full, gate_sems, at, 1, 4),
        place_copies(up_w[:1], up_w[1:], up_full, up_sems, at, 1, 2),
    )
    for group in groups:
        for copy in group:
            copy.start()
    for copy in groups[0]:
        copy.wait()
    projected = dot(attended[...], out_full[...])
    projected_ref[...] = projected
    residual = tokens[...].astype(F32) + projected * inverse_rms(projected) * gain_table[3:4, :]
    residual_ref[...] = residual
    ffn_in_ref[...] = (residual * inverse_rms(residual) * gain_table[4:5, :]).astype(BF16)
    writer.put(projected_ref, projected_out)
    writer.put(residual_ref, residual_out)
    width = gate_full.shape[1] // 4
    for k in range(4):
        waits = groups[1][1 + k :: 4] + (groups[2][1 + k // 2 :: 2] if k % 2 == 0 else [])
        if k == 0:
            waits = groups[1][:1] + groups[2][:1] + waits
        for copy in waits:
            copy.wait()
        core = at[0] if k < 2 else 1 - at[0]
        mid = at[1] if k % 2 == 0 else 1 - at[1]
        cut = pl.ds(multiple((core * 2 + mid) * width, width), width)
        gate = dot(ffn_in_ref[...], gate_full[:, cut])
        up = dot(ffn_in_ref[...], up_full[:, cut])
        square = gate * gate
        t = jnp.tanh(GELU_A * gate * (1.0 + GELU_B * square))
        cdf = 0.5 * (1.0 + t)
        act = gate * cdf
        slope = cdf + 0.5 * gate * (1.0 - t * t) * (GELU_A * (1.0 + 3.0 * GELU_B * square))
        mixed[:, cut] = (act * up).astype(BF16)
        gelu_out[:, cut] = act.astype(BF16)
        gate_slope[:, cut] = (up * slope).astype(BF16)
        writer.put(mixed.at[:, cut], mixed_out.at[:, cut])
        writer.put(gelu_out.at[:, cut], gelu_out_out.at[:, cut])
        writer.put(gate_slope.at[:, cut], gate_slope_out.at[:, cut])
    writer.wait()


def relative_blocks(at, fsdp):
    for c in range(2):
        core = c + at[0] - 2 * c * at[0]
        for f in range(fsdp):
            row = lax.rem(at[2] + f, fsdp)
            for x in range(2):
                mid = x + at[1] - 2 * x * at[1]
                yield c, f, x, core, row, mid


def column_blocks(at, fsdp, left_t, right, keep, send):
    tall, wide = left_t.shape[0] // fsdp, keep.shape[3]
    for c, f, x, core, row, mid in relative_blocks(at, fsdp):
        cut = pl.ds(multiple((core * 2 + mid) * wide, 128), wide)
        left = left_t[pl.ds(multiple(row * tall, 16), tall), :]
        target = keep if c == 0 else send
        target[f, x, :tall, :] = dot(left, right[:, cut]).astype(BF16)


def down_kernel(n_down, fsdp, *refs):
    at, mixed, residual, cotangent, gain_table = refs[:5]
    down_w = refs[5 : 5 + n_down]
    layer_out, d_down, grad_gain, keep, send = refs[5 + n_down : 10 + n_down]
    down_full, mixed_t, sems = refs[10 + n_down :]
    copies = place_copies(down_w[:1], down_w[1:], down_full, sems, at, 0, 2)
    for copy in copies:
        copy.start()
    mixed_t[...] = mixed[...].T
    for copy in copies:
        copy.wait()
    down = dot(mixed[...], down_full[...])
    r = inverse_rms(down)
    gain = gain_table[5:6, :]
    layer_out[...] = (residual[...] + down * r * gain).astype(BF16)
    du, dg = norm_back(down, gain, cotangent[...].astype(F32))
    grad_gain[...] = dg
    d_down[...] = du.astype(BF16)
    block = keep.shape[2]
    for c, f, x, core, row, mid in relative_blocks(at, fsdp):
        start = multiple(((row * 2 + core) * 2 + mid) * block, 16)
        target = keep if c == 0 else send
        target[f, x] = dot(mixed_t[pl.ds(start, block), :], d_down[...]).astype(BF16)


def gate_back_kernel(n_down, fsdp, *refs):
    at, d_down, gelu_out, gate_slope, ffn_in = refs[:5]
    down_w = refs[5 : 5 + n_down]
    d_gate, d_up, keep, send, up_keep, up_send = refs[5 + n_down : 11 + n_down]
    down_full, ffn_t, sems = refs[11 + n_down :]
    copies = place_copies(down_w[:1], down_w[1:], down_full, sems, at, 0, 2)
    for copy in copies:
        copy.start()
    ffn_t[...] = ffn_in[...].T
    for copy in copies:
        copy.wait()
    width = 256

    def step(i, _):
        cut = pl.ds(multiple(i * width, width), width)
        d_mixed = dot_nt(d_down[...], down_full[cut, :])
        d_gate[:, cut] = (d_mixed * gate_slope[:, cut].astype(F32)).astype(BF16)
        d_up[:, cut] = (d_mixed * gelu_out[:, cut].astype(F32)).astype(BF16)
        return 0

    lax.fori_loop(0, d_gate.shape[1] // width, step, 0)
    column_blocks(at, fsdp, ffn_t, d_gate, keep, send)
    column_blocks(at, fsdp, ffn_t, d_up, up_keep, up_send)


def middle_kernel(n_out, n_gate, n_up, fsdp, heads, *refs):
    at, d_gate, d_up, residual, projected, cotangent, gain_table, attended = refs[:8]
    refs = refs[8:]
    out_w, gate_w, up_w, refs = (
        refs[:n_out],
        refs[n_out : n_out + n_gate],
        refs[n_out + n_gate : n_out + n_gate + n_up],
        refs[n_out + n_gate + n_up :],
    )
    d_residual_ref, g_ffn, g_attn, d_att, keep, send = refs[:6]
    out_full, gate_full, up_full, att_t, out_sems, gate_sems, up_sems = refs[6:]
    groups = (
        place_copies(gate_w[:1], gate_w[1:], gate_full, gate_sems, at, 1, 4),
        place_copies(up_w[:1], up_w[1:], up_full, up_sems, at, 1, 2),
        place_copies(out_w[:1], out_w[1:], out_full, out_sems, at, 0, 2),
    )
    for group in groups:
        for copy in group:
            copy.start()
    att_t[...] = attended[...].T
    for copy in groups[0]:
        copy.wait()
    d_ffn_in = dot_nt(d_gate[...], gate_full[...])
    for copy in groups[1]:
        copy.wait()
    d_ffn_in = d_ffn_in + dot_nt(d_up[...], up_full[...])
    du, dg = norm_back(residual[...], gain_table[4:5, :], d_ffn_in)
    g_ffn[...] = dg
    d_residual = cotangent[...].astype(F32) + du
    d_residual_ref[...] = d_residual
    du, dg = norm_back(projected[...], gain_table[3:4, :], d_residual)
    g_attn[...] = dg
    d_proj = du.astype(BF16)
    rows, dim = d_proj.shape[0], d_att.shape[1]
    for copy in groups[2]:
        copy.wait()
    for h in range(heads):
        part = dot_nt(d_proj, out_full[h * dim : (h + 1) * dim, :]).astype(BF16)
        for b in range(rows // QBLOCK):
            start = (b * heads + h) * QBLOCK
            d_att[start : start + QBLOCK, :] = part[b * QBLOCK : (b + 1) * QBLOCK, :]
    block = att_t.shape[0] // (4 * fsdp)
    wide = keep.shape[3]
    parts = wide // LANES
    deep = block // parts
    for c, f, x, core, row, mid in relative_blocks(at, fsdp):
        start = multiple(((row * 2 + core) * 2 + mid) * block, 16)
        part = dot(att_t[pl.ds(start, block), :], d_proj).astype(BF16)
        target = keep if c == 0 else send
        target[f, x, :block, :] = part[:, :wide]
        for i in range(parts):
            target[f, x, block:, i * LANES : (i + 1) * LANES] = part[i * deep : (i + 1) * deep, wide:]


def attend_back_kernel(halo, heads, d_att, q_st, keys, values, probs, d_q, d_k, d_v, d_scores):
    rows = d_q.shape[0]
    dim = keys.shape[1]
    blocks = rows // QBLOCK
    span = WINDOW + QBLOCK
    scale = dim ** (-0.5)
    d_k[...] = jnp.zeros(d_k.shape, F32)
    d_v[...] = jnp.zeros(d_v.shape, F32)
    for b in range(blocks):
        first_key = halo - WINDOW + b * QBLOCK
        here = slice(first_key, first_key + span)
        for h in range(heads):
            start = (b * heads + h) * QBLOCK
            stack = slice(start, start + QBLOCK)
            d_probs = dot_nt(d_att[stack, :], values[here, :])
            p = probs[stack, :].astype(F32)
            row_terms = jnp.sum(p * d_probs, axis=-1, keepdims=True)
            ds = (p * (d_probs - row_terms) * scale).astype(BF16)
            d_scores[h * QBLOCK : (h + 1) * QBLOCK, :] = ds
            d_q[b * QBLOCK : (b + 1) * QBLOCK, h * dim : (h + 1) * dim] = dot(ds, keys[here, :])
        stack = slice(b * heads * QBLOCK, (b + 1) * heads * QBLOCK)
        d_k[here, :] += dot_tn(d_scores[...], q_st[stack, :])
        d_v[here, :] += dot_tn(probs[stack, :], d_att[stack, :])


def last_kernel(n_qkv, n_tok, fsdp, heads, *refs):
    (
        at, d_residual, d_q, d_k, d_v,
        q_raw, k_raw, cosine, sine, gain_table, normed, g_ffn, g_attn, g_out,
    ) = refs[:14]
    toks = refs[14 : 14 + n_tok]
    refs = refs[14 + n_tok :]
    qkv_w, refs = refs[:n_qkv], refs[n_qkv:]
    grad_tokens, d_halo, keep, send = refs[:4]
    w_full, normed_t, d_qkv, gain_rows, qkv_sems = refs[4:]
    copies = place_copies(qkv_w[:3], qkv_w[3:], w_full, qkv_sems, at, 1, 4)
    for copy in copies:
        copy.start()
    normed_t[...] = normed[...].T
    rows = toks[0].shape[0]
    halo = (n_tok - 1) * rows
    dim = k_raw.shape[1]
    gain_in, gain_q, gain_k = gain_table[0:1, :], gain_table[1:2, :dim], gain_table[2:3, :dim]
    half = dim // 2
    tall, wide = normed_t.shape[0] // fsdp, keep.shape[3]
    def turned_back(u, g, dz, cos, sin):
        first, second = dz[:, :half], dz[:, half:]
        dz = jnp.concatenate([first * cos + second * sin, second * cos - first * sin], axis=1)
        return norm_back(u, g, dz)

    total_q = jnp.zeros((1, dim), F32)
    if halo:
        d_qkv[:halo, : heads * dim] = jnp.zeros((halo, heads * dim), BF16)
    for h in range(heads):
        cut = slice(h * dim, (h + 1) * dim)
        du, dg = turned_back(q_raw[:, cut], gain_q, d_q[:, cut], cosine[halo:, :], sine[halo:, :])
        total_q += dg
        d_qkv[halo:, cut] = du.astype(BF16)
    total_k = jnp.zeros((1, dim), F32)
    for i in range(n_tok):
        here = slice(i * rows, (i + 1) * rows)
        du, dg = turned_back(k_raw[here, :], gain_k, d_k[here, :], cosine[here, :], sine[here, :])
        total_k += dg
        d_qkv[here, heads * dim : (heads + 1) * dim] = du.astype(BF16)
        d_qkv[here, (heads + 1) * dim :] = d_v[here, :].astype(BF16)
    column_blocks(at, fsdp, normed_t, d_qkv, keep, send)
    for copy in copies:
        copy.wait()
    total_in = jnp.zeros(gain_in.shape, F32)
    for i in range(n_tok):
        here = slice(i * rows, (i + 1) * rows)
        if i < n_tok - 1:
            d_normed = dot_nt(d_qkv[here, heads * dim :], w_full[:, heads * dim :])
        else:
            d_normed = dot_nt(d_qkv[here, :], w_full[...])
        du, dg = norm_back(toks[i][...].astype(F32), gain_in, d_normed)
        total_in += dg
        if i < n_tok - 1:
            d_halo[here, :] = du.astype(BF16)
        else:
            grad_tokens[...] = d_residual[...] + du
    gain_rows[...] = jnp.zeros(gain_rows.shape, F32)
    at_row = 0
    for total in (total_in, total_q, total_k, g_attn[...], g_ffn[...], g_out[...]):
        for i in range(total.shape[1] // LANES):
            gain_rows[at_row : at_row + 1, :LANES] = total[:, i * LANES : (i + 1) * LANES]
            at_row += 1
    packed = gain_rows[...].astype(BF16)
    for target in (keep, send):
        for f in range(fsdp):
            for x in range(2):
                target[f, x, tall:, :] = packed


def add(*terms):
    out = terms[0].astype(F32)
    for term in terms[1:]:
        out = out + term.astype(F32)
    return out


class Chunk:
    def __init__(self, here, keep, send):
        self.here, self.keep = here, keep
        self.other = here.core_swap(send)

    def over_fsdp(self, *earlier):
        here = self.here
        parts = [add(self.keep[by], self.other[by]).astype(BF16) for by in range(1, here.fsdp)]
        self.arrived = [here.fsdp_shift(after(part, *earlier), by + 1) for by, part in enumerate(parts)]

    def over_mid(self, *earlier):
        self.arrived = [after(a, *earlier) for a in self.arrived]
        terms = [self.keep[0, 1], self.other[0, 1]] + [a[1] for a in self.arrived]
        self.across = self.here.mid_swap(add(*terms).astype(BF16))
        self.mine = [self.keep[0, 0], self.other[0, 0]] + [a[0] for a in self.arrived]
        return self.arrived[0] if self.arrived else self.other

    def join(self, below, *earlier):
        for chunk in (self, below):
            chunk.arrived = [after(a, *earlier) for a in chunk.arrived]
        pairs = [
            [[c.keep[0, x], c.other[0, x]] + [a[x] for a in c.arrived] for c in (self, below)] for x in range(2)
        ]
        self.across_sent = jnp.concatenate([add(*terms).astype(BF16) for terms in pairs[1]])
        self.across = self.here.mid_swap(self.across_sent)
        self.mine = [jnp.concatenate([add(*terms).astype(BF16) for terms in pairs[0]])]

    def outer_sums(self, *earlier):
        here = self.here
        self.across = after(self.across, *earlier)
        mine = add(*self.mine, self.across).astype(BF16)
        n, w = mine.shape
        mine = mine.reshape(here.outer, n // here.outer, w)
        self.shares = [pick(mine, here.outer_ahead[0])]
        for by in range(1, here.outer):
            self.shares.append(here.outer_shift(pick(mine, here.outer_ahead[by]), by))
        return self.across

    def outer_gather(self, *earlier):
        here = self.here
        self.shares = list(after(tuple(self.shares), *earlier))
        own = add(*self.shares).astype(BF16)
        self.gathered = [own] + [here.outer_shift(own, by) for by in range(1, here.outer)]
        return self.shares[-1]

    def mid_gather(self, *earlier):
        here = self.here
        self.gathered = list(after(tuple(self.gathered), *earlier))
        block = ordered(self.gathered, here.outer_behind)
        block = block.reshape(-1, block.shape[-1])
        across = here.mid_swap(block)
        self.blocks = [[block, across], [here.core_swap(block), here.core_swap(across)]]
        return self.gathered[-1]


def by_place(here, blocks):
    own = [jnp.where(here.mid_at == 0, a, b) for a, b in blocks]
    other = [jnp.where(here.mid_at == 0, b, a) for a, b in blocks]
    pairs = list(zip(own, other))
    first = [jnp.where(here.core_at == 0, a, b) for a, b in zip(pairs[0], pairs[1])]
    second = [jnp.where(here.core_at == 0, b, a) for a, b in zip(pairs[0], pairs[1])]
    return first + second


def last_columns(blocks, start, count):
    wide = blocks[0].shape[1]
    pieces = []
    for i, block in enumerate(blocks):
        low, high = max(start - i * wide, 0), min(start + count - i * wide, wide)
        if low < high:
            pieces.append(block[:, low:high])
    return jnp.concatenate(pieces, axis=1).astype(F32)


def on_device(
    tokens, positions, cotangent, in_gain, w_query, w_key, w_value, query_gain, key_gain, w_out, attn_gain,
    ffn_gain_in, w_gate, w_up, w_down, ffn_gain_out,
):
    here = Places()
    fsdp = here.fsdp
    rows, width = tokens.shape
    dim = w_key.shape[1]
    query_cols = w_query.shape[1]
    heads = query_cols // dim
    hidden = w_gate.shape[1]
    hops = (WINDOW + rows - 1) // rows
    n_tok = hops + 1
    halo = hops * rows
    every = halo + rows
    at = here.vector

    gains = (in_gain, query_gain, key_gain, attn_gain, ffn_gain_in, ffn_gain_out)
    cuts = [0]
    for gain in gains:
        cuts.append(cuts[-1] + gain.shape[0])
    gain_row = jnp.concatenate(gains)
    gain_rows = ordered([gain_row] + [here.fsdp_shift(gain_row, by) for by in range(1, fsdp)], here.fsdp_behind)
    gain_rows = gain_rows.astype(F32)
    gain_table = jnp.concatenate(
        [
            jnp.pad(gain_rows[:, cuts[i] : cuts[i + 1]].reshape(1, -1), ((0, 0), (0, width - fsdp * gains[i].shape[0])))
            for i in range(6)
        ]
        + [jnp.zeros((2, width), F32)],
        axis=0,
    )
    qkv_w = [w_query, w_key, w_value]
    qkv_part = own_part(here, qkv_w, 1, 4)
    tokens_out = after(tokens, qkv_part)
    toks = [linear_shift(tokens_out, by) for by in range(hops, 0, -1)] + [tokens]
    qkv_w += on_chips(here, over_links(here, qkv_part), 4)
    out_arrived = over_links(here, after(own_part(here, [w_out], 0, 2), *toks[:-1]))
    gate_arrived = over_links(here, after(own_part(here, [w_gate], 1, 4), qkv_w[3]))
    up_arrived = over_links(here, after(own_part(here, [w_up], 1, 2), *gate_arrived))
    down_arrived = over_links(here, after(own_part(here, [w_down], 0, 2), *gate_arrived))

    all_positions = jnp.concatenate([positions[0] - halo + jnp.arange(halo, dtype=jnp.int32), positions])
    frequency = ROPE_BASE ** (-(jnp.arange(dim // 2, dtype=F32) * 2.0 / dim))
    angles = all_positions.astype(F32)[:, None] * frequency[None, :]
    cosine, sine = jnp.cos(angles), jnp.sin(angles)

    span = WINDOW + QBLOCK
    weight_bytes = 2 * fsdp * w_gate.size
    normed, q_raw, k_raw, q_st, keys, values, probs, attended = pl.pallas_call(
        functools.partial(attend_kernel, n_tok, len(qkv_w), heads),
        out_shape=(
            shape((every, width), BF16),
            shape((rows, query_cols), F32),
            shape((every, dim), F32),
            shape((heads * rows, dim), BF16),
            shape((every, dim), BF16),
            shape((every, dim), BF16),
            shape((heads * rows, span), BF16),
            shape((rows, query_cols), BF16),
        ),
        in_specs=[SMEM] + [VMEM] * (n_tok + 4) + [ANY] * len(qkv_w),
        out_specs=(VMEM,) * 8,
        scratch_shapes=[
            pltpu.VMEM((width, query_cols + 2 * dim), BF16),
            pltpu.SemaphoreType.DMA((len(qkv_w),)),
        ],
        compiler_params=params(),
        cost_estimate=cost(4e9, 1e7),
        name="attend",
    )(at, *toks, after(positions[:, None], *gate_arrived), cosine, sine, gain_table, *qkv_w)

    out_w = [w_out] + on_chips(here, [after(a, attended) for a in out_arrived], 2)
    gate_w = [w_gate] + on_chips(here, gate_arrived, 4)
    up_w = [w_up] + on_chips(here, [after(a, attended) for a in up_arrived], 2)
    projected, residual, ffn_in, mixed, gelu_out, gate_slope = pl.pallas_call(
        functools.partial(gate_kernel, len(out_w), len(gate_w), len(up_w)),
        out_shape=(
            shape((rows, width), F32),
            shape((rows, width), F32),
            shape((rows, width), BF16),
            shape((rows, hidden), BF16),
            shape((rows, hidden), BF16),
            shape((rows, hidden), BF16),
        ),
        in_specs=[SMEM] + [VMEM] * 3 + [ANY] * (len(out_w) + len(gate_w) + len(up_w)),
        out_specs=(ANY, ANY, VMEM, ANY, ANY, ANY),
        scratch_shapes=[
            pltpu.VMEM((rows, width), F32),
            pltpu.VMEM((rows, width), F32),
            pltpu.VMEM((rows, hidden), BF16),
            pltpu.VMEM((rows, hidden), BF16),
            pltpu.VMEM((rows, hidden), BF16),
            pltpu.VMEM((query_cols, width), BF16),
            pltpu.VMEM((width, hidden), BF16),
            pltpu.VMEM((width, hidden), BF16),
            pltpu.SemaphoreType.DMA((len(out_w),)),
            pltpu.SemaphoreType.DMA((len(gate_w),)),
            pltpu.SemaphoreType.DMA((len(up_w),)),
            pltpu.SemaphoreType.DMA((14,)),
        ],
        compiler_params=params(),
        cost_estimate=cost(1e6, 1e3),
        name="gate",
    )(at, attended, tokens, gain_table, *out_w, *gate_w, *up_w)

    down_w = [w_down] + on_chips(here, [after(a, mixed) for a in down_arrived], 2)
    down_block = w_down.shape[0] // 4
    down_shape = shape((fsdp, 2, down_block, width), BF16)
    layer_out, d_down, g_ffn_out, down_keep, down_send = pl.pallas_call(
        functools.partial(down_kernel, len(down_w), fsdp),
        out_shape=(
            shape((rows, width), BF16),
            shape((rows, width), BF16),
            shape((1, width), F32),
            down_shape,
            down_shape,
        ),
        in_specs=[SMEM] + [VMEM] * 4 + [ANY] * len(down_w),
        out_specs=(VMEM,) * 5,
        scratch_shapes=[
            pltpu.VMEM((hidden, width), BF16),
            pltpu.VMEM((hidden, rows), BF16),
            pltpu.SemaphoreType.DMA((len(down_w),)),
        ],
        compiler_params=params(),
        cost_estimate=cost(4e9, 2 * weight_bytes),
        name="down",
    )(at, mixed, residual, cotangent, gain_table, *down_w)

    down_sum = Chunk(here, down_keep, down_send)
    gate_shape = shape((fsdp, 2, w_gate.shape[0], hidden // 4), BF16)
    d_gate, d_up, gate_keep, gate_send, up_keep, up_send = pl.pallas_call(
        functools.partial(gate_back_kernel, len(down_w), fsdp),
        out_shape=(
            shape((rows, hidden), BF16),
            shape((rows, hidden), BF16),
            gate_shape,
            gate_shape,
            gate_shape,
            gate_shape,
        ),
        in_specs=[SMEM] + [VMEM] * 4 + [ANY] * len(down_w),
        out_specs=(VMEM,) * 6,
        scratch_shapes=[
            pltpu.VMEM((hidden, width), BF16),
            pltpu.VMEM((width, rows), BF16),
            pltpu.SemaphoreType.DMA((len(down_w),)),
        ],
        compiler_params=params(),
        cost_estimate=cost(6e9, 3 * weight_bytes),
        name="gate_back",
    )(at, d_down, gelu_out, gate_slope, ffn_in, *down_w)
    gate_sum = Chunk(here, gate_keep, gate_send)
    up_sum = Chunk(here, up_keep, up_send)
    down_sum.over_fsdp(d_gate)
    d_gate = after(d_gate, down_sum.other)
    qkv_cols = query_cols + 2 * dim
    last_wide = qkv_cols // 4
    shard_rows = w_query.shape[0]
    last_shape = shape((fsdp, 2, shard_rows + GAIN_ROWS, last_wide), BF16)
    out_block = w_out.shape[0] // 4
    out_shape = shape((fsdp, 2, out_block * width // (hidden // 4), hidden // 4), BF16)
    d_residual, g_ffn, g_attn, d_att, out_keep, out_send = pl.pallas_call(
        functools.partial(middle_kernel, len(out_w), len(gate_w), len(up_w), fsdp, heads),
        out_shape=(
            shape((rows, width), F32),
            shape((1, width), F32),
            shape((1, width), F32),
            shape((heads * rows, dim), BF16),
            out_shape,
            out_shape,
        ),
        in_specs=[SMEM] + [VMEM] * 7 + [ANY] * (len(out_w) + len(gate_w) + len(up_w)),
        out_specs=(VMEM,) * 6,
        scratch_shapes=[
            pltpu.VMEM((query_cols, width), BF16),
            pltpu.VMEM((width, hidden), BF16),
            pltpu.VMEM((width, hidden), BF16),
            pltpu.VMEM((query_cols, rows), BF16),
            pltpu.SemaphoreType.DMA((len(out_w),)),
            pltpu.SemaphoreType.DMA((len(gate_w),)),
            pltpu.SemaphoreType.DMA((len(up_w),)),
        ],
        compiler_params=params(),
        cost_estimate=cost(6e9, 4 * weight_bytes),
        name="middle",
    )(at, d_gate, d_up, residual, projected, cotangent, gain_table, attended, *out_w, *gate_w, *up_w)

    out_sum = Chunk(here, out_keep, out_send)
    gate_sum.over_fsdp(g_ffn)
    up_sum.over_fsdp(g_ffn)
    down_sum.over_mid(g_ffn)
    d_q, d_k, d_v = pl.pallas_call(
        functools.partial(attend_back_kernel, halo, heads),
        out_shape=(shape((rows, query_cols), F32), shape((every, dim), F32), shape((every, dim), F32)),
        in_specs=[VMEM] * 5,
        out_specs=(VMEM,) * 3,
        scratch_shapes=[pltpu.VMEM((heads * QBLOCK, span), BF16)],
        compiler_params=params(),
        cost_estimate=cost(6e9, 3 * weight_bytes),
        name="attend_back",
    )(after(d_att, gate_sum.other, up_sum.other, *down_sum.arrived), q_st, keys, values, probs)
    out_sum.over_fsdp(d_k)
    down_sum.outer_sums(d_k)
    d_q = after(d_q, out_sum.other, down_sum.across)
    grad_tokens, d_halo, last_keep, last_send = pl.pallas_call(
        functools.partial(last_kernel, len(qkv_w), n_tok, fsdp, heads),
        out_shape=(
            shape((rows, width), F32),
            shape((halo, width), BF16),
            last_shape,
            last_shape,
        ),
        in_specs=[SMEM] + [VMEM] * (13 + n_tok) + [ANY] * len(qkv_w),
        out_specs=(VMEM,) * 4,
        scratch_shapes=[
            pltpu.VMEM((width, qkv_cols), BF16),
            pltpu.VMEM((width, every), BF16),
            pltpu.VMEM((every, qkv_cols), BF16),
            pltpu.VMEM((GAIN_ROWS, last_wide), F32),
            pltpu.SemaphoreType.DMA((len(qkv_w),)),
        ],
        compiler_params=params(),
        cost_estimate=cost(15e9, 4 * weight_bytes),
        name="last",
    )(
        at, d_residual, d_q, d_k, d_v,
        q_raw, k_raw, cosine, sine, gain_table, normed, g_ffn, g_attn, g_ffn_out, *toks, *qkv_w,
    )

    last_sum = Chunk(here, last_keep, last_send)
    down_sum.outer_sums(last_keep)
    gate_sum.over_mid(last_keep, *up_sum.arrived)
    (last_sum.other,), (gate_sum.across,), down_sum.shares, out_sum.arrived = together(
        (last_sum.other,), (gate_sum.across,), down_sum.shares, out_sum.arrived
    )
    last_sum.over_fsdp()
    up_sum.join(out_sum)
    gate_sum.outer_sums()
    down_sum.outer_gather()
    last_sum.arrived, (up_sum.across,), gate_sum.shares, down_sum.gathered = together(
        last_sum.arrived, (up_sum.across,), gate_sum.shares, down_sum.gathered
    )
    last_sum.over_mid()
    up_sum.outer_sums()
    gate_sum.outer_gather()
    down_sum.mid_gather()
    (last_sum.across,), up_sum.shares, gate_sum.gathered, down_last = together(
        (last_sum.across,), up_sum.shares, gate_sum.gathered, down_sum.blocks[0]
    )
    down_sum.blocks[0] = list(down_last)
    last_sum.outer_sums()
    up_sum.outer_gather()
    gate_sum.mid_gather()
    last_sum.shares, up_sum.gathered, gate_last = together(last_sum.shares, up_sum.gathered, gate_sum.blocks[0])
    gate_sum.blocks[0] = list(gate_last)
    last_sum.outer_gather()
    up_sum.mid_gather()
    last_sum.mid_gather(up_sum.blocks[0][1])
    d_halo = after(d_halo, up_sum.blocks[0][1])
    halos = [linear_shift(d_halo[halo - by * rows :][:rows], -by) for by in range(1, hops + 1)]
    down_blocks, gate_blocks = by_place(here, down_sum.blocks), by_place(here, gate_sum.blocks)
    both_blocks, last_blocks = by_place(here, up_sum.blocks), by_place(here, last_sum.blocks)
    total_gains = last_sum.blocks[0][0][shard_rows:, :LANES].astype(F32)

    for came in halos:
        grad_tokens = grad_tokens + came.astype(F32)

    total_down = jnp.concatenate(down_blocks, axis=0).astype(F32)
    total_gate = jnp.concatenate(gate_blocks, axis=1).astype(F32)
    total_up = jnp.concatenate([b[:shard_rows] for b in both_blocks], axis=1).astype(F32)
    last_blocks = [b[:shard_rows] for b in last_blocks]
    total_qkv = [last_columns(last_blocks, 0, query_cols)]
    total_qkv += [last_columns(last_blocks, query_cols + i * dim, dim) for i in range(2)]
    wide = hidden // 4
    parts = wide // LANES
    total_out = []
    for block in both_blocks:
        below = block[shard_rows + out_block :].reshape(out_block // parts, parts, LANES)
        below = below.transpose(1, 0, 2).reshape(out_block, LANES)
        total_out.append(jnp.concatenate([block[shard_rows : shard_rows + out_block], below], axis=1))
    total_out = jnp.concatenate(total_out, axis=0).astype(F32)
    g, start = [], 0
    flat = total_gains.reshape(-1)
    for gain in gains:
        size = gain.shape[0]
        g.append(lax.dynamic_slice_in_dim(flat, start + here.fsdp_at * size, size, 0, allow_negative_indices=False))
        start += fsdp * size
    return (
        layer_out, grad_tokens, g[0],
        *total_qkv,
        g[1], g[2], total_out, g[3], g[4], total_gate, total_up, total_down, g[5],
    )


def solution(mesh):
    tok = P(("seq", "fsdp"), None)
    mat = P("fsdp", None)
    vec = P("fsdp")
    return jax.shard_map(
        on_device,
        mesh=mesh,
        in_specs=(tok, P(("seq", "fsdp")), tok, vec, mat, mat, mat, vec, vec, mat, vec, vec, mat, mat, mat, vec),
        out_specs=(tok, tok, vec, mat, mat, mat, vec, vec, mat, vec, vec, mat, mat, mat, vec),
        check_vma=False,
    )
```
